32 devices in a mesh: row: 4 (over z), col: 8 (over y, x, core).
Axes of the slice: x: 2, y: 2, z: 4, core: 2. Of those that a mesh axis runs over, the one named last changes fastest.
Arguments:
- val_wave: bfloat16 [8, 64, 64, 128], replicated, may hold values from -6 to 6
- cond_wave: bfloat16 [32, 64, 64, 128], P(('row', 'col')), may hold values from -6 to 6
- val_energy: float32 [8], replicated, may hold values from -12 to -0.5
- cond_energy: float32 [32], replicated, may hold values from 0.5 to 20
- band_owner: int32 [32], P(('row', 'col')), may hold values from 0 to 31, each once
- grid_map: int32 [30720], replicated, may hold values from 0 to 262143, as said below
Outputs:
- chi: float32 [2, 1024, 30720], P(None, 'row', 'col')
The draws below stay inside these ranges and needn't reach their ends.
Inputs may be any that keep to these rules, and one draw needn't show every extreme that they name: `band_owner`: every one of the 32 band numbers stands in exactly one slot. `grid_map`: 30720 distinct flat grid points: those of the shortest wave vectors, with indices above 32 read as negative frequencies, ordered by length with ties in random order.
All inputs are finite; a program needn't handle non-finite values.
Results may differ from the reference program's by a relative error of at most 0.0041.
Values may be sent and summed in bfloat16 or wider, within the bound.
No kernel may reach another device: no remote copies, remote signals or barrier semaphores. Data moves between devices by JAX's collectives and lax.ppermute only.
A program may use at most 576 MiB of HBM per device.

```python
import jax
import jax.numpy as jnp
from jax import lax

GRID = 64
NG = 30720
NV = 8
NC = 32
PAIRS = 256
SLAB = 1024


def signed_freq(index):
    return jnp.where(index < GRID // 2, index, index - GRID)


def draw_grid_map(key, part):
    points = jnp.arange(GRID * GRID * GRID, dtype=jnp.int32)
    first = signed_freq(points // (GRID * GRID))
    second = signed_freq(points // GRID % GRID)
    third = signed_freq(points % GRID)
    length = first * first + second * second + third * third
    shuffle = jax.random.permutation(key, GRID * GRID * GRID).astype(jnp.int32)
    scores = length * (GRID * GRID * GRID) + shuffle
    ranked, chosen = lax.top_k(-scores, NG)
    return chosen.astype(jnp.int32)


def shard_levels(rng, shape, shards, least, top_value):
    factor_of, own = 1.0, jax.random.fold_in(rng, 6)
    for dim, blocks in shards:
        steps = jnp.exp(jax.random.uniform(jax.random.fold_in(own, dim), (blocks,), jnp.float32, least / len(shards), top_value / len(shards)))
        factor_of = factor_of * jnp.repeat(steps, shape[dim] // blocks).reshape([-1 if axis == dim else 1 for axis in range(len(shape))])
    return factor_of


def centred(stream_key, shape, width, limit, shards=(), held_as=jnp.bfloat16):
    drawn = jax.random.normal(stream_key, shape, jnp.float32) * width
    if len(shards) > 0:
        drawn = shard_levels(stream_key, shape, shards, -0.22, 0.18) * drawn
    return jnp.clip(drawn, min=-limit, max=limit).astype(held_as)


def setup_inputs(seed: int = 0) -> dict:
    streams_of = jax.random.split(jax.random.key(seed), 7)
    val_wave = centred(streams_of[0], (NV, GRID, GRID, 2 * GRID), 1.0, 6.0)
    cond_wave = centred(streams_of[1], (NC, GRID, GRID, 2 * GRID), 1.0, 6.0, ((0, 32),))
    val_energy = jnp.clip(jax.random.uniform(streams_of[2], (NV,), jnp.float32, -12.0, -0.5), -12.0, -0.5)
    cond_energy = jnp.clip(jax.random.uniform(streams_of[3], (NC,), jnp.float32, 0.5, 20.0), 0.5, 20.0)
    band_owner = jax.random.permutation(streams_of[4], NC).astype(jnp.int32)
    grid_map = draw_grid_map(jax.random.fold_in(streams_of[6], 71), 0)
    return dict(val_wave=val_wave, cond_wave=cond_wave, val_energy=val_energy, cond_energy=cond_energy, band_owner=band_owner, grid_map=grid_map)


def reference(val_wave, cond_wave, val_energy, cond_energy, band_owner, grid_map):
    valence = val_wave.astype(jnp.float32)
    valence_re = valence[..., :GRID]
    valence_im = valence[..., GRID:]
    band_numbers = jnp.arange(NC, dtype=jnp.int32)
    scaling = 1.0 / float(GRID) ** 1.5

    def one_band(operands):
        wave, number = operands
        conduction = wave.astype(jnp.float32)
        conduction_re = conduction[..., :GRID]
        conduction_im = conduction[..., GRID:]
        dens_re = valence_re * conduction_re[None] + valence_im * conduction_im[None]
        dens_im = valence_re * conduction_im[None] - valence_im * conduction_re[None]
        spectrum = jnp.fft.fftn(lax.complex(dens_re, dens_im), axes=(1, 2, 3))
        picked = spectrum.reshape(NV, GRID * GRID * GRID)[:, grid_map]
        pair_dens = jnp.stack([jnp.real(picked) * scaling, jnp.imag(picked) * scaling])
        energy = jnp.sum(jnp.where(number == band_numbers, cond_energy, 0.0))
        weight = -2.0 / (PAIRS ** 0.5 * (energy - val_energy))
        weighted = (weight[None, :, None] * pair_dens[:, :, :SLAB]).astype(jnp.bfloat16)
        plain = pair_dens.astype(jnp.bfloat16)
        return weighted, plain

    weighted, plain = lax.map(one_band, (cond_wave, band_owner))
    weighted = weighted.transpose(1, 0, 2, 3).reshape(2, PAIRS, SLAB).astype(jnp.float32)
    plain = plain.transpose(1, 0, 2, 3).reshape(2, PAIRS, NG).astype(jnp.float32)
    left_re = jnp.concatenate([weighted[0], weighted[1]], 0)
    left_im = jnp.concatenate([weighted[1], -weighted[0]], 0)
    right = jnp.concatenate([plain[0], plain[1]], 0)
    chi_re = jnp.dot(left_re.T, right, precision=lax.Precision.HIGHEST, preferred_element_type=jnp.float32)
    chi_im = jnp.dot(left_im.T, right, precision=lax.Precision.HIGHEST, preferred_element_type=jnp.float32)
    return jnp.stack([chi_re, chi_im])
```

```python
import math

import jax
import jax.numpy as jnp
import numpy as np
from jax import lax
from jax.experimental import pallas as pl
from jax.experimental.pallas import tpu as pltpu
from jax.sharding import PartitionSpec as P

ROWS_DEV = 256
LANES = 128
VMEM_BYTES = 56 * 1024 * 1024
HALF = 64
KEEP = 40
ROWS_K = 48
ORIGIN = KEEP // 2


def round_up(value, step):
    return -(-value // step) * step


def length_counts(points):
    freq = np.arange(points) - points // 2
    square = freq * freq
    lengths = square[:, None, None] + square[None, :, None] + square[None, None, :]
    return np.cumsum(np.bincount(lengths.reshape(-1)))


def column_order(top):
    freq = np.arange(KEEP) - ORIGIN
    first, second = np.meshgrid(freq, freq, indexing="ij")
    length = (first * first + second * second).reshape(-1)
    order = np.argsort(length, kind="stable")
    order = order[length[order] <= top]
    return first.reshape(-1)[order], second.reshape(-1)[order], length[order]


class Bucket:
    def __init__(self, low, high, column_length):
        self.pieces = []
        offset = 0
        for index in range(KEEP):
            freq = index - ORIGIN
            start = int(np.searchsorted(column_length, low - freq * freq, side="left"))
            stop = int(np.searchsorted(column_length, high - freq * freq, side="right"))
            if stop > start:
                self.pieces.append((index, start, stop, offset))
                offset += stop - start
        self.size = offset

    def ids(self, column_2, column_3, points, width):
        out = np.full((width,), -1, np.int32)
        for index, start, stop, offset in self.pieces:
            k1 = (index - ORIGIN) % points
            k2 = column_2[start:stop] % points
            k3 = column_3[start:stop] % points
            out[offset : offset + stop - start] = (k1 * points + k2) * points + k3
        return out


def make_plan(points, total, blocks, slab):
    cumulative = length_counts(points)
    width = total // blocks
    top = int(np.searchsorted(cumulative, total, side="left"))
    column_2, column_3, column_length = column_order(top)
    buckets = []
    for block in range(blocks):
        low = int(np.searchsorted(cumulative, block * width, side="right"))
        high = int(np.searchsorted(cumulative, (block + 1) * width, side="left"))
        buckets.append(Bucket(low, high, column_length))
    slab_top = int(np.searchsorted(cumulative, slab, side="left"))
    slab_bucket = Bucket(0, slab_top, column_length)
    slab_columns = int(np.searchsorted(column_length, slab_top, side="right"))
    slab_edge = math.isqrt(slab_top)
    block_lanes = round_up(max(bucket.size for bucket in buckets), LANES)
    slab_lanes = round_up(slab_bucket.size, LANES)
    return dict(
        buckets=buckets,
        slab_bucket=slab_bucket,
        slab_columns=slab_columns,
        slab_edge=slab_edge,
        block_lanes=block_lanes,
        slab_lanes=slab_lanes,
        block_ids=np.stack([b.ids(column_2, column_3, points, block_lanes) for b in buckets]),
        slab_ids=slab_bucket.ids(column_2, column_3, points, slab_lanes),
        column_place=((column_3 + ORIGIN) * KEEP + column_2 + ORIGIN).astype(np.int32),
    )


def dft_table(points):
    n = np.arange(points)
    freq = np.arange(KEEP) - ORIGIN
    angle = (n[:, None] * freq[None, :] % points) * (2.0 * np.pi / points)
    cosine, sine = np.cos(angle), np.sin(angle)
    table = np.zeros((2 * HALF, 2 * HALF))
    table[:points, :KEEP] = cosine
    table[HALF : HALF + points, :KEEP] = sine
    table[:points, HALF : HALF + KEEP] = -sine
    table[HALF : HALF + points, HALF : HALF + KEEP] = cosine
    high = table.astype(jnp.bfloat16)
    low = (table - high.astype(np.float64)).astype(jnp.bfloat16)
    return np.block([[high, low], [high, np.zeros_like(low)]])


def split_parts(value):
    high = value.astype(jnp.bfloat16)
    low = (value - high.astype(jnp.float32)).astype(jnp.bfloat16)
    return high, low


def apply_table(parts, table):
    both = jnp.dot(parts, table, preferred_element_type=jnp.float32)
    return both[:, :LANES] + both[:, LANES:]


def stack_complex(turned, low_lanes):
    real, imag = turned[:KEEP], turned[HALF : HALF + KEEP]
    first = jnp.where(low_lanes, real, pltpu.roll(imag, HALF, 1))
    second = jnp.where(low_lanes, pltpu.roll(real, HALF, 1), imag)
    return jnp.concatenate([first, second], 0)


def pack_pieces(pieces, width, source, rows, lane, out):
    for tile in range(width // LANES):
        left, right = tile * LANES, (tile + 1) * LANES
        value = jnp.zeros((rows, LANES), jnp.float32)
        for index, start, stop, offset in pieces:
            begin, end = max(left, offset), min(right, offset + stop - start)
            while begin < end:
                at = start + begin - offset
                here = min(end, begin + LANES - at % LANES)
                block = source(index, at // LANES)
                shift = (begin - at) % LANES
                if shift:
                    block = pltpu.roll(block, shift, 1)
                inside = (lane >= begin - left) & (lane < here - left)
                value = jnp.where(inside, block, value)
                begin = here
        out(tile, value)


def spectrum_kernel(plan, points, bands, weight_ref, val_ref, cond_ref, table_ref, place_ref, send_ref, slab_ref,
                    cond_a, cond_b, middle, turned, last, sorter, plain_rows, weighted_rows, plain_sorted, weighted_sorted):
    band = pl.program_id(0)
    planes = 8
    lane = lax.broadcasted_iota(jnp.int32, (1, LANES), 1)
    low_lanes = lane < HALF
    depth = last.shape[0]

    @pl.when(band == 0)
    def _():
        scale = 1.0 / float(points) ** 1.5
        sign = jnp.where(low_lanes, scale, -scale)

        @pl.loop(0, points)
        def _(n):
            rows = pl.ds(pl.multiple_of(n * points, points), points)
            wave = cond_ref[0, n].astype(jnp.float32)
            cond_a[rows, :] = wave * scale
            cond_b[rows, :] = pltpu.roll(wave, HALF, 1) * sign

        columns = sorter.shape[1]
        for begin in range(0, depth, LANES):
            at = lax.broadcasted_iota(jnp.int32, (LANES, columns), 0) + begin
            sorter[begin : begin + LANES, :] = jnp.where(at == place_ref[...], 1.0, 0.0).astype(jnp.bfloat16)
        last[KEEP * KEEP :, :] = jnp.zeros((depth - KEEP * KEEP, 2 * LANES), jnp.bfloat16)
        plain_rows[...] = jnp.zeros_like(plain_rows)
        weighted_rows[...] = jnp.zeros_like(weighted_rows)

    table = table_ref[...]

    @pl.loop(0, points // planes)
    def _(block):
        rows = pl.ds(pl.multiple_of(block * planes * points, planes * points), planes * points)
        wave = val_ref[0, pl.ds(block * planes, planes)].reshape(planes * points, LANES).astype(jnp.float32)
        other = pltpu.roll(wave, HALF, 1)
        density = jnp.where(low_lanes, wave, other) * cond_a[rows, :] + jnp.where(low_lanes, other, wave) * cond_b[rows, :]
        high, low = split_parts(density)
        field = apply_table(jnp.concatenate([high, low], 1), table)
        for pair in range(planes // 2):
            both = field[pair * 2 * points : (pair + 1) * 2 * points].T
            high, low = split_parts(stack_complex(both, low_lanes))
            at = pl.ds(pl.multiple_of((block * planes + pair * 2) * KEEP, 2 * KEEP), 2 * KEEP)
            middle[at, :LANES] = high
            middle[at, LANES:] = low

    step = 8 * KEEP

    @pl.loop(0, points // 8)
    def _(block):
        rows = pl.ds(pl.multiple_of(block * step, step), step)
        turned[rows, :] = apply_table(middle[rows, :], table)

    for pair in range(KEEP // 2):
        both = jnp.concatenate(
            [turned[pl.ds(2 * pair, points, stride=KEEP), :], turned[pl.ds(2 * pair + 1, points, stride=KEEP), :]], 0
        ).T
        high, low = split_parts(stack_complex(both, low_lanes))
        at = slice(2 * pair * KEEP, (2 * pair + 2) * KEEP)
        last[at, :LANES] = high
        last[at, LANES:] = low

    weight = weight_ref[band]
    slab_rows = weighted_rows.shape[1]
    slab_first = (ORIGIN - plan["slab_edge"]) * KEEP // LANES
    slab_last = slab_first + weighted_rows.shape[2] // LANES
    for tile in range(depth // LANES):
        rows = slice(tile * LANES, (tile + 1) * LANES)
        field = apply_table(last[rows, :], table).T
        for part in range(2):
            value = field[part * HALF : part * HALF + ROWS_K]
            at = part * bands + band
            plain_rows[at, :, rows] = value.astype(jnp.bfloat16)
            if slab_first <= tile < slab_last:
                lanes = slice((tile - slab_first) * LANES, (tile - slab_first + 1) * LANES)
                weighted_rows[at, :, lanes] = (weight * value).astype(jnp.bfloat16)

    @pl.when(band == bands - 1)
    def _():
        count = 2 * bands
        for begin in range(0, count, 4):
            block = plain_rows[begin : begin + 4].reshape(4 * ROWS_K, depth)
            value = jnp.dot(block, sorter[...], preferred_element_type=jnp.float32)
            for tile in range(plain_sorted.shape[0]):
                rows = slice(begin * ROWS_K, (begin + 4) * ROWS_K)
                plain_sorted[tile, rows, :] = value[:, tile * LANES : (tile + 1) * LANES]
            block = weighted_rows[begin : begin + 4].reshape(4 * slab_rows, weighted_rows.shape[2])
            value = jnp.dot(
                block,
                sorter[slab_first * LANES : slab_last * LANES, : weighted_sorted.shape[0] * LANES],
                preferred_element_type=jnp.float32,
            )
            for tile in range(weighted_sorted.shape[0]):
                rows = slice(begin * slab_rows, (begin + 4) * slab_rows)
                weighted_sorted[tile, rows, :] = value[:, tile * LANES : (tile + 1) * LANES]

        def plain_at(index, tile):
            return plain_sorted[tile, pl.ds(index, count, stride=ROWS_K), :]

        def weighted_at(index, tile):
            return weighted_sorted[tile, pl.ds(index, count, stride=slab_rows), :]

        for block, bucket in enumerate(plan["buckets"]):

            def keep(tile, value):
                send_ref[block, :, tile * LANES : (tile + 1) * LANES] = value.astype(jnp.bfloat16)

            pack_pieces(bucket.pieces, plan["block_lanes"], plain_at, count, lane, keep)

        def keep_slab(tile, value):
            slab_ref[:, tile * LANES : (tile + 1) * LANES] = value.astype(jnp.bfloat16)

        pack_pieces(plan["slab_bucket"].pieces, plan["slab_lanes"], weighted_at, count, lane, keep_slab)


def spectra(plan, val_wave, cond_wave, weight):
    bands, points = val_wave.shape[0], val_wave.shape[1]
    depth = round_up(KEEP * KEEP, LANES)
    columns = round_up(plan["column_place"].shape[0], 256)
    place = np.full((1, columns), -1, np.int32)
    place[0, : plan["column_place"].shape[0]] = plan["column_place"]
    edge = plan["slab_edge"]
    slab_first = (ORIGIN - edge) * KEEP // LANES
    slab_last = round_up((ORIGIN + edge + 1) * KEEP, LANES) // LANES
    slab_depth = (slab_last - slab_first) * LANES
    slab_columns = round_up(plan["slab_columns"], LANES)
    grid_rows = points * points
    kernel = lambda *refs: spectrum_kernel(plan, points, bands, *refs)
    return pl.pallas_call(
        kernel,
        grid=(bands,),
        in_specs=[
            pl.BlockSpec(memory_space=pltpu.SMEM),
            pl.BlockSpec((1, points, points, 2 * points), lambda v: (v, 0, 0, 0)),
            pl.BlockSpec((1, points, points, 2 * points), lambda v: (0, 0, 0, 0)),
            pl.BlockSpec((4 * HALF, 4 * HALF), lambda v: (0, 0)),
            pl.BlockSpec((1, columns), lambda v: (0, 0)),
        ],
        out_specs=[
            pl.BlockSpec((len(plan["buckets"]), 2 * bands, plan["block_lanes"]), lambda v: (0, 0, 0)),
            pl.BlockSpec((2 * bands, plan["slab_lanes"]), lambda v: (0, 0)),
        ],
        out_shape=[
            jax.ShapeDtypeStruct((len(plan["buckets"]), 2 * bands, plan["block_lanes"]), jnp.bfloat16),
            jax.ShapeDtypeStruct((2 * bands, plan["slab_lanes"]), jnp.bfloat16),
        ],
        scratch_shapes=[
            pltpu.VMEM((grid_rows, LANES), jnp.float32),
            pltpu.VMEM((grid_rows, LANES), jnp.float32),
            pltpu.VMEM((points * KEEP, 2 * LANES), jnp.bfloat16),
            pltpu.VMEM((points * KEEP, LANES), jnp.float32),
            pltpu.VMEM((depth, 2 * LANES), jnp.bfloat16),
            pltpu.VMEM((depth, columns), jnp.bfloat16),
            pltpu.VMEM((2 * bands, ROWS_K, depth), jnp.bfloat16),
            pltpu.VMEM((2 * bands, ROWS_K, slab_depth), jnp.bfloat16),
            pltpu.VMEM((columns // LANES, 2 * bands * ROWS_K, LANES), jnp.float32),
            pltpu.VMEM((slab_columns // LANES, 2 * bands * ROWS_K, LANES), jnp.float32),
        ],
        compiler_params=pltpu.CompilerParams(vmem_limit_bytes=VMEM_BYTES, dimension_semantics=("arbitrary",)),
    )(weight, val_wave, cond_wave, jnp.asarray(dft_table(points)), jnp.asarray(place))


def one_hot(ids_ref, wanted):
    blocks = []
    for begin in range(0, ids_ref.shape[1], LANES):
        ids = jnp.broadcast_to(ids_ref[:, begin : begin + LANES], (LANES, LANES)).T
        ids = jnp.concatenate([ids] * (wanted.shape[1] // LANES), 1)
        blocks.append(jnp.where(ids == wanted, 1.0, 0.0).astype(jnp.bfloat16))
    return jnp.concatenate(blocks, 0)


def product_kernel(bands, panels_ref, slab_ref, ids_ref, slab_ids_ref, wanted_ref, slab_wanted_ref, out_ref, left, hot):
    rows = slab_wanted_ref.shape[1]

    @pl.when(pl.program_id(0) == 0)
    def _():
        chosen = jnp.dot(
            slab_ref[...], one_hot(slab_ids_ref, slab_wanted_ref[...]), preferred_element_type=jnp.float32
        )
        parts = chosen.reshape(-1, 2, bands, rows)
        swapped = jnp.concatenate([parts[:, 1:], -parts[:, :1]], 1).reshape(chosen.shape)
        left[:rows, :] = chosen.T.astype(jnp.bfloat16)
        left[rows:, :] = swapped.T.astype(jnp.bfloat16)

    wanted = wanted_ref[...]
    for begin in range(0, ids_ref.shape[1], LANES):
        ids = jnp.broadcast_to(ids_ref[:, begin : begin + LANES], (LANES, LANES)).T
        ids = jnp.concatenate([ids] * (wanted.shape[1] // LANES), 1)
        hot[begin : begin + LANES, :] = jnp.where(ids == wanted, 1.0, 0.0).astype(jnp.bfloat16)
    panel = jnp.dot(panels_ref[...], hot[...], preferred_element_type=jnp.float32).astype(jnp.bfloat16)
    chi = jnp.dot(left[...], panel, preferred_element_type=jnp.float32)
    out_ref[0] = chi[:rows]
    out_ref[1] = chi[rows:]


def product(bands, panels, slab, ids, slab_ids, wanted, slab_wanted):
    columns = wanted.shape[1]
    rows = slab_wanted.shape[1]
    block = 768
    whole = lambda array: pl.BlockSpec(array.shape, lambda n: (0, 0))
    kernel = lambda *refs: product_kernel(bands, *refs)
    return pl.pallas_call(
        kernel,
        grid=(columns // block,),
        in_specs=[
            whole(panels),
            whole(slab),
            whole(ids),
            whole(slab_ids),
            pl.BlockSpec((1, block), lambda n: (0, n)),
            whole(slab_wanted),
        ],
        out_specs=pl.BlockSpec((2, rows, block), lambda n: (0, 0, n)),
        out_shape=jax.ShapeDtypeStruct((2, rows, columns), jnp.float32),
        scratch_shapes=[
            pltpu.VMEM((2 * rows, panels.shape[0]), jnp.bfloat16),
            pltpu.VMEM((panels.shape[1], block), jnp.bfloat16),
        ],
        compiler_params=pltpu.CompilerParams(vmem_limit_bytes=VMEM_BYTES, dimension_semantics=("arbitrary",)),
    )(panels, slab, ids, slab_ids, wanted, slab_wanted)


def on_device(val_wave, cond_wave, val_energy, cond_energy, band_owner, grid_map):
    bands, points = val_wave.shape[0], val_wave.shape[1]
    band_total = cond_energy.shape[0]
    row_count = lax.axis_size("row")
    col_count = lax.axis_size("col")
    plan = make_plan(points, grid_map.shape[0], col_count, ROWS_DEV * row_count)
    energy = jnp.sum(jnp.where(band_owner[0] == jnp.arange(band_total, dtype=jnp.int32), cond_energy, 0.0))
    weight = -2.0 / (math.sqrt(bands * band_total) * (energy - val_energy))
    send, slab = spectra(plan, val_wave, cond_wave, weight)
    slab = lax.all_gather(slab, ("row", "col"), axis=0, tiled=True)
    by_columns = lax.all_to_all(send, "col", split_axis=0, concat_axis=0, tiled=True)
    panels = lax.all_gather(by_columns, "row", axis=0, tiled=True)
    panels = panels.reshape(-1, plan["block_lanes"])
    width = grid_map.shape[0] // col_count
    col, row = lax.axis_index("col"), lax.axis_index("row")
    ids = lax.dynamic_slice(jnp.asarray(plan["block_ids"]), (col, 0), (1, plan["block_lanes"]))
    slab_ids = jnp.asarray(plan["slab_ids"])[None]
    wanted = lax.dynamic_slice(grid_map, (col * width,), (width,))[None]
    slab_wanted = lax.dynamic_slice(grid_map, (row * ROWS_DEV,), (ROWS_DEV,))[None]
    return product(bands, panels, slab, ids, slab_ids, wanted, slab_wanted)


def solution(mesh):
    in_specs = (P(), P(("row", "col"), None, None, None), P(), P(), P(("row", "col")), P())
    out_specs = P(None, "row", "col")
    return jax.shard_map(
        on_device, mesh=mesh, in_specs=in_specs, out_specs=out_specs, check_vma=False
    )
```

```python
import math

import jax
import jax.numpy as jnp
import numpy as np
from jax import lax
from jax.experimental import pallas as pl
from jax.experimental.pallas import tpu as pltpu
from jax.sharding import PartitionSpec as P

ROWS_DEV = 256
LANES = 128
VMEM_BYTES = 56 * 1024 * 1024
HALF = 64
KEEP = 40
ROWS_K = 48
ORIGIN = KEEP // 2
PARTS = 3
CHUNKS = 2


def round_up(value, step):
    return -(-value // step) * step


def length_counts(points):
    freq = np.arange(points) - points // 2
    square = freq * freq
    lengths = square[:, None, None] + square[None, :, None] + square[None, None, :]
    return np.cumsum(np.bincount(lengths.reshape(-1)))


def column_order(top):
    freq = np.arange(KEEP) - ORIGIN
    first, second = np.meshgrid(freq, freq, indexing="ij")
    length = (first * first + second * second).reshape(-1)
    order = np.argsort(length, kind="stable")
    order = order[length[order] <= top]
    return first.reshape(-1)[order], second.reshape(-1)[order], length[order]


class Bucket:
    def __init__(self, ranges, column_length):
        self.pieces = []
        self.edges = {}
        offset = 0
        for low, high in ranges:
            begin = offset
            for index in range(KEEP):
                freq = index - ORIGIN
                start = int(np.searchsorted(column_length, low - freq * freq, side="left"))
                stop = int(np.searchsorted(column_length, high - freq * freq, side="right"))
                if stop > start:
                    self.pieces.append((index, start, stop, offset))
                    offset += stop - start
            for length in range(low, high + 1):
                self.edges[length] = (begin, offset)
        self.size = offset

    def ids(self, column_2, column_3, points, width):
        out = np.full((width,), -1, np.int32)
        for index, start, stop, offset in self.pieces:
            k1 = (index - ORIGIN) % points
            k2 = column_2[start:stop] % points
            k3 = column_3[start:stop] % points
            out[offset : offset + stop - start] = (k1 * points + k2) * points + k3
        return out


def length_ranges(cumulative, first, step, count):
    shell = lambda rank: int(np.searchsorted(cumulative, rank, side="right"))
    ranges, low = [], shell(first)
    for part in range(1, count):
        before, after = shell(first + part * step - 1), shell(first + part * step)
        if before == after:
            if low < before:
                ranges.append((low, before - 1))
            if low <= before:
                ranges.append((before, before))
        elif low <= before:
            ranges.append((low, before))
        low = before + 1
    high = shell(first + count * step - 1)
    if low <= high:
        ranges.append((low, high))
    return ranges


def make_plan(points, total, blocks, slab, slab_blocks):
    cumulative = length_counts(points)
    shell = lambda rank: int(np.searchsorted(cumulative, rank, side="right"))
    width, slab_width = total // blocks, slab // slab_blocks
    step = width // PARTS
    column_2, column_3, column_length = column_order(shell(total - 1))
    buckets = [Bucket(length_ranges(cumulative, n * width, step, PARTS), column_length) for n in range(blocks)]
    slabs = [Bucket(length_ranges(cumulative, n * slab_width, slab_width, 1), column_length) for n in range(slab_blocks)]
    slab_top = shell(slab - 1)
    lanes = round_up(max(bucket.size for bucket in buckets), LANES)
    slab_lanes = round_up(max(bucket.size for bucket in slabs), LANES)
    windows = np.zeros((blocks, PARTS, 2), np.int64)
    for n, bucket in enumerate(buckets):
        for part in range(PARTS):
            rank = n * width + part * step
            windows[n, part, 0] = bucket.edges[shell(rank)][0] // LANES * LANES
            windows[n, part, 1] = round_up(bucket.edges[shell(rank + step - 1)][1], LANES)
    window = int((windows[..., 1] - windows[..., 0]).max())
    return dict(
        buckets=buckets,
        slabs=slabs,
        slab_columns=int(np.searchsorted(column_length, slab_top, side="right")),
        slab_edge=math.isqrt(slab_top),
        lanes=lanes,
        slab_lanes=slab_lanes,
        window=window,
        starts=np.minimum(windows[..., 0], lanes - window).astype(np.int32),
        ids=np.stack([bucket.ids(column_2, column_3, points, lanes) for bucket in buckets]),
        slab_ids=np.stack([bucket.ids(column_2, column_3, points, slab_lanes) for bucket in slabs]),
        column_place=((column_3 + ORIGIN) * KEEP + column_2 + ORIGIN).astype(np.int32),
    )


def dft_table(points):
    n = np.arange(points)
    freq = np.arange(KEEP) - ORIGIN
    angle = (n[:, None] * freq[None, :] % points) * (2.0 * np.pi / points)
    cosine, sine = np.cos(angle), np.sin(angle)
    table = np.zeros((2 * HALF, 2 * HALF))
    table[:points, :KEEP] = cosine
    table[HALF : HALF + points, :KEEP] = sine
    table[:points, HALF : HALF + KEEP] = -sine
    table[HALF : HALF + points, HALF : HALF + KEEP] = cosine
    high = table.astype(jnp.bfloat16)
    low = (table - high.astype(np.float64)).astype(jnp.bfloat16)
    return np.block([[high, low], [high, np.zeros_like(low)]])


def split_parts(value):
    high = value.astype(jnp.bfloat16)
    low = (value - high.astype(jnp.float32)).astype(jnp.bfloat16)
    return high, low


def apply_table(parts, table):
    both = jnp.dot(parts, table, preferred_element_type=jnp.float32)
    return both[:, :LANES] + both[:, LANES:]


def stack_complex(turned, low_lanes):
    real, imag = turned[:KEEP], turned[HALF : HALF + KEEP]
    first = jnp.where(low_lanes, real, pltpu.roll(imag, HALF, 1))
    second = jnp.where(low_lanes, pltpu.roll(real, HALF, 1), imag)
    return jnp.concatenate([first, second], 0)


def pack_pieces(pieces, width, source, rows, lane, out):
    for tile in range(width // LANES):
        left, right = tile * LANES, (tile + 1) * LANES
        value = jnp.zeros((rows, LANES), jnp.float32)
        for index, start, stop, offset in pieces:
            begin, end = max(left, offset), min(right, offset + stop - start)
            while begin < end:
                at = start + begin - offset
                block = source(index, at // LANES)
                shift = (begin - at) % LANES
                if shift:
                    block = pltpu.roll(block, shift, 1)
                value = block if begin == left else jnp.where(lane >= begin - left, block, value)
                begin = min(end, begin + LANES - at % LANES)
        out(tile, value)


def slab_tiles(plan):
    first = (ORIGIN - plan["slab_edge"]) * KEEP // LANES
    last = round_up((ORIGIN + plan["slab_edge"] + 1) * KEEP, LANES) // LANES
    return first, last


def spectrum_kernel(plan, points, first_band, weight_ref, val_ref, cond_ref, table_ref, plain_ref, weighted_ref,
                    cond_a, cond_b, middle, turned, last):
    band = pl.program_id(0)
    planes = 8
    lane = lax.broadcasted_iota(jnp.int32, (1, LANES), 1)
    low_lanes = lane < HALF
    depth = last.shape[0]

    @pl.when(band == 0)
    def _():
        scale = 1.0 / float(points) ** 1.5
        sign = jnp.where(low_lanes, scale, -scale)

        @pl.loop(0, points // planes)
        def _(block):
            rows = pl.ds(pl.multiple_of(block * planes * points, planes * points), planes * points)
            wave = cond_ref[0, pl.ds(block * planes, planes)].reshape(planes * points, LANES).astype(jnp.float32)
            cond_a[rows, :] = wave * scale
            cond_b[rows, :] = pltpu.roll(wave, HALF, 1) * sign

        last[KEEP * KEEP :, :] = jnp.zeros((depth - KEEP * KEEP, 2 * LANES), jnp.bfloat16)

    table = table_ref[...]
    step = planes * KEEP

    def first_axis(block):
        rows = pl.ds(pl.multiple_of(block * planes * points, planes * points), planes * points)
        wave = val_ref[0, pl.ds(block * planes, planes)].reshape(planes * points, LANES).astype(jnp.float32)
        other = pltpu.roll(wave, HALF, 1)
        density = jnp.where(low_lanes, wave, other) * cond_a[rows, :] + jnp.where(low_lanes, other, wave) * cond_b[rows, :]
        high, low = split_parts(density)
        field = apply_table(jnp.concatenate([high, low], 1), table)
        for pair in range(planes // 2):
            both = field[pair * 2 * points : (pair + 1) * 2 * points].T
            high, low = split_parts(stack_complex(both, low_lanes))
            at = pl.ds(pl.multiple_of((block * planes + pair * 2) * KEEP, 2 * KEEP), 2 * KEEP)
            middle[at, :LANES] = high
            middle[at, LANES:] = low

    def second_axis(block):
        rows = pl.ds(pl.multiple_of(block * step, step), step)
        turned[rows, :] = apply_table(middle[rows, :], table)

    first_axis(0)

    @pl.loop(1, points // planes)
    def _(block):
        second_axis(block - 1)
        first_axis(block)

    second_axis(points // planes - 1)

    for pair in range(KEEP // 2):
        both = jnp.concatenate(
            [turned[pl.ds(2 * pair, points, stride=KEEP), :], turned[pl.ds(2 * pair + 1, points, stride=KEEP), :]], 0
        ).T
        high, low = split_parts(stack_complex(both, low_lanes))
        at = slice(2 * pair * KEEP, (2 * pair + 2) * KEEP)
        last[at, :LANES] = high
        last[at, LANES:] = low

    weight = weight_ref[first_band + band]
    slab_first, slab_last = slab_tiles(plan)
    for begin in range(0, depth // LANES, 5):
        end = min(begin + 5, depth // LANES)
        field = apply_table(last[begin * LANES : end * LANES, :], table)
        for tile in range(begin, end):
            turn = field[(tile - begin) * LANES : (tile - begin + 1) * LANES].T
            for part in range(2):
                value = turn[part * HALF : part * HALF + ROWS_K]
                plain_ref[part, 0, :, tile * LANES : (tile + 1) * LANES] = value.astype(jnp.bfloat16)
                if slab_first <= tile < slab_last:
                    lanes = slice((tile - slab_first) * LANES, (tile - slab_first + 1) * LANES)
                    weighted_ref[part, 0, :, lanes] = (weight * value).astype(jnp.bfloat16)


def spectra(plan, val_wave, cond_wave, weight, first_band, count):
    points = val_wave.shape[1]
    depth = round_up(KEEP * KEEP, LANES)
    slab_first, slab_last = slab_tiles(plan)
    slab_depth = (slab_last - slab_first) * LANES
    grid_rows = points * points
    kernel = lambda *refs: spectrum_kernel(plan, points, first_band, *refs)
    return pl.pallas_call(
        kernel,
        grid=(count,),
        in_specs=[
            pl.BlockSpec(memory_space=pltpu.SMEM),
            pl.BlockSpec((1, points, points, 2 * points), lambda v: (first_band + v, 0, 0, 0)),
            pl.BlockSpec((1, points, points, 2 * points), lambda v: (0, 0, 0, 0)),
            pl.BlockSpec((4 * HALF, 4 * HALF), lambda v: (0, 0)),
        ],
        out_specs=[
            pl.BlockSpec((2, 1, ROWS_K, depth), lambda v: (0, v, 0, 0)),
            pl.BlockSpec((2, 1, ROWS_K, slab_depth), lambda v: (0, v, 0, 0)),
        ],
        out_shape=[
            jax.ShapeDtypeStruct((2, count, ROWS_K, depth), jnp.bfloat16),
            jax.ShapeDtypeStruct((2, count, ROWS_K, slab_depth), jnp.bfloat16),
        ],
        scratch_shapes=[
            pltpu.VMEM((grid_rows, LANES), jnp.float32),
            pltpu.VMEM((grid_rows, LANES), jnp.float32),
            pltpu.VMEM((points * KEEP, 2 * LANES), jnp.bfloat16),
            pltpu.VMEM((points * KEEP, LANES), jnp.float32),
            pltpu.VMEM((depth, 2 * LANES), jnp.bfloat16),
        ],
        compiler_params=pltpu.CompilerParams(vmem_limit_bytes=VMEM_BYTES, dimension_semantics=("arbitrary",)),
        cost_estimate=pl.CostEstimate(flops=count * 1200000000, bytes_accessed=count * 2000000, transcendentals=0),
        name="spectra",
    )(weight, val_wave, cond_wave, jnp.asarray(dft_table(points)))


def pack_kernel(plan, groups, col_ref, place_ref, *refs):
    plains, weighteds = refs[:groups], refs[groups : 2 * groups]
    slots = len(plan["buckets"])
    outs = refs[2 * groups : 2 * groups + slots]
    slab_ref, sorter, plain_sorted, weighted_sorted, blocks = refs[2 * groups + slots :]
    depth, columns = sorter.shape
    count = 2 * sum(plain.shape[1] for plain in plains)
    lane = lax.broadcasted_iota(jnp.int32, (1, LANES), 1)
    for begin in range(0, depth, LANES):
        at = lax.broadcasted_iota(jnp.int32, (LANES, columns), 0) + begin
        sorter[begin : begin + LANES, :] = jnp.where(at == place_ref[...], 1.0, 0.0).astype(jnp.bfloat16)

    def sort_rows(parts, which, target):
        rows = jnp.concatenate([part[n] for n in range(2) for part in parts], 0)
        rows = rows.reshape(count * ROWS_K, rows.shape[2])
        value = jnp.dot(rows, which, preferred_element_type=jnp.float32)
        for tile in range(target.shape[0]):
            target[tile] = value[:, tile * LANES : (tile + 1) * LANES]

    slab_first, slab_last = slab_tiles(plan)
    sort_rows(plains, sorter[...], plain_sorted)
    sort_rows(weighteds, sorter[slab_first * LANES : slab_last * LANES, : weighted_sorted.shape[0] * LANES], weighted_sorted)

    def plain_at(index, tile):
        return plain_sorted[tile, pl.ds(index, count, stride=ROWS_K), :]

    def weighted_at(index, tile):
        return weighted_sorted[tile, pl.ds(index, count, stride=ROWS_K), :]

    col = col_ref[0]
    for block, bucket in enumerate(plan["buckets"]):
        slot = jnp.bitwise_xor(col, block)

        def keep(tile, value):
            blocks[slot, :, tile * LANES : (tile + 1) * LANES] = value.astype(jnp.bfloat16)

        pack_pieces(bucket.pieces, plan["lanes"], plain_at, count, lane, keep)
    for slot, out in enumerate(outs):
        out[...] = blocks[slot]
    for block, bucket in enumerate(plan["slabs"]):

        def keep_slab(tile, value):
            slab_ref[block, :, tile * LANES : (tile + 1) * LANES] = value.astype(jnp.bfloat16)

        pack_pieces(bucket.pieces, plan["slab_lanes"], weighted_at, count, lane, keep_slab)


def packed(plan, col, plains, weighteds):
    depth = plains[0].shape[3]
    count = 2 * sum(plain.shape[1] for plain in plains)
    columns = round_up(plan["column_place"].shape[0], 256)
    slab_columns = round_up(plan["slab_columns"], LANES)
    place = np.full((1, columns), -1, np.int32)
    place[0, : plan["column_place"].shape[0]] = plan["column_place"]
    slots, lanes = len(plan["buckets"]), plan["lanes"]
    kernel = lambda *refs: pack_kernel(plan, len(plains), *refs)
    vmem = pl.BlockSpec(memory_space=pltpu.VMEM)
    slab_shape = (len(plan["slabs"]), count, plan["slab_lanes"])
    return pl.pallas_call(
        kernel,
        in_specs=[pl.BlockSpec(memory_space=pltpu.SMEM)] + [vmem] * (1 + 2 * len(plains)),
        out_specs=[vmem] * (slots + 1),
        out_shape=[jax.ShapeDtypeStruct((count, lanes), jnp.bfloat16)] * slots
        + [jax.ShapeDtypeStruct(slab_shape, jnp.bfloat16)],
        scratch_shapes=[
            pltpu.VMEM((depth, columns), jnp.bfloat16),
            pltpu.VMEM((columns // LANES, count * ROWS_K, LANES), jnp.float32),
            pltpu.VMEM((slab_columns // LANES, count * ROWS_K, LANES), jnp.float32),
            pltpu.VMEM((slots, count, lanes), jnp.bfloat16),
        ],
        compiler_params=pltpu.CompilerParams(vmem_limit_bytes=VMEM_BYTES),
        cost_estimate=pl.CostEstimate(flops=4000000000, bytes_accessed=4000000, transcendentals=0),
        name="pack",
    )(col, jnp.asarray(place), *plains, *weighteds)


def one_hot(ids_ref, begin, wanted):
    ids = jnp.broadcast_to(ids_ref[:, pl.ds(begin, LANES)], (LANES, LANES)).T
    ids = jnp.concatenate([ids] * (wanted.shape[1] // LANES), 1)
    return jnp.where(ids == wanted, 1.0, 0.0).astype(jnp.bfloat16)


def product_kernel(shape, place_ref, slab_ref, ids_ref, slab_ids_ref, wanted_ref, slab_wanted_ref, *refs):
    rounds, chunks, slots, group = shape
    panels = refs[: chunks * (2 * rounds - 1)]
    out_ref, panel, chosen_rows, left, hot = refs[chunks * (2 * rounds - 1) :]
    rows = slab_wanted_ref.shape[1]
    window = hot.shape[0]

    @pl.when(pl.program_id(0) == 0)
    def _():
        size = slots * group
        col = place_ref[0]
        for chunk in range(chunks):
            own, *others = panels[chunk * (2 * rounds - 1) : (chunk + 1) * (2 * rounds - 1)]
            for turn in range(rounds):
                base = (turn * chunks + chunk) * size
                if turn == 0:
                    panel[base : base + size, :] = own[...]
                else:
                    panel[base : base + size, :] = others[turn - 1][...] + others[2 * rounds - 2 - turn][...]
                for slot in range(slots):
                    chosen_rows[base + slot * group : base + (slot + 1) * group, :] = slab_ref[
                        jnp.bitwise_xor(col, slot), turn, chunk
                    ].astype(jnp.float32)
        choice = jnp.concatenate(
            [one_hot(slab_ids_ref, begin, slab_wanted_ref[...]) for begin in range(0, slab_ids_ref.shape[1], LANES)], 0
        )
        chosen = jnp.dot(chosen_rows[...].astype(jnp.bfloat16), choice, preferred_element_type=jnp.float32)
        lane = lax.broadcasted_iota(jnp.int32, (1, LANES), 1)
        real_lanes = lane % group < group // 2
        for begin in range(0, chosen.shape[0], LANES):
            turned = chosen[begin : begin + LANES].T
            after = pltpu.roll(turned, LANES - group // 2, 1)
            before = pltpu.roll(turned, group // 2, 1)
            left[:rows, begin : begin + LANES] = turned.astype(jnp.bfloat16)
            left[rows:, begin : begin + LANES] = jnp.where(real_lanes, after, -before).astype(jnp.bfloat16)

    start = pl.multiple_of(place_ref[1 + pl.program_id(0)], LANES)
    wanted = wanted_ref[...]
    for begin in range(0, window, LANES):
        hot[begin : begin + LANES, :] = one_hot(ids_ref, pl.multiple_of(start + begin, LANES), wanted)
    ordered = jnp.dot(panel[:, pl.ds(start, window)], hot[...], preferred_element_type=jnp.float32).astype(jnp.bfloat16)
    chi = jnp.dot(left[...], ordered, preferred_element_type=jnp.float32)
    out_ref[0] = chi[:rows]
    out_ref[1] = chi[rows:]


def product(plan, shape, place, slab, ids, slab_ids, wanted, slab_wanted, panels):
    rounds, chunks, slots, group = shape
    columns, rows, pairs = wanted.shape[1], slab_wanted.shape[1], rounds * chunks * slots * group
    block = columns // PARTS
    whole = lambda array: pl.BlockSpec(array.shape, lambda n: (0,) * array.ndim)
    kernel = lambda *refs: product_kernel(shape, *refs)
    return pl.pallas_call(
        kernel,
        grid=(PARTS,),
        in_specs=[
            pl.BlockSpec(memory_space=pltpu.SMEM),
            whole(slab),
            whole(ids),
            whole(slab_ids),
            pl.BlockSpec((1, block), lambda n: (0, n)),
            whole(slab_wanted),
        ]
        + [whole(panel) for panel in panels],
        out_specs=pl.BlockSpec((2, rows, block), lambda n: (0, 0, n)),
        out_shape=jax.ShapeDtypeStruct((2, rows, columns), jnp.float32),
        scratch_shapes=[
            pltpu.VMEM((pairs, plan["lanes"]), jnp.bfloat16),
            pltpu.VMEM((pairs, plan["slab_lanes"]), jnp.float32),
            pltpu.VMEM((2 * rows, pairs), jnp.bfloat16),
            pltpu.VMEM((plan["window"], block), jnp.bfloat16),
        ],
        compiler_params=pltpu.CompilerParams(vmem_limit_bytes=VMEM_BYTES, dimension_semantics=("arbitrary",)),
        cost_estimate=pl.CostEstimate(flops=12000000000, bytes_accessed=16000000, transcendentals=0),
        name="product",
    )(place, slab, ids, slab_ids, wanted, slab_wanted, *panels)


def shifted(value, axis, step):
    size = lax.axis_size(axis)
    return lax.ppermute(value, axis, [(n, n + step) for n in range(size) if 0 <= n + step < size])


def from_planes(own):
    size = lax.axis_size("row")
    further, back = [], []
    for step in range(1, size):
        if step < 3:
            further.append(shifted(own, "row", -step))
            back.append(shifted(own, "row", step))
        else:
            further.append(shifted(further[-1], "row", -1))
            back.append(shifted(back[-1], "row", 1))
    return further, back


def within_plane(blocks):
    size = lax.axis_size("col")
    parts = [blocks[0]]
    for slot in range(1, size):
        parts.append(lax.ppermute(blocks[slot], "col", [(n, n ^ slot) for n in range(size)]))
    return jnp.concatenate(parts, 0)


def slab_to_rows(slab):
    size = lax.axis_size("row")
    row = lax.axis_index("row")
    out = [lax.dynamic_index_in_dim(slab, row, 0, keepdims=False)]
    sent = {}
    for step in range(1 - size, size):
        if step:
            block = lax.dynamic_index_in_dim(slab, jnp.clip(row + step, 0, size - 1), 0, keepdims=False)
            sent[step] = shifted(block, "row", step)
    for turn in range(1, size):
        out.append(sent[-turn] + sent[size - turn])
    return jnp.stack(out)


def on_device(val_wave, cond_wave, val_energy, cond_energy, band_owner, grid_map):
    bands, points = val_wave.shape[0], val_wave.shape[1]
    band_total = cond_energy.shape[0]
    row_count = lax.axis_size("row")
    col_count = lax.axis_size("col")
    col, row = lax.axis_index("col"), lax.axis_index("row")
    plan = make_plan(points, grid_map.shape[0], col_count, ROWS_DEV * row_count, row_count)
    energy = jnp.sum(jnp.where(band_owner[0] == jnp.arange(band_total, dtype=jnp.int32), cond_energy, 0.0))
    weight = -2.0 / (math.sqrt(bands * band_total) * (energy - val_energy))
    chunk = bands // CHUNKS
    panels, slabs = [], []
    for part in range(CHUNKS):
        pieces = []
        split = 1 if part == 0 else 2
        for piece in range(split):
            count = chunk // split
            pieces.append(spectra(plan, val_wave, cond_wave, weight, part * chunk + piece * count, count))
        *blocks, slab = packed(plan, col[None], [p[0] for p in pieces], [p[1] for p in pieces])
        own = within_plane(blocks)
        further, back = from_planes(own)
        panels += [own] + further + back
        slabs.append(slab)
    slab = slab_to_rows(jnp.stack(slabs, 1))
    slab = lax.all_gather(slab, "col", axis=0)
    width = grid_map.shape[0] // col_count
    place = jnp.concatenate([col[None], lax.dynamic_index_in_dim(jnp.asarray(plan["starts"]), col, 0, keepdims=False)])
    ids = lax.dynamic_slice(jnp.asarray(plan["ids"]), (col, 0), (1, plan["lanes"]))
    slab_ids = lax.dynamic_slice(jnp.asarray(plan["slab_ids"]), (row, 0), (1, plan["slab_lanes"]))
    wanted = lax.dynamic_slice(grid_map, (col * width,), (width,))[None]
    slab_wanted = lax.dynamic_slice(grid_map, (row * ROWS_DEV,), (ROWS_DEV,))[None]
    shape = (row_count, CHUNKS, col_count, 2 * chunk)
    return product(plan, shape, place, slab, ids, slab_ids, wanted, slab_wanted, panels)


def solution(mesh):
    in_specs = (P(), P(("row", "col"), None, None, None), P(), P(), P(("row", "col")), P())
    out_specs = P(None, "row", "col")
    return jax.shard_map(
        on_device, mesh=mesh, in_specs=in_specs, out_specs=out_specs, check_vma=False
    )
```

```python
import math

import jax
import jax.numpy as jnp
import numpy as np
from jax import lax
from jax.experimental import pallas as pl
from jax.experimental.pallas import tpu as pltpu
from jax.sharding import PartitionSpec as P

ROWS_DEV = 256
LANES = 128
VMEM_BYTES = 56 * 1024 * 1024
HALF = 64
KEEP = 40
ROWS_K = 48
ORIGIN = KEEP // 2
PARTS = 3
CHUNKS = 2


def round_up(value, step):
    return -(-value // step) * step


def length_counts(points):
    freq = np.arange(points) - points // 2
    square = freq * freq
    lengths = square[:, None, None] + square[None, :, None] + square[None, None, :]
    return np.cumsum(np.bincount(lengths.reshape(-1)))


def column_order(top):
    freq = np.arange(KEEP) - ORIGIN
    first, second = np.meshgrid(freq, freq, indexing="ij")
    length = (first * first + second * second).reshape(-1)
    order = np.argsort(length, kind="stable")
    order = order[length[order] <= top]
    return first.reshape(-1)[order], second.reshape(-1)[order], length[order]


class Bucket:
    def __init__(self, ranges, column_length):
        self.pieces = []
        self.edges = {}
        offset = 0
        for low, high in ranges:
            begin = offset
            for index in range(KEEP):
                freq = index - ORIGIN
                start = int(np.searchsorted(column_length, low - freq * freq, side="left"))
                stop = int(np.searchsorted(column_length, high - freq * freq, side="right"))
                if stop > start:
                    self.pieces.append((index, start, stop, offset))
                    offset += stop - start
            for length in range(low, high + 1):
                self.edges[length] = (begin, offset)
        self.size = offset

    def ids(self, column_2, column_3, points, width):
        out = np.full((width,), -1, np.int32)
        for index, start, stop, offset in self.pieces:
            k1 = (index - ORIGIN) % points
            k2 = column_2[start:stop] % points
            k3 = column_3[start:stop] % points
            out[offset : offset + stop - start] = (k1 * points + k2) * points + k3
        return out


def length_ranges(cumulative, first, step, count):
    shell = lambda rank: int(np.searchsorted(cumulative, rank, side="right"))
    ranges, low = [], shell(first)
    for part in range(1, count):
        before, after = shell(first + part * step - 1), shell(first + part * step)
        if before == after:
            if low < before:
                ranges.append((low, before - 1))
            if low <= before:
                ranges.append((before, before))
        elif low <= before:
            ranges.append((low, before))
        low = before + 1
    high = shell(first + count * step - 1)
    if low <= high:
        ranges.append((low, high))
    return ranges


def make_plan(points, total, blocks, slab, slab_blocks):
    cumulative = length_counts(points)
    shell = lambda rank: int(np.searchsorted(cumulative, rank, side="right"))
    width, slab_width = total // blocks, slab // slab_blocks
    step = width // PARTS
    column_2, column_3, column_length = column_order(shell(total - 1))
    buckets = [Bucket(length_ranges(cumulative, n * width, step, PARTS), column_length) for n in range(blocks)]
    slabs = [Bucket(length_ranges(cumulative, n * slab_width, slab_width, 1), column_length) for n in range(slab_blocks)]
    slab_top = shell(slab - 1)
    lanes = round_up(max(bucket.size for bucket in buckets), LANES)
    slab_lanes = round_up(max(bucket.size for bucket in slabs), LANES)
    windows = np.zeros((blocks, PARTS, 2), np.int64)
    for n, bucket in enumerate(buckets):
        for part in range(PARTS):
            rank = n * width + part * step
            windows[n, part, 0] = bucket.edges[shell(rank)][0] // LANES * LANES
            windows[n, part, 1] = round_up(bucket.edges[shell(rank + step - 1)][1], LANES)
    window = int((windows[..., 1] - windows[..., 0]).max())
    return dict(
        buckets=buckets,
        slabs=slabs,
        slab_columns=int(np.searchsorted(column_length, slab_top, side="right")),
        slab_edge=math.isqrt(slab_top),
        lanes=lanes,
        slab_lanes=slab_lanes,
        window=window,
        starts=np.minimum(windows[..., 0], lanes - window).astype(np.int32),
        ids=np.stack([bucket.ids(column_2, column_3, points, lanes) for bucket in buckets]),
        slab_ids=np.stack([bucket.ids(column_2, column_3, points, slab_lanes) for bucket in slabs]),
        column_place=((column_3 + ORIGIN) * KEEP + column_2 + ORIGIN).astype(np.int32),
    )


def dft_table(points):
    n = np.arange(points)
    freq = np.arange(KEEP) - ORIGIN
    angle = (n[:, None] * freq[None, :] % points) * (2.0 * np.pi / points)
    cosine, sine = np.cos(angle), np.sin(angle)
    table = np.zeros((2 * HALF, 2 * HALF))
    table[:points, :KEEP] = cosine
    table[HALF : HALF + points, :KEEP] = sine
    table[:points, HALF : HALF + KEEP] = -sine
    table[HALF : HALF + points, HALF : HALF + KEEP] = cosine
    high = table.astype(jnp.bfloat16)
    low = (table - high.astype(np.float64)).astype(jnp.bfloat16)
    return np.block([[high, low], [high, np.zeros_like(low)]])


def split_parts(value):
    high = value.astype(jnp.bfloat16)
    low = (value - high.astype(jnp.float32)).astype(jnp.bfloat16)
    return high, low


def apply_table(parts, table):
    both = jnp.dot(parts, table, preferred_element_type=jnp.float32)
    return both[:, :LANES] + both[:, LANES:]


def stack_complex(turned, low_lanes):
    real, imag = turned[:KEEP], turned[HALF : HALF + KEEP]
    first = jnp.where(low_lanes, real, pltpu.roll(imag, HALF, 1))
    second = jnp.where(low_lanes, pltpu.roll(real, HALF, 1), imag)
    return jnp.concatenate([first, second], 0)


def pack_pieces(pieces, width, source, rows, lane, out):
    for tile in range(width // LANES):
        left, right = tile * LANES, (tile + 1) * LANES
        value = jnp.zeros((rows, LANES), jnp.float32)
        for index, start, stop, offset in pieces:
            begin, end = max(left, offset), min(right, offset + stop - start)
            while begin < end:
                at = start + begin - offset
                block = source(index, at // LANES)
                shift = (begin - at) % LANES
                if shift:
                    block = pltpu.roll(block, shift, 1)
                value = block if begin == left else jnp.where(lane >= begin - left, block, value)
                begin = min(end, begin + LANES - at % LANES)
        out(tile, value)


def slab_tiles(plan):
    first = (ORIGIN - plan["slab_edge"]) * KEEP // LANES
    last = round_up((ORIGIN + plan["slab_edge"] + 1) * KEEP, LANES) // LANES
    return first, last


def spectrum_kernel(plan, points, first_band, weight_ref, val_ref, cond_ref, table_ref, plain_ref, weighted_ref,
                    cond_a, cond_b, middle, turned, last):
    band = pl.program_id(0)
    planes = 8
    lane = lax.broadcasted_iota(jnp.int32, (1, LANES), 1)
    low_lanes = lane < HALF
    depth = last.shape[0]

    @pl.when(band == 0)
    def _():
        scale = 1.0 / float(points) ** 1.5
        sign = jnp.where(low_lanes, scale, -scale)

        @pl.loop(0, points // planes)
        def _(block):
            rows = pl.ds(pl.multiple_of(block * planes * points, planes * points), planes * points)
            wave = cond_ref[0, pl.ds(block * planes, planes)].reshape(planes * points, LANES).astype(jnp.float32)
            cond_a[rows, :] = wave * scale
            cond_b[rows, :] = pltpu.roll(wave, HALF, 1) * sign

        last[KEEP * KEEP :, :] = jnp.zeros((depth - KEEP * KEEP, 2 * LANES), jnp.bfloat16)

    table = table_ref[...]
    step = planes * KEEP

    def first_axis(block):
        rows = pl.ds(pl.multiple_of(block * planes * points, planes * points), planes * points)
        wave = val_ref[0, pl.ds(block * planes, planes)].reshape(planes * points, LANES).astype(jnp.float32)
        other = pltpu.roll(wave, HALF, 1)
        density = jnp.where(low_lanes, wave, other) * cond_a[rows, :] + jnp.where(low_lanes, other, wave) * cond_b[rows, :]
        high, low = split_parts(density)
        field = apply_table(jnp.concatenate([high, low], 1), table)
        for pair in range(planes // 2):
            both = field[pair * 2 * points : (pair + 1) * 2 * points].T
            high, low = split_parts(stack_complex(both, low_lanes))
            at = pl.ds(pl.multiple_of((block * planes + pair * 2) * KEEP, 2 * KEEP), 2 * KEEP)
            middle[at, :LANES] = high
            middle[at, LANES:] = low

    def second_axis(block):
        rows = pl.ds(pl.multiple_of(block * step, step), step)
        turned[rows, :] = apply_table(middle[rows, :], table)

    first_axis(0)

    @pl.loop(1, points // planes)
    def _(block):
        second_axis(block - 1)
        first_axis(block)

    second_axis(points // planes - 1)

    for pair in range(KEEP // 2):
        both = jnp.concatenate(
            [turned[pl.ds(2 * pair, points, stride=KEEP), :], turned[pl.ds(2 * pair + 1, points, stride=KEEP), :]], 0
        ).T
        high, low = split_parts(stack_complex(both, low_lanes))
        at = slice(2 * pair * KEEP, (2 * pair + 2) * KEEP)
        last[at, :LANES] = high
        last[at, LANES:] = low

    weight = weight_ref[first_band + band]
    slab_first, slab_last = slab_tiles(plan)
    for begin in range(0, depth // LANES, 5):
        end = min(begin + 5, depth // LANES)
        field = apply_table(last[begin * LANES : end * LANES, :], table)
        for tile in range(begin, end):
            turn = field[(tile - begin) * LANES : (tile - begin + 1) * LANES].T
            for part in range(2):
                value = turn[part * HALF : part * HALF + ROWS_K]
                plain_ref[part, 0, :, tile * LANES : (tile + 1) * LANES] = value.astype(jnp.bfloat16)
                if slab_first <= tile < slab_last:
                    lanes = slice((tile - slab_first) * LANES, (tile - slab_first + 1) * LANES)
                    weighted_ref[part, 0, :, lanes] = (weight * value).astype(jnp.bfloat16)


def spectra(plan, val_wave, cond_wave, weight, first_band, count):
    points = val_wave.shape[1]
    depth = round_up(KEEP * KEEP, LANES)
    slab_first, slab_last = slab_tiles(plan)
    slab_depth = (slab_last - slab_first) * LANES
    grid_rows = points * points
    kernel = lambda *refs: spectrum_kernel(plan, points, first_band, *refs)
    return pl.pallas_call(
        kernel,
        grid=(count,),
        in_specs=[
            pl.BlockSpec(memory_space=pltpu.SMEM),
            pl.BlockSpec((1, points, points, 2 * points), lambda v: (first_band + v, 0, 0, 0)),
            pl.BlockSpec((1, points, points, 2 * points), lambda v: (0, 0, 0, 0)),
            pl.BlockSpec((4 * HALF, 4 * HALF), lambda v: (0, 0)),
        ],
        out_specs=[
            pl.BlockSpec((2, 1, ROWS_K, depth), lambda v: (0, v, 0, 0)),
            pl.BlockSpec((2, 1, ROWS_K, slab_depth), lambda v: (0, v, 0, 0)),
        ],
        out_shape=[
            jax.ShapeDtypeStruct((2, count, ROWS_K, depth), jnp.bfloat16),
            jax.ShapeDtypeStruct((2, count, ROWS_K, slab_depth), jnp.bfloat16),
        ],
        scratch_shapes=[
            pltpu.VMEM((grid_rows, LANES), jnp.float32),
            pltpu.VMEM((grid_rows, LANES), jnp.float32),
            pltpu.VMEM((points * KEEP, 2 * LANES), jnp.bfloat16),
            pltpu.VMEM((points * KEEP, LANES), jnp.float32),
            pltpu.VMEM((depth, 2 * LANES), jnp.bfloat16),
        ],
        compiler_params=pltpu.CompilerParams(vmem_limit_bytes=VMEM_BYTES, dimension_semantics=("arbitrary",)),
        cost_estimate=pl.CostEstimate(flops=count, bytes_accessed=count, transcendentals=0),
        name="spectra",
    )(weight, val_wave, cond_wave, jnp.asarray(dft_table(points)))


def pack_kernel(plan, groups, place_ref, *refs):
    plains, weighteds = refs[:groups], refs[groups : 2 * groups]
    send_ref, slab_ref, sorter, plain_sorted, weighted_sorted = refs[2 * groups :]
    depth, columns = sorter.shape
    count = 2 * sum(plain.shape[1] for plain in plains)
    lane = lax.broadcasted_iota(jnp.int32, (1, LANES), 1)
    for begin in range(0, depth, LANES):
        at = lax.broadcasted_iota(jnp.int32, (LANES, columns), 0) + begin
        sorter[begin : begin + LANES, :] = jnp.where(at == place_ref[...], 1.0, 0.0).astype(jnp.bfloat16)

    def sort_rows(parts, which, target):
        rows = jnp.concatenate([part[n] for n in range(2) for part in parts], 0)
        rows = rows.reshape(count * ROWS_K, rows.shape[2])
        value = jnp.dot(rows, which, preferred_element_type=jnp.float32)
        for tile in range(target.shape[0]):
            target[tile] = value[:, tile * LANES : (tile + 1) * LANES]

    slab_first, slab_last = slab_tiles(plan)
    sort_rows(plains, sorter[...], plain_sorted)
    sort_rows(weighteds, sorter[slab_first * LANES : slab_last * LANES, : weighted_sorted.shape[0] * LANES], weighted_sorted)

    def plain_at(index, tile):
        return plain_sorted[tile, pl.ds(index, count, stride=ROWS_K), :]

    def weighted_at(index, tile):
        return weighted_sorted[tile, pl.ds(index, count, stride=ROWS_K), :]

    for block, bucket in enumerate(plan["buckets"]):

        def keep(tile, value):
            send_ref[block, :, tile * LANES : (tile + 1) * LANES] = value.astype(jnp.bfloat16)

        pack_pieces(bucket.pieces, plan["lanes"], plain_at, count, lane, keep)
    for block, bucket in enumerate(plan["slabs"]):

        def keep_slab(tile, value):
            slab_ref[block, :, tile * LANES : (tile + 1) * LANES] = value.astype(jnp.bfloat16)

        pack_pieces(bucket.pieces, plan["slab_lanes"], weighted_at, count, lane, keep_slab)


def packed(plan, plains, weighteds):
    depth = plains[0].shape[3]
    count = 2 * sum(plain.shape[1] for plain in plains)
    columns = round_up(plan["column_place"].shape[0], 256)
    slab_columns = round_up(plan["slab_columns"], LANES)
    place = np.full((1, columns), -1, np.int32)
    place[0, : plan["column_place"].shape[0]] = plan["column_place"]
    kernel = lambda *refs: pack_kernel(plan, len(plains), *refs)
    vmem = pl.BlockSpec(memory_space=pltpu.VMEM)
    send_shape = (len(plan["buckets"]), count, plan["lanes"])
    slab_shape = (len(plan["slabs"]), count, plan["slab_lanes"])
    return pl.pallas_call(
        kernel,
        in_specs=[vmem] * (1 + 2 * len(plains)),
        out_specs=[vmem] * 2,
        out_shape=[jax.ShapeDtypeStruct(send_shape, jnp.bfloat16), jax.ShapeDtypeStruct(slab_shape, jnp.bfloat16)],
        scratch_shapes=[
            pltpu.VMEM((depth, columns), jnp.bfloat16),
            pltpu.VMEM((columns // LANES, count * ROWS_K, LANES), jnp.float32),
            pltpu.VMEM((slab_columns // LANES, count * ROWS_K, LANES), jnp.float32),
        ],
        compiler_params=pltpu.CompilerParams(vmem_limit_bytes=VMEM_BYTES),
        cost_estimate=pl.CostEstimate(flops=1, bytes_accessed=1, transcendentals=0),
        name="pack",
    )(jnp.asarray(place), *plains, *weighteds)


def one_hot(ids_ref, begin, wanted):
    ids = jnp.broadcast_to(ids_ref[:, pl.ds(begin, LANES)], (LANES, LANES)).T
    ids = jnp.concatenate([ids] * (wanted.shape[1] // LANES), 1)
    return jnp.where(ids == wanted, 1.0, 0.0).astype(jnp.bfloat16)


def left_kernel(group, slab_ref, slab_ids_ref, slab_wanted_ref, left_ref):
    rows = slab_wanted_ref.shape[1]
    choice = jnp.concatenate(
        [one_hot(slab_ids_ref, begin, slab_wanted_ref[...]) for begin in range(0, slab_ids_ref.shape[1], LANES)], 0
    )
    chosen = jnp.dot(slab_ref[...], choice, preferred_element_type=jnp.float32)
    lane = lax.broadcasted_iota(jnp.int32, (1, LANES), 1)
    real_lanes = lane % group < group // 2
    for begin in range(0, chosen.shape[0], LANES):
        turned = chosen[begin : begin + LANES].T
        after = pltpu.roll(turned, LANES - group // 2, 1)
        before = pltpu.roll(turned, group // 2, 1)
        left_ref[:rows, begin : begin + LANES] = turned.astype(jnp.bfloat16)
        left_ref[rows:, begin : begin + LANES] = jnp.where(real_lanes, after, -before).astype(jnp.bfloat16)


def left_side(group, slab, slab_ids, slab_wanted):
    vmem = pl.BlockSpec(memory_space=pltpu.VMEM)
    return pl.pallas_call(
        lambda *refs: left_kernel(group, *refs),
        in_specs=[vmem] * 3,
        out_specs=vmem,
        out_shape=jax.ShapeDtypeStruct((2 * slab_wanted.shape[1], slab.shape[0]), jnp.bfloat16),
        compiler_params=pltpu.CompilerParams(vmem_limit_bytes=VMEM_BYTES),
        cost_estimate=pl.CostEstimate(flops=1, bytes_accessed=1, transcendentals=0),
        name="left_side",
    )(slab, slab_ids, slab_wanted)


def in_order(start, panel_ref, ids_ref, wanted_ref, hot):
    wanted = wanted_ref[...]
    window = hot.shape[0]
    for begin in range(0, window, LANES):
        hot[begin : begin + LANES, :] = one_hot(ids_ref, pl.multiple_of(start + begin, LANES), wanted)
    return jnp.dot(panel_ref[:, pl.ds(start, window)], hot[...], preferred_element_type=jnp.float32).astype(jnp.bfloat16)


def order_kernel(starts_ref, ids_ref, wanted_ref, panel_ref, out_ref, hot):
    start = pl.multiple_of(starts_ref[pl.program_id(0)], LANES)
    out_ref[...] = in_order(start, panel_ref, ids_ref, wanted_ref, hot)


def product_kernel(starts_ref, ids_ref, wanted_ref, panel_ref, left_ref, *refs):
    *ordered, out_ref, hot = refs
    rows = out_ref.shape[1]
    start = pl.multiple_of(starts_ref[pl.program_id(0)], LANES)
    last = in_order(start, panel_ref, ids_ref, wanted_ref, hot)
    right = jnp.concatenate([part[...] for part in ordered] + [last], 0)
    chi = jnp.dot(left_ref[...], right, preferred_element_type=jnp.float32)
    out_ref[0] = chi[:rows]
    out_ref[1] = chi[rows:]


def put_in_order(plan, starts, ids, wanted, panel, left=None, ordered=()):
    columns = wanted.shape[1]
    block = columns // PARTS
    whole = lambda array: pl.BlockSpec(array.shape, lambda n: (0,) * array.ndim)
    in_specs = [
        pl.BlockSpec(memory_space=pltpu.SMEM),
        whole(ids),
        pl.BlockSpec((1, block), lambda n: (0, n)),
        whole(panel),
    ]
    operands = [starts, ids, wanted, panel]
    if left is None:
        out_spec = pl.BlockSpec((panel.shape[0], block), lambda n: (0, n))
        out_shape = jax.ShapeDtypeStruct((panel.shape[0], columns), jnp.bfloat16)
    else:
        rows = left.shape[0] // 2
        in_specs += [whole(left)] + [pl.BlockSpec((part.shape[0], block), lambda n: (0, n)) for part in ordered]
        operands += [left, *ordered]
        out_spec = pl.BlockSpec((2, rows, block), lambda n: (0, 0, n))
        out_shape = jax.ShapeDtypeStruct((2, rows, columns), jnp.float32)
    return pl.pallas_call(
        order_kernel if left is None else product_kernel,
        grid=(PARTS,),
        in_specs=in_specs,
        out_specs=out_spec,
        out_shape=out_shape,
        scratch_shapes=[pltpu.VMEM((plan["window"], block), jnp.bfloat16)],
        compiler_params=pltpu.CompilerParams(vmem_limit_bytes=VMEM_BYTES, dimension_semantics=("arbitrary",)),
        cost_estimate=pl.CostEstimate(flops=1, bytes_accessed=1, transcendentals=0),
        name="in_order" if left is None else "product",
    )(*operands)


def on_device(val_wave, cond_wave, val_energy, cond_energy, band_owner, grid_map):
    bands, points = val_wave.shape[0], val_wave.shape[1]
    band_total = cond_energy.shape[0]
    row_count = lax.axis_size("row")
    col_count = lax.axis_size("col")
    col, row = lax.axis_index("col"), lax.axis_index("row")
    plan = make_plan(points, grid_map.shape[0], col_count, ROWS_DEV * row_count, row_count)
    energy = jnp.sum(jnp.where(band_owner[0] == jnp.arange(band_total, dtype=jnp.int32), cond_energy, 0.0))
    weight = -2.0 / (math.sqrt(bands * band_total) * (energy - val_energy))
    width = grid_map.shape[0] // col_count
    starts = lax.dynamic_index_in_dim(jnp.asarray(plan["starts"]), col, 0, keepdims=False)
    ids = lax.dynamic_slice(jnp.asarray(plan["ids"]), (col, 0), (1, plan["lanes"]))
    slab_ids = lax.dynamic_slice(jnp.asarray(plan["slab_ids"]), (row, 0), (1, plan["slab_lanes"]))
    wanted = lax.dynamic_slice(grid_map, (col * width,), (width,))[None]
    slab_wanted = lax.dynamic_slice(grid_map, (row * ROWS_DEV,), (ROWS_DEV,))[None]
    chunk = bands // CHUNKS
    panels, slabs = [], []
    for part in range(CHUNKS):
        plain, weighted = spectra(plan, val_wave, cond_wave, weight, part * chunk, chunk)
        send, slab = packed(plan, [plain], [weighted])
        mine = lax.all_to_all(send, "col", split_axis=0, concat_axis=0, tiled=True)
        mine, slab, cond_wave = lax.optimization_barrier((mine, slab, cond_wave))
        panels.append(lax.all_gather(mine, "row", axis=0, tiled=True).reshape(-1, plan["lanes"]))
        slabs.append(slab)
    slab = lax.all_to_all(jnp.stack(slabs, 1), "row", split_axis=0, concat_axis=0, tiled=True)
    slab = lax.all_to_all(jnp.broadcast_to(slab, (col_count, *slab.shape)), "col", split_axis=0, concat_axis=0)
    slab = slab.transpose(2, 1, 0, 3, 4).reshape(-1, plan["slab_lanes"])
    left = left_side(2 * chunk, slab, slab_ids, slab_wanted)
    ordered = [put_in_order(plan, starts, ids, wanted, panel) for panel in panels[:-1]]
    return put_in_order(plan, starts, ids, wanted, panels[-1], left, ordered)


def solution(mesh):
    in_specs = (P(), P(("row", "col"), None, None, None), P(), P(), P(("row", "col")), P())
    out_specs = P(None, "row", "col")
    return jax.shard_map(
        on_device, mesh=mesh, in_specs=in_specs, out_specs=out_specs, check_vma=False
    )
```

```python
import math

import jax
import jax.numpy as jnp
import numpy as np
from jax import lax
from jax.experimental import pallas as pl
from jax.experimental.pallas import tpu as pltpu
from jax.sharding import PartitionSpec as P

ROWS_DEV = 256
LANES = 128
VMEM_BYTES = 56 * 1024 * 1024
HALF = 64
KEEP = 40
ROWS_K = 48
ORIGIN = KEEP // 2
PARTS = 3
CHUNKS = 2


def round_up(value, step):
    return -(-value // step) * step


def length_counts(points):
    freq = np.arange(points) - points // 2
    square = freq * freq
    lengths = square[:, None, None] + square[None, :, None] + square[None, None, :]
    return np.cumsum(np.bincount(lengths.reshape(-1)))


def column_order(top):
    freq = np.arange(KEEP) - ORIGIN
    first, second = np.meshgrid(freq, freq, indexing="ij")
    length = (first * first + second * second).reshape(-1)
    order = np.argsort(length, kind="stable")
    order = order[length[order] <= top]
    return first.reshape(-1)[order], second.reshape(-1)[order], length[order]


class Bucket:
    def __init__(self, ranges, column_length):
        self.pieces = []
        self.edges = {}
        offset = 0
        for low, high in ranges:
            begin = offset
            for index in range(KEEP):
                freq = index - ORIGIN
                start = int(np.searchsorted(column_length, low - freq * freq, side="left"))
                stop = int(np.searchsorted(column_length, high - freq * freq, side="right"))
                if stop > start:
                    self.pieces.append((index, start, stop, offset))
                    offset += stop - start
            for length in range(low, high + 1):
                self.edges[length] = (begin, offset)
        self.size = offset

    def ids(self, column_2, column_3, points, width):
        out = np.full((width,), -1, np.int32)
        for index, start, stop, offset in self.pieces:
            k1 = (index - ORIGIN) % points
            k2 = column_2[start:stop] % points
            k3 = column_3[start:stop] % points
            out[offset : offset + stop - start] = (k1 * points + k2) * points + k3
        return out


def length_ranges(cumulative, first, step, count):
    shell = lambda rank: int(np.searchsorted(cumulative, rank, side="right"))
    ranges, low = [], shell(first)
    for part in range(1, count):
        before, after = shell(first + part * step - 1), shell(first + part * step)
        if before == after:
            if low < before:
                ranges.append((low, before - 1))
            if low <= before:
                ranges.append((before, before))
        elif low <= before:
            ranges.append((low, before))
        low = before + 1
    high = shell(first + count * step - 1)
    if low <= high:
        ranges.append((low, high))
    return ranges


def make_plan(points, total, blocks, slab, slab_blocks):
    cumulative = length_counts(points)
    shell = lambda rank: int(np.searchsorted(cumulative, rank, side="right"))
    width, slab_width = total // blocks, slab // slab_blocks
    step = width // PARTS
    column_2, column_3, column_length = column_order(shell(total - 1))
    buckets = [Bucket(length_ranges(cumulative, n * width, step, PARTS), column_length) for n in range(blocks)]
    slabs = [Bucket(length_ranges(cumulative, n * slab_width, slab_width, 1), column_length) for n in range(slab_blocks)]
    slab_top = shell(slab - 1)
    lanes = round_up(max(bucket.size for bucket in buckets), LANES)
    slab_lanes = round_up(max(bucket.size for bucket in slabs), LANES)
    windows = np.zeros((blocks, PARTS, 2), np.int64)
    for n, bucket in enumerate(buckets):
        for part in range(PARTS):
            rank = n * width + part * step
            windows[n, part, 0] = bucket.edges[shell(rank)][0] // LANES * LANES
            windows[n, part, 1] = round_up(bucket.edges[shell(rank + step - 1)][1], LANES)
    window = int((windows[..., 1] - windows[..., 0]).max())
    return dict(
        buckets=buckets,
        slabs=slabs,
        slab_columns=int(np.searchsorted(column_length, slab_top, side="right")),
        slab_edge=math.isqrt(slab_top),
        lanes=lanes,
        slab_lanes=slab_lanes,
        window=window,
        starts=np.minimum(windows[..., 0], lanes - window).astype(np.int32),
        ids=np.stack([bucket.ids(column_2, column_3, points, lanes) for bucket in buckets]),
        slab_ids=np.stack([bucket.ids(column_2, column_3, points, slab_lanes) for bucket in slabs]),
        column_place=((column_3 + ORIGIN) * KEEP + column_2 + ORIGIN).astype(np.int32),
    )


def dft_table(points):
    n = np.arange(points)
    freq = np.arange(KEEP) - ORIGIN
    angle = (n[:, None] * freq[None, :] % points) * (2.0 * np.pi / points)
    cosine, sine = np.cos(angle), np.sin(angle)
    table = np.zeros((2 * HALF, 2 * HALF))
    table[:points, :KEEP] = cosine
    table[HALF : HALF + points, :KEEP] = sine
    table[:points, HALF : HALF + KEEP] = -sine
    table[HALF : HALF + points, HALF : HALF + KEEP] = cosine
    high = table.astype(jnp.bfloat16)
    low = (table - high.astype(np.float64)).astype(jnp.bfloat16)
    return np.block([[high, low], [high, np.zeros_like(low)]])


def split_parts(value):
    high = value.astype(jnp.bfloat16)
    low = (value - high.astype(jnp.float32)).astype(jnp.bfloat16)
    return high, low


def apply_table(parts, table):
    both = jnp.dot(parts, table, preferred_element_type=jnp.float32)
    return both[:, :LANES] + both[:, LANES:]


def stack_complex(turned, low_lanes):
    real, imag = turned[:KEEP], turned[HALF : HALF + KEEP]
    first = jnp.where(low_lanes, real, pltpu.roll(imag, HALF, 1))
    second = jnp.where(low_lanes, pltpu.roll(real, HALF, 1), imag)
    return jnp.concatenate([first, second], 0)


def pack_pieces(pieces, width, source, rows, lane, out):
    for tile in range(width // LANES):
        left, right = tile * LANES, (tile + 1) * LANES
        value = jnp.zeros((rows, LANES), jnp.float32)
        for index, start, stop, offset in pieces:
            begin, end = max(left, offset), min(right, offset + stop - start)
            while begin < end:
                at = start + begin - offset
                block = source(index, at // LANES)
                shift = (begin - at) % LANES
                if shift:
                    block = pltpu.roll(block, shift, 1)
                value = block if begin == left else jnp.where(lane >= begin - left, block, value)
                begin = min(end, begin + LANES - at % LANES)
        out(tile, value)


def slab_tiles(plan):
    first = (ORIGIN - plan["slab_edge"]) * KEEP // LANES
    last = round_up((ORIGIN + plan["slab_edge"] + 1) * KEEP, LANES) // LANES
    return first, last


def spectrum_kernel(plan, points, first_band, owner_ref, cond_energy_ref, val_energy_ref, val_ref, cond_ref, table_ref, plain_ref, weighted_ref,
                    cond_a, cond_b, middle, turned, last):
    band = pl.program_id(0)
    planes = 8
    lane = lax.broadcasted_iota(jnp.int32, (1, LANES), 1)
    low_lanes = lane < HALF
    depth = last.shape[0]

    @pl.when(band == 0)
    def _():
        scale = 1.0 / float(points) ** 1.5
        sign = jnp.where(low_lanes, scale, -scale)

        @pl.loop(0, points // planes)
        def _(block):
            rows = pl.ds(pl.multiple_of(block * planes * points, planes * points), planes * points)
            wave = cond_ref[0, pl.ds(block * planes, planes)].reshape(planes * points, LANES).astype(jnp.float32)
            cond_a[rows, :] = wave * scale
            cond_b[rows, :] = pltpu.roll(wave, HALF, 1) * sign

        last[KEEP * KEEP :, :] = jnp.zeros((depth - KEEP * KEEP, 2 * LANES), jnp.bfloat16)

    table = table_ref[...]
    step = planes * KEEP

    def first_axis(block):
        rows = pl.ds(pl.multiple_of(block * planes * points, planes * points), planes * points)
        wave = val_ref[0, pl.ds(block * planes, planes)].reshape(planes * points, LANES).astype(jnp.float32)
        other = pltpu.roll(wave, HALF, 1)
        density = jnp.where(low_lanes, wave, other) * cond_a[rows, :] + jnp.where(low_lanes, other, wave) * cond_b[rows, :]
        high, low = split_parts(density)
        field = apply_table(jnp.concatenate([high, low], 1), table)
        for pair in range(planes // 2):
            both = field[pair * 2 * points : (pair + 1) * 2 * points].T
            high, low = split_parts(stack_complex(both, low_lanes))
            at = pl.ds(pl.multiple_of((block * planes + pair * 2) * KEEP, 2 * KEEP), 2 * KEEP)
            middle[at, :LANES] = high
            middle[at, LANES:] = low

    def second_axis(block):
        rows = pl.ds(pl.multiple_of(block * step, step), step)
        turned[rows, :] = apply_table(middle[rows, :], table)

    first_axis(0)
    first_axis(1)

    @pl.loop(1, points // planes // 2)
    def _(block):
        for part in range(2):
            second_axis(2 * block - 2 + part)
        for part in range(2):
            first_axis(2 * block + part)

    second_axis(points // planes - 2)
    second_axis(points // planes - 1)

    for pair in range(KEEP // 2):
        both = jnp.concatenate(
            [turned[pl.ds(2 * pair, points, stride=KEEP), :], turned[pl.ds(2 * pair + 1, points, stride=KEEP), :]], 0
        ).T
        high, low = split_parts(stack_complex(both, low_lanes))
        at = slice(2 * pair * KEEP, (2 * pair + 2) * KEEP)
        last[at, :LANES] = high
        last[at, LANES:] = low

    pairs = val_energy_ref.shape[0] * cond_energy_ref.shape[0]
    gap = cond_energy_ref[owner_ref[0]] - val_energy_ref[first_band + band]
    weight = -2.0 / (math.sqrt(pairs) * jnp.full((1, LANES), gap, jnp.float32))
    slab_first, slab_last = slab_tiles(plan)
    for begin in range(0, depth // LANES, 5):
        end = min(begin + 5, depth // LANES)
        field = apply_table(last[begin * LANES : end * LANES, :], table)
        for tile in range(begin, end):
            turn = field[(tile - begin) * LANES : (tile - begin + 1) * LANES].T
            for part in range(2):
                value = turn[part * HALF : part * HALF + ROWS_K]
                plain_ref[part, 0, :, tile * LANES : (tile + 1) * LANES] = value.astype(jnp.bfloat16)
                if slab_first <= tile < slab_last:
                    lanes = slice((tile - slab_first) * LANES, (tile - slab_first + 1) * LANES)
                    weighted_ref[part, 0, :, lanes] = (weight * value).astype(jnp.bfloat16)


def spectra(plan, val_wave, cond_wave, energies, first_band, count):
    points = val_wave.shape[1]
    depth = round_up(KEEP * KEEP, LANES)
    slab_first, slab_last = slab_tiles(plan)
    slab_depth = (slab_last - slab_first) * LANES
    grid_rows = points * points
    kernel = lambda *refs: spectrum_kernel(plan, points, first_band, *refs)
    return pl.pallas_call(
        kernel,
        grid=(count,),
        in_specs=[
            pl.BlockSpec(memory_space=pltpu.SMEM),
            pl.BlockSpec(memory_space=pltpu.SMEM),
            pl.BlockSpec(memory_space=pltpu.SMEM),
            pl.BlockSpec((1, points, points, 2 * points), lambda v: (first_band + v, 0, 0, 0)),
            pl.BlockSpec((1, points, points, 2 * points), lambda v: (0, 0, 0, 0)),
            pl.BlockSpec((4 * HALF, 4 * HALF), lambda v: (0, 0)),
        ],
        out_specs=[
            pl.BlockSpec((2, 1, ROWS_K, depth), lambda v: (0, v, 0, 0)),
            pl.BlockSpec((2, 1, ROWS_K, slab_depth), lambda v: (0, v, 0, 0)),
        ],
        out_shape=[
            jax.ShapeDtypeStruct((2, count, ROWS_K, depth), jnp.bfloat16),
            jax.ShapeDtypeStruct((2, count, ROWS_K, slab_depth), jnp.bfloat16),
        ],
        scratch_shapes=[
            pltpu.VMEM((grid_rows, LANES), jnp.float32),
            pltpu.VMEM((grid_rows, LANES), jnp.float32),
            pltpu.VMEM((points * KEEP, 2 * LANES), jnp.bfloat16),
            pltpu.VMEM((points * KEEP, LANES), jnp.float32),
            pltpu.VMEM((depth, 2 * LANES), jnp.bfloat16),
        ],
        compiler_params=pltpu.CompilerParams(vmem_limit_bytes=VMEM_BYTES, dimension_semantics=("arbitrary",)),
        cost_estimate=pl.CostEstimate(flops=count, bytes_accessed=count, transcendentals=0),
        name="spectra",
    )(*energies, val_wave, cond_wave, jnp.asarray(dft_table(points)))


def pack_kernel(plan, groups, place_ref, *refs):
    plains, weighteds = refs[:groups], refs[groups : 2 * groups]
    send_ref, slab_ref, sorter, plain_sorted, weighted_sorted = refs[2 * groups :]
    depth, columns = sorter.shape
    count = 2 * sum(plain.shape[1] for plain in plains)
    lane = lax.broadcasted_iota(jnp.int32, (1, LANES), 1)
    for begin in range(0, depth, LANES):
        at = lax.broadcasted_iota(jnp.int32, (LANES, columns), 0) + begin
        sorter[begin : begin + LANES, :] = jnp.where(at == place_ref[...], 1.0, 0.0).astype(jnp.bfloat16)

    def sort_rows(parts, which, target):
        rows = jnp.concatenate([part[n] for n in range(2) for part in parts], 0)
        rows = rows.reshape(count * ROWS_K, rows.shape[2])
        value = jnp.dot(rows, which, preferred_element_type=jnp.float32)
        for tile in range(target.shape[0]):
            target[tile] = value[:, tile * LANES : (tile + 1) * LANES]

    slab_first, slab_last = slab_tiles(plan)
    sort_rows(plains, sorter[...], plain_sorted)
    sort_rows(weighteds, sorter[slab_first * LANES : slab_last * LANES, : weighted_sorted.shape[0] * LANES], weighted_sorted)

    def plain_at(index, tile):
        return plain_sorted[tile, pl.ds(index, count, stride=ROWS_K), :]

    def weighted_at(index, tile):
        return weighted_sorted[tile, pl.ds(index, count, stride=ROWS_K), :]

    for block, bucket in enumerate(plan["buckets"]):

        def keep(tile, value):
            send_ref[block, :, tile * LANES : (tile + 1) * LANES] = value.astype(jnp.bfloat16)

        pack_pieces(bucket.pieces, plan["lanes"], plain_at, count, lane, keep)
    for block, bucket in enumerate(plan["slabs"]):

        def keep_slab(tile, value):
            slab_ref[block, :, tile * LANES : (tile + 1) * LANES] = value.astype(jnp.bfloat16)

        pack_pieces(bucket.pieces, plan["slab_lanes"], weighted_at, count, lane, keep_slab)


def packed(plan, plains, weighteds):
    depth = plains[0].shape[3]
    count = 2 * sum(plain.shape[1] for plain in plains)
    columns = round_up(plan["column_place"].shape[0], 256)
    slab_columns = round_up(plan["slab_columns"], LANES)
    place = np.full((1, columns), -1, np.int32)
    place[0, : plan["column_place"].shape[0]] = plan["column_place"]
    kernel = lambda *refs: pack_kernel(plan, len(plains), *refs)
    vmem = pl.BlockSpec(memory_space=pltpu.VMEM)
    send_shape = (len(plan["buckets"]), count, plan["lanes"])
    slab_shape = (len(plan["slabs"]), count, plan["slab_lanes"])
    return pl.pallas_call(
        kernel,
        in_specs=[vmem] * (1 + 2 * len(plains)),
        out_specs=[vmem] * 2,
        out_shape=[jax.ShapeDtypeStruct(send_shape, jnp.bfloat16), jax.ShapeDtypeStruct(slab_shape, jnp.bfloat16)],
        scratch_shapes=[
            pltpu.VMEM((depth, columns), jnp.bfloat16),
            pltpu.VMEM((columns // LANES, count * ROWS_K, LANES), jnp.float32),
            pltpu.VMEM((slab_columns // LANES, count * ROWS_K, LANES), jnp.float32),
        ],
        compiler_params=pltpu.CompilerParams(vmem_limit_bytes=VMEM_BYTES),
        cost_estimate=pl.CostEstimate(flops=1, bytes_accessed=1, transcendentals=0),
        name="pack",
    )(jnp.asarray(place), *plains, *weighteds)


def one_hot(ids_ref, begin, wanted):
    ids = jnp.broadcast_to(ids_ref[:, pl.ds(begin, LANES)], (LANES, LANES)).T
    ids = jnp.concatenate([ids] * (wanted.shape[1] // LANES), 1)
    return jnp.where(ids == wanted, 1.0, 0.0).astype(jnp.bfloat16)


def left_kernel(group, slab_ref, slab_ids_ref, slab_wanted_ref, left_ref):
    rows = slab_wanted_ref.shape[1]
    choice = jnp.concatenate(
        [one_hot(slab_ids_ref, begin, slab_wanted_ref[...]) for begin in range(0, slab_ids_ref.shape[1], LANES)], 0
    )
    chosen = jnp.dot(slab_ref[...], choice, preferred_element_type=jnp.float32)
    lane = lax.broadcasted_iota(jnp.int32, (1, LANES), 1)
    real_lanes = lane % group < group // 2
    for begin in range(0, chosen.shape[0], LANES):
        turned = chosen[begin : begin + LANES].T
        after = pltpu.roll(turned, LANES - group // 2, 1)
        before = pltpu.roll(turned, group // 2, 1)
        left_ref[:rows, begin : begin + LANES] = turned.astype(jnp.bfloat16)
        left_ref[rows:, begin : begin + LANES] = jnp.where(real_lanes, after, -before).astype(jnp.bfloat16)


def left_side(group, slab, slab_ids, slab_wanted):
    vmem = pl.BlockSpec(memory_space=pltpu.VMEM)
    return pl.pallas_call(
        lambda *refs: left_kernel(group, *refs),
        in_specs=[vmem] * 3,
        out_specs=vmem,
        out_shape=jax.ShapeDtypeStruct((2 * slab_wanted.shape[1], slab.shape[0]), jnp.bfloat16),
        compiler_params=pltpu.CompilerParams(vmem_limit_bytes=VMEM_BYTES),
        cost_estimate=pl.CostEstimate(flops=1, bytes_accessed=1, transcendentals=0),
        name="left_side",
    )(slab, slab_ids, slab_wanted)


def in_order(start, panel_ref, ids_ref, wanted_ref, hot):
    wanted = wanted_ref[...]
    window = hot.shape[0]
    for begin in range(0, window, LANES):
        hot[begin : begin + LANES, :] = one_hot(ids_ref, pl.multiple_of(start + begin, LANES), wanted)
    return jnp.dot(panel_ref[:, pl.ds(start, window)], hot[...], preferred_element_type=jnp.float32).astype(jnp.bfloat16)


def order_kernel(starts_ref, ids_ref, wanted_ref, panel_ref, out_ref, hot):
    start = pl.multiple_of(starts_ref[pl.program_id(0)], LANES)
    out_ref[...] = in_order(start, panel_ref, ids_ref, wanted_ref, hot)


def product_kernel(starts_ref, ids_ref, wanted_ref, panel_ref, left_ref, *refs):
    *ordered, out_ref, hot = refs
    rows = out_ref.shape[1]
    start = pl.multiple_of(starts_ref[pl.program_id(0)], LANES)
    last = in_order(start, panel_ref, ids_ref, wanted_ref, hot)
    right = jnp.concatenate([part[...] for part in ordered] + [last], 0)
    chi = jnp.dot(left_ref[...], right, preferred_element_type=jnp.float32)
    out_ref[0] = chi[:rows]
    out_ref[1] = chi[rows:]


def put_in_order(plan, starts, ids, wanted, panel, left=None, ordered=()):
    columns = wanted.shape[1]
    block = columns // PARTS
    whole = lambda array: pl.BlockSpec(array.shape, lambda n: (0,) * array.ndim)
    in_specs = [
        pl.BlockSpec(memory_space=pltpu.SMEM),
        whole(ids),
        pl.BlockSpec((1, block), lambda n: (0, n)),
        whole(panel),
    ]
    operands = [starts, ids, wanted, panel]
    if left is None:
        out_spec = pl.BlockSpec((panel.shape[0], block), lambda n: (0, n))
        out_shape = jax.ShapeDtypeStruct((panel.shape[0], columns), jnp.bfloat16)
    else:
        rows = left.shape[0] // 2
        in_specs += [whole(left)] + [pl.BlockSpec((part.shape[0], block), lambda n: (0, n)) for part in ordered]
        operands += [left, *ordered]
        out_spec = pl.BlockSpec((2, rows, block), lambda n: (0, 0, n))
        out_shape = jax.ShapeDtypeStruct((2, rows, columns), jnp.float32)
    return pl.pallas_call(
        order_kernel if left is None else product_kernel,
        grid=(PARTS,),
        in_specs=in_specs,
        out_specs=out_spec,
        out_shape=out_shape,
        scratch_shapes=[pltpu.VMEM((plan["window"], block), jnp.bfloat16)],
        compiler_params=pltpu.CompilerParams(vmem_limit_bytes=VMEM_BYTES, dimension_semantics=("arbitrary",)),
        cost_estimate=pl.CostEstimate(flops=1, bytes_accessed=1, transcendentals=0),
        name="in_order" if left is None else "product",
    )(*operands)


def on_device(val_wave, cond_wave, val_energy, cond_energy, band_owner, grid_map):
    bands, points = val_wave.shape[0], val_wave.shape[1]
    row_count = lax.axis_size("row")
    col_count = lax.axis_size("col")
    col, row = lax.axis_index("col"), lax.axis_index("row")
    plan = make_plan(points, grid_map.shape[0], col_count, ROWS_DEV * row_count, row_count)
    width = grid_map.shape[0] // col_count
    starts = lax.dynamic_index_in_dim(jnp.asarray(plan["starts"]), col, 0, keepdims=False)
    ids = lax.dynamic_slice(jnp.asarray(plan["ids"]), (col, 0), (1, plan["lanes"]))
    slab_ids = lax.dynamic_slice(jnp.asarray(plan["slab_ids"]), (row, 0), (1, plan["slab_lanes"]))
    wanted = lax.dynamic_slice(grid_map, (col * width,), (width,))[None]
    slab_wanted = lax.dynamic_slice(grid_map, (row * ROWS_DEV,), (ROWS_DEV,))[None]
    chunk = bands // CHUNKS
    energies = (band_owner, cond_energy, val_energy)
    panels, slabs = [], []
    for part in range(CHUNKS):
        plain, weighted = spectra(plan, val_wave, cond_wave, energies, part * chunk, chunk)
        send, slab = packed(plan, [plain], [weighted])
        slabs.append(slab)
        if part < CHUNKS - 1:
            send, cond_wave = lax.optimization_barrier((send, cond_wave))
            panels.append(lax.all_gather(send, "row", axis=1))
        else:
            mine = lax.all_to_all(send, "col", split_axis=0, concat_axis=0, tiled=True)
            panels.append(lax.all_gather(mine, "row", axis=0, tiled=True).reshape(-1, plan["lanes"]))
    *early, slab, _ = lax.optimization_barrier((*panels[:-1], jnp.stack(slabs, 1), mine))
    for part, panel in enumerate(early):
        panel = lax.all_to_all(panel, "col", split_axis=0, concat_axis=0, tiled=True)
        panels[part] = panel.reshape(-1, plan["lanes"])
    slab = lax.all_to_all(slab, "row", split_axis=0, concat_axis=0, tiled=True)
    slab = lax.all_to_all(jnp.broadcast_to(slab, (col_count, *slab.shape)), "col", split_axis=0, concat_axis=0)
    slab = [slab[:, :, part] for part in range(CHUNKS)]
    slab[-1] = slab[-1].transpose(1, 0, 2, 3)
    slab = jnp.stack([part.reshape(-1, plan["slab_lanes"]) for part in slab]).reshape(-1, plan["slab_lanes"])
    left = left_side(2 * chunk, slab, slab_ids, slab_wanted)
    ordered = [put_in_order(plan, starts, ids, wanted, panel) for panel in panels[:-1]]
    return put_in_order(plan, starts, ids, wanted, panels[-1], left, ordered)


def solution(mesh):
    in_specs = (P(), P(("row", "col"), None, None, None), P(), P(), P(("row", "col")), P())
    out_specs = P(None, "row", "col")
    return jax.shard_map(
        on_device, mesh=mesh, in_specs=in_specs, out_specs=out_specs, check_vma=False
    )
```

```python
import math

import jax
import jax.numpy as jnp
import numpy as np
from jax import lax
from jax.experimental import pallas as pl
from jax.experimental.pallas import tpu as pltpu
from jax.sharding import PartitionSpec as P

ROWS_DEV = 256
LANES = 128
VMEM_BYTES = 56 * 1024 * 1024
HALF = 64
KEEP = 40
ROWS_K = 48
ORIGIN = KEEP // 2
PARTS = 3
CHUNKS = 2


def round_up(value, step):
    return -(-value // step) * step


def length_counts(points):
    freq = np.arange(points) - points // 2
    square = freq * freq
    lengths = square[:, None, None] + square[None, :, None] + square[None, None, :]
    return np.cumsum(np.bincount(lengths.reshape(-1)))


def column_order(top):
    freq = np.arange(KEEP) - ORIGIN
    first, second = np.meshgrid(freq, freq, indexing="ij")
    length = (first * first + second * second).reshape(-1)
    order = np.argsort(length, kind="stable")
    order = order[length[order] <= top]
    return first.reshape(-1)[order], second.reshape(-1)[order], length[order]


class Bucket:
    def __init__(self, ranges, column_length):
        self.pieces = []
        self.edges = {}
        offset = 0
        for low, high in ranges:
            begin = offset
            for index in range(KEEP):
                freq = index - ORIGIN
                start = int(np.searchsorted(column_length, low - freq * freq, side="left"))
                stop = int(np.searchsorted(column_length, high - freq * freq, side="right"))
                if stop > start:
                    self.pieces.append((index, start, stop, offset))
                    offset += stop - start
            for length in range(low, high + 1):
                self.edges[length] = (begin, offset)
        self.size = offset

    def ids(self, column_2, column_3, points, width):
        out = np.full((width,), -1, np.int32)
        for index, start, stop, offset in self.pieces:
            k1 = (index - ORIGIN) % points
            k2 = column_2[start:stop] % points
            k3 = column_3[start:stop] % points
            out[offset : offset + stop - start] = (k1 * points + k2) * points + k3
        return out


def length_ranges(cumulative, first, step, count):
    shell = lambda rank: int(np.searchsorted(cumulative, rank, side="right"))
    ranges, low = [], shell(first)
    for part in range(1, count):
        before, after = shell(first + part * step - 1), shell(first + part * step)
        if before == after:
            if low < before:
                ranges.append((low, before - 1))
            if low <= before:
                ranges.append((before, before))
        elif low <= before:
            ranges.append((low, before))
        low = before + 1
    high = shell(first + count * step - 1)
    if low <= high:
        ranges.append((low, high))
    return ranges


def make_plan(points, total, blocks, slab, slab_blocks):
    cumulative = length_counts(points)
    shell = lambda rank: int(np.searchsorted(cumulative, rank, side="right"))
    width, slab_width = total // blocks, slab // slab_blocks
    step = width // PARTS
    column_2, column_3, column_length = column_order(shell(total - 1))
    buckets = [Bucket(length_ranges(cumulative, n * width, step, PARTS), column_length) for n in range(blocks)]
    slabs = [Bucket(length_ranges(cumulative, n * slab_width, slab_width, 1), column_length) for n in range(slab_blocks)]
    slab_top = shell(slab - 1)
    lanes = round_up(max(bucket.size for bucket in buckets), LANES)
    slab_lanes = round_up(max(bucket.size for bucket in slabs), LANES)
    windows = np.zeros((blocks, PARTS, 2), np.int64)
    for n, bucket in enumerate(buckets):
        for part in range(PARTS):
            rank = n * width + part * step
            windows[n, part, 0] = bucket.edges[shell(rank)][0] // LANES * LANES
            windows[n, part, 1] = round_up(bucket.edges[shell(rank + step - 1)][1], LANES)
    window = int((windows[..., 1] - windows[..., 0]).max())
    return dict(
        buckets=buckets,
        slabs=slabs,
        slab_columns=int(np.searchsorted(column_length, slab_top, side="right")),
        slab_edge=math.isqrt(slab_top),
        lanes=lanes,
        slab_lanes=slab_lanes,
        window=window,
        starts=np.minimum(windows[..., 0], lanes - window).astype(np.int32),
        ids=np.stack([bucket.ids(column_2, column_3, points, lanes) for bucket in buckets]),
        slab_ids=np.stack([bucket.ids(column_2, column_3, points, slab_lanes) for bucket in slabs]),
        column_place=((column_3 + ORIGIN) * KEEP + column_2 + ORIGIN).astype(np.int32),
    )


def dft_table(points):
    n = np.arange(points)
    freq = np.arange(KEEP) - ORIGIN
    angle = (n[:, None] * freq[None, :] % points) * (2.0 * np.pi / points)
    cosine, sine = np.cos(angle), np.sin(angle)
    table = np.zeros((2 * HALF, 2 * HALF))
    table[:points, :KEEP] = cosine
    table[HALF : HALF + points, :KEEP] = sine
    table[:points, HALF : HALF + KEEP] = -sine
    table[HALF : HALF + points, HALF : HALF + KEEP] = cosine
    high = table.astype(jnp.bfloat16)
    low = (table - high.astype(np.float64)).astype(jnp.bfloat16)
    return np.block([[high, low], [high, np.zeros_like(low)]])


def split_parts(value):
    high = value.astype(jnp.bfloat16)
    low = (value - high.astype(jnp.float32)).astype(jnp.bfloat16)
    return high, low


def apply_table(parts, table):
    both = jnp.dot(parts, table, preferred_element_type=jnp.float32)
    return both[:, :LANES] + both[:, LANES:]


def stack_complex(turned, low_lanes):
    real, imag = turned[:KEEP], turned[HALF : HALF + KEEP]
    first = jnp.where(low_lanes, real, pltpu.roll(imag, HALF, 1))
    second = jnp.where(low_lanes, pltpu.roll(real, HALF, 1), imag)
    return jnp.concatenate([first, second], 0)


def pack_pieces(pieces, width, source, rows, lane, out):
    for tile in range(width // LANES):
        left, right = tile * LANES, (tile + 1) * LANES
        value = jnp.zeros((rows, LANES), jnp.float32)
        for index, start, stop, offset in pieces:
            begin, end = max(left, offset), min(right, offset + stop - start)
            while begin < end:
                at = start + begin - offset
                block = source(index, at // LANES)
                shift = (begin - at) % LANES
                if shift:
                    block = pltpu.roll(block, shift, 1)
                value = block if begin == left else jnp.where(lane >= begin - left, block, value)
                begin = min(end, begin + LANES - at % LANES)
        out(tile, value)


def slab_tiles(plan):
    first = (ORIGIN - plan["slab_edge"]) * KEEP // LANES
    last = round_up((ORIGIN + plan["slab_edge"] + 1) * KEEP, LANES) // LANES
    return first, last


def spectrum_kernel(plan, points, first_band, owner_ref, cond_energy_ref, val_energy_ref, val_ref, cond_ref, table_ref, plain_ref, weighted_ref,
                    cond_a, cond_b, middle, turned, last):
    band = pl.program_id(0)
    planes = 8
    lane = lax.broadcasted_iota(jnp.int32, (1, LANES), 1)
    low_lanes = lane < HALF
    depth = last.shape[0]

    @pl.when(band == 0)
    def _():
        scale = 1.0 / float(points) ** 1.5
        sign = jnp.where(low_lanes, scale, -scale)

        @pl.loop(0, points // planes)
        def _(block):
            rows = pl.ds(pl.multiple_of(block * planes * points, planes * points), planes * points)
            wave = cond_ref[0, pl.ds(block * planes, planes)].reshape(planes * points, LANES).astype(jnp.float32)
            cond_a[rows, :] = wave * scale
            cond_b[rows, :] = pltpu.roll(wave, HALF, 1) * sign

        last[KEEP * KEEP :, :] = jnp.zeros((depth - KEEP * KEEP, 2 * LANES), jnp.bfloat16)

    table = table_ref[...]
    step = planes * KEEP

    def first_axis(block):
        rows = slice(block * planes * points, (block + 1) * planes * points)
        wave = val_ref[0, block * planes : (block + 1) * planes].reshape(planes * points, LANES).astype(jnp.float32)
        other = pltpu.roll(wave, HALF, 1)
        density = jnp.where(low_lanes, wave, other) * cond_a[rows, :] + jnp.where(low_lanes, other, wave) * cond_b[rows, :]
        high, low = split_parts(density)
        field = apply_table(jnp.concatenate([high, low], 1), table)
        for pair in range(planes // 2):
            both = field[pair * 2 * points : (pair + 1) * 2 * points].T
            high, low = split_parts(stack_complex(both, low_lanes))
            at = slice((block * planes + pair * 2) * KEEP, (block * planes + pair * 2 + 2) * KEEP)
            middle[at, :LANES] = high
            middle[at, LANES:] = low

    def second_axis(block):
        rows = slice(block * step, (block + 1) * step)
        turned[rows, :] = apply_table(middle[rows, :], table)

    for block in range(points // planes):
        first_axis(block)
        if block:
            second_axis(block - 1)
    second_axis(points // planes - 1)

    for pair in range(KEEP // 2):
        both = jnp.concatenate(
            [turned[pl.ds(2 * pair, points, stride=KEEP), :], turned[pl.ds(2 * pair + 1, points, stride=KEEP), :]], 0
        ).T
        high, low = split_parts(stack_complex(both, low_lanes))
        at = slice(2 * pair * KEEP, (2 * pair + 2) * KEEP)
        last[at, :LANES] = high
        last[at, LANES:] = low

    pairs = val_energy_ref.shape[0] * cond_energy_ref.shape[0]
    gap = cond_energy_ref[owner_ref[0]] - val_energy_ref[first_band + band]
    weight = -2.0 / (math.sqrt(pairs) * jnp.full((1, LANES), gap, jnp.float32))
    slab_first, slab_last = slab_tiles(plan)
    for begin in range(0, depth // LANES, 5):
        end = min(begin + 5, depth // LANES)
        field = apply_table(last[begin * LANES : end * LANES, :], table)
        for tile in range(begin, end):
            turn = field[(tile - begin) * LANES : (tile - begin + 1) * LANES].T
            for part in range(2):
                value = turn[part * HALF : part * HALF + ROWS_K]
                plain_ref[part, 0, :, tile * LANES : (tile + 1) * LANES] = value.astype(jnp.bfloat16)
                if slab_first <= tile < slab_last:
                    lanes = slice((tile - slab_first) * LANES, (tile - slab_first + 1) * LANES)
                    weighted_ref[part, 0, :, lanes] = (weight * value).astype(jnp.bfloat16)


def spectra(plan, val_wave, cond_wave, energies, first_band, count):
    points = val_wave.shape[1]
    depth = round_up(KEEP * KEEP, LANES)
    slab_first, slab_last = slab_tiles(plan)
    slab_depth = (slab_last - slab_first) * LANES
    grid_rows = points * points
    kernel = lambda *refs: spectrum_kernel(plan, points, first_band, *refs)
    return pl.pallas_call(
        kernel,
        grid=(count,),
        in_specs=[
            pl.BlockSpec(memory_space=pltpu.SMEM),
            pl.BlockSpec(memory_space=pltpu.SMEM),
            pl.BlockSpec(memory_space=pltpu.SMEM),
            pl.BlockSpec((1, points, points, 2 * points), lambda v: (first_band + v, 0, 0, 0)),
            pl.BlockSpec((1, points, points, 2 * points), lambda v: (0, 0, 0, 0)),
            pl.BlockSpec((4 * HALF, 4 * HALF), lambda v: (0, 0)),
        ],
        out_specs=[
            pl.BlockSpec((2, 1, ROWS_K, depth), lambda v: (0, v, 0, 0)),
            pl.BlockSpec((2, 1, ROWS_K, slab_depth), lambda v: (0, v, 0, 0)),
        ],
        out_shape=[
            jax.ShapeDtypeStruct((2, count, ROWS_K, depth), jnp.bfloat16),
            jax.ShapeDtypeStruct((2, count, ROWS_K, slab_depth), jnp.bfloat16),
        ],
        scratch_shapes=[
            pltpu.VMEM((grid_rows, LANES), jnp.float32),
            pltpu.VMEM((grid_rows, LANES), jnp.float32),
            pltpu.VMEM((points * KEEP, 2 * LANES), jnp.bfloat16),
            pltpu.VMEM((points * KEEP, LANES), jnp.float32),
            pltpu.VMEM((depth, 2 * LANES), jnp.bfloat16),
        ],
        compiler_params=pltpu.CompilerParams(vmem_limit_bytes=VMEM_BYTES, dimension_semantics=("arbitrary",)),
        cost_estimate=pl.CostEstimate(flops=count, bytes_accessed=count, transcendentals=0),
        name="spectra",
    )(*energies, val_wave, cond_wave, jnp.asarray(dft_table(points)))


def pack_kernel(plan, groups, place_ref, *refs):
    plains, weighteds = refs[:groups], refs[groups : 2 * groups]
    send_ref, slab_ref, sorter, plain_sorted, weighted_sorted = refs[2 * groups :]
    depth, columns = sorter.shape
    count = 2 * sum(plain.shape[1] for plain in plains)
    lane = lax.broadcasted_iota(jnp.int32, (1, LANES), 1)
    for begin in range(0, depth, LANES):
        at = lax.broadcasted_iota(jnp.int32, (LANES, columns), 0) + begin
        sorter[begin : begin + LANES, :] = jnp.where(at == place_ref[...], 1.0, 0.0).astype(jnp.bfloat16)

    def sort_rows(parts, which, target):
        rows = jnp.concatenate([part[n] for n in range(2) for part in parts], 0)
        rows = rows.reshape(count * ROWS_K, rows.shape[2])
        value = jnp.dot(rows, which, preferred_element_type=jnp.float32)
        for tile in range(target.shape[0]):
            target[tile] = value[:, tile * LANES : (tile + 1) * LANES]

    slab_first, slab_last = slab_tiles(plan)
    sort_rows(plains, sorter[...], plain_sorted)
    sort_rows(weighteds, sorter[slab_first * LANES : slab_last * LANES, : weighted_sorted.shape[0] * LANES], weighted_sorted)

    def plain_at(index, tile):
        return plain_sorted[tile, pl.ds(index, count, stride=ROWS_K), :]

    def weighted_at(index, tile):
        return weighted_sorted[tile, pl.ds(index, count, stride=ROWS_K), :]

    for block, bucket in enumerate(plan["buckets"]):

        def keep(tile, value):
            send_ref[block, :, tile * LANES : (tile + 1) * LANES] = value.astype(jnp.bfloat16)

        pack_pieces(bucket.pieces, plan["lanes"], plain_at, count, lane, keep)
    for block, bucket in enumerate(plan["slabs"]):

        def keep_slab(tile, value):
            slab_ref[block, :, tile * LANES : (tile + 1) * LANES] = value.astype(jnp.bfloat16)

        pack_pieces(bucket.pieces, plan["slab_lanes"], weighted_at, count, lane, keep_slab)


def packed(plan, plains, weighteds):
    depth = plains[0].shape[3]
    count = 2 * sum(plain.shape[1] for plain in plains)
    columns = round_up(plan["column_place"].shape[0], 256)
    slab_columns = round_up(plan["slab_columns"], LANES)
    place = np.full((1, columns), -1, np.int32)
    place[0, : plan["column_place"].shape[0]] = plan["column_place"]
    kernel = lambda *refs: pack_kernel(plan, len(plains), *refs)
    vmem = pl.BlockSpec(memory_space=pltpu.VMEM)
    send_shape = (len(plan["buckets"]), count, plan["lanes"])
    slab_shape = (len(plan["slabs"]), count, plan["slab_lanes"])
    return pl.pallas_call(
        kernel,
        in_specs=[vmem] * (1 + 2 * len(plains)),
        out_specs=[vmem] * 2,
        out_shape=[jax.ShapeDtypeStruct(send_shape, jnp.bfloat16), jax.ShapeDtypeStruct(slab_shape, jnp.bfloat16)],
        scratch_shapes=[
            pltpu.VMEM((depth, columns), jnp.bfloat16),
            pltpu.VMEM((columns // LANES, count * ROWS_K, LANES), jnp.float32),
            pltpu.VMEM((slab_columns // LANES, count * ROWS_K, LANES), jnp.float32),
        ],
        compiler_params=pltpu.CompilerParams(vmem_limit_bytes=VMEM_BYTES),
        cost_estimate=pl.CostEstimate(flops=1, bytes_accessed=1, transcendentals=0),
        name="pack",
    )(jnp.asarray(place), *plains, *weighteds)


def one_hot(ids_ref, begin, wanted):
    ids = jnp.broadcast_to(ids_ref[:, pl.ds(begin, LANES)], (LANES, LANES)).T
    ids = jnp.concatenate([ids] * (wanted.shape[1] // LANES), 1)
    return jnp.where(ids == wanted, 1.0, 0.0).astype(jnp.bfloat16)


def left_kernel(group, slab_ref, slab_ids_ref, slab_wanted_ref, left_ref):
    rows = slab_wanted_ref.shape[1]
    choice = jnp.concatenate(
        [one_hot(slab_ids_ref, begin, slab_wanted_ref[...]) for begin in range(0, slab_ids_ref.shape[1], LANES)], 0
    )
    chosen = jnp.dot(slab_ref[...], choice, preferred_element_type=jnp.float32)
    lane = lax.broadcasted_iota(jnp.int32, (1, LANES), 1)
    real_lanes = lane % group < group // 2
    for begin in range(0, chosen.shape[0], LANES):
        turned = chosen[begin : begin + LANES].T
        after = pltpu.roll(turned, LANES - group // 2, 1)
        before = pltpu.roll(turned, group // 2, 1)
        left_ref[:rows, begin : begin + LANES] = turned.astype(jnp.bfloat16)
        left_ref[rows:, begin : begin + LANES] = jnp.where(real_lanes, after, -before).astype(jnp.bfloat16)


def left_side(group, slab, slab_ids, slab_wanted):
    vmem = pl.BlockSpec(memory_space=pltpu.VMEM)
    return pl.pallas_call(
        lambda *refs: left_kernel(group, *refs),
        in_specs=[vmem] * 3,
        out_specs=vmem,
        out_shape=jax.ShapeDtypeStruct((2 * slab_wanted.shape[1], slab.shape[0]), jnp.bfloat16),
        compiler_params=pltpu.CompilerParams(vmem_limit_bytes=VMEM_BYTES),
        cost_estimate=pl.CostEstimate(flops=1, bytes_accessed=1, transcendentals=0),
        name="left_side",
    )(slab, slab_ids, slab_wanted)


def order_kernel(starts_ref, ids_ref, wanted_ref, panel_ref, out_ref, hot):
    start = pl.multiple_of(starts_ref[pl.program_id(0)], LANES)
    wanted = wanted_ref[...]
    window = hot.shape[0]
    for begin in range(0, window, LANES):
        hot[begin : begin + LANES, :] = one_hot(ids_ref, pl.multiple_of(start + begin, LANES), wanted)
    ordered = jnp.dot(panel_ref[:, pl.ds(start, window)], hot[...], preferred_element_type=jnp.float32)
    out_ref[...] = ordered.astype(jnp.bfloat16)


def put_in_order(plan, starts, ids, wanted, panel):
    columns = wanted.shape[1]
    block = columns // PARTS
    whole = lambda array: pl.BlockSpec(array.shape, lambda n: (0,) * array.ndim)
    return pl.pallas_call(
        order_kernel,
        grid=(PARTS,),
        in_specs=[
            pl.BlockSpec(memory_space=pltpu.SMEM),
            whole(ids),
            pl.BlockSpec((1, block), lambda n: (0, n)),
            whole(panel),
        ],
        out_specs=pl.BlockSpec((panel.shape[0], block), lambda n: (0, n)),
        out_shape=jax.ShapeDtypeStruct((panel.shape[0], columns), jnp.bfloat16),
        scratch_shapes=[pltpu.VMEM((plan["window"], block), jnp.bfloat16)],
        compiler_params=pltpu.CompilerParams(vmem_limit_bytes=VMEM_BYTES, dimension_semantics=("arbitrary",)),
        cost_estimate=pl.CostEstimate(flops=1, bytes_accessed=1, transcendentals=0),
        name="in_order",
    )(starts, ids, wanted, panel)


def product_kernel(left_ref, *refs):
    *ordered, out_ref = refs
    rows = out_ref.shape[1]
    right = jnp.concatenate([part[...] for part in ordered], 0)
    chi = jnp.dot(left_ref[...], right, preferred_element_type=jnp.float32)
    out_ref[0] = chi[:rows]
    out_ref[1] = chi[rows:]


def product(left, ordered):
    rows, columns = left.shape[0] // 2, ordered[0].shape[1]
    block = columns // (2 * PARTS) // LANES * LANES
    return pl.pallas_call(
        product_kernel,
        grid=(pl.cdiv(columns, block),),
        in_specs=[pl.BlockSpec(left.shape, lambda n: (0, 0))]
        + [pl.BlockSpec((part.shape[0], block), lambda n: (0, n)) for part in ordered],
        out_specs=pl.BlockSpec((2, rows, block), lambda n: (0, 0, n)),
        out_shape=jax.ShapeDtypeStruct((2, rows, columns), jnp.float32),
        compiler_params=pltpu.CompilerParams(vmem_limit_bytes=VMEM_BYTES, dimension_semantics=("arbitrary",)),
        cost_estimate=pl.CostEstimate(flops=1, bytes_accessed=1, transcendentals=0),
        name="product",
    )(left, *ordered)


def on_device(val_wave, cond_wave, val_energy, cond_energy, band_owner, grid_map):
    bands, points = val_wave.shape[0], val_wave.shape[1]
    row_count = lax.axis_size("row")
    col_count = lax.axis_size("col")
    col, row = lax.axis_index("col"), lax.axis_index("row")
    plan = make_plan(points, grid_map.shape[0], col_count, ROWS_DEV * row_count, row_count)
    width = grid_map.shape[0] // col_count
    starts = lax.dynamic_index_in_dim(jnp.asarray(plan["starts"]), col, 0, keepdims=False)
    ids = lax.dynamic_slice(jnp.asarray(plan["ids"]), (col, 0), (1, plan["lanes"]))
    slab_ids = lax.dynamic_slice(jnp.asarray(plan["slab_ids"]), (row, 0), (1, plan["slab_lanes"]))
    wanted = lax.dynamic_slice(grid_map, (col * width,), (width,))[None]
    slab_wanted = lax.dynamic_slice(grid_map, (row * ROWS_DEV,), (ROWS_DEV,))[None]
    chunk = bands // CHUNKS
    energies = (band_owner, cond_energy, val_energy)
    panels, slabs = [], []
    for part in range(CHUNKS):
        plain, weighted = spectra(plan, val_wave, cond_wave, energies, part * chunk, chunk)
        send, slab = packed(plan, [plain], [weighted])
        slabs.append(slab)
        if part < CHUNKS - 1:
            send, cond_wave = lax.optimization_barrier((send, cond_wave))
            panels.append(lax.all_gather(send, "row", axis=1))
        else:
            mine = lax.all_to_all(send, "col", split_axis=0, concat_axis=0, tiled=True).reshape(-1, plan["lanes"])
            mine = put_in_order(plan, starts, ids, wanted, mine)
            last = lax.all_gather(mine, "row", axis=0, tiled=True)
    slab, _ = lax.optimization_barrier((jnp.stack(slabs, 1), mine))
    slab = lax.all_to_all(slab, "row", split_axis=0, concat_axis=0, tiled=True)
    slab = lax.all_to_all(jnp.broadcast_to(slab, (col_count, *slab.shape)), "col", split_axis=0, concat_axis=0)
    *panels, slab = lax.optimization_barrier((*panels, slab))
    slab = [slab[:, :, part] for part in range(CHUNKS)]
    slab[-1] = slab[-1].transpose(1, 0, 2, 3)
    slab = jnp.stack([part.reshape(-1, plan["slab_lanes"]) for part in slab]).reshape(-1, plan["slab_lanes"])
    left = left_side(2 * chunk, slab, slab_ids, slab_wanted)
    ordered = []
    for panel in panels:
        panel = lax.all_to_all(panel, "col", split_axis=0, concat_axis=0, tiled=True)
        ordered.append(put_in_order(plan, starts, ids, wanted, panel.reshape(-1, plan["lanes"])))
    return product(left, [*ordered, last])


def solution(mesh):
    in_specs = (P(), P(("row", "col"), None, None, None), P(), P(), P(("row", "col")), P())
    out_specs = P(None, "row", "col")
    return jax.shard_map(
        on_device, mesh=mesh, in_specs=in_specs, out_specs=out_specs, check_vma=False
    )
```

```python
import math

import jax
import jax.numpy as jnp
import numpy as np
from jax import lax
from jax.experimental import pallas as pl
from jax.experimental.pallas import tpu as pltpu
from jax.sharding import PartitionSpec as P

ROWS_DEV = 256
LANES = 128
VMEM_BYTES = 56 * 1024 * 1024
HALF = 64
KEEP = 40
ROWS_K = 48
ORIGIN = KEEP // 2
PARTS = 3
CHUNKS = 2


def round_up(value, step):
    return -(-value // step) * step


def length_counts(points):
    freq = np.arange(points) - points // 2
    square = freq * freq
    lengths = square[:, None, None] + square[None, :, None] + square[None, None, :]
    return np.cumsum(np.bincount(lengths.reshape(-1)))


def column_order(top):
    freq = np.arange(KEEP) - ORIGIN
    first, second = np.meshgrid(freq, freq, indexing="ij")
    length = (first * first + second * second).reshape(-1)
    order = np.argsort(length, kind="stable")
    order = order[length[order] <= top]
    return first.reshape(-1)[order], second.reshape(-1)[order], length[order]


class Bucket:
    def __init__(self, ranges, column_length):
        self.pieces = []
        self.edges = {}
        offset = 0
        for low, high in ranges:
            begin = offset
            for index in range(KEEP):
                freq = index - ORIGIN
                start = int(np.searchsorted(column_length, low - freq * freq, side="left"))
                stop = int(np.searchsorted(column_length, high - freq * freq, side="right"))
                if stop > start:
                    self.pieces.append((index, start, stop, offset))
                    offset += stop - start
            for length in range(low, high + 1):
                self.edges[length] = (begin, offset)
        self.size = offset

    def ids(self, column_2, column_3, points, width):
        out = np.full((width,), -1, np.int32)
        for index, start, stop, offset in self.pieces:
            k1 = (index - ORIGIN) % points
            k2 = column_2[start:stop] % points
            k3 = column_3[start:stop] % points
            out[offset : offset + stop - start] = (k1 * points + k2) * points + k3
        return out


def length_ranges(cumulative, first, step, count):
    shell = lambda rank: int(np.searchsorted(cumulative, rank, side="right"))
    ranges, low = [], shell(first)
    for part in range(1, count):
        before, after = shell(first + part * step - 1), shell(first + part * step)
        if before == after:
            if low < before:
                ranges.append((low, before - 1))
            if low <= before:
                ranges.append((before, before))
        elif low <= before:
            ranges.append((low, before))
        low = before + 1
    high = shell(first + count * step - 1)
    if low <= high:
        ranges.append((low, high))
    return ranges


def make_plan(points, total, blocks, slab, slab_blocks):
    cumulative = length_counts(points)
    shell = lambda rank: int(np.searchsorted(cumulative, rank, side="right"))
    width, slab_width = total // blocks, slab // slab_blocks
    step = width // PARTS
    column_2, column_3, column_length = column_order(shell(total - 1))
    buckets = [Bucket(length_ranges(cumulative, n * width, step, PARTS), column_length) for n in range(blocks)]
    slabs = [Bucket(length_ranges(cumulative, n * slab_width, slab_width, 1), column_length) for n in range(slab_blocks)]
    slab_top = shell(slab - 1)
    lanes = round_up(max(bucket.size for bucket in buckets), LANES)
    slab_lanes = round_up(max(bucket.size for bucket in slabs), LANES)
    windows = np.zeros((blocks, PARTS, 2), np.int64)
    for n, bucket in enumerate(buckets):
        for part in range(PARTS):
            rank = n * width + part * step
            windows[n, part, 0] = bucket.edges[shell(rank)][0] // LANES * LANES
            windows[n, part, 1] = round_up(bucket.edges[shell(rank + step - 1)][1], LANES)
    window = int((windows[..., 1] - windows[..., 0]).max())
    return dict(
        buckets=buckets,
        slabs=slabs,
        slab_columns=int(np.searchsorted(column_length, slab_top, side="right")),
        slab_edge=math.isqrt(slab_top),
        lanes=lanes,
        slab_lanes=slab_lanes,
        window=window,
        starts=np.minimum(windows[..., 0], lanes - window).astype(np.int32),
        ids=np.stack([bucket.ids(column_2, column_3, points, lanes) for bucket in buckets]),
        slab_ids=np.stack([bucket.ids(column_2, column_3, points, slab_lanes) for bucket in slabs]),
        column_place=((column_3 + ORIGIN) * KEEP + column_2 + ORIGIN).astype(np.int32),
    )


def dft_table(points):
    n = np.arange(points)
    freq = np.arange(KEEP) - ORIGIN
    angle = (n[:, None] * freq[None, :] % points) * (2.0 * np.pi / points)
    cosine, sine = np.cos(angle), np.sin(angle)
    table = np.zeros((2 * HALF, 2 * HALF))
    table[:points, :KEEP] = cosine
    table[HALF : HALF + points, :KEEP] = sine
    table[:points, HALF : HALF + KEEP] = -sine
    table[HALF : HALF + points, HALF : HALF + KEEP] = cosine
    high = table.astype(jnp.bfloat16)
    low = (table - high.astype(np.float64)).astype(jnp.bfloat16)
    return np.block([[high, low], [high, np.zeros_like(low)]])


def split_parts(value):
    high = value.astype(jnp.bfloat16)
    low = (value - high.astype(jnp.float32)).astype(jnp.bfloat16)
    return high, low


def apply_table(parts, table):
    both = jnp.dot(parts, table, preferred_element_type=jnp.float32)
    return both[:, :LANES] + both[:, LANES:]


def stack_complex(turned, low_lanes):
    real, imag = turned[:KEEP], turned[HALF : HALF + KEEP]
    first = jnp.where(low_lanes, real, pltpu.roll(imag, HALF, 1))
    second = jnp.where(low_lanes, pltpu.roll(real, HALF, 1), imag)
    return jnp.concatenate([first, second], 0)


def pack_pieces(pieces, width, source, rows, lane, out):
    for tile in range(width // LANES):
        left, right = tile * LANES, (tile + 1) * LANES
        value = jnp.zeros((rows, LANES), jnp.float32)
        for index, start, stop, offset in pieces:
            begin, end = max(left, offset), min(right, offset + stop - start)
            while begin < end:
                at = start + begin - offset
                block = source(index, at // LANES)
                shift = (begin - at) % LANES
                if shift:
                    block = pltpu.roll(block, shift, 1)
                value = block if begin == left else jnp.where(lane >= begin - left, block, value)
                begin = min(end, begin + LANES - at % LANES)
        out(tile, value)


def slab_tiles(plan):
    first = (ORIGIN - plan["slab_edge"]) * KEEP // LANES
    last = round_up((ORIGIN + plan["slab_edge"] + 1) * KEEP, LANES) // LANES
    return first, last


def spectrum_kernel(plan, points, first_band, owner_ref, cond_energy_ref, val_energy_ref, val_ref, cond_ref, table_ref, plain_ref, weighted_ref,
                    cond_a, cond_b, middle, turned, last):
    band = pl.program_id(0)
    planes = 8
    lane = lax.broadcasted_iota(jnp.int32, (1, LANES), 1)
    low_lanes = lane < HALF
    depth = last.shape[0]

    @pl.when(band == 0)
    def _():
        scale = 1.0 / float(points) ** 1.5
        sign = jnp.where(low_lanes, scale, -scale)

        @pl.loop(0, points // planes)
        def _(block):
            rows = pl.ds(pl.multiple_of(block * planes * points, planes * points), planes * points)
            wave = cond_ref[0, pl.ds(block * planes, planes)].reshape(planes * points, LANES).astype(jnp.float32)
            cond_a[rows, :] = wave * scale
            cond_b[rows, :] = pltpu.roll(wave, HALF, 1) * sign

        last[KEEP * KEEP :, :] = jnp.zeros((depth - KEEP * KEEP, 2 * LANES), jnp.bfloat16)

    table = table_ref[...]
    step = planes * KEEP

    def first_axis(block):
        rows = pl.ds(pl.multiple_of(block * planes * points, planes * points), planes * points)
        wave = val_ref[0, pl.ds(block * planes, planes)].reshape(planes * points, LANES).astype(jnp.float32)
        other = pltpu.roll(wave, HALF, 1)
        density = jnp.where(low_lanes, wave, other) * cond_a[rows, :] + jnp.where(low_lanes, other, wave) * cond_b[rows, :]
        high, low = split_parts(density)
        field = apply_table(jnp.concatenate([high, low], 1), table)
        for pair in range(planes // 2):
            both = field[pair * 2 * points : (pair + 1) * 2 * points].T
            high, low = split_parts(stack_complex(both, low_lanes))
            at = pl.ds(pl.multiple_of((block * planes + pair * 2) * KEEP, 2 * KEEP), 2 * KEEP)
            middle[at, :LANES] = high
            middle[at, LANES:] = low

    def second_axis(block):
        rows = pl.ds(pl.multiple_of(block * step, step), step)
        turned[rows, :] = apply_table(middle[rows, :], table)

    blocks = points // planes

    @pl.loop(0, blocks // 2)
    def _(turn):
        for part in range(2):
            second_axis((2 * turn - 2 + part + blocks) % blocks)
        for part in range(2):
            first_axis(2 * turn + part)

    @pl.loop(blocks - 2, blocks)
    def _(block):
        second_axis(block)

    @pl.loop(0, KEEP // 8)
    def _(turn):
        for part in range(4):
            pair = turn * 4 + part
            both = jnp.concatenate(
                [turned[pl.ds(2 * pair, points, stride=KEEP), :], turned[pl.ds(2 * pair + 1, points, stride=KEEP), :]], 0
            ).T
            high, low = split_parts(stack_complex(both, low_lanes))
            at = pl.ds(pl.multiple_of(pair * 2 * KEEP, 2 * KEEP), 2 * KEEP)
            last[at, :LANES] = high
            last[at, LANES:] = low

    pairs = val_energy_ref.shape[0] * cond_energy_ref.shape[0]
    gap = cond_energy_ref[owner_ref[0]] - val_energy_ref[first_band + band]
    weight = -2.0 / (math.sqrt(pairs) * jnp.full((1, LANES), gap, jnp.float32))

    @pl.loop(0, depth // (2 * LANES))
    def _(turn):
        field = apply_table(last[pl.ds(pl.multiple_of(turn * 2 * LANES, 2 * LANES), 2 * LANES), :], table)
        for half in range(2):
            turn_lanes = pl.ds(pl.multiple_of(turn * 2 * LANES, 2 * LANES) + half * LANES, LANES)
            spectrum = field[half * LANES : (half + 1) * LANES].T
            for part in range(2):
                value = spectrum[part * HALF : part * HALF + ROWS_K]
                plain_ref[part, 0, :, turn_lanes] = value.astype(jnp.bfloat16)
                weighted_ref[part, 0, :, turn_lanes] = (weight * value).astype(jnp.bfloat16)


def spectra(plan, val_wave, cond_wave, energies, first_band, count):
    points = val_wave.shape[1]
    depth = round_up(KEEP * KEEP, 2 * LANES)
    grid_rows = points * points
    kernel = lambda *refs: spectrum_kernel(plan, points, first_band, *refs)
    return pl.pallas_call(
        kernel,
        grid=(count,),
        in_specs=[
            pl.BlockSpec(memory_space=pltpu.SMEM),
            pl.BlockSpec(memory_space=pltpu.SMEM),
            pl.BlockSpec(memory_space=pltpu.SMEM),
            pl.BlockSpec((1, points, points, 2 * points), lambda v: (first_band + v, 0, 0, 0)),
            pl.BlockSpec((1, points, points, 2 * points), lambda v: (0, 0, 0, 0)),
            pl.BlockSpec((4 * HALF, 4 * HALF), lambda v: (0, 0)),
        ],
        out_specs=[
            pl.BlockSpec((2, 1, ROWS_K, depth), lambda v: (0, v, 0, 0)),
            pl.BlockSpec((2, 1, ROWS_K, depth), lambda v: (0, v, 0, 0)),
        ],
        out_shape=[
            jax.ShapeDtypeStruct((2, count, ROWS_K, depth), jnp.bfloat16),
            jax.ShapeDtypeStruct((2, count, ROWS_K, depth), jnp.bfloat16),
        ],
        scratch_shapes=[
            pltpu.VMEM((grid_rows, LANES), jnp.float32),
            pltpu.VMEM((grid_rows, LANES), jnp.float32),
            pltpu.VMEM((points * KEEP, 2 * LANES), jnp.bfloat16),
            pltpu.VMEM((points * KEEP, LANES), jnp.float32),
            pltpu.VMEM((depth, 2 * LANES), jnp.bfloat16),
        ],
        compiler_params=pltpu.CompilerParams(vmem_limit_bytes=VMEM_BYTES, dimension_semantics=("arbitrary",)),
        cost_estimate=pl.CostEstimate(flops=count, bytes_accessed=count, transcendentals=0),
        name="spectra",
    )(*energies, val_wave, cond_wave, jnp.asarray(dft_table(points)))


def pack_kernel(plan, place_ref, plain_ref, weighted_ref, *refs):
    *slab_refs, send_ref, slab_ref, sorter, plain_sorted, weighted_sorted = refs
    depth, columns = sorter.shape
    count = 2 * plain_ref.shape[1]
    lane = lax.broadcasted_iota(jnp.int32, (1, LANES), 1)
    for begin in range(0, depth, LANES):
        at = lax.broadcasted_iota(jnp.int32, (LANES, columns), 0) + begin
        sorter[begin : begin + LANES, :] = jnp.where(at == place_ref[...], 1.0, 0.0).astype(jnp.bfloat16)

    def sort_rows(rows, which, target):
        value = jnp.dot(rows.reshape(count * ROWS_K, rows.shape[3]), which, preferred_element_type=jnp.float32)
        for tile in range(target.shape[0]):
            target[tile] = value[:, tile * LANES : (tile + 1) * LANES]

    slab_first, slab_last = slab_tiles(plan)
    slab_places = slice(slab_first * LANES, slab_last * LANES)
    sort_rows(plain_ref[...], sorter[...], plain_sorted)
    sort_rows(weighted_ref[:, :, :, slab_places], sorter[slab_places, : weighted_sorted.shape[0] * LANES], weighted_sorted)

    def plain_at(index, tile):
        return plain_sorted[tile, pl.ds(index, count, stride=ROWS_K), :]

    def weighted_at(index, tile):
        return weighted_sorted[tile, pl.ds(index, count, stride=ROWS_K), :]

    for block, bucket in enumerate(plan["buckets"]):

        def keep(tile, value):
            send_ref[block, :, tile * LANES : (tile + 1) * LANES] = value.astype(jnp.bfloat16)

        pack_pieces(bucket.pieces, plan["lanes"], plain_at, count, lane, keep)
    for block, bucket in enumerate(plan["slabs"]):

        def keep_slab(tile, value):
            slab_ref[block, :, tile * LANES : (tile + 1) * LANES] = value.astype(jnp.bfloat16)

        pack_pieces(bucket.pieces, plan["slab_lanes"], weighted_at, count, lane, keep_slab)
    if slab_refs:
        lanes = plan["slab_lanes"]
        for part, ref in enumerate([*slab_refs, slab_ref]):
            for row in range(len(plan["slabs"])):
                at = plan["lanes"] + (part * len(plan["slabs"]) + row) * lanes
                for block in range(len(plan["buckets"])):
                    send_ref[block, :, at : at + lanes] = ref[row]


def packed(plan, plain, weighted, slabs):
    depth, count = plain.shape[3], 2 * plain.shape[1]
    columns = round_up(plan["column_place"].shape[0], 256)
    slab_columns = round_up(plan["slab_columns"], LANES)
    place = np.full((1, columns), -1, np.int32)
    place[0, : plan["column_place"].shape[0]] = plan["column_place"]
    vmem = pl.BlockSpec(memory_space=pltpu.VMEM)
    slab_shape = (len(plan["slabs"]), count, plan["slab_lanes"])
    riders = (len(slabs) + 1) * len(plan["slabs"]) * plan["slab_lanes"] if slabs else 0
    send_shape = (len(plan["buckets"]), count, plan["lanes"] + riders)
    return pl.pallas_call(
        lambda *refs: pack_kernel(plan, *refs),
        in_specs=[vmem] * (3 + len(slabs)),
        out_specs=[vmem] * 2,
        out_shape=[jax.ShapeDtypeStruct(send_shape, jnp.bfloat16), jax.ShapeDtypeStruct(slab_shape, jnp.bfloat16)],
        scratch_shapes=[
            pltpu.VMEM((depth, columns), jnp.bfloat16),
            pltpu.VMEM((columns // LANES, count * ROWS_K, LANES), jnp.float32),
            pltpu.VMEM((slab_columns // LANES, count * ROWS_K, LANES), jnp.float32),
        ],
        compiler_params=pltpu.CompilerParams(vmem_limit_bytes=VMEM_BYTES),
        cost_estimate=pl.CostEstimate(flops=1, bytes_accessed=1, transcendentals=0),
        name="pack",
    )(jnp.asarray(place), plain, weighted, *slabs)


def one_hot(ids_ref, begin, wanted):
    ids = jnp.broadcast_to(ids_ref[:, pl.ds(begin, LANES)], (LANES, LANES)).T
    ids = jnp.concatenate([ids] * (wanted.shape[1] // LANES), 1)
    return jnp.where(ids == wanted, 1.0, 0.0).astype(jnp.bfloat16)


def left_kernel(slab_ref, slab_ids_ref, slab_wanted_ref, left_ref):
    rows = slab_wanted_ref.shape[1]
    row_count, chunks, col_count, group, _ = slab_ref.shape
    order = [(row, part, col) for part in range(chunks - 1) for col in range(col_count) for row in range(row_count)]
    order += [(row, chunks - 1, col) for row in range(row_count) for col in range(col_count)]
    slab = jnp.concatenate([slab_ref[place].astype(jnp.float32) for place in order], 0).astype(jnp.bfloat16)
    choice = jnp.concatenate(
        [one_hot(slab_ids_ref, begin, slab_wanted_ref[...]) for begin in range(0, slab_ids_ref.shape[1], LANES)], 0
    )
    chosen = jnp.dot(slab, choice, preferred_element_type=jnp.float32)
    lane = lax.broadcasted_iota(jnp.int32, (1, LANES), 1)
    real_lanes = lane % group < group // 2
    for begin in range(0, chosen.shape[0], LANES):
        turned = chosen[begin : begin + LANES].T
        after = pltpu.roll(turned, LANES - group // 2, 1)
        before = pltpu.roll(turned, group // 2, 1)
        left_ref[:rows, begin : begin + LANES] = turned.astype(jnp.bfloat16)
        left_ref[rows:, begin : begin + LANES] = jnp.where(real_lanes, after, -before).astype(jnp.bfloat16)


def left_side(slab, slab_ids, slab_wanted):
    vmem = pl.BlockSpec(memory_space=pltpu.VMEM)
    return pl.pallas_call(
        left_kernel,
        in_specs=[vmem] * 3,
        out_specs=vmem,
        out_shape=jax.ShapeDtypeStruct((2 * slab_wanted.shape[1], math.prod(slab.shape[:4])), jnp.bfloat16),
        compiler_params=pltpu.CompilerParams(vmem_limit_bytes=VMEM_BYTES),
        cost_estimate=pl.CostEstimate(flops=1, bytes_accessed=1, transcendentals=0),
        name="left_side",
    )(slab, slab_ids, slab_wanted)


def order_kernel(starts_ref, ids_ref, wanted_ref, panel_ref, out_ref, hot):
    start = pl.multiple_of(starts_ref[pl.program_id(0)], LANES)
    wanted = wanted_ref[...]
    window = hot.shape[0]
    for begin in range(0, window, LANES):
        hot[begin : begin + LANES, :] = one_hot(ids_ref, pl.multiple_of(start + begin, LANES), wanted)
    ordered = jnp.dot(panel_ref[:, pl.ds(start, window)], hot[...], preferred_element_type=jnp.float32)
    out_ref[...] = ordered.astype(jnp.bfloat16)


def put_in_order(plan, starts, ids, wanted, panel):
    columns = wanted.shape[1]
    block = columns // PARTS
    whole = lambda array: pl.BlockSpec(array.shape, lambda n: (0,) * array.ndim)
    return pl.pallas_call(
        order_kernel,
        grid=(PARTS,),
        in_specs=[
            pl.BlockSpec(memory_space=pltpu.SMEM),
            whole(ids),
            pl.BlockSpec((1, block), lambda n: (0, n)),
            whole(panel),
        ],
        out_specs=pl.BlockSpec((panel.shape[0], block), lambda n: (0, n)),
        out_shape=jax.ShapeDtypeStruct((panel.shape[0], columns), jnp.bfloat16),
        scratch_shapes=[pltpu.VMEM((plan["window"], block), jnp.bfloat16)],
        compiler_params=pltpu.CompilerParams(vmem_limit_bytes=VMEM_BYTES, dimension_semantics=("arbitrary",)),
        cost_estimate=pl.CostEstimate(flops=1, bytes_accessed=1, transcendentals=0),
        name="in_order",
    )(starts, ids, wanted, panel)


def product_kernel(left_ref, *refs):
    *ordered, out_ref = refs
    rows = out_ref.shape[1]
    right = jnp.concatenate([part[...] for part in ordered], 0)
    chi = jnp.dot(left_ref[...], right, preferred_element_type=jnp.float32)
    out_ref[0] = chi[:rows]
    out_ref[1] = chi[rows:]


def product(left, ordered):
    rows, columns = left.shape[0] // 2, ordered[0].shape[1]
    block = columns // (2 * PARTS) // LANES * LANES
    return pl.pallas_call(
        product_kernel,
        grid=(pl.cdiv(columns, block),),
        in_specs=[pl.BlockSpec(left.shape, lambda n: (0, 0))]
        + [pl.BlockSpec((part.shape[0], block), lambda n: (0, n)) for part in ordered],
        out_specs=pl.BlockSpec((2, rows, block), lambda n: (0, 0, n)),
        out_shape=jax.ShapeDtypeStruct((2, rows, columns), jnp.float32),
        compiler_params=pltpu.CompilerParams(vmem_limit_bytes=VMEM_BYTES, dimension_semantics=("arbitrary",)),
        cost_estimate=pl.CostEstimate(flops=1, bytes_accessed=1, transcendentals=0),
        name="product",
    )(left, *ordered)


def on_device(val_wave, cond_wave, val_energy, cond_energy, band_owner, grid_map):
    bands, points = val_wave.shape[0], val_wave.shape[1]
    row_count = lax.axis_size("row")
    col_count = lax.axis_size("col")
    col, row = lax.axis_index("col"), lax.axis_index("row")
    plan = make_plan(points, grid_map.shape[0], col_count, ROWS_DEV * row_count, row_count)
    width = grid_map.shape[0] // col_count
    starts = lax.dynamic_index_in_dim(jnp.asarray(plan["starts"]), col, 0, keepdims=False)
    ids = lax.dynamic_slice(jnp.asarray(plan["ids"]), (col, 0), (1, plan["lanes"]))
    slab_ids = lax.dynamic_slice(jnp.asarray(plan["slab_ids"]), (row, 0), (1, plan["slab_lanes"]))
    wanted = lax.dynamic_slice(grid_map, (col * width,), (width,))[None]
    slab_wanted = lax.dynamic_slice(grid_map, (row * ROWS_DEV,), (ROWS_DEV,))[None]
    chunk = bands // CHUNKS
    energies = (band_owner, cond_energy, val_energy)
    panels, slabs = [], []
    for part in range(CHUNKS):
        plain, weighted = spectra(plan, val_wave, cond_wave, energies, part * chunk, chunk)
        send, slab = packed(plan, plain, weighted, slabs if part == CHUNKS - 1 else [])
        slabs.append(slab)
        if part < CHUNKS - 1:
            send, cond_wave = lax.optimization_barrier((send, cond_wave))
            panels.append(lax.all_gather(send, "row", axis=1))
        else:
            mine = lax.all_to_all(send, "col", split_axis=0, concat_axis=0, tiled=True).reshape(-1, send.shape[2])
            ordered_mine = put_in_order(plan, starts, ids, wanted, mine)
            last = lax.all_gather(ordered_mine, "row", axis=0, tiled=True)
    slab, _ = lax.optimization_barrier((mine[:, plan["lanes"] :], ordered_mine))
    slab = slab.reshape(col_count, 2 * chunk, CHUNKS, row_count, plan["slab_lanes"]).transpose(3, 2, 0, 1, 4)
    slab = lax.all_to_all(slab, "row", split_axis=0, concat_axis=0, tiled=True)
    *panels, slab = lax.optimization_barrier((*panels, slab))
    left = left_side(slab, slab_ids, slab_wanted)
    ordered = []
    for panel in panels:
        panel = lax.all_to_all(panel, "col", split_axis=0, concat_axis=0, tiled=True)
        ordered.append(put_in_order(plan, starts, ids, wanted, panel.reshape(-1, plan["lanes"])))
    return product(left, [*ordered, last])


def solution(mesh):
    in_specs = (P(), P(("row", "col"), None, None, None), P(), P(), P(("row", "col")), P())
    out_specs = P(None, "row", "col")
    return jax.shard_map(
        on_device, mesh=mesh, in_specs=in_specs, out_specs=out_specs, check_vma=False
    )
```

```python
import math

import jax
import jax.numpy as jnp
import numpy as np
from jax import lax
from jax.experimental import pallas as pl
from jax.experimental.pallas import tpu as pltpu
from jax.sharding import PartitionSpec as P

ROWS_DEV = 256
LANES = 128
VMEM_BYTES = 56 * 1024 * 1024
HALF = 64
KEEP = 40
ROWS_K = 48
ORIGIN = KEEP // 2
PARTS = 3


def round_up(value, step):
    return -(-value // step) * step


def length_counts(points):
    freq = np.arange(points) - points // 2
    square = freq * freq
    lengths = square[:, None, None] + square[None, :, None] + square[None, None, :]
    return np.cumsum(np.bincount(lengths.reshape(-1)))


def column_order(top):
    freq = np.arange(KEEP) - ORIGIN
    first, second = np.meshgrid(freq, freq, indexing="ij")
    length = (first * first + second * second).reshape(-1)
    order = np.argsort(length, kind="stable")
    order = order[length[order] <= top]
    return first.reshape(-1)[order], second.reshape(-1)[order], length[order]


class Bucket:
    def __init__(self, ranges, column_length):
        self.pieces = []
        self.edges = {}
        offset = 0
        for low, high in ranges:
            begin = offset
            for index in range(KEEP):
                freq = index - ORIGIN
                start = int(np.searchsorted(column_length, low - freq * freq, side="left"))
                stop = int(np.searchsorted(column_length, high - freq * freq, side="right"))
                if stop > start:
                    self.pieces.append((index, start, stop, offset))
                    offset += stop - start
            for length in range(low, high + 1):
                self.edges[length] = (begin, offset)
        self.size = offset

    def ids(self, column_2, column_3, points, width):
        out = np.full((width,), -1, np.int32)
        for index, start, stop, offset in self.pieces:
            k1 = (index - ORIGIN) % points
            k2 = column_2[start:stop] % points
            k3 = column_3[start:stop] % points
            out[offset : offset + stop - start] = (k1 * points + k2) * points + k3
        return out


def length_ranges(cumulative, first, step, count):
    shell = lambda rank: int(np.searchsorted(cumulative, rank, side="right"))
    ranges, low = [], shell(first)
    for part in range(1, count):
        before, after = shell(first + part * step - 1), shell(first + part * step)
        if before == after:
            if low < before:
                ranges.append((low, before - 1))
            if low <= before:
                ranges.append((before, before))
        elif low <= before:
            ranges.append((low, before))
        low = before + 1
    high = shell(first + count * step - 1)
    if low <= high:
        ranges.append((low, high))
    return ranges


def make_plan(points, total, blocks, slab, slab_blocks):
    cumulative = length_counts(points)
    shell = lambda rank: int(np.searchsorted(cumulative, rank, side="right"))
    width, slab_width = total // blocks, slab // slab_blocks
    step = width // PARTS
    column_2, column_3, column_length = column_order(shell(total - 1))
    buckets = [Bucket(length_ranges(cumulative, n * width, step, PARTS), column_length) for n in range(blocks)]
    slabs = [Bucket(length_ranges(cumulative, n * slab_width, slab_width, 1), column_length) for n in range(slab_blocks)]
    slab_top = shell(slab - 1)
    lanes = round_up(max(bucket.size for bucket in buckets), LANES)
    slab_lanes = round_up(max(bucket.size for bucket in slabs), LANES)
    windows = np.zeros((blocks, PARTS, 2), np.int64)
    for n, bucket in enumerate(buckets):
        for part in range(PARTS):
            rank = n * width + part * step
            windows[n, part, 0] = bucket.edges[shell(rank)][0] // LANES * LANES
            windows[n, part, 1] = round_up(bucket.edges[shell(rank + step - 1)][1], LANES)
    window = int((windows[..., 1] - windows[..., 0]).max())
    return dict(
        buckets=buckets,
        slabs=slabs,
        slab_columns=int(np.searchsorted(column_length, slab_top, side="right")),
        slab_edge=math.isqrt(slab_top),
        lanes=lanes,
        slab_lanes=slab_lanes,
        window=window,
        starts=np.minimum(windows[..., 0], lanes - window).astype(np.int32),
        ids=np.stack([bucket.ids(column_2, column_3, points, lanes) for bucket in buckets]),
        slab_ids=np.stack([bucket.ids(column_2, column_3, points, slab_lanes) for bucket in slabs]),
        column_place=((column_3 + ORIGIN) * KEEP + column_2 + ORIGIN).astype(np.int32),
    )


def dft_table(points):
    n = np.arange(points)
    freq = np.arange(KEEP) - ORIGIN
    angle = (n[:, None] * freq[None, :] % points) * (2.0 * np.pi / points)
    cosine, sine = np.cos(angle), np.sin(angle)
    table = np.zeros((2 * HALF, 2 * HALF))
    table[:points, :KEEP] = cosine
    table[HALF : HALF + points, :KEEP] = sine
    table[:points, HALF : HALF + KEEP] = -sine
    table[HALF : HALF + points, HALF : HALF + KEEP] = cosine
    high = table.astype(jnp.bfloat16)
    low = (table - high.astype(np.float64)).astype(jnp.bfloat16)
    return np.block([[high, low], [high, np.zeros_like(low)]])


def split_parts(value):
    high = value.astype(jnp.bfloat16)
    low = (value - high.astype(jnp.float32)).astype(jnp.bfloat16)
    return high, low


def apply_table(parts, table):
    both = jnp.dot(parts, table, preferred_element_type=jnp.float32)
    return both[:, :LANES] + both[:, LANES:]


def stack_complex(turned, low_lanes):
    real, imag = turned[:KEEP], turned[HALF : HALF + KEEP]
    first = jnp.where(low_lanes, real, pltpu.roll(imag, HALF, 1))
    second = jnp.where(low_lanes, pltpu.roll(real, HALF, 1), imag)
    return jnp.concatenate([first, second], 0)


def pack_pieces(pieces, width, source, rows, lane, out):
    for tile in range(width // LANES):
        left, right = tile * LANES, (tile + 1) * LANES
        value = jnp.zeros((rows, LANES), jnp.float32)
        for index, start, stop, offset in pieces:
            begin, end = max(left, offset), min(right, offset + stop - start)
            while begin < end:
                at = start + begin - offset
                block = source(index, at // LANES)
                shift = (begin - at) % LANES
                if shift:
                    block = pltpu.roll(block, shift, 1)
                value = block if begin == left else jnp.where(lane >= begin - left, block, value)
                begin = min(end, begin + LANES - at % LANES)
        out(tile, value)


def slab_tiles(plan):
    first = (ORIGIN - plan["slab_edge"]) * KEEP // LANES
    last = round_up((ORIGIN + plan["slab_edge"] + 1) * KEEP, LANES) // LANES
    return first, last


def spectrum_kernel(plan, points, first_band, owner_ref, cond_energy_ref, val_energy_ref, val_ref, cond_ref, table_ref, plain_ref, weighted_ref,
                    cond_a, cond_b, middle, turned, last):
    band = pl.program_id(0)
    planes = 8
    lane = lax.broadcasted_iota(jnp.int32, (1, LANES), 1)
    low_lanes = lane < HALF
    depth = last.shape[0]

    @pl.when(band == 0)
    def _():
        scale = 1.0 / float(points) ** 1.5
        sign = jnp.where(low_lanes, scale, -scale)

        @pl.loop(0, points // planes)
        def _(block):
            rows = pl.ds(pl.multiple_of(block * planes * points, planes * points), planes * points)
            wave = cond_ref[0, pl.ds(block * planes, planes)].reshape(planes * points, LANES).astype(jnp.float32)
            cond_a[rows, :] = wave * scale
            cond_b[rows, :] = pltpu.roll(wave, HALF, 1) * sign

        last[KEEP * KEEP :, :] = jnp.zeros((depth - KEEP * KEEP, 2 * LANES), jnp.bfloat16)

    table = table_ref[...]
    step = planes * KEEP

    def first_axis(block):
        rows = pl.ds(pl.multiple_of(block * planes * points, planes * points), planes * points)
        wave = val_ref[0, pl.ds(block * planes, planes)].reshape(planes * points, LANES).astype(jnp.float32)
        other = pltpu.roll(wave, HALF, 1)
        density = jnp.where(low_lanes, wave, other) * cond_a[rows, :] + jnp.where(low_lanes, other, wave) * cond_b[rows, :]
        high, low = split_parts(density)
        field = apply_table(jnp.concatenate([high, low], 1), table)
        for pair in range(planes // 2):
            both = field[pair * 2 * points : (pair + 1) * 2 * points].T
            high, low = split_parts(stack_complex(both, low_lanes))
            at = pl.ds(pl.multiple_of((block * planes + pair * 2) * KEEP, 2 * KEEP), 2 * KEEP)
            middle[at, :LANES] = high
            middle[at, LANES:] = low

    def second_axis(block):
        rows = pl.ds(pl.multiple_of(block * step, step), step)
        turned[rows, :] = apply_table(middle[rows, :], table)

    first_axis(0)
    first_axis(1)

    @pl.loop(1, points // planes // 2)
    def _(turn):
        for part in range(2):
            second_axis(2 * turn - 2 + part)
        for part in range(2):
            first_axis(2 * turn + part)

    second_axis(points // planes - 2)
    second_axis(points // planes - 1)

    for pair in range(KEEP // 2):
        both = jnp.concatenate(
            [turned[pl.ds(2 * pair, points, stride=KEEP), :], turned[pl.ds(2 * pair + 1, points, stride=KEEP), :]], 0
        ).T
        high, low = split_parts(stack_complex(both, low_lanes))
        at = slice(2 * pair * KEEP, (2 * pair + 2) * KEEP)
        last[at, :LANES] = high
        last[at, LANES:] = low

    pairs = val_energy_ref.shape[0] * cond_energy_ref.shape[0]
    gap = cond_energy_ref[owner_ref[0]] - val_energy_ref[first_band + band]
    weight = -2.0 / (math.sqrt(pairs) * jnp.full((1, LANES), gap, jnp.float32))
    slab_first, slab_last = slab_tiles(plan)
    for begin in range(0, depth // LANES, 5):
        end = min(begin + 5, depth // LANES)
        field = apply_table(last[begin * LANES : end * LANES, :], table)
        for tile in range(begin, end):
            turn = field[(tile - begin) * LANES : (tile - begin + 1) * LANES].T
            for part in range(2):
                value = turn[part * HALF : part * HALF + ROWS_K]
                plain_ref[part, 0, :, tile * LANES : (tile + 1) * LANES] = value.astype(jnp.bfloat16)
                if slab_first <= tile < slab_last:
                    lanes = slice((tile - slab_first) * LANES, (tile - slab_first + 1) * LANES)
                    weighted_ref[part, 0, :, lanes] = (weight * value).astype(jnp.bfloat16)


def spectra(plan, val_wave, cond_wave, energies, first_band, count):
    points = val_wave.shape[1]
    depth = round_up(KEEP * KEEP, LANES)
    slab_first, slab_last = slab_tiles(plan)
    slab_depth = (slab_last - slab_first) * LANES
    grid_rows = points * points
    kernel = lambda *refs: spectrum_kernel(plan, points, first_band, *refs)
    return pl.pallas_call(
        kernel,
        grid=(count,),
        in_specs=[
            pl.BlockSpec(memory_space=pltpu.SMEM),
            pl.BlockSpec(memory_space=pltpu.SMEM),
            pl.BlockSpec(memory_space=pltpu.SMEM),
            pl.BlockSpec((1, points, points, 2 * points), lambda v: (first_band + v, 0, 0, 0)),
            pl.BlockSpec((1, points, points, 2 * points), lambda v: (0, 0, 0, 0)),
            pl.BlockSpec((4 * HALF, 4 * HALF), lambda v: (0, 0)),
        ],
        out_specs=[
            pl.BlockSpec((2, 1, ROWS_K, depth), lambda v: (0, v, 0, 0)),
            pl.BlockSpec((2, 1, ROWS_K, slab_depth), lambda v: (0, v, 0, 0)),
        ],
        out_shape=[
            jax.ShapeDtypeStruct((2, count, ROWS_K, depth), jnp.bfloat16),
            jax.ShapeDtypeStruct((2, count, ROWS_K, slab_depth), jnp.bfloat16),
        ],
        scratch_shapes=[
            pltpu.VMEM((grid_rows, LANES), jnp.float32),
            pltpu.VMEM((grid_rows, LANES), jnp.float32),
            pltpu.VMEM((points * KEEP, 2 * LANES), jnp.bfloat16),
            pltpu.VMEM((points * KEEP, LANES), jnp.float32),
            pltpu.VMEM((depth, 2 * LANES), jnp.bfloat16),
        ],
        compiler_params=pltpu.CompilerParams(vmem_limit_bytes=VMEM_BYTES, dimension_semantics=("arbitrary",)),
        cost_estimate=pl.CostEstimate(flops=count, bytes_accessed=count, transcendentals=0),
        name="spectra",
    )(*energies, val_wave, cond_wave, jnp.asarray(dft_table(points)))


def pack_kernel(plan, groups, place_ref, *refs):
    plains, weighteds = refs[:groups], refs[groups : 2 * groups]
    send_ref, slab_ref, sorter, plain_sorted, weighted_sorted = refs[2 * groups :]
    depth, columns = sorter.shape
    count = 2 * sum(plain.shape[1] for plain in plains)
    lane = lax.broadcasted_iota(jnp.int32, (1, LANES), 1)
    for begin in range(0, depth, LANES):
        at = lax.broadcasted_iota(jnp.int32, (LANES, columns), 0) + begin
        sorter[begin : begin + LANES, :] = jnp.where(at == place_ref[...], 1.0, 0.0).astype(jnp.bfloat16)

    def sort_rows(parts, which, target):
        rows = jnp.concatenate([part[n] for n in range(2) for part in parts], 0)
        rows = rows.reshape(count * ROWS_K, rows.shape[2])
        value = jnp.dot(rows, which, preferred_element_type=jnp.float32)
        for tile in range(target.shape[0]):
            target[tile] = value[:, tile * LANES : (tile + 1) * LANES]

    slab_first, slab_last = slab_tiles(plan)
    sort_rows(plains, sorter[...], plain_sorted)
    sort_rows(weighteds, sorter[slab_first * LANES : slab_last * LANES, : weighted_sorted.shape[0] * LANES], weighted_sorted)

    def plain_at(index, tile):
        return plain_sorted[tile, pl.ds(index, count, stride=ROWS_K), :]

    def weighted_at(index, tile):
        return weighted_sorted[tile, pl.ds(index, count, stride=ROWS_K), :]

    for block, bucket in enumerate(plan["buckets"]):

        def keep(tile, value):
            send_ref[block, :, tile * LANES : (tile + 1) * LANES] = value.astype(jnp.bfloat16)

        pack_pieces(bucket.pieces, plan["lanes"], plain_at, count, lane, keep)
    for block, bucket in enumerate(plan["slabs"]):

        def keep_slab(tile, value):
            slab_ref[block, :, tile * LANES : (tile + 1) * LANES] = value.astype(jnp.bfloat16)

        pack_pieces(bucket.pieces, plan["slab_lanes"], weighted_at, count, lane, keep_slab)


def packed(plan, plains, weighteds):
    depth = plains[0].shape[3]
    count = 2 * sum(plain.shape[1] for plain in plains)
    columns = round_up(plan["column_place"].shape[0], 256)
    slab_columns = round_up(plan["slab_columns"], LANES)
    place = np.full((1, columns), -1, np.int32)
    place[0, : plan["column_place"].shape[0]] = plan["column_place"]
    kernel = lambda *refs: pack_kernel(plan, len(plains), *refs)
    vmem = pl.BlockSpec(memory_space=pltpu.VMEM)
    send_shape = (len(plan["buckets"]), count, plan["lanes"])
    slab_shape = (len(plan["slabs"]), count, plan["slab_lanes"])
    return pl.pallas_call(
        kernel,
        in_specs=[vmem] * (1 + 2 * len(plains)),
        out_specs=[vmem] * 2,
        out_shape=[jax.ShapeDtypeStruct(send_shape, jnp.bfloat16), jax.ShapeDtypeStruct(slab_shape, jnp.bfloat16)],
        scratch_shapes=[
            pltpu.VMEM((depth, columns), jnp.bfloat16),
            pltpu.VMEM((columns // LANES, count * ROWS_K, LANES), jnp.float32),
            pltpu.VMEM((slab_columns // LANES, count * ROWS_K, LANES), jnp.float32),
        ],
        compiler_params=pltpu.CompilerParams(vmem_limit_bytes=VMEM_BYTES),
        cost_estimate=pl.CostEstimate(flops=1, bytes_accessed=1, transcendentals=0),
        name="pack",
    )(jnp.asarray(place), *plains, *weighteds)


def one_hot(ids_ref, begin, wanted):
    ids = jnp.broadcast_to(ids_ref[:, pl.ds(begin, LANES)], (LANES, LANES)).T
    ids = jnp.concatenate([ids] * (wanted.shape[1] // LANES), 1)
    return jnp.where(ids == wanted, 1.0, 0.0).astype(jnp.bfloat16)


def left_kernel(group, slab_ref, slab_ids_ref, slab_wanted_ref, left_ref):
    rows = slab_wanted_ref.shape[1]
    choice = jnp.concatenate(
        [one_hot(slab_ids_ref, begin, slab_wanted_ref[...]) for begin in range(0, slab_ids_ref.shape[1], LANES)], 0
    )
    chosen = jnp.dot(slab_ref[...], choice, preferred_element_type=jnp.float32)
    lane = lax.broadcasted_iota(jnp.int32, (1, LANES), 1)
    real_lanes = lane % group < group // 2
    for begin in range(0, chosen.shape[0], LANES):
        turned = chosen[begin : begin + LANES].T
        after = pltpu.roll(turned, LANES - group // 2, 1)
        before = pltpu.roll(turned, group // 2, 1)
        left_ref[:rows, begin : begin + LANES] = turned.astype(jnp.bfloat16)
        left_ref[rows:, begin : begin + LANES] = jnp.where(real_lanes, after, -before).astype(jnp.bfloat16)


def left_side(group, slab, slab_ids, slab_wanted):
    vmem = pl.BlockSpec(memory_space=pltpu.VMEM)
    return pl.pallas_call(
        lambda *refs: left_kernel(group, *refs),
        in_specs=[vmem] * 3,
        out_specs=vmem,
        out_shape=jax.ShapeDtypeStruct((2 * slab_wanted.shape[1], slab.shape[0]), jnp.bfloat16),
        compiler_params=pltpu.CompilerParams(vmem_limit_bytes=VMEM_BYTES),
        cost_estimate=pl.CostEstimate(flops=1, bytes_accessed=1, transcendentals=0),
        name="left_side",
    )(slab, slab_ids, slab_wanted)


def in_order(starts_ref, ids_ref, wanted_ref, panel_ref, hot):
    start = pl.multiple_of(starts_ref[pl.program_id(0)], LANES)
    wanted = wanted_ref[...]
    window = hot.shape[0]
    for begin in range(0, window, LANES):
        hot[begin : begin + LANES, :] = one_hot(ids_ref, pl.multiple_of(start + begin, LANES), wanted)
    return jnp.dot(panel_ref[:, pl.ds(start, window)], hot[...], preferred_element_type=jnp.float32).astype(jnp.bfloat16)


def order_kernel(starts_ref, ids_ref, wanted_ref, panel_ref, out_ref, hot):
    out_ref[...] = in_order(starts_ref, ids_ref, wanted_ref, panel_ref, hot)


def product_kernel(starts_ref, ids_ref, wanted_ref, panel_ref, left_ref, last_ref, out_ref, hot):
    rows = out_ref.shape[1]
    right = jnp.concatenate([in_order(starts_ref, ids_ref, wanted_ref, panel_ref, hot), last_ref[...]], 0)
    chi = jnp.dot(left_ref[...], right, preferred_element_type=jnp.float32)
    out_ref[0] = chi[:rows]
    out_ref[1] = chi[rows:]


def put_in_order(plan, starts, ids, wanted, panel, left=None, last=None):
    columns = wanted.shape[1]
    block = columns // PARTS
    whole = lambda array: pl.BlockSpec(array.shape, lambda n: (0,) * array.ndim)
    in_specs = [
        pl.BlockSpec(memory_space=pltpu.SMEM),
        whole(ids),
        pl.BlockSpec((1, block), lambda n: (0, n)),
        whole(panel),
    ]
    operands = [starts, ids, wanted, panel]
    if left is None:
        out_spec = pl.BlockSpec((panel.shape[0], block), lambda n: (0, n))
        out_shape = jax.ShapeDtypeStruct((panel.shape[0], columns), jnp.bfloat16)
    else:
        rows = left.shape[0] // 2
        in_specs += [whole(left), pl.BlockSpec((last.shape[0], block), lambda n: (0, n))]
        operands += [left, last]
        out_spec = pl.BlockSpec((2, rows, block), lambda n: (0, 0, n))
        out_shape = jax.ShapeDtypeStruct((2, rows, columns), jnp.float32)
    return pl.pallas_call(
        order_kernel if left is None else product_kernel,
        grid=(PARTS,),
        in_specs=in_specs,
        out_specs=out_spec,
        out_shape=out_shape,
        scratch_shapes=[pltpu.VMEM((plan["window"], block), jnp.bfloat16)],
        compiler_params=pltpu.CompilerParams(vmem_limit_bytes=VMEM_BYTES, dimension_semantics=("arbitrary",)),
        cost_estimate=pl.CostEstimate(flops=1, bytes_accessed=1, transcendentals=0),
        name="in_order" if left is None else "product",
    )(*operands)


def on_device(val_wave, cond_wave, val_energy, cond_energy, band_owner, grid_map):
    bands, points = val_wave.shape[0], val_wave.shape[1]
    row_count = lax.axis_size("row")
    col_count = lax.axis_size("col")
    col, row = lax.axis_index("col"), lax.axis_index("row")
    plan = make_plan(points, grid_map.shape[0], col_count, ROWS_DEV * row_count, row_count)
    width = grid_map.shape[0] // col_count
    starts = lax.dynamic_index_in_dim(jnp.asarray(plan["starts"]), col, 0, keepdims=False)
    ids = lax.dynamic_slice(jnp.asarray(plan["ids"]), (col, 0), (1, plan["lanes"]))
    slab_ids = lax.dynamic_slice(jnp.asarray(plan["slab_ids"]), (row, 0), (1, plan["slab_lanes"]))
    wanted = lax.dynamic_slice(grid_map, (col * width,), (width,))[None]
    slab_wanted = lax.dynamic_slice(grid_map, (row * ROWS_DEV,), (ROWS_DEV,))[None]
    chunk = bands // 2
    energies = (band_owner, cond_energy, val_energy)
    slabs = []
    for part in range(2):
        plain, weighted = spectra(plan, val_wave, cond_wave, energies, part * chunk, chunk)
        send, slab = packed(plan, [plain], [weighted])
        slabs.append(slab)
        if part == 0:
            send, cond_wave = lax.optimization_barrier((send, cond_wave))
            early = lax.all_gather(send, "row", axis=1)
        else:
            mine = lax.all_to_all(send, "col", split_axis=0, concat_axis=0, tiled=True).reshape(-1, plan["lanes"])
            mine = put_in_order(plan, starts, ids, wanted, mine)
            last = lax.all_gather(mine, "row", axis=0, tiled=True)
    slab, _ = lax.optimization_barrier((jnp.stack(slabs, 1), mine))
    slab = lax.all_to_all(slab, "row", split_axis=0, concat_axis=0, tiled=True)
    slab = lax.all_to_all(jnp.broadcast_to(slab, (col_count, *slab.shape)), "col", split_axis=0, concat_axis=0)
    early, slab = lax.optimization_barrier((early, slab))
    slab = [slab[:, :, 0], slab[:, :, 1].transpose(1, 0, 2, 3)]
    slab = jnp.stack([part.reshape(-1, plan["slab_lanes"]) for part in slab]).reshape(-1, plan["slab_lanes"])
    left = left_side(2 * chunk, slab, slab_ids, slab_wanted)
    early = lax.all_to_all(early, "col", split_axis=0, concat_axis=0, tiled=True).reshape(-1, plan["lanes"])
    return put_in_order(plan, starts, ids, wanted, early, left, last)


def solution(mesh):
    in_specs = (P(), P(("row", "col"), None, None, None), P(), P(), P(("row", "col")), P())
    out_specs = P(None, "row", "col")
    return jax.shard_map(
        on_device, mesh=mesh, in_specs=in_specs, out_specs=out_specs, check_vma=False
    )
```

```python
import math

import jax
import jax.numpy as jnp
import numpy as np
from jax import lax
from jax.experimental import pallas as pl
from jax.experimental.pallas import tpu as pltpu
from jax.sharding import PartitionSpec as P

ROWS_DEV = 256
LANES = 128
VMEM_BYTES = 56 * 1024 * 1024
HALF = 64
KEEP = 40
ROWS_K = 48
ORIGIN = KEEP // 2
PARITY_LANES = 896
PARTS = 3


def round_up(value, step):
    return -(-value // step) * step


def length_counts(points):
    freq = np.arange(points) - points // 2
    square = freq * freq
    lengths = square[:, None, None] + square[None, :, None] + square[None, None, :]
    return np.cumsum(np.bincount(lengths.reshape(-1)))


def column_order(top):
    freq = np.arange(KEEP) - ORIGIN
    first, second = np.meshgrid(freq, freq, indexing="ij")
    length = (first * first + second * second).reshape(-1)
    order = np.argsort(length, kind="stable")
    order = order[length[order] <= top]
    return first.reshape(-1)[order], second.reshape(-1)[order], length[order]


def column_place(index_2, index_3):
    return index_3 % 2 * PARITY_LANES + index_3 // 2 * KEEP + index_2


class Bucket:
    def __init__(self, ranges, column_length):
        self.pieces = []
        self.edges = {}
        offset = 0
        for low, high in ranges:
            begin = offset
            for index in range(KEEP):
                freq = index - ORIGIN
                start = int(np.searchsorted(column_length, low - freq * freq, side="left"))
                stop = int(np.searchsorted(column_length, high - freq * freq, side="right"))
                if stop > start:
                    self.pieces.append((index, start, stop, offset))
                    offset += stop - start
            for length in range(low, high + 1):
                self.edges[length] = (begin, offset)
        self.size = offset

    def ids(self, column_2, column_3, points, width):
        out = np.full((width,), -1, np.int32)
        for index, start, stop, offset in self.pieces:
            k1 = (index - ORIGIN) % points
            k2 = column_2[start:stop] % points
            k3 = column_3[start:stop] % points
            out[offset : offset + stop - start] = (k1 * points + k2) * points + k3
        return out


def length_ranges(cumulative, first, step, count):
    shell = lambda rank: int(np.searchsorted(cumulative, rank, side="right"))
    ranges, low = [], shell(first)
    for part in range(1, count):
        before, after = shell(first + part * step - 1), shell(first + part * step)
        if before == after:
            if low < before:
                ranges.append((low, before - 1))
            if low <= before:
                ranges.append((before, before))
        elif low <= before:
            ranges.append((low, before))
        low = before + 1
    high = shell(first + count * step - 1)
    if low <= high:
        ranges.append((low, high))
    return ranges


def make_plan(points, total, blocks, slab, slab_blocks):
    cumulative = length_counts(points)
    shell = lambda rank: int(np.searchsorted(cumulative, rank, side="right"))
    width, slab_width = total // blocks, slab // slab_blocks
    step = width // PARTS
    column_2, column_3, column_length = column_order(shell(total - 1))
    buckets = [Bucket(length_ranges(cumulative, n * width, step, PARTS), column_length) for n in range(blocks)]
    slabs = [Bucket(length_ranges(cumulative, n * slab_width, slab_width, 1), column_length) for n in range(slab_blocks)]
    slab_top = shell(slab - 1)
    lanes = round_up(max(bucket.size for bucket in buckets), LANES)
    slab_lanes = round_up(max(bucket.size for bucket in slabs), LANES)
    windows = np.zeros((blocks, PARTS, 2), np.int64)
    for n, bucket in enumerate(buckets):
        for part in range(PARTS):
            rank = n * width + part * step
            windows[n, part, 0] = bucket.edges[shell(rank)][0] // LANES * LANES
            windows[n, part, 1] = round_up(bucket.edges[shell(rank + step - 1)][1], LANES)
    window = int((windows[..., 1] - windows[..., 0]).max())
    return dict(
        buckets=buckets,
        slabs=slabs,
        slab_columns=int(np.searchsorted(column_length, slab_top, side="right")),
        slab_edge=math.isqrt(slab_top),
        lanes=lanes,
        slab_lanes=slab_lanes,
        window=window,
        starts=np.minimum(windows[..., 0], lanes - window).astype(np.int32),
        ids=np.stack([bucket.ids(column_2, column_3, points, lanes) for bucket in buckets]),
        slab_ids=np.stack([bucket.ids(column_2, column_3, points, slab_lanes) for bucket in slabs]),
        column_place=column_place(column_2 + ORIGIN, column_3 + ORIGIN).astype(np.int32),
    )


def dft_tables(points):
    n = np.arange(points)
    freq = np.arange(KEEP) - ORIGIN
    angle = (n[:, None] * freq[None, :] % points) * (2.0 * np.pi / points)
    cosine, sine = np.cos(angle), np.sin(angle)
    table = np.zeros((2, points, 2, 2, 2, HALF))
    for item in range(2):
        table[0, :, item, item, 0, :KEEP] = cosine
        table[1, :, item, item, 0, :KEEP] = sine
        table[0, :, item, item, 1, :KEEP] = -sine
        table[1, :, item, item, 1, :KEEP] = cosine
    table = table.reshape(2, points, 2, 4 * HALF)
    halves = table.reshape(2, points // 2, 2, 2, 4 * HALF).transpose(0, 3, 2, 1, 4)
    orders = [table.transpose(2, 0, 1, 3), table.transpose(0, 2, 1, 3), halves]
    out = []
    for order in orders:
        order = order.reshape(4 * points, 4 * HALF)
        high = order.astype(jnp.bfloat16)
        low = (order - high.astype(np.float64)).astype(jnp.bfloat16)
        out.append(np.concatenate([high, low]))
    return np.stack(out)


def split_parts(value):
    high = value.astype(jnp.bfloat16)
    low = (value - high.astype(jnp.float32)).astype(jnp.bfloat16)
    return high, low


def store_split(target, rows, blocks):
    for part, block in enumerate(blocks):
        high, low = split_parts(jnp.concatenate(block, 0))
        target[rows, part * LANES : (part + 1) * LANES] = high
        target[rows, (part + 2) * LANES : (part + 3) * LANES] = low


def apply_table(stored, table):
    high = table[: 2 * LANES]
    both = jnp.concatenate([stored, stored[:, : 2 * LANES]], 1)
    return jnp.dot(both, jnp.concatenate([high, high, table[2 * LANES :]], 0), preferred_element_type=jnp.float32)


def parts_of(turned):
    return turned[:KEEP], turned[HALF : HALF + KEEP]


def pack_pieces(pieces, width, source, rows, lane, out):
    for tile in range(width // LANES):
        left, right = tile * LANES, (tile + 1) * LANES
        value = jnp.zeros((rows, LANES), jnp.float32)
        for index, start, stop, offset in pieces:
            begin, end = max(left, offset), min(right, offset + stop - start)
            while begin < end:
                at = start + begin - offset
                block = source(index, at // LANES)
                shift = (begin - at) % LANES
                if shift:
                    block = pltpu.roll(block, shift, 1)
                value = block if begin == left else jnp.where(lane >= begin - left, block, value)
                begin = min(end, begin + LANES - at % LANES)
        out(tile, value)


def slab_tiles(plan):
    first = (ORIGIN - plan["slab_edge"]) // 2 * KEEP // LANES
    last = round_up(((ORIGIN + plan["slab_edge"]) // 2 + 1) * KEEP, LANES) // LANES
    return [odd * PARITY_LANES // LANES + tile for odd in range(2) for tile in range(first, last)]


def spectrum_kernel(plan, points, first_band, owner_ref, cond_energy_ref, val_energy_ref, val_ref, cond_ref, table_ref,
                    plain_ref, weighted_ref, cond_a, cond_b, middle, turned, last):
    band = pl.program_id(0)
    planes = 8
    pairs = planes // 2
    lane = lax.broadcasted_iota(jnp.int32, (1, LANES), 1)
    low_lanes = lane < HALF

    @pl.when(band == 0)
    def _():
        scale = 1.0 / float(points) ** 1.5
        sign = jnp.where(low_lanes, scale, -scale)

        @pl.loop(0, points // planes)
        def _(block):
            rows = pl.ds(pl.multiple_of(block * planes * points, planes * points), planes * points)
            wave = cond_ref[0, pl.ds(block * planes, planes)].reshape(planes * points, LANES).astype(jnp.float32)
            cond_a[rows, :] = wave * scale
            cond_b[rows, :] = pltpu.roll(wave, HALF, 1) * sign

        last[KEEP * KEEP // 2 :, :] = jnp.zeros((last.shape[0] - KEEP * KEEP // 2, 4 * LANES), jnp.bfloat16)

    def first_axis(block):
        rows = pl.ds(pl.multiple_of(block * planes * points, planes * points), planes * points)
        wave = val_ref[0, pl.ds(block * planes, planes)].reshape(planes * points, LANES).astype(jnp.float32)
        other = pltpu.roll(wave, HALF, 1)
        density = jnp.where(low_lanes, wave, other) * cond_a[rows, :] + jnp.where(low_lanes, other, wave) * cond_b[rows, :]
        high, low = split_parts(density)
        half = planes * points // 2
        stored = jnp.concatenate([high[:half], high[half:], low[:half], low[half:]], 1)
        field = apply_table(stored, table_ref[0])
        for item in range(2):
            both = [
                parts_of(field[pair * 2 * points : (pair + 1) * 2 * points, item * LANES : (item + 1) * LANES].T)
                for pair in range(pairs // 2)
            ]
            at = pl.ds(pl.multiple_of((block * pairs + item * pairs // 2) * KEEP, 2 * KEEP), 2 * KEEP)
            store_split(middle, at, list(zip(*both)))

    def second_axis(block):
        rows = pl.ds(pl.multiple_of(block * pairs * KEEP, pairs * KEEP), pairs * KEEP)
        field = apply_table(middle[rows, :], table_ref[1])
        for item in range(2):
            turned[item, rows, :] = field[:, item * LANES : (item + 1) * LANES]

    first_axis(0)
    first_axis(1)

    @pl.loop(1, points // planes // 2)
    def _(turn):
        for part in range(2):
            second_axis(2 * turn - 2 + part)
        for part in range(2):
            first_axis(2 * turn + part)

    second_axis(points // planes - 2)
    second_axis(points // planes - 1)

    for begin in range(0, KEEP, 4):
        both = []
        for pair in range(2):
            items = [
                turned[item, pl.ds(begin + 2 * pair + k3, points // 2, stride=KEEP), :]
                for k3 in range(2)
                for item in range(2)
            ]
            both.append(parts_of(jnp.concatenate(items, 0).T))
        store_split(last, slice(begin // 2 * KEEP, (begin // 2 + 2) * KEEP), list(zip(*both)))

    bands = val_energy_ref.shape[0] * cond_energy_ref.shape[0]
    gap = cond_energy_ref[owner_ref[0]] - val_energy_ref[first_band + band]
    weight = -2.0 / (math.sqrt(bands) * jnp.full((1, LANES), gap, jnp.float32))
    slab = slab_tiles(plan)
    tiles = PARITY_LANES // LANES
    for begin, end in ((0, tiles // 2), (tiles // 2, tiles)):
        field = apply_table(last[begin * LANES : end * LANES, :], table_ref[2])
        for odd in range(2):
            for row in range(begin, end):
                tile = odd * tiles + row
                turn = field[(row - begin) * LANES : (row - begin + 1) * LANES, odd * LANES : (odd + 1) * LANES].T
                for part in range(2):
                    value = turn[part * HALF : part * HALF + ROWS_K]
                    plain_ref[part, 0, :, tile * LANES : (tile + 1) * LANES] = value.astype(jnp.bfloat16)
                    if tile in slab:
                        lanes = slice(slab.index(tile) * LANES, (slab.index(tile) + 1) * LANES)
                        weighted_ref[part, 0, :, lanes] = (weight * value).astype(jnp.bfloat16)


def spectra(plan, val_wave, cond_wave, energies, first_band, count):
    points = val_wave.shape[1]
    depth = 2 * PARITY_LANES
    slab_depth = len(slab_tiles(plan)) * LANES
    grid_rows = points * points
    kernel = lambda *refs: spectrum_kernel(plan, points, first_band, *refs)
    return pl.pallas_call(
        kernel,
        grid=(count,),
        in_specs=[
            pl.BlockSpec(memory_space=pltpu.SMEM),
            pl.BlockSpec(memory_space=pltpu.SMEM),
            pl.BlockSpec(memory_space=pltpu.SMEM),
            pl.BlockSpec((1, points, points, 2 * points), lambda v: (first_band + v, 0, 0, 0)),
            pl.BlockSpec((1, points, points, 2 * points), lambda v: (0, 0, 0, 0)),
            pl.BlockSpec((3, 8 * points, 4 * HALF), lambda v: (0, 0, 0)),
        ],
        out_specs=[
            pl.BlockSpec((2, 1, ROWS_K, depth), lambda v: (0, v, 0, 0)),
            pl.BlockSpec((2, 1, ROWS_K, slab_depth), lambda v: (0, v, 0, 0)),
        ],
        out_shape=[
            jax.ShapeDtypeStruct((2, count, ROWS_K, depth), jnp.bfloat16),
            jax.ShapeDtypeStruct((2, count, ROWS_K, slab_depth), jnp.bfloat16),
        ],
        scratch_shapes=[
            pltpu.VMEM((grid_rows, LANES), jnp.float32),
            pltpu.VMEM((grid_rows, LANES), jnp.float32),
            pltpu.VMEM((points // 2 * KEEP, 4 * LANES), jnp.bfloat16),
            pltpu.VMEM((2, points // 2 * KEEP, LANES), jnp.float32),
            pltpu.VMEM((PARITY_LANES, 4 * LANES), jnp.bfloat16),
        ],
        compiler_params=pltpu.CompilerParams(vmem_limit_bytes=VMEM_BYTES, dimension_semantics=("arbitrary",)),
        cost_estimate=pl.CostEstimate(flops=count, bytes_accessed=count, transcendentals=0),
        name="spectra",
    )(*energies, val_wave, cond_wave, jnp.asarray(dft_tables(points)))


def pack_kernel(plan, groups, place_ref, *refs):
    plains, weighteds = refs[:groups], refs[groups : 2 * groups]
    send_ref, slab_ref, sorter, plain_sorted, weighted_sorted = refs[2 * groups :]
    depth, columns = sorter.shape
    count = 2 * sum(plain.shape[1] for plain in plains)
    lane = lax.broadcasted_iota(jnp.int32, (1, LANES), 1)
    for begin in range(0, depth, LANES):
        at = lax.broadcasted_iota(jnp.int32, (LANES, columns), 0) + begin
        sorter[begin : begin + LANES, :] = jnp.where(at == place_ref[...], 1.0, 0.0).astype(jnp.bfloat16)

    def sort_rows(parts, which, target):
        rows = jnp.concatenate([part[n] for n in range(2) for part in parts], 0)
        rows = rows.reshape(count * ROWS_K, rows.shape[2])
        value = jnp.dot(rows, which, preferred_element_type=jnp.float32)
        for tile in range(target.shape[0]):
            target[tile] = value[:, tile * LANES : (tile + 1) * LANES]

    slab = [sorter[tile * LANES : (tile + 1) * LANES, : weighted_sorted.shape[0] * LANES] for tile in slab_tiles(plan)]
    sort_rows(plains, sorter[...], plain_sorted)
    sort_rows(weighteds, jnp.concatenate(slab, 0), weighted_sorted)

    def plain_at(index, tile):
        return plain_sorted[tile, pl.ds(index, count, stride=ROWS_K), :]

    def weighted_at(index, tile):
        return weighted_sorted[tile, pl.ds(index, count, stride=ROWS_K), :]

    for block, bucket in enumerate(plan["buckets"]):

        def keep(tile, value):
            send_ref[block, :, tile * LANES : (tile + 1) * LANES] = value.astype(jnp.bfloat16)

        pack_pieces(bucket.pieces, plan["lanes"], plain_at, count, lane, keep)
    for block, bucket in enumerate(plan["slabs"]):

        def keep_slab(tile, value):
            slab_ref[block, :, tile * LANES : (tile + 1) * LANES] = value.astype(jnp.bfloat16)

        pack_pieces(bucket.pieces, plan["slab_lanes"], weighted_at, count, lane, keep_slab)


def packed(plan, plains, weighteds):
    depth = plains[0].shape[3]
    count = 2 * sum(plain.shape[1] for plain in plains)
    columns = round_up(plan["column_place"].shape[0], 256)
    slab_columns = round_up(plan["slab_columns"], LANES)
    place = np.full((1, columns), -1, np.int32)
    place[0, : plan["column_place"].shape[0]] = plan["column_place"]
    kernel = lambda *refs: pack_kernel(plan, len(plains), *refs)
    vmem = pl.BlockSpec(memory_space=pltpu.VMEM)
    send_shape = (len(plan["buckets"]), count, plan["lanes"])
    slab_shape = (len(plan["slabs"]), count, plan["slab_lanes"])
    return pl.pallas_call(
        kernel,
        in_specs=[vmem] * (1 + 2 * len(plains)),
        out_specs=[vmem] * 2,
        out_shape=[jax.ShapeDtypeStruct(send_shape, jnp.bfloat16), jax.ShapeDtypeStruct(slab_shape, jnp.bfloat16)],
        scratch_shapes=[
            pltpu.VMEM((depth, columns), jnp.bfloat16),
            pltpu.VMEM((columns // LANES, count * ROWS_K, LANES), jnp.float32),
            pltpu.VMEM((slab_columns // LANES, count * ROWS_K, LANES), jnp.float32),
        ],
        compiler_params=pltpu.CompilerParams(vmem_limit_bytes=VMEM_BYTES),
        cost_estimate=pl.CostEstimate(flops=1, bytes_accessed=1, transcendentals=0),
        name="pack",
    )(jnp.asarray(place), *plains, *weighteds)


def one_hot(ids_ref, begin, wanted):
    ids = jnp.broadcast_to(ids_ref[:, pl.ds(begin, LANES)], (LANES, LANES)).T
    ids = jnp.concatenate([ids] * (wanted.shape[1] // LANES), 1)
    return jnp.where(ids == wanted, 1.0, 0.0).astype(jnp.bfloat16)


def left_kernel(group, slab_ref, slab_ids_ref, slab_wanted_ref, left_ref):
    rows = slab_wanted_ref.shape[1]
    choice = jnp.concatenate(
        [one_hot(slab_ids_ref, begin, slab_wanted_ref[...]) for begin in range(0, slab_ids_ref.shape[1], LANES)], 0
    )
    chosen = jnp.dot(slab_ref[...], choice, preferred_element_type=jnp.float32)
    lane = lax.broadcasted_iota(jnp.int32, (1, LANES), 1)
    real_lanes = lane % group < group // 2
    for begin in range(0, chosen.shape[0], LANES):
        turned = chosen[begin : begin + LANES].T
        after = pltpu.roll(turned, LANES - group // 2, 1)
        before = pltpu.roll(turned, group // 2, 1)
        left_ref[:rows, begin : begin + LANES] = turned.astype(jnp.bfloat16)
        left_ref[rows:, begin : begin + LANES] = jnp.where(real_lanes, after, -before).astype(jnp.bfloat16)


def left_side(group, slab, slab_ids, slab_wanted):
    vmem = pl.BlockSpec(memory_space=pltpu.VMEM)
    return pl.pallas_call(
        lambda *refs: left_kernel(group, *refs),
        in_specs=[vmem] * 3,
        out_specs=vmem,
        out_shape=jax.ShapeDtypeStruct((2 * slab_wanted.shape[1], slab.shape[0]), jnp.bfloat16),
        compiler_params=pltpu.CompilerParams(vmem_limit_bytes=VMEM_BYTES),
        cost_estimate=pl.CostEstimate(flops=1, bytes_accessed=1, transcendentals=0),
        name="left_side",
    )(slab, slab_ids, slab_wanted)


def in_order(starts_ref, ids_ref, wanted_ref, panel_ref, hot):
    start = pl.multiple_of(starts_ref[pl.program_id(0)], LANES)
    wanted = wanted_ref[...]
    window = hot.shape[0]
    for begin in range(0, window, LANES):
        hot[begin : begin + LANES, :] = one_hot(ids_ref, pl.multiple_of(start + begin, LANES), wanted)
    return jnp.dot(panel_ref[:, pl.ds(start, window)], hot[...], preferred_element_type=jnp.float32).astype(jnp.bfloat16)


def order_kernel(starts_ref, ids_ref, wanted_ref, panel_ref, out_ref, hot):
    out_ref[...] = in_order(starts_ref, ids_ref, wanted_ref, panel_ref, hot)


def product_kernel(starts_ref, ids_ref, wanted_ref, panel_ref, left_ref, last_ref, out_ref, hot):
    rows = out_ref.shape[1]
    right = jnp.concatenate([in_order(starts_ref, ids_ref, wanted_ref, panel_ref, hot), last_ref[...]], 0)
    chi = jnp.dot(left_ref[...], right, preferred_element_type=jnp.float32)
    out_ref[0] = chi[:rows]
    out_ref[1] = chi[rows:]


def put_in_order(plan, starts, ids, wanted, panel, left=None, last=None):
    columns = wanted.shape[1]
    block = columns // PARTS
    whole = lambda array: pl.BlockSpec(array.shape, lambda n: (0,) * array.ndim)
    in_specs = [
        pl.BlockSpec(memory_space=pltpu.SMEM),
        whole(ids),
        pl.BlockSpec((1, block), lambda n: (0, n)),
        whole(panel),
    ]
    operands = [starts, ids, wanted, panel]
    if left is None:
        out_spec = pl.BlockSpec((panel.shape[0], block), lambda n: (0, n))
        out_shape = jax.ShapeDtypeStruct((panel.shape[0], columns), jnp.bfloat16)
    else:
        rows = left.shape[0] // 2
        in_specs += [whole(left), pl.BlockSpec((last.shape[0], block), lambda n: (0, n))]
        operands += [left, last]
        out_spec = pl.BlockSpec((2, rows, block), lambda n: (0, 0, n))
        out_shape = jax.ShapeDtypeStruct((2, rows, columns), jnp.float32)
    return pl.pallas_call(
        order_kernel if left is None else product_kernel,
        grid=(PARTS,),
        in_specs=in_specs,
        out_specs=out_spec,
        out_shape=out_shape,
        scratch_shapes=[pltpu.VMEM((plan["window"], block), jnp.bfloat16)],
        compiler_params=pltpu.CompilerParams(vmem_limit_bytes=VMEM_BYTES, dimension_semantics=("arbitrary",)),
        cost_estimate=pl.CostEstimate(flops=1, bytes_accessed=1, transcendentals=0),
        name="in_order" if left is None else "product",
    )(*operands)


def on_device(val_wave, cond_wave, val_energy, cond_energy, band_owner, grid_map):
    bands, points = val_wave.shape[0], val_wave.shape[1]
    row_count = lax.axis_size("row")
    col_count = lax.axis_size("col")
    col, row = lax.axis_index("col"), lax.axis_index("row")
    plan = make_plan(points, grid_map.shape[0], col_count, ROWS_DEV * row_count, row_count)
    width = grid_map.shape[0] // col_count
    starts = lax.dynamic_index_in_dim(jnp.asarray(plan["starts"]), col, 0, keepdims=False)
    ids = lax.dynamic_slice(jnp.asarray(plan["ids"]), (col, 0), (1, plan["lanes"]))
    slab_ids = lax.dynamic_slice(jnp.asarray(plan["slab_ids"]), (row, 0), (1, plan["slab_lanes"]))
    wanted = lax.dynamic_slice(grid_map, (col * width,), (width,))[None]
    slab_wanted = lax.dynamic_slice(grid_map, (row * ROWS_DEV,), (ROWS_DEV,))[None]
    chunk = bands // 2
    energies = (band_owner, cond_energy, val_energy)
    slabs = []
    for part in range(2):
        plain, weighted = spectra(plan, val_wave, cond_wave, energies, part * chunk, chunk)
        send, slab = packed(plan, [plain], [weighted])
        slabs.append(slab)
        if part == 0:
            send, cond_wave = lax.optimization_barrier((send, cond_wave))
            early = lax.all_gather(send, "row", axis=1)
        else:
            mine = lax.all_to_all(send, "col", split_axis=0, concat_axis=0, tiled=True).reshape(-1, plan["lanes"])
            mine = put_in_order(plan, starts, ids, wanted, mine)
            last = lax.all_gather(mine, "row", axis=0, tiled=True)
    slab, _ = lax.optimization_barrier((jnp.stack(slabs, 1), mine))
    slab = lax.all_to_all(slab, "row", split_axis=0, concat_axis=0, tiled=True)
    slab = lax.all_to_all(jnp.broadcast_to(slab, (col_count, *slab.shape)), "col", split_axis=0, concat_axis=0)
    early, slab = lax.optimization_barrier((early, slab))
    slab = [slab[:, :, 0], slab[:, :, 1].transpose(1, 0, 2, 3)]
    slab = jnp.stack([part.reshape(-1, plan["slab_lanes"]) for part in slab]).reshape(-1, plan["slab_lanes"])
    left = left_side(2 * chunk, slab, slab_ids, slab_wanted)
    early = lax.all_to_all(early, "col", split_axis=0, concat_axis=0, tiled=True).reshape(-1, plan["lanes"])
    return put_in_order(plan, starts, ids, wanted, early, left, last)


def solution(mesh):
    in_specs = (P(), P(("row", "col"), None, None, None), P(), P(), P(("row", "col")), P())
    out_specs = P(None, "row", "col")
    return jax.shard_map(
        on_device, mesh=mesh, in_specs=in_specs, out_specs=out_specs, check_vma=False
    )
```

```python
import math

import jax
import jax.numpy as jnp
import numpy as np
from jax import lax
from jax.experimental import pallas as pl
from jax.experimental.pallas import tpu as pltpu
from jax.sharding import PartitionSpec as P

ROWS_DEV = 256
LANES = 128
VMEM_BYTES = 56 * 1024 * 1024
HALF = 64
KEEP = 40
ROWS_K = 48
ORIGIN = KEEP // 2
PARITY_LANES = 896
PARTS = 3


def round_up(value, step):
    return -(-value // step) * step


def length_counts(points):
    freq = np.arange(points) - points // 2
    square = freq * freq
    lengths = square[:, None, None] + square[None, :, None] + square[None, None, :]
    return np.cumsum(np.bincount(lengths.reshape(-1)))


def column_order(top):
    freq = np.arange(KEEP) - ORIGIN
    first, second = np.meshgrid(freq, freq, indexing="ij")
    length = (first * first + second * second).reshape(-1)
    order = np.argsort(length, kind="stable")
    order = order[length[order] <= top]
    return first.reshape(-1)[order], second.reshape(-1)[order], length[order]


def column_place(index_2, index_3):
    return index_3 % 2 * PARITY_LANES + index_3 // 2 * KEEP + index_2


class Bucket:
    def __init__(self, ranges, column_length):
        self.pieces = []
        self.edges = {}
        offset = 0
        for low, high in ranges:
            begin = offset
            for index in range(KEEP):
                freq = index - ORIGIN
                start = int(np.searchsorted(column_length, low - freq * freq, side="left"))
                stop = int(np.searchsorted(column_length, high - freq * freq, side="right"))
                if stop > start:
                    self.pieces.append((index, start, stop, offset))
                    offset += stop - start
            for length in range(low, high + 1):
                self.edges[length] = (begin, offset)
        self.size = offset

    def ids(self, column_2, column_3, points, width):
        out = np.full((width,), -1, np.int32)
        for index, start, stop, offset in self.pieces:
            k1 = (index - ORIGIN) % points
            k2 = column_2[start:stop] % points
            k3 = column_3[start:stop] % points
            out[offset : offset + stop - start] = (k1 * points + k2) * points + k3
        return out


def length_ranges(cumulative, first, step, count):
    shell = lambda rank: int(np.searchsorted(cumulative, rank, side="right"))
    ranges, low = [], shell(first)
    for part in range(1, count):
        before, after = shell(first + part * step - 1), shell(first + part * step)
        if before == after:
            if low < before:
                ranges.append((low, before - 1))
            if low <= before:
                ranges.append((before, before))
        elif low <= before:
            ranges.append((low, before))
        low = before + 1
    high = shell(first + count * step - 1)
    if low <= high:
        ranges.append((low, high))
    return ranges


def make_plan(points, total, blocks, slab, slab_blocks):
    cumulative = length_counts(points)
    shell = lambda rank: int(np.searchsorted(cumulative, rank, side="right"))
    width, slab_width = total // blocks, slab // slab_blocks
    step = width // PARTS
    column_2, column_3, column_length = column_order(shell(total - 1))
    buckets = [Bucket(length_ranges(cumulative, n * width, step, PARTS), column_length) for n in range(blocks)]
    slabs = [Bucket(length_ranges(cumulative, n * slab_width, slab_width, 1), column_length) for n in range(slab_blocks)]
    slab_top = shell(slab - 1)
    lanes = round_up(max(bucket.size for bucket in buckets), LANES)
    slab_lanes = round_up(max(bucket.size for bucket in slabs), LANES)
    windows = np.zeros((blocks, PARTS, 2), np.int64)
    for n, bucket in enumerate(buckets):
        for part in range(PARTS):
            rank = n * width + part * step
            windows[n, part, 0] = bucket.edges[shell(rank)][0] // LANES * LANES
            windows[n, part, 1] = round_up(bucket.edges[shell(rank + step - 1)][1], LANES)
    window = int((windows[..., 1] - windows[..., 0]).max())
    return dict(
        buckets=buckets,
        slabs=slabs,
        slab_columns=int(np.searchsorted(column_length, slab_top, side="right")),
        slab_edge=math.isqrt(slab_top),
        lanes=lanes,
        slab_lanes=slab_lanes,
        window=window,
        starts=np.minimum(windows[..., 0], lanes - window).astype(np.int32),
        ids=np.stack([bucket.ids(column_2, column_3, points, lanes) for bucket in buckets]),
        slab_ids=np.stack([bucket.ids(column_2, column_3, points, slab_lanes) for bucket in slabs]),
        column_place=column_place(column_2 + ORIGIN, column_3 + ORIGIN).astype(np.int32),
    )


def dft_tables(points):
    n = np.arange(points)
    freq = np.arange(KEEP) - ORIGIN
    angle = (n[:, None] * freq[None, :] % points) * (2.0 * np.pi / points)
    cosine, sine = np.cos(angle), np.sin(angle)
    one = np.zeros((2, points, 2, HALF))
    one[0, :, 0, :KEEP] = cosine
    one[1, :, 0, :KEEP] = sine
    one[0, :, 1, :KEEP] = -sine
    one[1, :, 1, :KEEP] = cosine
    two = np.zeros((2, 2, points, 2, 2, HALF))
    for item in range(2):
        two[:, item, :, item] = one

    def parts(table):
        high = table.astype(jnp.bfloat16)
        return high, (table - high.astype(np.float64)).astype(jnp.bfloat16)

    high, low = parts(one[..., :KEEP].reshape(2 * points, 2 * KEEP).T)
    first = np.concatenate([high, high, low], 1)
    second = np.concatenate(parts(two.reshape(4 * points, 4 * HALF)), 0)
    halves = two[..., :ROWS_K].reshape(2, 2, points // 2, 2, 4 * ROWS_K).transpose(0, 1, 3, 2, 4)
    high, low = parts(halves.reshape(4 * points, 4 * ROWS_K).T)
    third = np.concatenate([high, high, low], 1)
    return [jnp.asarray(table) for table in (first, second, third)]


def split_parts(value):
    high = value.astype(jnp.bfloat16)
    low = (value - high.astype(jnp.float32)).astype(jnp.bfloat16)
    return high, low


def store_split(target, rows, blocks):
    for part, block in enumerate(blocks):
        high, low = split_parts(jnp.concatenate(block, 0))
        target[rows, part * LANES : (part + 1) * LANES] = high
        target[rows, (part + 2) * LANES : (part + 3) * LANES] = low


def doubled(stored):
    return jnp.concatenate([stored, stored[:, : stored.shape[1] // 2]], 1)


def contract_last(table, stored):
    return lax.dot_general(table, doubled(stored), (((1,), (1,)), ((), ())), preferred_element_type=jnp.float32)


def pack_pieces(pieces, width, source, rows, lane, out):
    for tile in range(width // LANES):
        left, right = tile * LANES, (tile + 1) * LANES
        value = jnp.zeros((rows, LANES), jnp.float32)
        for index, start, stop, offset in pieces:
            begin, end = max(left, offset), min(right, offset + stop - start)
            while begin < end:
                at = start + begin - offset
                block = source(index, at // LANES)
                shift = (begin - at) % LANES
                if shift:
                    block = pltpu.roll(block, shift, 1)
                value = block if begin == left else jnp.where(lane >= begin - left, block, value)
                begin = min(end, begin + LANES - at % LANES)
        out(tile, value)


def slab_tiles(plan):
    first = (ORIGIN - plan["slab_edge"]) // 2 * KEEP // LANES
    last = round_up(((ORIGIN + plan["slab_edge"]) // 2 + 1) * KEEP, LANES) // LANES
    return [odd * PARITY_LANES // LANES + tile for odd in range(2) for tile in range(first, last)]


def spectrum_kernel(plan, points, first_band, owner_ref, cond_energy_ref, val_energy_ref, val_ref, cond_ref, first_ref,
                    second_ref, third_ref, plain_ref, weighted_ref, cond_a, cond_b, middle, turned, last):
    band = pl.program_id(0)
    planes = 8
    pairs = planes // 2
    lane = lax.broadcasted_iota(jnp.int32, (1, LANES), 1)
    low_lanes = lane < HALF

    @pl.when(band == 0)
    def _():
        scale = 1.0 / float(points) ** 1.5
        sign = jnp.where(low_lanes, scale, -scale)

        @pl.loop(0, points // planes)
        def _(block):
            rows = pl.ds(pl.multiple_of(block * planes * points, planes * points), planes * points)
            wave = cond_ref[0, pl.ds(block * planes, planes)].reshape(planes * points, LANES).astype(jnp.float32)
            cond_a[rows, :] = wave * scale
            cond_b[rows, :] = pltpu.roll(wave, HALF, 1) * sign

        last[KEEP * KEEP // 2 :, :] = jnp.zeros((last.shape[0] - KEEP * KEEP // 2, 4 * LANES), jnp.bfloat16)

    def first_axis(block):
        rows = pl.ds(pl.multiple_of(block * planes * points, planes * points), planes * points)
        wave = val_ref[0, pl.ds(block * planes, planes)].reshape(planes * points, LANES).astype(jnp.float32)
        other = pltpu.roll(wave, HALF, 1)
        density = jnp.where(low_lanes, wave, other) * cond_a[rows, :] + jnp.where(low_lanes, other, wave) * cond_b[rows, :]
        high, low = split_parts(density)
        field = contract_last(first_ref[...], jnp.concatenate([high, low], 1))
        for begin in range(0, pairs, 2):
            blocks = [
                [field[part * KEEP : (part + 1) * KEEP, pair * LANES : (pair + 1) * LANES] for pair in (begin, begin + 1)]
                for part in range(2)
            ]
            at = pl.ds(pl.multiple_of((block * pairs + begin) * KEEP, 2 * KEEP), 2 * KEEP)
            store_split(middle, at, blocks)

    def second_axis(block):
        rows = pl.ds(pl.multiple_of(block * pairs * KEEP, pairs * KEEP), pairs * KEEP)
        high = second_ref[: 2 * LANES]
        table = jnp.concatenate([high, high, second_ref[2 * LANES :]], 0)
        field = jnp.dot(doubled(middle[rows, :]), table, preferred_element_type=jnp.float32)
        for item in range(2):
            turned[item, rows, :] = field[:, item * LANES : (item + 1) * LANES]

    first_axis(0)
    first_axis(1)

    @pl.loop(1, points // planes // 2)
    def _(turn):
        for part in range(2):
            second_axis(2 * turn - 2 + part)
        for part in range(2):
            first_axis(2 * turn + part)

    second_axis(points // planes - 2)
    second_axis(points // planes - 1)

    for begin in range(0, KEEP, 4):
        both = []
        for pair in range(2):
            items = [
                turned[item, pl.ds(begin + 2 * pair + k3, points // 2, stride=KEEP), :]
                for k3 in range(2)
                for item in range(2)
            ]
            turn = jnp.concatenate(items, 0).T
            both.append((turn[:KEEP], turn[HALF : HALF + KEEP]))
        store_split(last, slice(begin // 2 * KEEP, (begin // 2 + 2) * KEEP), list(zip(*both)))

    bands = val_energy_ref.shape[0] * cond_energy_ref.shape[0]
    gap = cond_energy_ref[owner_ref[0]] - val_energy_ref[first_band + band]
    weight = -2.0 / (math.sqrt(bands) * jnp.full((1, LANES), gap, jnp.float32))
    slab = slab_tiles(plan)
    tiles = PARITY_LANES // LANES
    field = contract_last(third_ref[...], last[...])
    for odd in range(2):
        for part in range(2):
            at = (odd * 2 + part) * ROWS_K
            value = field[at : at + ROWS_K]
            plain_ref[part, 0, :, odd * PARITY_LANES : (odd + 1) * PARITY_LANES] = value.astype(jnp.bfloat16)
            for place, tile in enumerate(slab):
                if tile // tiles == odd:
                    inside = value[:, tile % tiles * LANES : (tile % tiles + 1) * LANES]
                    weighted_ref[part, 0, :, place * LANES : (place + 1) * LANES] = (weight * inside).astype(jnp.bfloat16)


def spectra(plan, val_wave, cond_wave, energies, first_band, count):
    points = val_wave.shape[1]
    depth = 2 * PARITY_LANES
    slab_depth = len(slab_tiles(plan)) * LANES
    grid_rows = points * points
    tables = dft_tables(points)
    kernel = lambda *refs: spectrum_kernel(plan, points, first_band, *refs)
    return pl.pallas_call(
        kernel,
        grid=(count,),
        in_specs=[
            pl.BlockSpec(memory_space=pltpu.SMEM),
            pl.BlockSpec(memory_space=pltpu.SMEM),
            pl.BlockSpec(memory_space=pltpu.SMEM),
            pl.BlockSpec((1, points, points, 2 * points), lambda v: (first_band + v, 0, 0, 0)),
            pl.BlockSpec((1, points, points, 2 * points), lambda v: (0, 0, 0, 0)),
            *[pl.BlockSpec(table.shape, lambda v: (0, 0)) for table in tables],
        ],
        out_specs=[
            pl.BlockSpec((2, 1, ROWS_K, depth), lambda v: (0, v, 0, 0)),
            pl.BlockSpec((2, 1, ROWS_K, slab_depth), lambda v: (0, v, 0, 0)),
        ],
        out_shape=[
            jax.ShapeDtypeStruct((2, count, ROWS_K, depth), jnp.bfloat16),
            jax.ShapeDtypeStruct((2, count, ROWS_K, slab_depth), jnp.bfloat16),
        ],
        scratch_shapes=[
            pltpu.VMEM((grid_rows, LANES), jnp.float32),
            pltpu.VMEM((grid_rows, LANES), jnp.float32),
            pltpu.VMEM((points // 2 * KEEP, 4 * LANES), jnp.bfloat16),
            pltpu.VMEM((2, points // 2 * KEEP, LANES), jnp.float32),
            pltpu.VMEM((PARITY_LANES, 4 * LANES), jnp.bfloat16),
        ],
        compiler_params=pltpu.CompilerParams(vmem_limit_bytes=VMEM_BYTES, dimension_semantics=("arbitrary",)),
        cost_estimate=pl.CostEstimate(flops=count, bytes_accessed=count, transcendentals=0),
        name="spectra",
    )(*energies, val_wave, cond_wave, *tables)


def pack_kernel(plan, groups, place_ref, *refs):
    plains, weighteds = refs[:groups], refs[groups : 2 * groups]
    send_ref, slab_ref, sorter, plain_sorted, weighted_sorted = refs[2 * groups :]
    depth, columns = sorter.shape
    count = 2 * sum(plain.shape[1] for plain in plains)
    lane = lax.broadcasted_iota(jnp.int32, (1, LANES), 1)
    for begin in range(0, depth, LANES):
        at = lax.broadcasted_iota(jnp.int32, (LANES, columns), 0) + begin
        sorter[begin : begin + LANES, :] = jnp.where(at == place_ref[...], 1.0, 0.0).astype(jnp.bfloat16)

    def sort_rows(parts, which, target):
        rows = jnp.concatenate([part[n] for n in range(2) for part in parts], 0)
        rows = rows.reshape(count * ROWS_K, rows.shape[2])
        value = jnp.dot(rows, which, preferred_element_type=jnp.float32)
        for tile in range(target.shape[0]):
            target[tile] = value[:, tile * LANES : (tile + 1) * LANES]

    slab = [sorter[tile * LANES : (tile + 1) * LANES, : weighted_sorted.shape[0] * LANES] for tile in slab_tiles(plan)]
    sort_rows(plains, sorter[...], plain_sorted)
    sort_rows(weighteds, jnp.concatenate(slab, 0), weighted_sorted)

    def plain_at(index, tile):
        return plain_sorted[tile, pl.ds(index, count, stride=ROWS_K), :]

    def weighted_at(index, tile):
        return weighted_sorted[tile, pl.ds(index, count, stride=ROWS_K), :]

    for block, bucket in enumerate(plan["buckets"]):

        def keep(tile, value):
            send_ref[block, :, tile * LANES : (tile + 1) * LANES] = value.astype(jnp.bfloat16)

        pack_pieces(bucket.pieces, plan["lanes"], plain_at, count, lane, keep)
    for block, bucket in enumerate(plan["slabs"]):

        def keep_slab(tile, value):
            slab_ref[block, :, tile * LANES : (tile + 1) * LANES] = value.astype(jnp.bfloat16)

        pack_pieces(bucket.pieces, plan["slab_lanes"], weighted_at, count, lane, keep_slab)


def packed(plan, plains, weighteds):
    depth = plains[0].shape[3]
    count = 2 * sum(plain.shape[1] for plain in plains)
    columns = round_up(plan["column_place"].shape[0], 256)
    slab_columns = round_up(plan["slab_columns"], LANES)
    place = np.full((1, columns), -1, np.int32)
    place[0, : plan["column_place"].shape[0]] = plan["column_place"]
    kernel = lambda *refs: pack_kernel(plan, len(plains), *refs)
    vmem = pl.BlockSpec(memory_space=pltpu.VMEM)
    send_shape = (len(plan["buckets"]), count, plan["lanes"])
    slab_shape = (len(plan["slabs"]), count, plan["slab_lanes"])
    return pl.pallas_call(
        kernel,
        in_specs=[vmem] * (1 + 2 * len(plains)),
        out_specs=[vmem] * 2,
        out_shape=[jax.ShapeDtypeStruct(send_shape, jnp.bfloat16), jax.ShapeDtypeStruct(slab_shape, jnp.bfloat16)],
        scratch_shapes=[
            pltpu.VMEM((depth, columns), jnp.bfloat16),
            pltpu.VMEM((columns // LANES, count * ROWS_K, LANES), jnp.float32),
            pltpu.VMEM((slab_columns // LANES, count * ROWS_K, LANES), jnp.float32),
        ],
        compiler_params=pltpu.CompilerParams(vmem_limit_bytes=VMEM_BYTES),
        cost_estimate=pl.CostEstimate(flops=1, bytes_accessed=1, transcendentals=0),
        name="pack",
    )(jnp.asarray(place), *plains, *weighteds)


def one_hot(ids_ref, begin, wanted):
    ids = jnp.broadcast_to(ids_ref[:, pl.ds(begin, LANES)], (LANES, LANES)).T
    ids = jnp.concatenate([ids] * (wanted.shape[1] // LANES), 1)
    return jnp.where(ids == wanted, 1.0, 0.0).astype(jnp.bfloat16)


def left_kernel(group, slab_ref, slab_ids_ref, slab_wanted_ref, left_ref):
    rows = slab_wanted_ref.shape[1]
    choice = jnp.concatenate(
        [one_hot(slab_ids_ref, begin, slab_wanted_ref[...]) for begin in range(0, slab_ids_ref.shape[1], LANES)], 0
    )
    chosen = jnp.dot(slab_ref[...], choice, preferred_element_type=jnp.float32)
    lane = lax.broadcasted_iota(jnp.int32, (1, LANES), 1)
    real_lanes = lane % group < group // 2
    for begin in range(0, chosen.shape[0], LANES):
        turned = chosen[begin : begin + LANES].T
        after = pltpu.roll(turned, LANES - group // 2, 1)
        before = pltpu.roll(turned, group // 2, 1)
        left_ref[:rows, begin : begin + LANES] = turned.astype(jnp.bfloat16)
        left_ref[rows:, begin : begin + LANES] = jnp.where(real_lanes, after, -before).astype(jnp.bfloat16)


def left_side(group, slab, slab_ids, slab_wanted):
    vmem = pl.BlockSpec(memory_space=pltpu.VMEM)
    return pl.pallas_call(
        lambda *refs: left_kernel(group, *refs),
        in_specs=[vmem] * 3,
        out_specs=vmem,
        out_shape=jax.ShapeDtypeStruct((2 * slab_wanted.shape[1], slab.shape[0]), jnp.bfloat16),
        compiler_params=pltpu.CompilerParams(vmem_limit_bytes=VMEM_BYTES),
        cost_estimate=pl.CostEstimate(flops=1, bytes_accessed=1, transcendentals=0),
        name="left_side",
    )(slab, slab_ids, slab_wanted)


def in_order(starts_ref, ids_ref, wanted_ref, panel_ref, hot):
    start = pl.multiple_of(starts_ref[pl.program_id(0)], LANES)
    wanted = wanted_ref[...]
    window = hot.shape[0]
    for begin in range(0, window, LANES):
        hot[begin : begin + LANES, :] = one_hot(ids_ref, pl.multiple_of(start + begin, LANES), wanted)
    return jnp.dot(panel_ref[:, pl.ds(start, window)], hot[...], preferred_element_type=jnp.float32).astype(jnp.bfloat16)


def order_kernel(starts_ref, ids_ref, wanted_ref, panel_ref, out_ref, hot):
    out_ref[...] = in_order(starts_ref, ids_ref, wanted_ref, panel_ref, hot)


def product_kernel(starts_ref, ids_ref, wanted_ref, panel_ref, left_ref, last_ref, out_ref, hot):
    rows = out_ref.shape[1]
    right = jnp.concatenate([in_order(starts_ref, ids_ref, wanted_ref, panel_ref, hot), last_ref[...]], 0)
    chi = jnp.dot(left_ref[...], right, preferred_element_type=jnp.float32)
    out_ref[0] = chi[:rows]
    out_ref[1] = chi[rows:]


def put_in_order(plan, starts, ids, wanted, panel, left=None, last=None):
    columns = wanted.shape[1]
    block = columns // PARTS
    whole = lambda array: pl.BlockSpec(array.shape, lambda n: (0,) * array.ndim)
    in_specs = [
        pl.BlockSpec(memory_space=pltpu.SMEM),
        whole(ids),
        pl.BlockSpec((1, block), lambda n: (0, n)),
        whole(panel),
    ]
    operands = [starts, ids, wanted, panel]
    if left is None:
        out_spec = pl.BlockSpec((panel.shape[0], block), lambda n: (0, n))
        out_shape = jax.ShapeDtypeStruct((panel.shape[0], columns), jnp.bfloat16)
    else:
        rows = left.shape[0] // 2
        in_specs += [whole(left), pl.BlockSpec((last.shape[0], block), lambda n: (0, n))]
        operands += [left, last]
        out_spec = pl.BlockSpec((2, rows, block), lambda n: (0, 0, n))
        out_shape = jax.ShapeDtypeStruct((2, rows, columns), jnp.float32)
    return pl.pallas_call(
        order_kernel if left is None else product_kernel,
        grid=(PARTS,),
        in_specs=in_specs,
        out_specs=out_spec,
        out_shape=out_shape,
        scratch_shapes=[pltpu.VMEM((plan["window"], block), jnp.bfloat16)],
        compiler_params=pltpu.CompilerParams(vmem_limit_bytes=VMEM_BYTES, dimension_semantics=("arbitrary",)),
        cost_estimate=pl.CostEstimate(flops=1, bytes_accessed=1, transcendentals=0),
        name="in_order" if left is None else "product",
    )(*operands)


def on_device(val_wave, cond_wave, val_energy, cond_energy, band_owner, grid_map):
    bands, points = val_wave.shape[0], val_wave.shape[1]
    row_count = lax.axis_size("row")
    col_count = lax.axis_size("col")
    col, row = lax.axis_index("col"), lax.axis_index("row")
    plan = make_plan(points, grid_map.shape[0], col_count, ROWS_DEV * row_count, row_count)
    width = grid_map.shape[0] // col_count
    starts = lax.dynamic_index_in_dim(jnp.asarray(plan["starts"]), col, 0, keepdims=False)
    ids = lax.dynamic_slice(jnp.asarray(plan["ids"]), (col, 0), (1, plan["lanes"]))
    slab_ids = lax.dynamic_slice(jnp.asarray(plan["slab_ids"]), (row, 0), (1, plan["slab_lanes"]))
    wanted = lax.dynamic_slice(grid_map, (col * width,), (width,))[None]
    slab_wanted = lax.dynamic_slice(grid_map, (row * ROWS_DEV,), (ROWS_DEV,))[None]
    chunk = bands // 2
    energies = (band_owner, cond_energy, val_energy)
    slabs = []
    for part in range(2):
        plain, weighted = spectra(plan, val_wave, cond_wave, energies, part * chunk, chunk)
        send, slab = packed(plan, [plain], [weighted])
        slabs.append(slab)
        if part == 0:
            send, cond_wave = lax.optimization_barrier((send, cond_wave))
            early = lax.all_gather(send, "row", axis=1)
        else:
            mine = lax.all_to_all(send, "col", split_axis=0, concat_axis=0, tiled=True).reshape(-1, plan["lanes"])
            mine = put_in_order(plan, starts, ids, wanted, mine)
            last = lax.all_gather(mine, "row", axis=0, tiled=True)
    slab, _ = lax.optimization_barrier((jnp.stack(slabs, 1), mine))
    slab = lax.all_to_all(slab, "row", split_axis=0, concat_axis=0, tiled=True)
    slab = lax.all_to_all(jnp.broadcast_to(slab, (col_count, *slab.shape)), "col", split_axis=0, concat_axis=0)
    early, slab = lax.optimization_barrier((early, slab))
    slab = [slab[:, :, 0], slab[:, :, 1].transpose(1, 0, 2, 3)]
    slab = jnp.stack([part.reshape(-1, plan["slab_lanes"]) for part in slab]).reshape(-1, plan["slab_lanes"])
    left = left_side(2 * chunk, slab, slab_ids, slab_wanted)
    early = lax.all_to_all(early, "col", split_axis=0, concat_axis=0, tiled=True).reshape(-1, plan["lanes"])
    return put_in_order(plan, starts, ids, wanted, early, left, last)


def solution(mesh):
    in_specs = (P(), P(("row", "col"), None, None, None), P(), P(), P(("row", "col")), P())
    out_specs = P(None, "row", "col")
    return jax.shard_map(
        on_device, mesh=mesh, in_specs=in_specs, out_specs=out_specs, check_vma=False
    )
```

```python
import math

import jax
import jax.numpy as jnp
import numpy as np
from jax import lax
from jax.experimental import pallas as pl
from jax.experimental.pallas import tpu as pltpu
from jax.sharding import PartitionSpec as P

ROWS_DEV = 256
LANES = 128
VMEM_BYTES = 56 * 1024 * 1024
HALF = 64
KEEP = 40
ROWS_K = 48
ORIGIN = KEEP // 2
PARITY_LANES = 896
PARTS = 3


def round_up(value, step):
    return -(-value // step) * step


def length_counts(points):
    freq = np.arange(points) - points // 2
    square = freq * freq
    lengths = square[:, None, None] + square[None, :, None] + square[None, None, :]
    return np.cumsum(np.bincount(lengths.reshape(-1)))


def column_order(top):
    freq = np.arange(KEEP) - ORIGIN
    first, second = np.meshgrid(freq, freq, indexing="ij")
    length = (first * first + second * second).reshape(-1)
    order = np.argsort(length, kind="stable")
    order = order[length[order] <= top]
    return first.reshape(-1)[order], second.reshape(-1)[order], length[order]


def column_place(index_2, index_3):
    return index_3 % 2 * PARITY_LANES + index_3 // 2 * KEEP + index_2


class Bucket:
    def __init__(self, ranges, column_length):
        self.pieces = []
        self.edges = {}
        offset = 0
        for low, high in ranges:
            begin = offset
            for index in range(KEEP):
                freq = index - ORIGIN
                start = int(np.searchsorted(column_length, low - freq * freq, side="left"))
                stop = int(np.searchsorted(column_length, high - freq * freq, side="right"))
                if stop > start:
                    self.pieces.append((index, start, stop, offset))
                    offset += stop - start
            for length in range(low, high + 1):
                self.edges[length] = (begin, offset)
        self.size = offset

    def ids(self, column_2, column_3, points, width):
        out = np.full((width,), -1, np.int32)
        for index, start, stop, offset in self.pieces:
            k1 = (index - ORIGIN) % points
            k2 = column_2[start:stop] % points
            k3 = column_3[start:stop] % points
            out[offset : offset + stop - start] = (k1 * points + k2) * points + k3
        return out


def length_ranges(cumulative, first, step, count):
    shell = lambda rank: int(np.searchsorted(cumulative, rank, side="right"))
    ranges, low = [], shell(first)
    for part in range(1, count):
        before, after = shell(first + part * step - 1), shell(first + part * step)
        if before == after:
            if low < before:
                ranges.append((low, before - 1))
            if low <= before:
                ranges.append((before, before))
        elif low <= before:
            ranges.append((low, before))
        low = before + 1
    high = shell(first + count * step - 1)
    if low <= high:
        ranges.append((low, high))
    return ranges


def make_plan(points, total, blocks, slab, slab_blocks):
    cumulative = length_counts(points)
    shell = lambda rank: int(np.searchsorted(cumulative, rank, side="right"))
    width, slab_width = total // blocks, slab // slab_blocks
    step = width // PARTS
    column_2, column_3, column_length = column_order(shell(total - 1))
    buckets = [Bucket(length_ranges(cumulative, n * width, step, PARTS), column_length) for n in range(blocks)]
    slabs = [Bucket(length_ranges(cumulative, n * slab_width, slab_width, 1), column_length) for n in range(slab_blocks)]
    slab_top = shell(slab - 1)
    lanes = round_up(max(bucket.size for bucket in buckets), LANES)
    slab_lanes = round_up(max(bucket.size for bucket in slabs), LANES)
    windows = np.zeros((blocks, PARTS, 2), np.int64)
    for n, bucket in enumerate(buckets):
        for part in range(PARTS):
            rank = n * width + part * step
            windows[n, part, 0] = bucket.edges[shell(rank)][0] // LANES * LANES
            windows[n, part, 1] = round_up(bucket.edges[shell(rank + step - 1)][1], LANES)
    window = int((windows[..., 1] - windows[..., 0]).max())
    return dict(
        buckets=buckets,
        slabs=slabs,
        slab_columns=int(np.searchsorted(column_length, slab_top, side="right")),
        slab_edge=math.isqrt(slab_top),
        lanes=lanes,
        slab_lanes=slab_lanes,
        window=window,
        starts=np.minimum(windows[..., 0], lanes - window).astype(np.int32),
        ids=np.stack([bucket.ids(column_2, column_3, points, lanes) for bucket in buckets]),
        slab_ids=np.stack([bucket.ids(column_2, column_3, points, slab_lanes) for bucket in slabs]),
        column_place=column_place(column_2 + ORIGIN, column_3 + ORIGIN).astype(np.int32),
    )


def dft_tables(points):
    n = np.arange(points)
    freq = np.arange(KEEP) - ORIGIN
    angle = (n[:, None] * freq[None, :] % points) * (2.0 * np.pi / points)
    cosine, sine = np.cos(angle), np.sin(angle)
    one = np.zeros((2, points, 2, HALF))
    one[0, :, 0, :KEEP] = cosine
    one[1, :, 0, :KEEP] = sine
    one[0, :, 1, :KEEP] = -sine
    one[1, :, 1, :KEEP] = cosine
    two = np.zeros((2, 2, points, 2, 2, HALF))
    for item in range(2):
        two[:, item, :, item] = one

    def parts(table):
        high = table.astype(jnp.bfloat16)
        return high, (table - high.astype(np.float64)).astype(jnp.bfloat16)

    high, low = parts(one[..., :KEEP].reshape(2 * points, 2 * KEEP).T)
    first = np.concatenate([high, high, low], 1)
    second = np.concatenate(parts(two.reshape(4 * points, 4 * HALF)), 0)
    halves = two[..., :ROWS_K].reshape(2, 2, points // 2, 2, 4 * ROWS_K).transpose(0, 1, 3, 2, 4)
    high, low = parts(halves.reshape(4 * points, 4 * ROWS_K).T)
    third = np.concatenate([high, high, low], 1)
    return [jnp.asarray(table) for table in (first, second, third)]


def split_parts(value):
    high = value.astype(jnp.bfloat16)
    low = (value - high.astype(jnp.float32)).astype(jnp.bfloat16)
    return high, low


def store_split(target, rows, blocks):
    for part, block in enumerate(blocks):
        high, low = split_parts(jnp.concatenate(block, 0))
        target[rows, part * LANES : (part + 1) * LANES] = high
        target[rows, (part + 2) * LANES : (part + 3) * LANES] = low


def doubled(stored):
    return jnp.concatenate([stored, stored[:, : stored.shape[1] // 2]], 1)


def contract_last(table, stored):
    return lax.dot_general(table, doubled(stored), (((1,), (1,)), ((), ())), preferred_element_type=jnp.float32)


def pack_pieces(pieces, width, source, rows, lane, out):
    for tile in range(width // LANES):
        left, right = tile * LANES, (tile + 1) * LANES
        value = jnp.zeros((rows, LANES), jnp.float32)
        for index, start, stop, offset in pieces:
            begin, end = max(left, offset), min(right, offset + stop - start)
            while begin < end:
                at = start + begin - offset
                block = source(index, at // LANES)
                shift = (begin - at) % LANES
                if shift:
                    block = pltpu.roll(block, shift, 1)
                value = block if begin == left else jnp.where(lane >= begin - left, block, value)
                begin = min(end, begin + LANES - at % LANES)
        out(tile, value)


def slab_tiles(plan):
    first = (ORIGIN - plan["slab_edge"]) // 2 * KEEP // LANES
    last = round_up(((ORIGIN + plan["slab_edge"]) // 2 + 1) * KEEP, LANES) // LANES
    return [odd * PARITY_LANES // LANES + tile for odd in range(2) for tile in range(first, last)]


def spectrum_kernel(plan, points, first_band, owner_ref, cond_energy_ref, val_energy_ref, val_ref, cond_ref, first_ref,
                    second_ref, third_ref, plain_ref, weighted_ref, cond_a, cond_b, middle, turned, last):
    band = pl.program_id(0)
    planes = 8
    pairs = planes // 2
    lane = lax.broadcasted_iota(jnp.int32, (1, LANES), 1)
    low_lanes = lane < HALF

    @pl.when(band == 0)
    def _():
        scale = 1.0 / float(points) ** 1.5
        sign = jnp.where(low_lanes, scale, -scale)

        @pl.loop(0, points // planes)
        def _(block):
            rows = pl.ds(pl.multiple_of(block * planes * points, planes * points), planes * points)
            wave = cond_ref[0, pl.ds(block * planes, planes)].reshape(planes * points, LANES).astype(jnp.float32)
            cond_a[rows, :] = wave * scale
            cond_b[rows, :] = pltpu.roll(wave, HALF, 1) * sign

        last[KEEP * KEEP // 2 :, :] = jnp.zeros((last.shape[0] - KEEP * KEEP // 2, 4 * LANES), jnp.bfloat16)

    def first_axis(block):
        rows = pl.ds(pl.multiple_of(block * planes * points, planes * points), planes * points)
        wave = val_ref[0, pl.ds(block * planes, planes)].reshape(planes * points, LANES).astype(jnp.float32)
        other = pltpu.roll(wave, HALF, 1)
        density = jnp.where(low_lanes, wave, other) * cond_a[rows, :] + jnp.where(low_lanes, other, wave) * cond_b[rows, :]
        high, low = split_parts(density)
        field = contract_last(first_ref[...], jnp.concatenate([high, low], 1))
        for begin in range(0, pairs, 2):
            blocks = [
                [field[part * KEEP : (part + 1) * KEEP, pair * LANES : (pair + 1) * LANES] for pair in (begin, begin + 1)]
                for part in range(2)
            ]
            at = pl.ds(pl.multiple_of((block * pairs + begin) * KEEP, 2 * KEEP), 2 * KEEP)
            store_split(middle, at, blocks)

    def second_axis(block):
        rows = pl.ds(pl.multiple_of(block * pairs * KEEP, pairs * KEEP), pairs * KEEP)
        high = second_ref[: 2 * LANES]
        table = jnp.concatenate([high, high, second_ref[2 * LANES :]], 0)
        field = jnp.dot(doubled(middle[rows, :]), table, preferred_element_type=jnp.float32)
        for item in range(2):
            turned[item, rows, :] = field[:, item * LANES : (item + 1) * LANES]

    first_axis(0)
    first_axis(1)

    @pl.loop(1, points // planes // 2)
    def _(turn):
        for part in range(2):
            second_axis(2 * turn - 2 + part)
        for part in range(2):
            first_axis(2 * turn + part)

    second_axis(points // planes - 2)
    second_axis(points // planes - 1)

    for begin in range(0, KEEP, 4):
        both = []
        for pair in range(2):
            items = [
                turned[item, pl.ds(begin + 2 * pair + k3, points // 2, stride=KEEP), :]
                for k3 in range(2)
                for item in range(2)
            ]
            turn = jnp.concatenate(items, 0).T
            both.append((turn[:KEEP], turn[HALF : HALF + KEEP]))
        store_split(last, slice(begin // 2 * KEEP, (begin // 2 + 2) * KEEP), list(zip(*both)))

    bands = val_energy_ref.shape[0] * cond_energy_ref.shape[0]
    gap = cond_energy_ref[owner_ref[0]] - val_energy_ref[first_band + band]
    weight = -2.0 / (math.sqrt(bands) * jnp.full((1, LANES), gap, jnp.float32))
    slab = slab_tiles(plan)
    tiles = PARITY_LANES // LANES
    field = contract_last(third_ref[...], last[...])
    for odd in range(2):
        for part in range(2):
            at = (odd * 2 + part) * ROWS_K
            value = field[at : at + ROWS_K]
            plain_ref[part, 0, :, odd * PARITY_LANES : (odd + 1) * PARITY_LANES] = value.astype(jnp.bfloat16)
            for place, tile in enumerate(slab):
                if tile // tiles == odd:
                    inside = value[:, tile % tiles * LANES : (tile % tiles + 1) * LANES]
                    weighted_ref[part, 0, :, place * LANES : (place + 1) * LANES] = (weight * inside).astype(jnp.bfloat16)


def spectra(plan, val_wave, cond_wave, energies, first_band, count):
    points = val_wave.shape[1]
    depth = 2 * PARITY_LANES
    slab_depth = len(slab_tiles(plan)) * LANES
    grid_rows = points * points
    tables = dft_tables(points)
    kernel = lambda *refs: spectrum_kernel(plan, points, first_band, *refs)
    return pl.pallas_call(
        kernel,
        grid=(count,),
        in_specs=[
            pl.BlockSpec(memory_space=pltpu.SMEM),
            pl.BlockSpec(memory_space=pltpu.SMEM),
            pl.BlockSpec(memory_space=pltpu.SMEM),
            pl.BlockSpec((1, points, points, 2 * points), lambda v: (first_band + v, 0, 0, 0)),
            pl.BlockSpec((1, points, points, 2 * points), lambda v: (0, 0, 0, 0)),
            *[pl.BlockSpec(table.shape, lambda v: (0, 0)) for table in tables],
        ],
        out_specs=[
            pl.BlockSpec((2, 1, ROWS_K, depth), lambda v: (0, v, 0, 0)),
            pl.BlockSpec((2, 1, ROWS_K, slab_depth), lambda v: (0, v, 0, 0)),
        ],
        out_shape=[
            jax.ShapeDtypeStruct((2, count, ROWS_K, depth), jnp.bfloat16),
            jax.ShapeDtypeStruct((2, count, ROWS_K, slab_depth), jnp.bfloat16),
        ],
        scratch_shapes=[
            pltpu.VMEM((grid_rows, LANES), jnp.float32),
            pltpu.VMEM((grid_rows, LANES), jnp.float32),
            pltpu.VMEM((points // 2 * KEEP, 4 * LANES), jnp.bfloat16),
            pltpu.VMEM((2, points // 2 * KEEP, LANES), jnp.float32),
            pltpu.VMEM((PARITY_LANES, 4 * LANES), jnp.bfloat16),
        ],
        compiler_params=pltpu.CompilerParams(vmem_limit_bytes=VMEM_BYTES, dimension_semantics=("arbitrary",)),
        cost_estimate=pl.CostEstimate(flops=count, bytes_accessed=count, transcendentals=0),
        name="spectra",
    )(*energies, val_wave, cond_wave, *tables)


def pack_kernel(plan, groups, place_ref, *refs):
    plains, weighteds = refs[:groups], refs[groups : 2 * groups]
    send_ref, slab_ref, sorter, plain_sorted, weighted_sorted = refs[2 * groups :]
    depth, columns = sorter.shape
    count = 2 * sum(plain.shape[1] for plain in plains)
    lane = lax.broadcasted_iota(jnp.int32, (1, LANES), 1)
    for begin in range(0, depth, LANES):
        at = lax.broadcasted_iota(jnp.int32, (LANES, columns), 0) + begin
        sorter[begin : begin + LANES, :] = jnp.where(at == place_ref[...], 1.0, 0.0).astype(jnp.bfloat16)

    def sort_rows(parts, which, target):
        rows = jnp.concatenate([part[n] for n in range(2) for part in parts], 0)
        rows = rows.reshape(count * ROWS_K, rows.shape[2])
        value = jnp.dot(rows, which, preferred_element_type=jnp.float32)
        for tile in range(target.shape[0]):
            target[tile] = value[:, tile * LANES : (tile + 1) * LANES]

    slab = [sorter[tile * LANES : (tile + 1) * LANES, : weighted_sorted.shape[0] * LANES] for tile in slab_tiles(plan)]
    sort_rows(plains, sorter[...], plain_sorted)
    sort_rows(weighteds, jnp.concatenate(slab, 0), weighted_sorted)

    def plain_at(index, tile):
        return plain_sorted[tile, pl.ds(index, count, stride=ROWS_K), :]

    def weighted_at(index, tile):
        return weighted_sorted[tile, pl.ds(index, count, stride=ROWS_K), :]

    for block, bucket in enumerate(plan["buckets"]):

        def keep(tile, value):
            send_ref[block, :, tile * LANES : (tile + 1) * LANES] = value.astype(jnp.bfloat16)

        pack_pieces(bucket.pieces, plan["lanes"], plain_at, count, lane, keep)
    for block, bucket in enumerate(plan["slabs"]):

        def keep_slab(tile, value):
            slab_ref[block, :, tile * LANES : (tile + 1) * LANES] = value.astype(jnp.bfloat16)

        pack_pieces(bucket.pieces, plan["slab_lanes"], weighted_at, count, lane, keep_slab)


def packed(plan, plains, weighteds):
    depth = plains[0].shape[3]
    count = 2 * sum(plain.shape[1] for plain in plains)
    columns = round_up(plan["column_place"].shape[0], 256)
    slab_columns = round_up(plan["slab_columns"], LANES)
    place = np.full((1, columns), -1, np.int32)
    place[0, : plan["column_place"].shape[0]] = plan["column_place"]
    kernel = lambda *refs: pack_kernel(plan, len(plains), *refs)
    vmem = pl.BlockSpec(memory_space=pltpu.VMEM)
    send_shape = (len(plan["buckets"]), count, plan["lanes"])
    slab_shape = (len(plan["slabs"]), count, plan["slab_lanes"])
    return pl.pallas_call(
        kernel,
        in_specs=[vmem] * (1 + 2 * len(plains)),
        out_specs=[vmem] * 2,
        out_shape=[jax.ShapeDtypeStruct(send_shape, jnp.bfloat16), jax.ShapeDtypeStruct(slab_shape, jnp.bfloat16)],
        scratch_shapes=[
            pltpu.VMEM((depth, columns), jnp.bfloat16),
            pltpu.VMEM((columns // LANES, count * ROWS_K, LANES), jnp.float32),
            pltpu.VMEM((slab_columns // LANES, count * ROWS_K, LANES), jnp.float32),
        ],
        compiler_params=pltpu.CompilerParams(vmem_limit_bytes=VMEM_BYTES),
        cost_estimate=pl.CostEstimate(flops=1, bytes_accessed=1, transcendentals=0),
        name="pack",
    )(jnp.asarray(place), *plains, *weighteds)


def one_hot(ids_ref, begin, wanted):
    ids = jnp.broadcast_to(ids_ref[:, pl.ds(begin, LANES)], (LANES, LANES)).T
    ids = jnp.concatenate([ids] * (wanted.shape[1] // LANES), 1)
    return jnp.where(ids == wanted, 1.0, 0.0).astype(jnp.bfloat16)


def left_kernel(group, slab_ref, slab_ids_ref, slab_wanted_ref, left_ref):
    rows = slab_wanted_ref.shape[1]
    choice = jnp.concatenate(
        [one_hot(slab_ids_ref, begin, slab_wanted_ref[...]) for begin in range(0, slab_ids_ref.shape[1], LANES)], 0
    )
    chosen = jnp.dot(slab_ref[...], choice, preferred_element_type=jnp.float32)
    lane = lax.broadcasted_iota(jnp.int32, (1, LANES), 1)
    real_lanes = lane % group < group // 2
    for begin in range(0, chosen.shape[0], LANES):
        turned = chosen[begin : begin + LANES].T
        after = pltpu.roll(turned, LANES - group // 2, 1)
        before = pltpu.roll(turned, group // 2, 1)
        left_ref[:rows, begin : begin + LANES] = turned.astype(jnp.bfloat16)
        left_ref[rows:, begin : begin + LANES] = jnp.where(real_lanes, after, -before).astype(jnp.bfloat16)


def left_side(group, slab, slab_ids, slab_wanted):
    vmem = pl.BlockSpec(memory_space=pltpu.VMEM)
    return pl.pallas_call(
        lambda *refs: left_kernel(group, *refs),
        in_specs=[vmem] * 3,
        out_specs=vmem,
        out_shape=jax.ShapeDtypeStruct((2 * slab_wanted.shape[1], slab.shape[0]), jnp.bfloat16),
        compiler_params=pltpu.CompilerParams(vmem_limit_bytes=VMEM_BYTES),
        cost_estimate=pl.CostEstimate(flops=1, bytes_accessed=1, transcendentals=0),
        name="left_side",
    )(slab, slab_ids, slab_wanted)


def order_kernel(starts_ref, ids_ref, wanted_ref, panel_ref, out_ref, hot):
    start = pl.multiple_of(starts_ref[pl.program_id(0)], LANES)
    wanted = wanted_ref[...]
    window = hot.shape[0]
    for begin in range(0, window, LANES):
        hot[begin : begin + LANES, :] = one_hot(ids_ref, pl.multiple_of(start + begin, LANES), wanted)
    ordered = jnp.dot(panel_ref[:, pl.ds(start, window)], hot[...], preferred_element_type=jnp.float32)
    out_ref[...] = ordered.astype(jnp.bfloat16)


def put_in_order(plan, starts, ids, wanted, panel):
    columns = wanted.shape[1]
    block = columns // PARTS
    whole = lambda array: pl.BlockSpec(array.shape, lambda n: (0,) * array.ndim)
    return pl.pallas_call(
        order_kernel,
        grid=(PARTS,),
        in_specs=[
            pl.BlockSpec(memory_space=pltpu.SMEM),
            whole(ids),
            pl.BlockSpec((1, block), lambda n: (0, n)),
            whole(panel),
        ],
        out_specs=pl.BlockSpec((panel.shape[0], block), lambda n: (0, n)),
        out_shape=jax.ShapeDtypeStruct((panel.shape[0], columns), jnp.bfloat16),
        scratch_shapes=[pltpu.VMEM((plan["window"], block), jnp.bfloat16)],
        compiler_params=pltpu.CompilerParams(vmem_limit_bytes=VMEM_BYTES, dimension_semantics=("arbitrary",)),
        cost_estimate=pl.CostEstimate(flops=1, bytes_accessed=1, transcendentals=0),
        name="in_order",
    )(starts, ids, wanted, panel)


def product_kernel(left_ref, *refs):
    *ordered, out_ref = refs
    rows = out_ref.shape[1]
    right = jnp.concatenate([part[...] for part in ordered], 0)
    chi = jnp.dot(left_ref[...], right, preferred_element_type=jnp.float32)
    out_ref[0] = chi[:rows]
    out_ref[1] = chi[rows:]


def product(left, ordered):
    rows, columns = left.shape[0] // 2, ordered[0].shape[1]
    block = columns // (2 * PARTS) // LANES * LANES
    return pl.pallas_call(
        product_kernel,
        grid=(pl.cdiv(columns, block),),
        in_specs=[pl.BlockSpec(left.shape, lambda n: (0, 0))]
        + [pl.BlockSpec((part.shape[0], block), lambda n: (0, n)) for part in ordered],
        out_specs=pl.BlockSpec((2, rows, block), lambda n: (0, 0, n)),
        out_shape=jax.ShapeDtypeStruct((2, rows, columns), jnp.float32),
        compiler_params=pltpu.CompilerParams(vmem_limit_bytes=VMEM_BYTES, dimension_semantics=("arbitrary",)),
        cost_estimate=pl.CostEstimate(flops=1, bytes_accessed=1, transcendentals=0),
        name="product",
    )(left, *ordered)


def on_device(val_wave, cond_wave, val_energy, cond_energy, band_owner, grid_map):
    bands, points = val_wave.shape[0], val_wave.shape[1]
    row_count = lax.axis_size("row")
    col_count = lax.axis_size("col")
    col, row = lax.axis_index("col"), lax.axis_index("row")
    plan = make_plan(points, grid_map.shape[0], col_count, ROWS_DEV * row_count, row_count)
    width = grid_map.shape[0] // col_count
    starts = lax.dynamic_index_in_dim(jnp.asarray(plan["starts"]), col, 0, keepdims=False)
    ids = lax.dynamic_slice(jnp.asarray(plan["ids"]), (col, 0), (1, plan["lanes"]))
    slab_ids = lax.dynamic_slice(jnp.asarray(plan["slab_ids"]), (row, 0), (1, plan["slab_lanes"]))
    wanted = lax.dynamic_slice(grid_map, (col * width,), (width,))[None]
    slab_wanted = lax.dynamic_slice(grid_map, (row * ROWS_DEV,), (ROWS_DEV,))[None]
    chunk = bands // 2
    energies = (band_owner, cond_energy, val_energy)
    slabs = []
    for part in range(2):
        plain, weighted = spectra(plan, val_wave, cond_wave, energies, part * chunk, chunk)
        send, slab = packed(plan, [plain], [weighted])
        slabs.append(slab)
        if part == 0:
            send, cond_wave = lax.optimization_barrier((send, cond_wave))
            early = lax.all_gather(send, "row", axis=0)
        else:
            mine = lax.all_to_all(send, "col", split_axis=0, concat_axis=0, tiled=True).reshape(-1, plan["lanes"])
            mine = put_in_order(plan, starts, ids, wanted, mine)
            last = lax.all_gather(mine, "row", axis=0, tiled=True)
    slab, _ = lax.optimization_barrier((jnp.stack(slabs, 1), mine))
    slab = lax.all_to_all(slab, "row", split_axis=0, concat_axis=0, tiled=True)
    early, slab = lax.optimization_barrier((early, slab))
    early = lax.all_to_all(early, "col", split_axis=1, concat_axis=1, tiled=True)
    early = early.transpose(1, 0, 2, 3).reshape(-1, plan["lanes"])
    early, slab = lax.optimization_barrier((early, slab))
    slab = lax.all_to_all(jnp.broadcast_to(slab, (col_count, *slab.shape)), "col", split_axis=0, concat_axis=0)
    slab = [slab[:, :, 0], slab[:, :, 1].transpose(1, 0, 2, 3)]
    slab = jnp.stack([part.reshape(-1, plan["slab_lanes"]) for part in slab]).reshape(-1, plan["slab_lanes"])
    left = left_side(2 * chunk, slab, slab_ids, slab_wanted)
    return product(left, [put_in_order(plan, starts, ids, wanted, early), last])


def solution(mesh):
    in_specs = (P(), P(("row", "col"), None, None, None), P(), P(), P(("row", "col")), P())
    out_specs = P(None, "row", "col")
    return jax.shard_map(
        on_device, mesh=mesh, in_specs=in_specs, out_specs=out_specs, check_vma=False
    )
```

```python
import math

import jax
import jax.numpy as jnp
import numpy as np
from jax import lax
from jax.experimental import pallas as pl
from jax.experimental.pallas import tpu as pltpu
from jax.sharding import PartitionSpec as P

ROWS_DEV = 256
LANES = 128
VMEM_BYTES = 56 * 1024 * 1024
HALF = 64
KEEP = 40
ORIGIN = KEEP // 2
PARITY_LANES = 896
PARTS = 3


def round_up(value, step):
    return -(-value // step) * step


def length_counts(points):
    freq = np.arange(points) - points // 2
    square = freq * freq
    lengths = square[:, None, None] + square[None, :, None] + square[None, None, :]
    return np.cumsum(np.bincount(lengths.reshape(-1)))


def column_order(top):
    freq = np.arange(KEEP) - ORIGIN
    first, second = np.meshgrid(freq, freq, indexing="ij")
    length = (first * first + second * second).reshape(-1)
    order = np.argsort(length, kind="stable")
    order = order[length[order] <= top]
    return first.reshape(-1)[order], second.reshape(-1)[order], length[order]


def column_place(index_2, index_3):
    return index_3 % 2 * PARITY_LANES + index_3 // 2 * KEEP + index_2


class Bucket:
    def __init__(self, ranges, column_length):
        self.pieces = []
        self.edges = {}
        offset = 0
        for low, high in ranges:
            begin = offset
            for index in range(KEEP):
                freq = index - ORIGIN
                start = int(np.searchsorted(column_length, low - freq * freq, side="left"))
                stop = int(np.searchsorted(column_length, high - freq * freq, side="right"))
                if stop > start:
                    self.pieces.append((index, start, stop, offset))
                    offset += stop - start
            for length in range(low, high + 1):
                self.edges[length] = (begin, offset)
        self.size = offset

    def ids(self, column_2, column_3, points, width):
        out = np.full((width,), -1, np.int32)
        for index, start, stop, offset in self.pieces:
            k1 = (index - ORIGIN) % points
            k2 = column_2[start:stop] % points
            k3 = column_3[start:stop] % points
            out[offset : offset + stop - start] = (k1 * points + k2) * points + k3
        return out


def length_ranges(cumulative, first, step, count):
    shell = lambda rank: int(np.searchsorted(cumulative, rank, side="right"))
    ranges, low = [], shell(first)
    for part in range(1, count):
        before, after = shell(first + part * step - 1), shell(first + part * step)
        if before == after:
            if low < before:
                ranges.append((low, before - 1))
            if low <= before:
                ranges.append((before, before))
        elif low <= before:
            ranges.append((low, before))
        low = before + 1
    high = shell(first + count * step - 1)
    if low <= high:
        ranges.append((low, high))
    return ranges


def make_plan(points, total, blocks, slab, slab_blocks):
    cumulative = length_counts(points)
    shell = lambda rank: int(np.searchsorted(cumulative, rank, side="right"))
    width, slab_width = total // blocks, slab // slab_blocks
    step = width // PARTS
    column_2, column_3, column_length = column_order(shell(total - 1))
    buckets = [Bucket(length_ranges(cumulative, n * width, step, PARTS), column_length) for n in range(blocks)]
    slabs = [Bucket(length_ranges(cumulative, n * slab_width, slab_width, 1), column_length) for n in range(slab_blocks)]
    slab_top = shell(slab - 1)
    lanes = round_up(max(bucket.size for bucket in buckets), LANES)
    slab_lanes = round_up(max(bucket.size for bucket in slabs), LANES)
    windows = np.zeros((blocks, PARTS, 2), np.int64)
    for n, bucket in enumerate(buckets):
        for part in range(PARTS):
            rank = n * width + part * step
            windows[n, part, 0] = bucket.edges[shell(rank)][0] // LANES * LANES
            windows[n, part, 1] = round_up(bucket.edges[shell(rank + step - 1)][1], LANES)
    window = int((windows[..., 1] - windows[..., 0]).max())
    return dict(
        buckets=buckets,
        slabs=slabs,
        slab_columns=int(np.searchsorted(column_length, slab_top, side="right")),
        slab_edge=math.isqrt(slab_top),
        lanes=lanes,
        slab_lanes=slab_lanes,
        window=window,
        starts=np.minimum(windows[..., 0], lanes - window).astype(np.int32),
        ids=np.stack([bucket.ids(column_2, column_3, points, lanes) for bucket in buckets]),
        slab_ids=np.stack([bucket.ids(column_2, column_3, points, slab_lanes) for bucket in slabs]),
        column_place=column_place(column_2 + ORIGIN, column_3 + ORIGIN).astype(np.int32),
    )


def dft_tables(points):
    n = np.arange(points)
    freq = np.arange(KEEP) - ORIGIN
    angle = (n[:, None] * freq[None, :] % points) * (2.0 * np.pi / points)
    cosine, sine = np.cos(angle), np.sin(angle)
    one = np.zeros((2, points, 2, HALF))
    one[0, :, 0, :KEEP] = cosine
    one[1, :, 0, :KEEP] = sine
    one[0, :, 1, :KEEP] = -sine
    one[1, :, 1, :KEEP] = cosine
    two = np.zeros((2, 2, points, 2, 2, HALF))
    for item in range(2):
        two[:, item, :, item] = one

    def parts(table):
        high = table.astype(jnp.bfloat16)
        return high, (table - high.astype(np.float64)).astype(jnp.bfloat16)

    high, low = parts(one[..., :KEEP].reshape(2 * points, 2 * KEEP).T)
    first = np.concatenate([high, high, low], 1)
    second = np.concatenate(parts(two.reshape(4 * points, 4 * HALF)), 0)
    halves = two[..., :KEEP].reshape(2, 2, points // 2, 2, 4 * KEEP).transpose(0, 1, 3, 2, 4)
    high, low = parts(halves.reshape(4 * points, 4 * KEEP).T)
    third = np.concatenate([high, high, low], 1)
    return [jnp.asarray(table) for table in (first, second, third)]


def split_parts(value):
    high = value.astype(jnp.bfloat16)
    low = (value - high.astype(jnp.float32)).astype(jnp.bfloat16)
    return high, low


def store_split(target, rows, blocks):
    for part, block in enumerate(blocks):
        high, low = split_parts(jnp.concatenate(block, 0))
        target[rows, part * LANES : (part + 1) * LANES] = high
        target[rows, (part + 2) * LANES : (part + 3) * LANES] = low


def doubled(stored):
    return jnp.concatenate([stored, stored[:, : stored.shape[1] // 2]], 1)


def contract_last(table, stored):
    return lax.dot_general(table, doubled(stored), (((1,), (1,)), ((), ())), preferred_element_type=jnp.float32)


def pack_pieces(pieces, width, source, rows, lane, out):
    for tile in range(width // LANES):
        left, right = tile * LANES, (tile + 1) * LANES
        value = jnp.zeros((rows, LANES), jnp.float32)
        for index, start, stop, offset in pieces:
            begin, end = max(left, offset), min(right, offset + stop - start)
            while begin < end:
                at = start + begin - offset
                block = source(index, at // LANES)
                shift = (begin - at) % LANES
                if shift:
                    block = pltpu.roll(block, shift, 1)
                value = block if begin == left else jnp.where(lane >= begin - left, block, value)
                begin = min(end, begin + LANES - at % LANES)
        out(tile, value)


def slab_tiles(plan):
    first = (ORIGIN - plan["slab_edge"]) // 2 * KEEP // LANES
    last = round_up(((ORIGIN + plan["slab_edge"]) // 2 + 1) * KEEP, LANES) // LANES
    return [odd * PARITY_LANES // LANES + tile for odd in range(2) for tile in range(first, last)]


def spectrum_kernel(plan, points, first_band, count, owner_ref, cond_energy_ref, val_energy_ref, val_ref, cond_ref, place_ref, first_ref,
                    second_ref, third_ref, send_ref, slab_ref, cond_a, cond_b, middle, turned, last, sorter, plain_rows, weighted_rows,
                    plain_sorted, weighted_sorted):
    band = pl.program_id(0)
    planes = 8
    pairs = planes // 2
    lane = lax.broadcasted_iota(jnp.int32, (1, LANES), 1)
    low_lanes = lane < HALF

    @pl.when(band == 0)
    def _():
        scale = 1.0 / float(points) ** 1.5
        sign = jnp.where(low_lanes, scale, -scale)

        @pl.loop(0, points // planes)
        def _(block):
            rows = pl.ds(pl.multiple_of(block * planes * points, planes * points), planes * points)
            wave = cond_ref[0, pl.ds(block * planes, planes)].reshape(planes * points, LANES).astype(jnp.float32)
            cond_a[rows, :] = wave * scale
            cond_b[rows, :] = pltpu.roll(wave, HALF, 1) * sign

        last[KEEP * KEEP // 2 :, :] = jnp.zeros((last.shape[0] - KEEP * KEEP // 2, 4 * LANES), jnp.bfloat16)

    def first_axis(block):
        rows = pl.ds(pl.multiple_of(block * planes * points, planes * points), planes * points)
        wave = val_ref[0, pl.ds(block * planes, planes)].reshape(planes * points, LANES).astype(jnp.float32)
        other = pltpu.roll(wave, HALF, 1)
        density = jnp.where(low_lanes, wave, other) * cond_a[rows, :] + jnp.where(low_lanes, other, wave) * cond_b[rows, :]
        high, low = split_parts(density)
        field = contract_last(first_ref[...], jnp.concatenate([high, low], 1))
        for begin in range(0, pairs, 2):
            blocks = [
                [field[part * KEEP : (part + 1) * KEEP, pair * LANES : (pair + 1) * LANES] for pair in (begin, begin + 1)]
                for part in range(2)
            ]
            at = pl.ds(pl.multiple_of((block * pairs + begin) * KEEP, 2 * KEEP), 2 * KEEP)
            store_split(middle, at, blocks)

    def second_axis(block):
        rows = pl.ds(pl.multiple_of(block * pairs * KEEP, pairs * KEEP), pairs * KEEP)
        high = second_ref[: 2 * LANES]
        table = jnp.concatenate([high, high, second_ref[2 * LANES :]], 0)
        field = jnp.dot(doubled(middle[rows, :]), table, preferred_element_type=jnp.float32)
        for item in range(2):
            turned[item, rows, :] = field[:, item * LANES : (item + 1) * LANES]

    turns = points // planes // 2 - 1
    piece = sorter.shape[0] // (count * turns)
    first_axis(0)
    first_axis(1)

    @pl.loop(1, turns + 1)
    def _(turn):
        begin = pl.multiple_of((band * turns + turn - 1) * piece, 16)
        at = lax.broadcasted_iota(jnp.int32, (piece, sorter.shape[1]), 0) + begin
        sorter[pl.ds(begin, piece), :] = jnp.where(at == place_ref[...], 1.0, 0.0).astype(jnp.bfloat16)
        for part in range(2):
            second_axis(2 * turn - 2 + part)
        for part in range(2):
            first_axis(2 * turn + part)

    second_axis(points // planes - 2)
    second_axis(points // planes - 1)

    for begin in range(0, KEEP, 4):
        both = []
        for pair in range(2):
            items = [
                turned[item, pl.ds(begin + 2 * pair + k3, points // 2, stride=KEEP), :]
                for k3 in range(2)
                for item in range(2)
            ]
            turn = jnp.concatenate(items, 0).T
            both.append((turn[:KEEP], turn[HALF : HALF + KEEP]))
        store_split(last, slice(begin // 2 * KEEP, (begin // 2 + 2) * KEEP), list(zip(*both)))

    bands = val_energy_ref.shape[0] * cond_energy_ref.shape[0]
    gap = cond_energy_ref[owner_ref[0]] - val_energy_ref[first_band + band]
    weight = -2.0 / (math.sqrt(bands) * jnp.full((1, LANES), gap, jnp.float32))
    slab = slab_tiles(plan)
    tiles = PARITY_LANES // LANES
    field = contract_last(third_ref[...], last[...])
    band_rows = pl.ds(pl.multiple_of(band * 2 * KEEP, 2 * KEEP), 2 * KEEP)
    for odd in range(2):
        value = field[odd * 2 * KEEP : (odd + 1) * 2 * KEEP]
        plain_rows[band_rows, odd * PARITY_LANES : (odd + 1) * PARITY_LANES] = value.astype(jnp.bfloat16)
        for place, tile in enumerate(slab):
            if tile // tiles == odd:
                inside = value[:, tile % tiles * LANES : (tile % tiles + 1) * LANES]
                weighted_rows[band_rows, place * LANES : (place + 1) * LANES] = (weight * inside).astype(jnp.bfloat16)

    @pl.when(band == count - 1)
    def _():
        def sort_rows(rows, which, target):
            value = jnp.dot(rows, which, preferred_element_type=jnp.float32)
            for tile in range(target.shape[0]):
                target[tile] = value[:, tile * LANES : (tile + 1) * LANES]

        which = [sorter[tile * LANES : (tile + 1) * LANES, : weighted_sorted.shape[0] * LANES] for tile in slab]
        sort_rows(plain_rows[...], sorter[: 2 * PARITY_LANES, :], plain_sorted)
        sort_rows(weighted_rows[...], jnp.concatenate(which, 0), weighted_sorted)

        def plain_at(index, tile):
            return plain_sorted[tile, pl.ds(index, 2 * count, stride=KEEP), :]

        def weighted_at(index, tile):
            return weighted_sorted[tile, pl.ds(index, 2 * count, stride=KEEP), :]

        for block, bucket in enumerate(plan["buckets"]):

            def keep(tile, value):
                send_ref[block, :, tile * LANES : (tile + 1) * LANES] = value.astype(jnp.bfloat16)

            pack_pieces(bucket.pieces, plan["lanes"], plain_at, 2 * count, lane, keep)
        for block, bucket in enumerate(plan["slabs"]):

            def keep_slab(tile, value):
                slab_ref[block, :, tile * LANES : (tile + 1) * LANES] = value.astype(jnp.bfloat16)

            pack_pieces(bucket.pieces, plan["slab_lanes"], weighted_at, 2 * count, lane, keep_slab)


def spectra(plan, val_wave, cond_wave, energies, first_band, count):
    points = val_wave.shape[1]
    turns = points // 16 - 1
    depth = round_up(-(-2 * PARITY_LANES // (count * turns)), 16) * count * turns
    columns = round_up(plan["column_place"].shape[0], 256)
    slab_columns = round_up(plan["slab_columns"], LANES)
    slab_depth = len(slab_tiles(plan)) * LANES
    place = np.full((1, columns), -1, np.int32)
    place[0, : plan["column_place"].shape[0]] = plan["column_place"]
    grid_rows = points * points
    tables = dft_tables(points)
    send_shape = (len(plan["buckets"]), 2 * count, plan["lanes"])
    slab_shape = (len(plan["slabs"]), 2 * count, plan["slab_lanes"])
    kernel = lambda *refs: spectrum_kernel(plan, points, first_band, count, *refs)
    return pl.pallas_call(
        kernel,
        grid=(count,),
        in_specs=[
            pl.BlockSpec(memory_space=pltpu.SMEM),
            pl.BlockSpec(memory_space=pltpu.SMEM),
            pl.BlockSpec(memory_space=pltpu.SMEM),
            pl.BlockSpec((1, points, points, 2 * points), lambda v: (first_band + v, 0, 0, 0)),
            pl.BlockSpec((1, points, points, 2 * points), lambda v: (0, 0, 0, 0)),
            pl.BlockSpec((1, columns), lambda v: (0, 0)),
            *[pl.BlockSpec(table.shape, lambda v: (0, 0)) for table in tables],
        ],
        out_specs=[pl.BlockSpec(send_shape, lambda v: (0, 0, 0)), pl.BlockSpec(slab_shape, lambda v: (0, 0, 0))],
        out_shape=[jax.ShapeDtypeStruct(send_shape, jnp.bfloat16), jax.ShapeDtypeStruct(slab_shape, jnp.bfloat16)],
        scratch_shapes=[
            pltpu.VMEM((grid_rows, LANES), jnp.float32),
            pltpu.VMEM((grid_rows, LANES), jnp.float32),
            pltpu.VMEM((points // 2 * KEEP, 4 * LANES), jnp.bfloat16),
            pltpu.VMEM((2, points // 2 * KEEP, LANES), jnp.float32),
            pltpu.VMEM((PARITY_LANES, 4 * LANES), jnp.bfloat16),
            pltpu.VMEM((depth, columns), jnp.bfloat16),
            pltpu.VMEM((2 * count * KEEP, 2 * PARITY_LANES), jnp.bfloat16),
            pltpu.VMEM((2 * count * KEEP, slab_depth), jnp.bfloat16),
            pltpu.VMEM((columns // LANES, 2 * count * KEEP, LANES), jnp.float32),
            pltpu.VMEM((slab_columns // LANES, 2 * count * KEEP, LANES), jnp.float32),
        ],
        compiler_params=pltpu.CompilerParams(vmem_limit_bytes=VMEM_BYTES, dimension_semantics=("arbitrary",)),
        cost_estimate=pl.CostEstimate(flops=1, bytes_accessed=1, transcendentals=0),
        name="spectra",
    )(*energies, val_wave, cond_wave, jnp.asarray(place), *tables)


def one_hot(ids_ref, begin, wanted):
    ids = jnp.broadcast_to(ids_ref[:, pl.ds(begin, LANES)], (LANES, LANES)).T
    ids = jnp.concatenate([ids] * (wanted.shape[1] // LANES), 1)
    return jnp.where(ids == wanted, 1.0, 0.0).astype(jnp.bfloat16)


def left_kernel(slab_ref, slab_ids_ref, slab_wanted_ref, left_ref):
    rows = slab_wanted_ref.shape[1]
    choice = jnp.concatenate(
        [one_hot(slab_ids_ref, begin, slab_wanted_ref[...]) for begin in range(0, slab_ids_ref.shape[1], LANES)], 0
    )
    chosen = jnp.dot(slab_ref[...], choice, preferred_element_type=jnp.float32)
    lane = lax.broadcasted_iota(jnp.int32, (1, LANES), 1)
    real_lanes = lane % 2 == 0
    for begin in range(0, chosen.shape[0], LANES):
        turned = chosen[begin : begin + LANES].T
        after = pltpu.roll(turned, LANES - 1, 1)
        before = pltpu.roll(turned, 1, 1)
        left_ref[:rows, begin : begin + LANES] = turned.astype(jnp.bfloat16)
        left_ref[rows:, begin : begin + LANES] = jnp.where(real_lanes, after, -before).astype(jnp.bfloat16)


def left_side(slab, slab_ids, slab_wanted):
    vmem = pl.BlockSpec(memory_space=pltpu.VMEM)
    return pl.pallas_call(
        left_kernel,
        in_specs=[vmem] * 3,
        out_specs=vmem,
        out_shape=jax.ShapeDtypeStruct((2 * slab_wanted.shape[1], slab.shape[0]), jnp.bfloat16),
        compiler_params=pltpu.CompilerParams(vmem_limit_bytes=VMEM_BYTES),
        cost_estimate=pl.CostEstimate(flops=1, bytes_accessed=1, transcendentals=0),
        name="left_side",
    )(slab, slab_ids, slab_wanted)


def order_kernel(starts_ref, ids_ref, wanted_ref, panel_ref, out_ref, hot):
    start = pl.multiple_of(starts_ref[pl.program_id(0)], LANES)
    wanted = wanted_ref[...]
    window = hot.shape[0]
    for begin in range(0, window, LANES):
        hot[begin : begin + LANES, :] = one_hot(ids_ref, pl.multiple_of(start + begin, LANES), wanted)
    ordered = jnp.dot(panel_ref[:, pl.ds(start, window)], hot[...], preferred_element_type=jnp.float32)
    out_ref[...] = ordered.astype(jnp.bfloat16)


def put_in_order(plan, starts, ids, wanted, panel):
    columns = wanted.shape[1]
    block = columns // PARTS
    whole = lambda array: pl.BlockSpec(array.shape, lambda n: (0,) * array.ndim)
    return pl.pallas_call(
        order_kernel,
        grid=(PARTS,),
        in_specs=[
            pl.BlockSpec(memory_space=pltpu.SMEM),
            whole(ids),
            pl.BlockSpec((1, block), lambda n: (0, n)),
            whole(panel),
        ],
        out_specs=pl.BlockSpec((panel.shape[0], block), lambda n: (0, n)),
        out_shape=jax.ShapeDtypeStruct((panel.shape[0], columns), jnp.bfloat16),
        scratch_shapes=[pltpu.VMEM((plan["window"], block), jnp.bfloat16)],
        compiler_params=pltpu.CompilerParams(vmem_limit_bytes=VMEM_BYTES, dimension_semantics=("arbitrary",)),
        cost_estimate=pl.CostEstimate(flops=1, bytes_accessed=1, transcendentals=0),
        name="in_order",
    )(starts, ids, wanted, panel)


def product_kernel(left_ref, *refs):
    *ordered, out_ref = refs
    rows = out_ref.shape[1]
    right = jnp.concatenate([part[...] for part in ordered], 0)
    chi = jnp.dot(left_ref[...], right, preferred_element_type=jnp.float32)
    out_ref[0] = chi[:rows]
    out_ref[1] = chi[rows:]


def product(left, ordered):
    rows, columns = left.shape[0] // 2, ordered[0].shape[1]
    block = columns // (2 * PARTS) // LANES * LANES
    return pl.pallas_call(
        product_kernel,
        grid=(pl.cdiv(columns, block),),
        in_specs=[pl.BlockSpec(left.shape, lambda n: (0, 0))]
        + [pl.BlockSpec((part.shape[0], block), lambda n: (0, n)) for part in ordered],
        out_specs=pl.BlockSpec((2, rows, block), lambda n: (0, 0, n)),
        out_shape=jax.ShapeDtypeStruct((2, rows, columns), jnp.float32),
        compiler_params=pltpu.CompilerParams(vmem_limit_bytes=VMEM_BYTES, dimension_semantics=("arbitrary",)),
        cost_estimate=pl.CostEstimate(flops=1, bytes_accessed=1, transcendentals=0),
        name="product",
    )(left, *ordered)


def on_device(val_wave, cond_wave, val_energy, cond_energy, band_owner, grid_map):
    bands, points = val_wave.shape[0], val_wave.shape[1]
    row_count = lax.axis_size("row")
    col_count = lax.axis_size("col")
    col, row = lax.axis_index("col"), lax.axis_index("row")
    plan = make_plan(points, grid_map.shape[0], col_count, ROWS_DEV * row_count, row_count)
    width = grid_map.shape[0] // col_count
    starts = lax.dynamic_index_in_dim(jnp.asarray(plan["starts"]), col, 0, keepdims=False)
    ids = lax.dynamic_slice(jnp.asarray(plan["ids"]), (col, 0), (1, plan["lanes"]))
    slab_ids = lax.dynamic_slice(jnp.asarray(plan["slab_ids"]), (row, 0), (1, plan["slab_lanes"]))
    wanted = lax.dynamic_slice(grid_map, (col * width,), (width,))[None]
    slab_wanted = lax.dynamic_slice(grid_map, (row * ROWS_DEV,), (ROWS_DEV,))[None]
    chunk = bands // 2
    energies = (band_owner, cond_energy, val_energy)
    slabs = []
    for part in range(2):
        send, slab = spectra(plan, val_wave, cond_wave, energies, part * chunk, chunk)
        slabs.append(slab)
        if part == 0:
            send, cond_wave = lax.optimization_barrier((send, cond_wave))
            early = lax.all_gather(send, "row", axis=1)
        else:
            mine = lax.all_to_all(send, "col", split_axis=0, concat_axis=0, tiled=True).reshape(-1, plan["lanes"])
            mine = put_in_order(plan, starts, ids, wanted, mine)
            last = lax.all_gather(mine, "row", axis=0, tiled=True)
    slab, _ = lax.optimization_barrier((jnp.stack(slabs, 1), mine))
    slab = lax.all_to_all(slab, "row", split_axis=0, concat_axis=0, tiled=True)
    slab = lax.all_to_all(jnp.broadcast_to(slab, (col_count, *slab.shape)), "col", split_axis=0, concat_axis=0)
    early, slab = lax.optimization_barrier((early, slab))
    slab = [slab[:, :, 0], slab[:, :, 1].transpose(1, 0, 2, 3)]
    slab = jnp.stack([part.reshape(-1, plan["slab_lanes"]) for part in slab]).reshape(-1, plan["slab_lanes"])
    left = left_side(slab, slab_ids, slab_wanted)
    early = lax.all_to_all(early, "col", split_axis=0, concat_axis=0, tiled=True).reshape(-1, plan["lanes"])
    return product(left, [put_in_order(plan, starts, ids, wanted, early), last])


def solution(mesh):
    in_specs = (P(), P(("row", "col"), None, None, None), P(), P(), P(("row", "col")), P())
    out_specs = P(None, "row", "col")
    return jax.shard_map(
        on_device, mesh=mesh, in_specs=in_specs, out_specs=out_specs, check_vma=False
    )
```

```python
import math

import jax
import jax.numpy as jnp
import numpy as np
from jax import lax
from jax.experimental import pallas as pl
from jax.experimental.pallas import tpu as pltpu
from jax.sharding import PartitionSpec as P

ROWS_DEV = 256
LANES = 128
VMEM_BYTES = 56 * 1024 * 1024
HALF = 64
KEEP = 40
ORIGIN = KEEP // 2
PARITY_LANES = 896
PARTS = 3


def round_up(value, step):
    return -(-value // step) * step


def length_counts(points):
    freq = np.arange(points) - points // 2
    square = freq * freq
    lengths = square[:, None, None] + square[None, :, None] + square[None, None, :]
    return np.cumsum(np.bincount(lengths.reshape(-1)))


def column_order(top):
    freq = np.arange(KEEP) - ORIGIN
    first, second = np.meshgrid(freq, freq, indexing="ij")
    length = (first * first + second * second).reshape(-1)
    order = np.argsort(length, kind="stable")
    order = order[length[order] <= top]
    return first.reshape(-1)[order], second.reshape(-1)[order], length[order]


def column_place(index_2, index_3):
    return index_3 % 2 * PARITY_LANES + index_3 // 2 * KEEP + index_2


class Bucket:
    def __init__(self, ranges, column_length):
        self.pieces = []
        self.edges = {}
        offset = 0
        for low, high in ranges:
            begin = offset
            for index in range(KEEP):
                freq = index - ORIGIN
                start = int(np.searchsorted(column_length, low - freq * freq, side="left"))
                stop = int(np.searchsorted(column_length, high - freq * freq, side="right"))
                if stop > start:
                    self.pieces.append((index, start, stop, offset))
                    offset += stop - start
            for length in range(low, high + 1):
                self.edges[length] = (begin, offset)
        self.size = offset

    def ids(self, column_2, column_3, points, width):
        out = np.full((width,), -1, np.int32)
        for index, start, stop, offset in self.pieces:
            k1 = (index - ORIGIN) % points
            k2 = column_2[start:stop] % points
            k3 = column_3[start:stop] % points
            out[offset : offset + stop - start] = (k1 * points + k2) * points + k3
        return out


def length_ranges(cumulative, first, step, count):
    shell = lambda rank: int(np.searchsorted(cumulative, rank, side="right"))
    ranges, low = [], shell(first)
    for part in range(1, count):
        before, after = shell(first + part * step - 1), shell(first + part * step)
        if before == after:
            if low < before:
                ranges.append((low, before - 1))
            if low <= before:
                ranges.append((before, before))
        elif low <= before:
            ranges.append((low, before))
        low = before + 1
    high = shell(first + count * step - 1)
    if low <= high:
        ranges.append((low, high))
    return ranges


def make_plan(points, total, blocks, slab, slab_blocks):
    cumulative = length_counts(points)
    shell = lambda rank: int(np.searchsorted(cumulative, rank, side="right"))
    width, slab_width = total // blocks, slab // slab_blocks
    step = width // PARTS
    column_2, column_3, column_length = column_order(shell(total - 1))
    buckets = [Bucket(length_ranges(cumulative, n * width, step, PARTS), column_length) for n in range(blocks)]
    slabs = [Bucket(length_ranges(cumulative, n * slab_width, slab_width, 1), column_length) for n in range(slab_blocks)]
    slab_top = shell(slab - 1)
    lanes = round_up(max(bucket.size for bucket in buckets), LANES)
    slab_lanes = round_up(max(bucket.size for bucket in slabs), LANES)
    windows = np.zeros((blocks, PARTS, 2), np.int64)
    for n, bucket in enumerate(buckets):
        for part in range(PARTS):
            rank = n * width + part * step
            windows[n, part, 0] = bucket.edges[shell(rank)][0] // LANES * LANES
            windows[n, part, 1] = round_up(bucket.edges[shell(rank + step - 1)][1], LANES)
    window = int((windows[..., 1] - windows[..., 0]).max())
    return dict(
        buckets=buckets,
        slabs=slabs,
        slab_columns=int(np.searchsorted(column_length, slab_top, side="right")),
        slab_edge=math.isqrt(slab_top),
        lanes=lanes,
        slab_lanes=slab_lanes,
        window=window,
        starts=np.minimum(windows[..., 0], lanes - window).astype(np.int32),
        ids=np.stack([bucket.ids(column_2, column_3, points, lanes) for bucket in buckets]),
        slab_ids=np.stack([bucket.ids(column_2, column_3, points, slab_lanes) for bucket in slabs]),
        column_place=column_place(column_2 + ORIGIN, column_3 + ORIGIN).astype(np.int32),
    )


def dft_tables(points):
    n = np.arange(points)
    freq = np.arange(KEEP) - ORIGIN
    angle = (n[:, None] * freq[None, :] % points) * (2.0 * np.pi / points)
    cosine, sine = np.cos(angle), np.sin(angle)
    one = np.zeros((2, points, 2, HALF))
    one[0, :, 0, :KEEP] = cosine
    one[1, :, 0, :KEEP] = sine
    one[0, :, 1, :KEEP] = -sine
    one[1, :, 1, :KEEP] = cosine
    two = np.zeros((2, 2, points, 2, 2, HALF))
    for item in range(2):
        two[:, item, :, item] = one

    def parts(table):
        high = table.astype(jnp.bfloat16)
        return high, (table - high.astype(np.float64)).astype(jnp.bfloat16)

    high, low = parts(one[..., :KEEP].reshape(2 * points, 2 * KEEP).T)
    first = np.concatenate([high, high, low], 1)
    second = np.concatenate(parts(two.reshape(4 * points, 4 * HALF)), 0)
    halves = two[..., :KEEP].reshape(2, 2, points // 2, 2, 4 * KEEP).transpose(0, 1, 3, 2, 4)
    high, low = parts(halves.reshape(4 * points, 4 * KEEP).T)
    third = np.concatenate([high, high, low], 1)
    return [jnp.asarray(table) for table in (first, second, third)]


def split_parts(value):
    high = value.astype(jnp.bfloat16)
    low = (value - high.astype(jnp.float32)).astype(jnp.bfloat16)
    return high, low


def store_split(target, rows, blocks):
    for part, block in enumerate(blocks):
        high, low = split_parts(jnp.concatenate(block, 0))
        target[rows, part * LANES : (part + 1) * LANES] = high
        target[rows, (part + 2) * LANES : (part + 3) * LANES] = low


def doubled(stored):
    return jnp.concatenate([stored, stored[:, : stored.shape[1] // 2]], 1)


def contract_last(table, stored):
    return lax.dot_general(table, doubled(stored), (((1,), (1,)), ((), ())), preferred_element_type=jnp.float32)


def pack_pieces(pieces, width, source, rows, lane, out):
    for tile in range(width // LANES):
        left, right = tile * LANES, (tile + 1) * LANES
        value = jnp.zeros((rows, LANES), jnp.float32)
        for index, start, stop, offset in pieces:
            begin, end = max(left, offset), min(right, offset + stop - start)
            while begin < end:
                at = start + begin - offset
                block = source(index, at // LANES)
                shift = (begin - at) % LANES
                if shift:
                    block = pltpu.roll(block, shift, 1)
                value = block if begin == left else jnp.where(lane >= begin - left, block, value)
                begin = min(end, begin + LANES - at % LANES)
        out(tile, value)


def slab_tiles(plan):
    first = (ORIGIN - plan["slab_edge"]) // 2 * KEEP // LANES
    last = round_up(((ORIGIN + plan["slab_edge"]) // 2 + 1) * KEEP, LANES) // LANES
    return [odd * PARITY_LANES // LANES + tile for odd in range(2) for tile in range(first, last)]


def spectrum_kernel(plan, points, first_band, count, owner_ref, cond_energy_ref, val_energy_ref, val_ref, cond_ref, place_ref, first_ref,
                    second_ref, third_ref, send_ref, slab_ref, cond_a, cond_b, middle, turned, last, sorter, plain_rows, weighted_rows,
                    plain_sorted, weighted_sorted):
    band = pl.program_id(0)
    planes = 16
    pairs = planes // 2
    blocks = points // planes
    lane = lax.broadcasted_iota(jnp.int32, (1, LANES), 1)
    low_lanes = lane < HALF

    @pl.when(band == 0)
    def _():
        scale = 1.0 / float(points) ** 1.5
        sign = jnp.where(low_lanes, scale, -scale)

        @pl.loop(0, points // planes)
        def _(block):
            rows = pl.ds(pl.multiple_of(block * planes * points, planes * points), planes * points)
            wave = cond_ref[0, pl.ds(block * planes, planes)].reshape(planes * points, LANES).astype(jnp.float32)
            cond_a[rows, :] = wave * scale
            cond_b[rows, :] = pltpu.roll(wave, HALF, 1) * sign

        last[KEEP * KEEP // 2 :, :] = jnp.zeros((last.shape[0] - KEEP * KEEP // 2, 4 * LANES), jnp.bfloat16)

    def first_axis(block):
        rows = pl.ds(pl.multiple_of(block * planes * points, planes * points), planes * points)
        wave = val_ref[0, pl.ds(block * planes, planes)].reshape(planes * points, LANES).astype(jnp.float32)
        other = pltpu.roll(wave, HALF, 1)
        density = jnp.where(low_lanes, wave, other) * cond_a[rows, :] + jnp.where(low_lanes, other, wave) * cond_b[rows, :]
        high, low = split_parts(density)
        field = contract_last(first_ref[...], jnp.concatenate([high, low], 1))
        for begin in range(0, pairs, 2):
            blocks = [
                [field[part * KEEP : (part + 1) * KEEP, pair * LANES : (pair + 1) * LANES] for pair in (begin, begin + 1)]
                for part in range(2)
            ]
            at = pl.ds(pl.multiple_of((block * pairs + begin) * KEEP, 2 * KEEP), 2 * KEEP)
            store_split(middle, at, blocks)

    def second_axis(block):
        rows = pl.ds(pl.multiple_of(block * pairs * KEEP, pairs * KEEP), pairs * KEEP)
        high = second_ref[: 2 * LANES]
        table = jnp.concatenate([high, high, second_ref[2 * LANES :]], 0)
        field = jnp.dot(doubled(middle[rows, :]), table, preferred_element_type=jnp.float32)
        for item in range(2):
            turned[item, rows, :] = field[:, item * LANES : (item + 1) * LANES]

    piece = sorter.shape[0] // (count * (blocks - 1))
    first_axis(0)

    @pl.loop(1, blocks)
    def _(turn):
        begin = pl.multiple_of((band * (blocks - 1) + turn - 1) * piece, 16)
        at = lax.broadcasted_iota(jnp.int32, (piece, sorter.shape[1]), 0) + begin
        sorter[pl.ds(begin, piece), :] = jnp.where(at == place_ref[...], 1.0, 0.0).astype(jnp.bfloat16)
        second_axis(turn - 1)
        first_axis(turn)

    second_axis(blocks - 1)

    for begin in range(0, KEEP, 4):
        both = []
        for pair in range(2):
            items = [
                turned[item, pl.ds(begin + 2 * pair + k3, points // 2, stride=KEEP), :]
                for k3 in range(2)
                for item in range(2)
            ]
            turn = jnp.concatenate(items, 0).T
            both.append((turn[:KEEP], turn[HALF : HALF + KEEP]))
        store_split(last, slice(begin // 2 * KEEP, (begin // 2 + 2) * KEEP), list(zip(*both)))

    bands = val_energy_ref.shape[0] * cond_energy_ref.shape[0]
    gap = cond_energy_ref[owner_ref[0]] - val_energy_ref[first_band + band]
    weight = -2.0 / (math.sqrt(bands) * jnp.full((1, LANES), gap, jnp.float32))
    slab = slab_tiles(plan)
    tiles = PARITY_LANES // LANES
    field = contract_last(third_ref[...], last[...])
    band_rows = pl.ds(pl.multiple_of(band * 2 * KEEP, 2 * KEEP), 2 * KEEP)
    for odd in range(2):
        value = field[odd * 2 * KEEP : (odd + 1) * 2 * KEEP]
        plain_rows[band_rows, odd * PARITY_LANES : (odd + 1) * PARITY_LANES] = value.astype(jnp.bfloat16)
        for place, tile in enumerate(slab):
            if tile // tiles == odd:
                inside = value[:, tile % tiles * LANES : (tile % tiles + 1) * LANES]
                weighted_rows[band_rows, place * LANES : (place + 1) * LANES] = (weight * inside).astype(jnp.bfloat16)

    @pl.when(band == count - 1)
    def _():
        def sort_rows(rows, which, target):
            value = jnp.dot(rows, which, preferred_element_type=jnp.float32)
            for tile in range(target.shape[0]):
                target[tile] = value[:, tile * LANES : (tile + 1) * LANES]

        which = [sorter[tile * LANES : (tile + 1) * LANES, : weighted_sorted.shape[0] * LANES] for tile in slab]
        sort_rows(plain_rows[...], sorter[: 2 * PARITY_LANES, :], plain_sorted)
        sort_rows(weighted_rows[...], jnp.concatenate(which, 0), weighted_sorted)

        def plain_at(index, tile):
            return plain_sorted[tile, pl.ds(index, 2 * count, stride=KEEP), :]

        def weighted_at(index, tile):
            return weighted_sorted[tile, pl.ds(index, 2 * count, stride=KEEP), :]

        for block, bucket in enumerate(plan["buckets"]):

            def keep(tile, value):
                send_ref[block, :, tile * LANES : (tile + 1) * LANES] = value.astype(jnp.bfloat16)

            pack_pieces(bucket.pieces, plan["lanes"], plain_at, 2 * count, lane, keep)
        for block, bucket in enumerate(plan["slabs"]):

            def keep_slab(tile, value):
                slab_ref[block, :, tile * LANES : (tile + 1) * LANES] = value.astype(jnp.bfloat16)

            pack_pieces(bucket.pieces, plan["slab_lanes"], weighted_at, 2 * count, lane, keep_slab)


def spectra(plan, val_wave, cond_wave, energies, first_band, count):
    points = val_wave.shape[1]
    turns = points // 16 - 1
    depth = round_up(-(-2 * PARITY_LANES // (count * turns)), 16) * count * turns
    columns = round_up(plan["column_place"].shape[0], 256)
    slab_columns = round_up(plan["slab_columns"], LANES)
    slab_depth = len(slab_tiles(plan)) * LANES
    place = np.full((1, columns), -1, np.int32)
    place[0, : plan["column_place"].shape[0]] = plan["column_place"]
    grid_rows = points * points
    tables = dft_tables(points)
    send_shape = (len(plan["buckets"]), 2 * count, plan["lanes"])
    slab_shape = (len(plan["slabs"]), 2 * count, plan["slab_lanes"])
    kernel = lambda *refs: spectrum_kernel(plan, points, first_band, count, *refs)
    return pl.pallas_call(
        kernel,
        grid=(count,),
        in_specs=[
            pl.BlockSpec(memory_space=pltpu.SMEM),
            pl.BlockSpec(memory_space=pltpu.SMEM),
            pl.BlockSpec(memory_space=pltpu.SMEM),
            pl.BlockSpec((1, points, points, 2 * points), lambda v: (first_band + v, 0, 0, 0)),
            pl.BlockSpec((1, points, points, 2 * points), lambda v: (0, 0, 0, 0)),
            pl.BlockSpec((1, columns), lambda v: (0, 0)),
            *[pl.BlockSpec(table.shape, lambda v: (0, 0)) for table in tables],
        ],
        out_specs=[pl.BlockSpec(send_shape, lambda v: (0, 0, 0)), pl.BlockSpec(slab_shape, lambda v: (0, 0, 0))],
        out_shape=[jax.ShapeDtypeStruct(send_shape, jnp.bfloat16), jax.ShapeDtypeStruct(slab_shape, jnp.bfloat16)],
        scratch_shapes=[
            pltpu.VMEM((grid_rows, LANES), jnp.float32),
            pltpu.VMEM((grid_rows, LANES), jnp.float32),
            pltpu.VMEM((points // 2 * KEEP, 4 * LANES), jnp.bfloat16),
            pltpu.VMEM((2, points // 2 * KEEP, LANES), jnp.float32),
            pltpu.VMEM((PARITY_LANES, 4 * LANES), jnp.bfloat16),
            pltpu.VMEM((depth, columns), jnp.bfloat16),
            pltpu.VMEM((2 * count * KEEP, 2 * PARITY_LANES), jnp.bfloat16),
            pltpu.VMEM((2 * count * KEEP, slab_depth), jnp.bfloat16),
            pltpu.VMEM((columns // LANES, 2 * count * KEEP, LANES), jnp.float32),
            pltpu.VMEM((slab_columns // LANES, 2 * count * KEEP, LANES), jnp.float32),
        ],
        compiler_params=pltpu.CompilerParams(vmem_limit_bytes=VMEM_BYTES, dimension_semantics=("arbitrary",)),
        cost_estimate=pl.CostEstimate(flops=1, bytes_accessed=1, transcendentals=0),
        name="spectra",
    )(*energies, val_wave, cond_wave, jnp.asarray(place), *tables)


def one_hot(ids_ref, begin, wanted):
    ids = jnp.broadcast_to(ids_ref[:, pl.ds(begin, LANES)], (LANES, LANES)).T
    ids = jnp.concatenate([ids] * (wanted.shape[1] // LANES), 1)
    return jnp.where(ids == wanted, 1.0, 0.0).astype(jnp.bfloat16)


def left_kernel(slab_ref, slab_ids_ref, slab_wanted_ref, left_ref):
    rows = slab_wanted_ref.shape[1]
    choice = jnp.concatenate(
        [one_hot(slab_ids_ref, begin, slab_wanted_ref[...]) for begin in range(0, slab_ids_ref.shape[1], LANES)], 0
    )
    chosen = jnp.dot(slab_ref[...], choice, preferred_element_type=jnp.float32)
    lane = lax.broadcasted_iota(jnp.int32, (1, LANES), 1)
    real_lanes = lane % 2 == 0
    for begin in range(0, chosen.shape[0], LANES):
        turned = chosen[begin : begin + LANES].T
        after = pltpu.roll(turned, LANES - 1, 1)
        before = pltpu.roll(turned, 1, 1)
        left_ref[:rows, begin : begin + LANES] = turned.astype(jnp.bfloat16)
        left_ref[rows:, begin : begin + LANES] = jnp.where(real_lanes, after, -before).astype(jnp.bfloat16)


def left_side(slab, slab_ids, slab_wanted):
    vmem = pl.BlockSpec(memory_space=pltpu.VMEM)
    return pl.pallas_call(
        left_kernel,
        in_specs=[vmem] * 3,
        out_specs=vmem,
        out_shape=jax.ShapeDtypeStruct((2 * slab_wanted.shape[1], slab.shape[0]), jnp.bfloat16),
        compiler_params=pltpu.CompilerParams(vmem_limit_bytes=VMEM_BYTES),
        cost_estimate=pl.CostEstimate(flops=1, bytes_accessed=1, transcendentals=0),
        name="left_side",
    )(slab, slab_ids, slab_wanted)


def order_kernel(starts_ref, ids_ref, wanted_ref, panel_ref, out_ref, hot):
    start = pl.multiple_of(starts_ref[pl.program_id(0)], LANES)
    wanted = wanted_ref[...]
    window = hot.shape[0]
    for begin in range(0, window, LANES):
        hot[begin : begin + LANES, :] = one_hot(ids_ref, pl.multiple_of(start + begin, LANES), wanted)
    ordered = jnp.dot(panel_ref[:, pl.ds(start, window)], hot[...], preferred_element_type=jnp.float32)
    out_ref[...] = ordered.astype(jnp.bfloat16)


def put_in_order(plan, starts, ids, wanted, panel):
    columns = wanted.shape[1]
    block = columns // PARTS
    whole = lambda array: pl.BlockSpec(array.shape, lambda n: (0,) * array.ndim)
    return pl.pallas_call(
        order_kernel,
        grid=(PARTS,),
        in_specs=[
            pl.BlockSpec(memory_space=pltpu.SMEM),
            whole(ids),
            pl.BlockSpec((1, block), lambda n: (0, n)),
            whole(panel),
        ],
        out_specs=pl.BlockSpec((panel.shape[0], block), lambda n: (0, n)),
        out_shape=jax.ShapeDtypeStruct((panel.shape[0], columns), jnp.bfloat16),
        scratch_shapes=[pltpu.VMEM((plan["window"], block), jnp.bfloat16)],
        compiler_params=pltpu.CompilerParams(vmem_limit_bytes=VMEM_BYTES, dimension_semantics=("arbitrary",)),
        cost_estimate=pl.CostEstimate(flops=1, bytes_accessed=1, transcendentals=0),
        name="in_order",
    )(starts, ids, wanted, panel)


def product_kernel(left_ref, *refs):
    *ordered, out_ref = refs
    rows = out_ref.shape[1]
    right = jnp.concatenate([part[...] for part in ordered], 0)
    chi = jnp.dot(left_ref[...], right, preferred_element_type=jnp.float32)
    out_ref[0] = chi[:rows]
    out_ref[1] = chi[rows:]


def product(left, ordered):
    rows, columns = left.shape[0] // 2, ordered[0].shape[1]
    block = 6 * LANES
    return pl.pallas_call(
        product_kernel,
        grid=(pl.cdiv(columns, block),),
        in_specs=[pl.BlockSpec(left.shape, lambda n: (0, 0))]
        + [pl.BlockSpec((part.shape[0], block), lambda n: (0, n)) for part in ordered],
        out_specs=pl.BlockSpec((2, rows, block), lambda n: (0, 0, n)),
        out_shape=jax.ShapeDtypeStruct((2, rows, columns), jnp.float32),
        compiler_params=pltpu.CompilerParams(vmem_limit_bytes=VMEM_BYTES, dimension_semantics=("arbitrary",)),
        cost_estimate=pl.CostEstimate(flops=1, bytes_accessed=1, transcendentals=0),
        name="product",
    )(left, *ordered)


def on_device(val_wave, cond_wave, val_energy, cond_energy, band_owner, grid_map):
    bands, points = val_wave.shape[0], val_wave.shape[1]
    row_count = lax.axis_size("row")
    col_count = lax.axis_size("col")
    col, row = lax.axis_index("col"), lax.axis_index("row")
    plan = make_plan(points, grid_map.shape[0], col_count, ROWS_DEV * row_count, row_count)
    width = grid_map.shape[0] // col_count
    starts = lax.dynamic_index_in_dim(jnp.asarray(plan["starts"]), col, 0, keepdims=False)
    ids = lax.dynamic_slice(jnp.asarray(plan["ids"]), (col, 0), (1, plan["lanes"]))
    slab_ids = lax.dynamic_slice(jnp.asarray(plan["slab_ids"]), (row, 0), (1, plan["slab_lanes"]))
    wanted = lax.dynamic_slice(grid_map, (col * width,), (width,))[None]
    slab_wanted = lax.dynamic_slice(grid_map, (row * ROWS_DEV,), (ROWS_DEV,))[None]
    chunk = bands // 2
    energies = (band_owner, cond_energy, val_energy)
    slabs = []
    for part in range(2):
        send, slab = spectra(plan, val_wave, cond_wave, energies, part * chunk, chunk)
        slabs.append(slab)
        if part == 0:
            send, cond_wave = lax.optimization_barrier((send, cond_wave))
            early = lax.all_gather(send, "row", axis=1)
        else:
            mine = lax.all_to_all(send, "col", split_axis=0, concat_axis=0, tiled=True).reshape(-1, plan["lanes"])
            last = lax.all_gather(put_in_order(plan, starts, ids, wanted, mine), "row", axis=0, tiled=True)
    slab, _ = lax.optimization_barrier((jnp.stack(slabs, 1), mine))
    slab = lax.all_to_all(slab, "row", split_axis=0, concat_axis=0, tiled=True)
    slab = lax.all_to_all(jnp.broadcast_to(slab, (col_count, *slab.shape)), "col", split_axis=0, concat_axis=0)
    early, slab = lax.optimization_barrier((early, slab))
    slab = [slab[:, :, 0], slab[:, :, 1].transpose(1, 0, 2, 3)]
    slab = jnp.stack([part.reshape(-1, plan["slab_lanes"]) for part in slab]).reshape(-1, plan["slab_lanes"])
    left = left_side(slab, slab_ids, slab_wanted)
    early = lax.all_to_all(early, "col", split_axis=0, concat_axis=0, tiled=True).reshape(-1, plan["lanes"])
    return product(left, [put_in_order(plan, starts, ids, wanted, early), last])


def solution(mesh):
    in_specs = (P(), P(("row", "col"), None, None, None), P(), P(), P(("row", "col")), P())
    out_specs = P(None, "row", "col")
    return jax.shard_map(
        on_device, mesh=mesh, in_specs=in_specs, out_specs=out_specs, check_vma=False
    )
```

```python
import math

import jax
import jax.numpy as jnp
import numpy as np
from jax import lax
from jax.experimental import pallas as pl
from jax.experimental.pallas import tpu as pltpu
from jax.sharding import PartitionSpec as P

ROWS_DEV = 256
LANES = 128
VMEM_BYTES = 56 * 1024 * 1024
HALF = 64
KEEP = 40
ORIGIN = KEEP // 2
PARITY_LANES = 896
PARTS = 3


def round_up(value, step):
    return -(-value // step) * step


def length_counts(points):
    freq = np.arange(points) - points // 2
    square = freq * freq
    lengths = square[:, None, None] + square[None, :, None] + square[None, None, :]
    return np.cumsum(np.bincount(lengths.reshape(-1)))


def column_order(top):
    freq = np.arange(KEEP) - ORIGIN
    first, second = np.meshgrid(freq, freq, indexing="ij")
    length = (first * first + second * second).reshape(-1)
    order = np.argsort(length, kind="stable")
    order = order[length[order] <= top]
    return first.reshape(-1)[order], second.reshape(-1)[order], length[order]


def column_place(index_2, index_3):
    return index_3 % 2 * PARITY_LANES + index_3 // 2 * KEEP + index_2


class Bucket:
    def __init__(self, ranges, column_length):
        self.pieces = []
        self.edges = {}
        offset = 0
        for low, high in ranges:
            begin = offset
            for index in range(KEEP):
                freq = index - ORIGIN
                start = int(np.searchsorted(column_length, low - freq * freq, side="left"))
                stop = int(np.searchsorted(column_length, high - freq * freq, side="right"))
                if stop > start:
                    self.pieces.append((index, start, stop, offset))
                    offset += stop - start
            for length in range(low, high + 1):
                self.edges[length] = (begin, offset)
        self.size = offset

    def ids(self, column_2, column_3, points, width):
        out = np.full((width,), -1, np.int32)
        for index, start, stop, offset in self.pieces:
            k1 = (index - ORIGIN) % points
            k2 = column_2[start:stop] % points
            k3 = column_3[start:stop] % points
            out[offset : offset + stop - start] = (k1 * points + k2) * points + k3
        return out


def length_ranges(cumulative, first, step, count):
    shell = lambda rank: int(np.searchsorted(cumulative, rank, side="right"))
    ranges, low = [], shell(first)
    for part in range(1, count):
        before, after = shell(first + part * step - 1), shell(first + part * step)
        if before == after:
            if low < before:
                ranges.append((low, before - 1))
            if low <= before:
                ranges.append((before, before))
        elif low <= before:
            ranges.append((low, before))
        low = before + 1
    high = shell(first + count * step - 1)
    if low <= high:
        ranges.append((low, high))
    return ranges


def make_plan(points, total, blocks, slab, slab_blocks):
    cumulative = length_counts(points)
    shell = lambda rank: int(np.searchsorted(cumulative, rank, side="right"))
    width, slab_width = total // blocks, slab // slab_blocks
    step = width // PARTS
    column_2, column_3, column_length = column_order(shell(total - 1))
    buckets = [Bucket(length_ranges(cumulative, n * width, step, PARTS), column_length) for n in range(blocks)]
    slabs = [Bucket(length_ranges(cumulative, n * slab_width, slab_width, 1), column_length) for n in range(slab_blocks)]
    slab_top = shell(slab - 1)
    lanes = round_up(max(bucket.size for bucket in buckets), LANES)
    slab_lanes = round_up(max(bucket.size for bucket in slabs), LANES)
    windows = np.zeros((blocks, PARTS, 2), np.int64)
    for n, bucket in enumerate(buckets):
        for part in range(PARTS):
            rank = n * width + part * step
            windows[n, part, 0] = bucket.edges[shell(rank)][0] // LANES * LANES
            windows[n, part, 1] = round_up(bucket.edges[shell(rank + step - 1)][1], LANES)
    window = int((windows[..., 1] - windows[..., 0]).max())
    return dict(
        buckets=buckets,
        slabs=slabs,
        slab_columns=int(np.searchsorted(column_length, slab_top, side="right")),
        slab_edge=math.isqrt(slab_top),
        lanes=lanes,
        slab_lanes=slab_lanes,
        window=window,
        starts=np.minimum(windows[..., 0], lanes - window).astype(np.int32),
        ids=np.stack([bucket.ids(column_2, column_3, points, lanes) for bucket in buckets]),
        slab_ids=np.stack([bucket.ids(column_2, column_3, points, slab_lanes) for bucket in slabs]),
        column_place=column_place(column_2 + ORIGIN, column_3 + ORIGIN).astype(np.int32),
    )


def dft_tables(points):
    n = np.arange(points)
    freq = np.arange(KEEP) - ORIGIN
    angle = (n[:, None] * freq[None, :] % points) * (2.0 * np.pi / points)
    cosine, sine = np.cos(angle), np.sin(angle)
    one = np.zeros((2, points, 2, HALF))
    one[0, :, 0, :KEEP] = cosine
    one[1, :, 0, :KEEP] = sine
    one[0, :, 1, :KEEP] = -sine
    one[1, :, 1, :KEEP] = cosine
    two = np.zeros((2, 2, points, 2, 2, HALF))
    for item in range(2):
        two[:, item, :, item] = one

    def parts(table):
        high = table.astype(jnp.bfloat16)
        return high, (table - high.astype(np.float64)).astype(jnp.bfloat16)

    high, low = parts(one[..., :KEEP].reshape(2 * points, 2 * KEEP).T)
    first = np.concatenate([high, high, low], 1)
    second = np.concatenate(parts(two.reshape(4 * points, 4 * HALF)), 0)
    halves = two[..., :KEEP].reshape(2, 2, points // 2, 2, 4 * KEEP).transpose(0, 1, 3, 2, 4)
    high, low = parts(halves.reshape(4 * points, 4 * KEEP).T)
    third = np.concatenate([high, high, low], 1)
    return [jnp.asarray(table) for table in (first, second, third)]


def split_parts(value):
    high = value.astype(jnp.bfloat16)
    low = (value - high.astype(jnp.float32)).astype(jnp.bfloat16)
    return high, low


def store_split(target, rows, blocks):
    for part, block in enumerate(blocks):
        high, low = split_parts(jnp.concatenate(block, 0))
        target[rows, part * LANES : (part + 1) * LANES] = high
        target[rows, (part + 2) * LANES : (part + 3) * LANES] = low


def doubled(stored):
    return jnp.concatenate([stored, stored[:, : stored.shape[1] // 2]], 1)


def contract_last(table, stored):
    return lax.dot_general(table, doubled(stored), (((1,), (1,)), ((), ())), preferred_element_type=jnp.float32)


def pack_pieces(pieces, width, source, rows, lane, out):
    for tile in range(width // LANES):
        left, right = tile * LANES, (tile + 1) * LANES
        value = jnp.zeros((rows, LANES), jnp.float32)
        for index, start, stop, offset in pieces:
            begin, end = max(left, offset), min(right, offset + stop - start)
            while begin < end:
                at = start + begin - offset
                block = source(index, at // LANES)
                shift = (begin - at) % LANES
                if shift:
                    block = pltpu.roll(block, shift, 1)
                value = block if begin == left else jnp.where(lane >= begin - left, block, value)
                begin = min(end, begin + LANES - at % LANES)
        out(tile, value)


def slab_tiles(plan):
    first = (ORIGIN - plan["slab_edge"]) // 2 * KEEP // LANES
    last = round_up(((ORIGIN + plan["slab_edge"]) // 2 + 1) * KEEP, LANES) // LANES
    return [odd * PARITY_LANES // LANES + tile for odd in range(2) for tile in range(first, last)]


def spectrum_kernel(plan, points, first_band, count, owner_ref, cond_energy_ref, val_energy_ref, val_ref, cond_ref, place_ref, first_ref,
                    second_ref, third_ref, send_ref, slab_ref, cond_a, cond_b, middle, turned, last, sorter, plain_rows, weighted_rows,
                    plain_sorted, weighted_sorted):
    band = pl.program_id(0)
    planes = 4
    pairs = planes // 2
    lane = lax.broadcasted_iota(jnp.int32, (1, LANES), 1)
    low_lanes = lane < HALF

    @pl.when(band == 0)
    def _():
        scale = 1.0 / float(points) ** 1.5
        sign = jnp.where(low_lanes, scale, -scale)

        @pl.loop(0, points // planes)
        def _(block):
            rows = pl.ds(pl.multiple_of(block * planes * points, planes * points), planes * points)
            wave = cond_ref[0, pl.ds(block * planes, planes)].reshape(planes * points, LANES).astype(jnp.float32)
            cond_a[rows, :] = wave * scale
            cond_b[rows, :] = pltpu.roll(wave, HALF, 1) * sign

        last[KEEP * KEEP // 2 :, :] = jnp.zeros((last.shape[0] - KEEP * KEEP // 2, 4 * LANES), jnp.bfloat16)

    def first_axis(block):
        rows = pl.ds(pl.multiple_of(block * planes * points, planes * points), planes * points)
        wave = val_ref[0, pl.ds(block * planes, planes)].reshape(planes * points, LANES).astype(jnp.float32)
        other = pltpu.roll(wave, HALF, 1)
        density = jnp.where(low_lanes, wave, other) * cond_a[rows, :] + jnp.where(low_lanes, other, wave) * cond_b[rows, :]
        high, low = split_parts(density)
        field = contract_last(first_ref[...], jnp.concatenate([high, low], 1))
        for begin in range(0, pairs, 2):
            blocks = [
                [field[part * KEEP : (part + 1) * KEEP, pair * LANES : (pair + 1) * LANES] for pair in (begin, begin + 1)]
                for part in range(2)
            ]
            at = pl.ds(pl.multiple_of((block * pairs + begin) * KEEP, 2 * KEEP), 2 * KEEP)
            store_split(middle, at, blocks)

    def second_axis(block):
        rows = pl.ds(pl.multiple_of(block * 4 * KEEP, 4 * KEEP), 4 * KEEP)
        high = second_ref[: 2 * LANES]
        table = jnp.concatenate([high, high, second_ref[2 * LANES :]], 0)
        field = jnp.dot(doubled(middle[rows, :]), table, preferred_element_type=jnp.float32)
        for item in range(2):
            turned[item, rows, :] = field[:, item * LANES : (item + 1) * LANES]

    turns = points // 16 - 1
    piece = sorter.shape[0] // (count * turns)
    for part in range(4):
        first_axis(part)

    @pl.loop(1, turns + 1)
    def _(turn):
        begin = pl.multiple_of((band * turns + turn - 1) * piece, 16)
        at = lax.broadcasted_iota(jnp.int32, (piece, sorter.shape[1]), 0) + begin
        sorter[pl.ds(begin, piece), :] = jnp.where(at == place_ref[...], 1.0, 0.0).astype(jnp.bfloat16)
        for part in range(2):
            second_axis(2 * turn - 2 + part)
        for part in range(4):
            first_axis(4 * turn + part)

    for part in range(2):
        second_axis(2 * turns + part)

    for begin in range(0, KEEP, 4):
        both = []
        for pair in range(2):
            items = [
                turned[item, pl.ds(begin + 2 * pair + k3, points // 2, stride=KEEP), :]
                for k3 in range(2)
                for item in range(2)
            ]
            turn = jnp.concatenate(items, 0).T
            both.append((turn[:KEEP], turn[HALF : HALF + KEEP]))
        store_split(last, slice(begin // 2 * KEEP, (begin // 2 + 2) * KEEP), list(zip(*both)))

    bands = val_energy_ref.shape[0] * cond_energy_ref.shape[0]
    gap = cond_energy_ref[owner_ref[0]] - val_energy_ref[first_band + band]
    weight = -2.0 / (math.sqrt(bands) * jnp.full((1, LANES), gap, jnp.float32))
    slab = slab_tiles(plan)
    tiles = PARITY_LANES // LANES
    field = contract_last(third_ref[...], last[...])
    band_rows = pl.ds(pl.multiple_of(band * 2 * KEEP, 2 * KEEP), 2 * KEEP)
    for odd in range(2):
        value = field[odd * 2 * KEEP : (odd + 1) * 2 * KEEP]
        plain_rows[band_rows, odd * PARITY_LANES : (odd + 1) * PARITY_LANES] = value.astype(jnp.bfloat16)
        for place, tile in enumerate(slab):
            if tile // tiles == odd:
                inside = value[:, tile % tiles * LANES : (tile % tiles + 1) * LANES]
                weighted_rows[band_rows, place * LANES : (place + 1) * LANES] = (weight * inside).astype(jnp.bfloat16)

    @pl.when(band == count - 1)
    def _():
        def sort_rows(rows, which, target):
            value = jnp.dot(rows, which, preferred_element_type=jnp.float32)
            for tile in range(target.shape[0]):
                target[tile] = value[:, tile * LANES : (tile + 1) * LANES]

        which = [sorter[tile * LANES : (tile + 1) * LANES, : weighted_sorted.shape[0] * LANES] for tile in slab]
        sort_rows(plain_rows[...], sorter[: 2 * PARITY_LANES, :], plain_sorted)
        sort_rows(weighted_rows[...], jnp.concatenate(which, 0), weighted_sorted)

        def plain_at(index, tile):
            return plain_sorted[tile, pl.ds(index, 2 * count, stride=KEEP), :]

        def weighted_at(index, tile):
            return weighted_sorted[tile, pl.ds(index, 2 * count, stride=KEEP), :]

        for block, bucket in enumerate(plan["buckets"]):

            def keep(tile, value):
                send_ref[block, :, tile * LANES : (tile + 1) * LANES] = value.astype(jnp.bfloat16)

            pack_pieces(bucket.pieces, plan["lanes"], plain_at, 2 * count, lane, keep)
        for block, bucket in enumerate(plan["slabs"]):

            def keep_slab(tile, value):
                slab_ref[block, :, tile * LANES : (tile + 1) * LANES] = value.astype(jnp.bfloat16)

            pack_pieces(bucket.pieces, plan["slab_lanes"], weighted_at, 2 * count, lane, keep_slab)


def spectra(plan, val_wave, cond_wave, energies, first_band, count):
    points = val_wave.shape[1]
    turns = points // 16 - 1
    depth = round_up(-(-2 * PARITY_LANES // (count * turns)), 16) * count * turns
    columns = round_up(plan["column_place"].shape[0], 256)
    slab_columns = round_up(plan["slab_columns"], LANES)
    slab_depth = len(slab_tiles(plan)) * LANES
    place = np.full((1, columns), -1, np.int32)
    place[0, : plan["column_place"].shape[0]] = plan["column_place"]
    grid_rows = points * points
    tables = dft_tables(points)
    send_shape = (len(plan["buckets"]), 2 * count, plan["lanes"])
    slab_shape = (len(plan["slabs"]), 2 * count, plan["slab_lanes"])
    kernel = lambda *refs: spectrum_kernel(plan, points, first_band, count, *refs)
    return pl.pallas_call(
        kernel,
        grid=(count,),
        in_specs=[
            pl.BlockSpec(memory_space=pltpu.SMEM),
            pl.BlockSpec(memory_space=pltpu.SMEM),
            pl.BlockSpec(memory_space=pltpu.SMEM),
            pl.BlockSpec((1, points, points, 2 * points), lambda v: (first_band + v, 0, 0, 0)),
            pl.BlockSpec((1, points, points, 2 * points), lambda v: (0, 0, 0, 0)),
            pl.BlockSpec((1, columns), lambda v: (0, 0)),
            *[pl.BlockSpec(table.shape, lambda v: (0, 0)) for table in tables],
        ],
        out_specs=[pl.BlockSpec(send_shape, lambda v: (0, 0, 0)), pl.BlockSpec(slab_shape, lambda v: (0, 0, 0))],
        out_shape=[jax.ShapeDtypeStruct(send_shape, jnp.bfloat16), jax.ShapeDtypeStruct(slab_shape, jnp.bfloat16)],
        scratch_shapes=[
            pltpu.VMEM((grid_rows, LANES), jnp.float32),
            pltpu.VMEM((grid_rows, LANES), jnp.float32),
            pltpu.VMEM((points // 2 * KEEP, 4 * LANES), jnp.bfloat16),
            pltpu.VMEM((2, points // 2 * KEEP, LANES), jnp.float32),
            pltpu.VMEM((PARITY_LANES, 4 * LANES), jnp.bfloat16),
            pltpu.VMEM((depth, columns), jnp.bfloat16),
            pltpu.VMEM((2 * count * KEEP, 2 * PARITY_LANES), jnp.bfloat16),
            pltpu.VMEM((2 * count * KEEP, slab_depth), jnp.bfloat16),
            pltpu.VMEM((columns // LANES, 2 * count * KEEP, LANES), jnp.float32),
            pltpu.VMEM((slab_columns // LANES, 2 * count * KEEP, LANES), jnp.float32),
        ],
        compiler_params=pltpu.CompilerParams(vmem_limit_bytes=VMEM_BYTES, dimension_semantics=("arbitrary",)),
        cost_estimate=pl.CostEstimate(flops=1, bytes_accessed=1, transcendentals=0),
        name="spectra",
    )(*energies, val_wave, cond_wave, jnp.asarray(place), *tables)


def one_hot(ids, wanted):
    ids = jnp.broadcast_to(ids, (LANES, LANES)).T
    ids = jnp.concatenate([ids] * (wanted.shape[1] // LANES), 1)
    return jnp.where(ids == wanted, 1.0, 0.0).astype(jnp.bfloat16)


def left_kernel(row_count, place_ref, slab_ref, ids_ref, wanted_ref, left_ref):
    rows = wanted_ref.shape[1]
    col_count = slab_ref.shape[0]
    group = slab_ref.shape[1] // (2 * row_count)
    order = [(col, 2 * row) for col in range(col_count) for row in range(row_count)]
    order += [(col, 2 * row + 1) for row in range(row_count) for col in range(col_count)]
    slab = [slab_ref[col, at * group : (at + 1) * group, :].astype(jnp.float32) for col, at in order]
    ids = ids_ref[0]
    choice = [one_hot(ids[:, begin : begin + LANES], wanted_ref[...]) for begin in range(0, ids.shape[1], LANES)]
    chosen = jnp.dot(
        jnp.concatenate(slab, 0).astype(jnp.bfloat16), jnp.concatenate(choice, 0), preferred_element_type=jnp.float32
    )
    lane = lax.broadcasted_iota(jnp.int32, (1, LANES), 1)
    real_lanes = lane % 2 == 0
    for begin in range(0, chosen.shape[0], LANES):
        turned = chosen[begin : begin + LANES].T
        after = pltpu.roll(turned, LANES - 1, 1)
        before = pltpu.roll(turned, 1, 1)
        left_ref[:rows, begin : begin + LANES] = turned.astype(jnp.bfloat16)
        left_ref[rows:, begin : begin + LANES] = jnp.where(real_lanes, after, -before).astype(jnp.bfloat16)


def left_side(plan, place, points_map, slab):
    pairs = slab.shape[0] * slab.shape[1]
    ids = jnp.asarray(plan["slab_ids"])[:, None]
    return pl.pallas_call(
        lambda *refs: left_kernel(ids.shape[0], *refs),
        grid_spec=pltpu.PrefetchScalarGridSpec(
            num_scalar_prefetch=1,
            grid=(1,),
            in_specs=[
                pl.BlockSpec(slab.shape, lambda n, place: (0, 0, 0)),
                pl.BlockSpec((1, *ids.shape[1:]), lambda n, place: (place[1], 0, 0)),
                pl.BlockSpec((1, ROWS_DEV), lambda n, place: (0, place[1])),
            ],
            out_specs=pl.BlockSpec((2 * ROWS_DEV, pairs), lambda n, place: (0, 0)),
        ),
        out_shape=jax.ShapeDtypeStruct((2 * ROWS_DEV, pairs), jnp.bfloat16),
        compiler_params=pltpu.CompilerParams(vmem_limit_bytes=VMEM_BYTES),
        cost_estimate=pl.CostEstimate(flops=1, bytes_accessed=1, transcendentals=0),
        name="left_side",
    )(place, slab, ids, points_map)


def order_kernel(window_starts, place_ref, ids_ref, wanted_ref, panel_ref, out_ref, hot):
    part = pl.program_id(0)
    col = place_ref[0]
    start = 0
    for block, starts in enumerate(window_starts):
        for n, value in enumerate(starts):
            start = jnp.where((col == block) & (part == n), int(value), start)
    start = pl.multiple_of(start, LANES)
    wanted = wanted_ref[...]
    window = hot.shape[0]
    for begin in range(0, window, LANES):
        ids = ids_ref[0, :, pl.ds(pl.multiple_of(start + begin, LANES), LANES)]
        hot[begin : begin + LANES, :] = one_hot(ids, wanted)
    ordered = jnp.dot(panel_ref[:, pl.ds(start, window)], hot[...], preferred_element_type=jnp.float32)
    out_ref[...] = ordered.astype(jnp.bfloat16)


def put_in_order(plan, place, points_map, panel):
    columns = points_map.shape[1] // len(plan["buckets"])
    block = columns // PARTS
    ids = jnp.asarray(plan["ids"])[:, None]
    return pl.pallas_call(
        lambda *refs: order_kernel(plan["starts"].tolist(), *refs),
        grid_spec=pltpu.PrefetchScalarGridSpec(
            num_scalar_prefetch=1,
            grid=(PARTS,),
            in_specs=[
                pl.BlockSpec((1, *ids.shape[1:]), lambda n, place: (place[0], 0, 0)),
                pl.BlockSpec((1, block), lambda n, place: (0, place[0] * PARTS + n)),
                pl.BlockSpec(panel.shape, lambda n, place: (0, 0)),
            ],
            out_specs=pl.BlockSpec((panel.shape[0], block), lambda n, place: (0, n)),
            scratch_shapes=[pltpu.VMEM((plan["window"], block), jnp.bfloat16)],
        ),
        out_shape=jax.ShapeDtypeStruct((panel.shape[0], columns), jnp.bfloat16),
        compiler_params=pltpu.CompilerParams(vmem_limit_bytes=VMEM_BYTES, dimension_semantics=("arbitrary",)),
        cost_estimate=pl.CostEstimate(flops=1, bytes_accessed=1, transcendentals=0),
        name="in_order",
    )(place, ids, points_map, panel)


def product_kernel(left_ref, *refs):
    *ordered, out_ref = refs
    rows = out_ref.shape[1]
    right = jnp.concatenate([part[...] for part in ordered], 0)
    chi = jnp.dot(left_ref[...], right, preferred_element_type=jnp.float32)
    out_ref[0] = chi[:rows]
    out_ref[1] = chi[rows:]


def product(left, ordered):
    rows, columns = left.shape[0] // 2, ordered[0].shape[1]
    block = 6 * LANES
    return pl.pallas_call(
        product_kernel,
        grid=(pl.cdiv(columns, block),),
        in_specs=[pl.BlockSpec(left.shape, lambda n: (0, 0))]
        + [pl.BlockSpec((part.shape[0], block), lambda n: (0, n)) for part in ordered],
        out_specs=pl.BlockSpec((2, rows, block), lambda n: (0, 0, n)),
        out_shape=jax.ShapeDtypeStruct((2, rows, columns), jnp.float32),
        compiler_params=pltpu.CompilerParams(vmem_limit_bytes=VMEM_BYTES, dimension_semantics=("arbitrary",)),
        cost_estimate=pl.CostEstimate(flops=1, bytes_accessed=1, transcendentals=0),
        name="product",
    )(left, *ordered)


def on_device(val_wave, cond_wave, val_energy, cond_energy, band_owner, grid_map):
    bands, points = val_wave.shape[0], val_wave.shape[1]
    row_count = lax.axis_size("row")
    col_count = lax.axis_size("col")
    col, row = lax.axis_index("col"), lax.axis_index("row")
    plan = make_plan(points, grid_map.shape[0], col_count, ROWS_DEV * row_count, row_count)
    place = jnp.stack([col, row]).astype(jnp.int32)
    points_map = grid_map[None]
    chunk = bands // 2
    energies = (band_owner, cond_energy, val_energy)
    slabs = []
    for part in range(2):
        send, slab = spectra(plan, val_wave, cond_wave, energies, part * chunk, chunk)
        slabs.append(slab)
        if part == 0:
            send, cond_wave = lax.optimization_barrier((send, cond_wave))
            early = lax.all_gather(send, "row", axis=1)
        else:
            mine = lax.all_to_all(send, "col", split_axis=0, concat_axis=0, tiled=True).reshape(-1, plan["lanes"])
            mine = put_in_order(plan, place, points_map, mine)
            last = lax.all_gather(mine, "row", axis=0, tiled=True)
    slab, _ = lax.optimization_barrier((jnp.concatenate(slabs, 1), mine))
    slab = lax.all_to_all(slab, "row", split_axis=0, concat_axis=0, tiled=True).reshape(-1, plan["slab_lanes"])
    slab = jnp.broadcast_to(slab, (col_count, *slab.shape))
    early, slab = lax.optimization_barrier((early, slab))
    early = lax.all_to_all(early, "col", split_axis=0, concat_axis=0, tiled=True).reshape(-1, plan["lanes"])
    early, slab = lax.optimization_barrier((early, slab))
    slab = lax.all_to_all(slab, "col", split_axis=0, concat_axis=0, tiled=True)
    early = put_in_order(plan, place, points_map, early)
    return product(left_side(plan, place, points_map, slab), [early, last])


def solution(mesh):
    in_specs = (P(), P(("row", "col"), None, None, None), P(), P(), P(("row", "col")), P())
    out_specs = P(None, "row", "col")
    return jax.shard_map(
        on_device, mesh=mesh, in_specs=in_specs, out_specs=out_specs, check_vma=False
    )
```

```python
import math

import jax
import jax.numpy as jnp
import numpy as np
from jax import lax
from jax.experimental import pallas as pl
from jax.experimental.pallas import tpu as pltpu
from jax.sharding import PartitionSpec as P

ROWS_DEV = 256
LANES = 128
VMEM_BYTES = 56 * 1024 * 1024
HALF = 64
KEEP = 40
ORIGIN = KEEP // 2
PARITY_LANES = 896
PARTS = 3


def round_up(value, step):
    return -(-value // step) * step


def length_counts(points):
    freq = np.arange(points) - points // 2
    square = freq * freq
    lengths = square[:, None, None] + square[None, :, None] + square[None, None, :]
    return np.cumsum(np.bincount(lengths.reshape(-1)))


def column_order(top):
    freq = np.arange(KEEP) - ORIGIN
    first, second = np.meshgrid(freq, freq, indexing="ij")
    length = (first * first + second * second).reshape(-1)
    order = np.argsort(length, kind="stable")
    order = order[length[order] <= top]
    return first.reshape(-1)[order], second.reshape(-1)[order], length[order]


def column_place(index_2, index_3):
    return index_3 % 2 * PARITY_LANES + index_3 // 2 * KEEP + index_2


class Bucket:
    def __init__(self, ranges, column_length):
        self.pieces = []
        self.edges = {}
        offset = 0
        for low, high in ranges:
            begin = offset
            for index in range(KEEP):
                freq = index - ORIGIN
                start = int(np.searchsorted(column_length, low - freq * freq, side="left"))
                stop = int(np.searchsorted(column_length, high - freq * freq, side="right"))
                if stop > start:
                    self.pieces.append((index, start, stop, offset))
                    offset += stop - start
            for length in range(low, high + 1):
                self.edges[length] = (begin, offset)
        self.size = offset

    def ids(self, column_2, column_3, points, width):
        out = np.full((width,), -1, np.int32)
        for index, start, stop, offset in self.pieces:
            k1 = (index - ORIGIN) % points
            k2 = column_2[start:stop] % points
            k3 = column_3[start:stop] % points
            out[offset : offset + stop - start] = (k1 * points + k2) * points + k3
        return out


def length_ranges(cumulative, first, step, count):
    shell = lambda rank: int(np.searchsorted(cumulative, rank, side="right"))
    ranges, low = [], shell(first)
    for part in range(1, count):
        before, after = shell(first + part * step - 1), shell(first + part * step)
        if before == after:
            if low < before:
                ranges.append((low, before - 1))
            if low <= before:
                ranges.append((before, before))
        elif low <= before:
            ranges.append((low, before))
        low = before + 1
    high = shell(first + count * step - 1)
    if low <= high:
        ranges.append((low, high))
    return ranges


def make_plan(points, total, blocks, slab, slab_blocks):
    cumulative = length_counts(points)
    shell = lambda rank: int(np.searchsorted(cumulative, rank, side="right"))
    width, slab_width = total // blocks, slab // slab_blocks
    step = width // PARTS
    column_2, column_3, column_length = column_order(shell(total - 1))
    buckets = [Bucket(length_ranges(cumulative, n * width, step, PARTS), column_length) for n in range(blocks)]
    slabs = [Bucket(length_ranges(cumulative, n * slab_width, slab_width, 1), column_length) for n in range(slab_blocks)]
    slab_top = shell(slab - 1)
    lanes = round_up(max(bucket.size for bucket in buckets), LANES)
    slab_lanes = round_up(max(bucket.size for bucket in slabs), LANES)
    windows = np.zeros((blocks, PARTS, 2), np.int64)
    for n, bucket in enumerate(buckets):
        for part in range(PARTS):
            rank = n * width + part * step
            windows[n, part, 0] = bucket.edges[shell(rank)][0] // LANES * LANES
            windows[n, part, 1] = round_up(bucket.edges[shell(rank + step - 1)][1], LANES)
    window = int((windows[..., 1] - windows[..., 0]).max())
    return dict(
        buckets=buckets,
        slabs=slabs,
        slab_columns=int(np.searchsorted(column_length, slab_top, side="right")),
        slab_edge=math.isqrt(slab_top),
        lanes=lanes,
        slab_lanes=slab_lanes,
        window=window,
        starts=np.minimum(windows[..., 0], lanes - window).astype(np.int32),
        ids=np.stack([bucket.ids(column_2, column_3, points, lanes) for bucket in buckets]),
        slab_ids=np.stack([bucket.ids(column_2, column_3, points, slab_lanes) for bucket in slabs]),
        column_place=column_place(column_2 + ORIGIN, column_3 + ORIGIN).astype(np.int32),
    )


def dft_tables(points):
    n = np.arange(points)
    freq = np.arange(KEEP) - ORIGIN
    angle = (n[:, None] * freq[None, :] % points) * (2.0 * np.pi / points)
    cosine, sine = np.cos(angle), np.sin(angle)
    one = np.zeros((2, points, 2, HALF))
    one[0, :, 0, :KEEP] = cosine
    one[1, :, 0, :KEEP] = sine
    one[0, :, 1, :KEEP] = -sine
    one[1, :, 1, :KEEP] = cosine
    two = np.zeros((2, 2, points, 2, 2, HALF))
    for item in range(2):
        two[:, item, :, item] = one

    def parts(table):
        high = table.astype(jnp.bfloat16)
        return high, (table - high.astype(np.float64)).astype(jnp.bfloat16)

    high, low = parts(one[..., :KEEP].reshape(2 * points, 2 * KEEP).T)
    first = np.block([[high, high], [low, np.zeros_like(low)]])
    second = np.concatenate(parts(two.reshape(4 * points, 4 * HALF)), 0)
    halves = two[..., :KEEP].reshape(2, 2, points // 2, 2, 4 * KEEP).transpose(0, 1, 3, 2, 4)
    high, low = parts(halves.reshape(4 * points, 4 * KEEP).T)
    third = np.block([[high, high], [low, np.zeros_like(low)]])
    return [jnp.asarray(table) for table in (first, second, third)]


def split_parts(value):
    high = value.astype(jnp.bfloat16)
    low = (value - high.astype(jnp.float32)).astype(jnp.bfloat16)
    return high, low


def store_split(target, rows, blocks):
    for part, block in enumerate(blocks):
        high, low = split_parts(jnp.concatenate(block, 0))
        target[rows, part * LANES : (part + 1) * LANES] = high
        target[rows, (part + 2) * LANES : (part + 3) * LANES] = low


def doubled(stored):
    return jnp.concatenate([stored, stored[:, : stored.shape[1] // 2]], 1)


def contract_last(table, stored):
    both = lax.dot_general(table, stored, (((1,), (1,)), ((), ())), preferred_element_type=jnp.float32)
    rows = both.shape[0] // 2
    return both[:rows] + both[rows:]


def pack_pieces(pieces, width, source, rows, lane, out):
    for tile in range(width // LANES):
        left, right = tile * LANES, (tile + 1) * LANES
        value = jnp.zeros((rows, LANES), jnp.float32)
        for index, start, stop, offset in pieces:
            begin, end = max(left, offset), min(right, offset + stop - start)
            while begin < end:
                at = start + begin - offset
                block = source(index, at // LANES)
                shift = (begin - at) % LANES
                if shift:
                    block = pltpu.roll(block, shift, 1)
                value = block if begin == left else jnp.where(lane >= begin - left, block, value)
                begin = min(end, begin + LANES - at % LANES)
        out(tile, value)


def slab_tiles(plan):
    first = (ORIGIN - plan["slab_edge"]) // 2 * KEEP // LANES
    last = round_up(((ORIGIN + plan["slab_edge"]) // 2 + 1) * KEEP, LANES) // LANES
    return [odd * PARITY_LANES // LANES + tile for odd in range(2) for tile in range(first, last)]


def spectrum_kernel(plan, points, first_band, count, owner_ref, cond_energy_ref, val_energy_ref, val_ref, cond_ref, place_ref, first_ref,
                    second_ref, third_ref, send_ref, slab_ref, cond_a, cond_b, middle, turned, last, sorter, plain_rows, weighted_rows,
                    plain_sorted, weighted_sorted):
    band = pl.program_id(0)
    planes = 8
    pairs = planes // 2
    lane = lax.broadcasted_iota(jnp.int32, (1, LANES), 1)
    low_lanes = lane < HALF

    @pl.when(band == 0)
    def _():
        scale = 1.0 / float(points) ** 1.5
        sign = jnp.where(low_lanes, scale, -scale)

        @pl.loop(0, points // planes)
        def _(block):
            rows = pl.ds(pl.multiple_of(block * planes * points, planes * points), planes * points)
            wave = cond_ref[0, pl.ds(block * planes, planes)].reshape(planes * points, LANES).astype(jnp.float32)
            cond_a[rows, :] = wave * scale
            cond_b[rows, :] = pltpu.roll(wave, HALF, 1) * sign

        last[KEEP * KEEP // 2 :, :] = jnp.zeros((last.shape[0] - KEEP * KEEP // 2, 4 * LANES), jnp.bfloat16)

    def first_axis(block):
        rows = pl.ds(pl.multiple_of(block * planes * points, planes * points), planes * points)
        wave = val_ref[0, pl.ds(block * planes, planes)].reshape(planes * points, LANES).astype(jnp.float32)
        other = pltpu.roll(wave, HALF, 1)
        density = jnp.where(low_lanes, wave, other) * cond_a[rows, :] + jnp.where(low_lanes, other, wave) * cond_b[rows, :]
        high, low = split_parts(density)
        field = contract_last(first_ref[...], jnp.concatenate([high, low], 1))
        for begin in range(0, pairs, 2):
            blocks = [
                [field[part * KEEP : (part + 1) * KEEP, pair * LANES : (pair + 1) * LANES] for pair in (begin, begin + 1)]
                for part in range(2)
            ]
            at = pl.ds(pl.multiple_of((block * pairs + begin) * KEEP, 2 * KEEP), 2 * KEEP)
            store_split(middle, at, blocks)

    def second_axis(block):
        rows = pl.ds(pl.multiple_of(block * 4 * KEEP, 4 * KEEP), 4 * KEEP)
        high = second_ref[: 2 * LANES]
        table = jnp.concatenate([high, high, second_ref[2 * LANES :]], 0)
        field = jnp.dot(doubled(middle[rows, :]), table, preferred_element_type=jnp.float32)
        for item in range(2):
            turned[item, rows, :] = field[:, item * LANES : (item + 1) * LANES]

    turns = points // 16 - 1
    piece = sorter.shape[0] // (count * turns)
    for part in range(2):
        first_axis(part)

    @pl.loop(1, turns + 1)
    def _(turn):
        begin = pl.multiple_of((band * turns + turn - 1) * piece, 16)
        at = lax.broadcasted_iota(jnp.int32, (piece, sorter.shape[1]), 0) + begin
        sorter[pl.ds(begin, piece), :] = jnp.where(at == place_ref[...], 1.0, 0.0).astype(jnp.bfloat16)
        for part in range(2):
            second_axis(2 * turn - 2 + part)
        for part in range(2):
            first_axis(2 * turn + part)

    for part in range(2):
        second_axis(2 * turns + part)

    for begin in range(0, KEEP, 4):
        both = []
        for pair in range(2):
            items = [
                turned[item, pl.ds(begin + 2 * pair + k3, points // 2, stride=KEEP), :]
                for k3 in range(2)
                for item in range(2)
            ]
            turn = jnp.concatenate(items, 0).T
            both.append((turn[:KEEP], turn[HALF : HALF + KEEP]))
        store_split(last, slice(begin // 2 * KEEP, (begin // 2 + 2) * KEEP), list(zip(*both)))

    bands = val_energy_ref.shape[0] * cond_energy_ref.shape[0]
    gap = cond_energy_ref[owner_ref[0]] - val_energy_ref[first_band + band]
    weight = -2.0 / (math.sqrt(bands) * jnp.full((1, LANES), gap, jnp.float32))
    slab = slab_tiles(plan)
    tiles = PARITY_LANES // LANES
    field = contract_last(third_ref[...], last[...])
    band_rows = pl.ds(pl.multiple_of(band * 2 * KEEP, 2 * KEEP), 2 * KEEP)
    for odd in range(2):
        value = field[odd * 2 * KEEP : (odd + 1) * 2 * KEEP]
        plain_rows[band_rows, odd * PARITY_LANES : (odd + 1) * PARITY_LANES] = value.astype(jnp.bfloat16)
        for place, tile in enumerate(slab):
            if tile // tiles == odd:
                inside = value[:, tile % tiles * LANES : (tile % tiles + 1) * LANES]
                weighted_rows[band_rows, place * LANES : (place + 1) * LANES] = (weight * inside).astype(jnp.bfloat16)

    @pl.when(band == count - 1)
    def _():
        def sort_rows(rows, which, target):
            value = jnp.dot(rows, which, preferred_element_type=jnp.float32)
            for tile in range(target.shape[0]):
                target[tile] = value[:, tile * LANES : (tile + 1) * LANES]

        which = [sorter[tile * LANES : (tile + 1) * LANES, : weighted_sorted.shape[0] * LANES] for tile in slab]
        sort_rows(plain_rows[...], sorter[: 2 * PARITY_LANES, :], plain_sorted)
        sort_rows(weighted_rows[...], jnp.concatenate(which, 0), weighted_sorted)

        def plain_at(index, tile):
            return plain_sorted[tile, pl.ds(index, 2 * count, stride=KEEP), :]

        def weighted_at(index, tile):
            return weighted_sorted[tile, pl.ds(index, 2 * count, stride=KEEP), :]

        for block, bucket in enumerate(plan["buckets"]):

            def keep(tile, value):
                send_ref[block, :, tile * LANES : (tile + 1) * LANES] = value.astype(jnp.bfloat16)

            pack_pieces(bucket.pieces, plan["lanes"], plain_at, 2 * count, lane, keep)
        for block, bucket in enumerate(plan["slabs"]):

            def keep_slab(tile, value):
                slab_ref[block, :, tile * LANES : (tile + 1) * LANES] = value.astype(jnp.bfloat16)

            pack_pieces(bucket.pieces, plan["slab_lanes"], weighted_at, 2 * count, lane, keep_slab)


def spectra(plan, val_wave, cond_wave, energies, first_band, count):
    points = val_wave.shape[1]
    turns = points // 16 - 1
    depth = round_up(-(-2 * PARITY_LANES // (count * turns)), 16) * count * turns
    columns = round_up(plan["column_place"].shape[0], 256)
    slab_columns = round_up(plan["slab_columns"], LANES)
    slab_depth = len(slab_tiles(plan)) * LANES
    place = np.full((1, columns), -1, np.int32)
    place[0, : plan["column_place"].shape[0]] = plan["column_place"]
    grid_rows = points * points
    tables = dft_tables(points)
    send_shape = (len(plan["buckets"]), 2 * count, plan["lanes"])
    slab_shape = (len(plan["slabs"]), 2 * count, plan["slab_lanes"])
    kernel = lambda *refs: spectrum_kernel(plan, points, first_band, count, *refs)
    return pl.pallas_call(
        kernel,
        grid=(count,),
        in_specs=[
            pl.BlockSpec(memory_space=pltpu.SMEM),
            pl.BlockSpec(memory_space=pltpu.SMEM),
            pl.BlockSpec(memory_space=pltpu.SMEM),
            pl.BlockSpec((1, points, points, 2 * points), lambda v: (first_band + v, 0, 0, 0)),
            pl.BlockSpec((1, points, points, 2 * points), lambda v: (0, 0, 0, 0)),
            pl.BlockSpec((1, columns), lambda v: (0, 0)),
            *[pl.BlockSpec(table.shape, lambda v: (0, 0)) for table in tables],
        ],
        out_specs=[pl.BlockSpec(send_shape, lambda v: (0, 0, 0)), pl.BlockSpec(slab_shape, lambda v: (0, 0, 0))],
        out_shape=[jax.ShapeDtypeStruct(send_shape, jnp.bfloat16), jax.ShapeDtypeStruct(slab_shape, jnp.bfloat16)],
        scratch_shapes=[
            pltpu.VMEM((grid_rows, LANES), jnp.float32),
            pltpu.VMEM((grid_rows, LANES), jnp.float32),
            pltpu.VMEM((points // 2 * KEEP, 4 * LANES), jnp.bfloat16),
            pltpu.VMEM((2, points // 2 * KEEP, LANES), jnp.float32),
            pltpu.VMEM((PARITY_LANES, 4 * LANES), jnp.bfloat16),
            pltpu.VMEM((depth, columns), jnp.bfloat16),
            pltpu.VMEM((2 * count * KEEP, 2 * PARITY_LANES), jnp.bfloat16),
            pltpu.VMEM((2 * count * KEEP, slab_depth), jnp.bfloat16),
            pltpu.VMEM((columns // LANES, 2 * count * KEEP, LANES), jnp.float32),
            pltpu.VMEM((slab_columns // LANES, 2 * count * KEEP, LANES), jnp.float32),
        ],
        compiler_params=pltpu.CompilerParams(vmem_limit_bytes=VMEM_BYTES, dimension_semantics=("arbitrary",)),
        cost_estimate=pl.CostEstimate(flops=1, bytes_accessed=1, transcendentals=0),
        name="spectra",
    )(*energies, val_wave, cond_wave, jnp.asarray(place), *tables)


def one_hot(ids, wanted):
    ids = jnp.broadcast_to(ids, (LANES, LANES)).T
    ids = jnp.concatenate([ids] * (wanted.shape[1] // LANES), 1)
    return jnp.where(ids == wanted, 1.0, 0.0).astype(jnp.bfloat16)


def left_kernel(row_count, place_ref, slab_ref, ids_ref, wanted_ref, left_ref):
    rows = wanted_ref.shape[1]
    col_count = slab_ref.shape[0]
    group = slab_ref.shape[1] // (2 * row_count)
    order = [(col, 2 * row) for col in range(col_count) for row in range(row_count)]
    order += [(col, 2 * row + 1) for row in range(row_count) for col in range(col_count)]
    slab = [slab_ref[col, at * group : (at + 1) * group, :].astype(jnp.float32) for col, at in order]
    ids = ids_ref[0]
    choice = [one_hot(ids[:, begin : begin + LANES], wanted_ref[...]) for begin in range(0, ids.shape[1], LANES)]
    chosen = jnp.dot(
        jnp.concatenate(slab, 0).astype(jnp.bfloat16), jnp.concatenate(choice, 0), preferred_element_type=jnp.float32
    )
    lane = lax.broadcasted_iota(jnp.int32, (1, LANES), 1)
    real_lanes = lane % 2 == 0
    for begin in range(0, chosen.shape[0], LANES):
        turned = chosen[begin : begin + LANES].T
        after = pltpu.roll(turned, LANES - 1, 1)
        before = pltpu.roll(turned, 1, 1)
        left_ref[:rows, begin : begin + LANES] = turned.astype(jnp.bfloat16)
        left_ref[rows:, begin : begin + LANES] = jnp.where(real_lanes, after, -before).astype(jnp.bfloat16)


def left_side(plan, place, points_map, slab):
    pairs = slab.shape[0] * slab.shape[1]
    ids = jnp.asarray(plan["slab_ids"])[:, None]
    return pl.pallas_call(
        lambda *refs: left_kernel(ids.shape[0], *refs),
        grid_spec=pltpu.PrefetchScalarGridSpec(
            num_scalar_prefetch=1,
            grid=(1,),
            in_specs=[
                pl.BlockSpec(slab.shape, lambda n, place: (0, 0, 0)),
                pl.BlockSpec((1, *ids.shape[1:]), lambda n, place: (place[1], 0, 0)),
                pl.BlockSpec((1, ROWS_DEV), lambda n, place: (0, place[1])),
            ],
            out_specs=pl.BlockSpec((2 * ROWS_DEV, pairs), lambda n, place: (0, 0)),
        ),
        out_shape=jax.ShapeDtypeStruct((2 * ROWS_DEV, pairs), jnp.bfloat16),
        compiler_params=pltpu.CompilerParams(vmem_limit_bytes=VMEM_BYTES),
        cost_estimate=pl.CostEstimate(flops=1, bytes_accessed=1, transcendentals=0),
        name="left_side",
    )(place, slab, ids, points_map)


def order_kernel(place_ref, starts_ref, ids_ref, wanted_ref, panel_ref, out_ref, hot):
    start = pl.multiple_of(starts_ref[place_ref[0] * PARTS + pl.program_id(0)], LANES)
    wanted = wanted_ref[...]
    window = hot.shape[0]
    for begin in range(0, window, LANES):
        ids = ids_ref[0, :, pl.ds(pl.multiple_of(start + begin, LANES), LANES)]
        hot[begin : begin + LANES, :] = one_hot(ids, wanted)
    ordered = jnp.dot(panel_ref[:, pl.ds(start, window)], hot[...], preferred_element_type=jnp.float32)
    out_ref[...] = ordered.astype(jnp.bfloat16)


def put_in_order(plan, place, points_map, panel):
    columns = points_map.shape[1] // len(plan["buckets"])
    block = columns // PARTS
    ids = jnp.asarray(plan["ids"])[:, None]
    return pl.pallas_call(
        order_kernel,
        grid_spec=pltpu.PrefetchScalarGridSpec(
            num_scalar_prefetch=2,
            grid=(PARTS,),
            in_specs=[
                pl.BlockSpec((1, *ids.shape[1:]), lambda n, place, starts: (place[0], 0, 0)),
                pl.BlockSpec((1, block), lambda n, place, starts: (0, place[0] * PARTS + n)),
                pl.BlockSpec(panel.shape, lambda n, place, starts: (0, 0)),
            ],
            out_specs=pl.BlockSpec((panel.shape[0], block), lambda n, place, starts: (0, n)),
            scratch_shapes=[pltpu.VMEM((plan["window"], block), jnp.bfloat16)],
        ),
        out_shape=jax.ShapeDtypeStruct((panel.shape[0], columns), jnp.bfloat16),
        compiler_params=pltpu.CompilerParams(vmem_limit_bytes=VMEM_BYTES, dimension_semantics=("arbitrary",)),
        cost_estimate=pl.CostEstimate(flops=1, bytes_accessed=1, transcendentals=0),
        name="in_order",
    )(place, jnp.asarray(plan["starts"].reshape(-1)), ids, points_map, panel)


def product_kernel(left_ref, *refs):
    *ordered, out_ref = refs
    rows = out_ref.shape[1]
    right = jnp.concatenate([part[...] for part in ordered], 0)
    chi = jnp.dot(left_ref[...], right, preferred_element_type=jnp.float32)
    out_ref[0] = chi[:rows]
    out_ref[1] = chi[rows:]


def product(left, ordered):
    rows, columns = left.shape[0] // 2, ordered[0].shape[1]
    block = 6 * LANES
    return pl.pallas_call(
        product_kernel,
        grid=(pl.cdiv(columns, block),),
        in_specs=[pl.BlockSpec(left.shape, lambda n: (0, 0))]
        + [pl.BlockSpec((part.shape[0], block), lambda n: (0, n)) for part in ordered],
        out_specs=pl.BlockSpec((2, rows, block), lambda n: (0, 0, n)),
        out_shape=jax.ShapeDtypeStruct((2, rows, columns), jnp.float32),
        compiler_params=pltpu.CompilerParams(vmem_limit_bytes=VMEM_BYTES, dimension_semantics=("arbitrary",)),
        cost_estimate=pl.CostEstimate(flops=1, bytes_accessed=1, transcendentals=0),
        name="product",
    )(left, *ordered)


def on_device(val_wave, cond_wave, val_energy, cond_energy, band_owner, grid_map):
    bands, points = val_wave.shape[0], val_wave.shape[1]
    row_count = lax.axis_size("row")
    col_count = lax.axis_size("col")
    col, row = lax.axis_index("col"), lax.axis_index("row")
    plan = make_plan(points, grid_map.shape[0], col_count, ROWS_DEV * row_count, row_count)
    place = jnp.stack([col, row]).astype(jnp.int32)
    points_map = grid_map[None]
    chunk = bands // 2
    energies = (band_owner, cond_energy, val_energy)
    slabs = []
    for part in range(2):
        send, slab = spectra(plan, val_wave, cond_wave, energies, part * chunk, chunk)
        slabs.append(slab)
        if part == 0:
            send, cond_wave = lax.optimization_barrier((send, cond_wave))
            early = lax.all_gather(send, "row", axis=1)
        else:
            mine = lax.all_to_all(send, "col", split_axis=0, concat_axis=0, tiled=True).reshape(-1, plan["lanes"])
            mine = put_in_order(plan, place, points_map, mine)
            last = lax.all_gather(mine, "row", axis=0, tiled=True)
    slab, _ = lax.optimization_barrier((jnp.concatenate(slabs, 1), mine))
    slab = lax.all_to_all(slab, "row", split_axis=0, concat_axis=0, tiled=True).reshape(-1, plan["slab_lanes"])
    slab = jnp.broadcast_to(slab, (col_count, *slab.shape))
    early, slab = lax.optimization_barrier((early, slab))
    early = lax.all_to_all(early, "col", split_axis=0, concat_axis=0, tiled=True).reshape(-1, plan["lanes"])
    early, slab = lax.optimization_barrier((early, slab))
    slab = lax.all_to_all(slab, "col", split_axis=0, concat_axis=0, tiled=True)
    early = put_in_order(plan, place, points_map, early)
    return product(left_side(plan, place, points_map, slab), [early, last])


def solution(mesh):
    in_specs = (P(), P(("row", "col"), None, None, None), P(), P(), P(("row", "col")), P())
    out_specs = P(None, "row", "col")
    return jax.shard_map(
        on_device, mesh=mesh, in_specs=in_specs, out_specs=out_specs, check_vma=False
    )
```

```python
import math

import jax
import jax.numpy as jnp
import numpy as np
from jax import lax
from jax.experimental import pallas as pl
from jax.experimental.pallas import tpu as pltpu
from jax.sharding import PartitionSpec as P

ROWS_DEV = 256
LANES = 128
VMEM_BYTES = 56 * 1024 * 1024
HALF = 64
KEEP = 40
ORIGIN = KEEP // 2
PARITY_LANES = 896
PARTS = 5


def round_up(value, step):
    return -(-value // step) * step


def length_counts(points):
    freq = np.arange(points) - points // 2
    square = freq * freq
    lengths = square[:, None, None] + square[None, :, None] + square[None, None, :]
    return np.cumsum(np.bincount(lengths.reshape(-1)))


def column_order(top):
    freq = np.arange(KEEP) - ORIGIN
    first, second = np.meshgrid(freq, freq, indexing="ij")
    length = (first * first + second * second).reshape(-1)
    order = np.argsort(length, kind="stable")
    order = order[length[order] <= top]
    return first.reshape(-1)[order], second.reshape(-1)[order], length[order]


def column_place(index_2, index_3):
    return index_3 % 2 * PARITY_LANES + index_3 // 2 * KEEP + index_2


class Bucket:
    def __init__(self, ranges, column_length):
        self.pieces = []
        self.edges = {}
        offset = 0
        for low, high in ranges:
            begin = offset
            for index in range(KEEP):
                freq = index - ORIGIN
                start = int(np.searchsorted(column_length, low - freq * freq, side="left"))
                stop = int(np.searchsorted(column_length, high - freq * freq, side="right"))
                if stop > start:
                    self.pieces.append((index, start, stop, offset))
                    offset += stop - start
            for length in range(low, high + 1):
                self.edges[length] = (begin, offset)
        self.size = offset

    def ids(self, column_2, column_3, points, width):
        out = np.full((width,), -1, np.int32)
        for index, start, stop, offset in self.pieces:
            k1 = (index - ORIGIN) % points
            k2 = column_2[start:stop] % points
            k3 = column_3[start:stop] % points
            out[offset : offset + stop - start] = (k1 * points + k2) * points + k3
        return out


def length_ranges(cumulative, first, step, count):
    shell = lambda rank: int(np.searchsorted(cumulative, rank, side="right"))
    ranges, low = [], shell(first)
    for part in range(1, count):
        before, after = shell(first + part * step - 1), shell(first + part * step)
        if before == after:
            if low < before:
                ranges.append((low, before - 1))
            if low <= before:
                ranges.append((before, before))
        elif low <= before:
            ranges.append((low, before))
        low = before + 1
    high = shell(first + count * step - 1)
    if low <= high:
        ranges.append((low, high))
    return ranges


def make_plan(points, total, blocks, slab, slab_blocks):
    cumulative = length_counts(points)
    shell = lambda rank: int(np.searchsorted(cumulative, rank, side="right"))
    width, slab_width = total // blocks, slab // slab_blocks
    step = width // PARTS
    column_2, column_3, column_length = column_order(shell(total - 1))
    buckets = [Bucket(length_ranges(cumulative, n * width, step, PARTS), column_length) for n in range(blocks)]
    slabs = [Bucket(length_ranges(cumulative, n * slab_width, slab_width, 1), column_length) for n in range(slab_blocks)]
    slab_top = shell(slab - 1)
    lanes = round_up(max(bucket.size for bucket in buckets), LANES)
    slab_lanes = round_up(max(bucket.size for bucket in slabs), LANES)
    windows = np.zeros((blocks, PARTS, 2), np.int64)
    for n, bucket in enumerate(buckets):
        for part in range(PARTS):
            rank = n * width + part * step
            windows[n, part, 0] = bucket.edges[shell(rank)][0] // LANES * LANES
            windows[n, part, 1] = round_up(bucket.edges[shell(rank + step - 1)][1], LANES)
    window = int((windows[..., 1] - windows[..., 0]).max())
    return dict(
        buckets=buckets,
        slabs=slabs,
        slab_columns=int(np.searchsorted(column_length, slab_top, side="right")),
        slab_edge=math.isqrt(slab_top),
        lanes=lanes,
        slab_lanes=slab_lanes,
        window=window,
        starts=np.minimum(windows[..., 0], lanes - window).astype(np.int32),
        ids=np.stack([bucket.ids(column_2, column_3, points, lanes) for bucket in buckets]),
        slab_ids=np.stack([bucket.ids(column_2, column_3, points, slab_lanes) for bucket in slabs]),
        column_place=column_place(column_2 + ORIGIN, column_3 + ORIGIN).astype(np.int32),
    )


def dft_tables(points):
    n = np.arange(points)
    freq = np.arange(KEEP) - ORIGIN
    angle = (n[:, None] * freq[None, :] % points) * (2.0 * np.pi / points)
    cosine, sine = np.cos(angle), np.sin(angle)
    one = np.zeros((2, points, 2, HALF))
    one[0, :, 0, :KEEP] = cosine
    one[1, :, 0, :KEEP] = sine
    one[0, :, 1, :KEEP] = -sine
    one[1, :, 1, :KEEP] = cosine
    two = np.zeros((2, 2, points, 2, 2, HALF))
    for item in range(2):
        two[:, item, :, item] = one

    def parts(table):
        high = table.astype(jnp.bfloat16)
        return high, (table - high.astype(np.float64)).astype(jnp.bfloat16)

    high, low = parts(one[..., :KEEP].reshape(2 * points, 2 * KEEP).T)
    first = np.block([[high, high], [low, np.zeros_like(low)]])
    second = np.concatenate(parts(two.reshape(4 * points, 4 * HALF)), 0)
    halves = two[..., :KEEP].reshape(2, 2, points // 2, 2, 4 * KEEP).transpose(0, 1, 3, 2, 4)
    high, low = parts(halves.reshape(4 * points, 4 * KEEP).T)
    third = np.block([[high, high], [low, np.zeros_like(low)]])
    return [jnp.asarray(table) for table in (first, second, third)]


def split_parts(value):
    high = value.astype(jnp.bfloat16)
    low = (value - high.astype(jnp.float32)).astype(jnp.bfloat16)
    return high, low


def store_split(target, rows, blocks):
    for part, block in enumerate(blocks):
        high, low = split_parts(jnp.concatenate(block, 0))
        target[rows, part * LANES : (part + 1) * LANES] = high
        target[rows, (part + 2) * LANES : (part + 3) * LANES] = low


def doubled(stored):
    return jnp.concatenate([stored, stored[:, : stored.shape[1] // 2]], 1)


def contract_last(table, stored):
    both = lax.dot_general(table, stored, (((1,), (1,)), ((), ())), preferred_element_type=jnp.float32)
    rows = both.shape[0] // 2
    return both[:rows] + both[rows:]


def pack_pieces(pieces, width, source, rows, lane, out):
    for tile in range(width // LANES):
        left, right = tile * LANES, (tile + 1) * LANES
        value = jnp.zeros((rows, LANES), jnp.float32)
        for index, start, stop, offset in pieces:
            begin, end = max(left, offset), min(right, offset + stop - start)
            while begin < end:
                at = start + begin - offset
                block = source(index, at // LANES)
                shift = (begin - at) % LANES
                if shift:
                    block = pltpu.roll(block, shift, 1)
                value = block if begin == left else jnp.where(lane >= begin - left, block, value)
                begin = min(end, begin + LANES - at % LANES)
        out(tile, value)


def slab_tiles(plan):
    first = (ORIGIN - plan["slab_edge"]) // 2 * KEEP // LANES
    last = round_up(((ORIGIN + plan["slab_edge"]) // 2 + 1) * KEEP, LANES) // LANES
    return [odd * PARITY_LANES // LANES + tile for odd in range(2) for tile in range(first, last)]


def spectrum_kernel(plan, points, first_band, count, owner_ref, cond_energy_ref, val_energy_ref, val_ref, cond_ref, place_ref, first_ref,
                    second_ref, third_ref, send_ref, slab_ref, cond_a, cond_b, middle, turned, last, sorter, plain_rows, weighted_rows,
                    plain_sorted, weighted_sorted):
    band = pl.program_id(0)
    planes = 8
    pairs = planes // 2
    lane = lax.broadcasted_iota(jnp.int32, (1, LANES), 1)
    low_lanes = lane < HALF

    @pl.when(band == 0)
    def _():
        scale = 1.0 / float(points) ** 1.5
        sign = jnp.where(low_lanes, scale, -scale)

        @pl.loop(0, points // planes)
        def _(block):
            rows = pl.ds(pl.multiple_of(block * planes * points, planes * points), planes * points)
            wave = cond_ref[0, pl.ds(block * planes, planes)].reshape(planes * points, LANES).astype(jnp.float32)
            cond_a[rows, :] = wave * scale
            cond_b[rows, :] = pltpu.roll(wave, HALF, 1) * sign

        last[KEEP * KEEP // 2 :, :] = jnp.zeros((last.shape[0] - KEEP * KEEP // 2, 4 * LANES), jnp.bfloat16)

    def first_axis(block):
        rows = pl.ds(pl.multiple_of(block * planes * points, planes * points), planes * points)
        wave = val_ref[0, pl.ds(block * planes, planes)].reshape(planes * points, LANES).astype(jnp.float32)
        other = pltpu.roll(wave, HALF, 1)
        density = jnp.where(low_lanes, wave, other) * cond_a[rows, :] + jnp.where(low_lanes, other, wave) * cond_b[rows, :]
        high, low = split_parts(density)
        field = contract_last(first_ref[...], jnp.concatenate([high, low], 1))
        for begin in range(0, pairs, 2):
            blocks = [
                [field[part * KEEP : (part + 1) * KEEP, pair * LANES : (pair + 1) * LANES] for pair in (begin, begin + 1)]
                for part in range(2)
            ]
            at = pl.ds(pl.multiple_of((block * pairs + begin) * KEEP, 2 * KEEP), 2 * KEEP)
            store_split(middle, at, blocks)

    def second_axis(block):
        rows = pl.ds(pl.multiple_of(block * 4 * KEEP, 4 * KEEP), 4 * KEEP)
        high = second_ref[: 2 * LANES]
        table = jnp.concatenate([high, high, second_ref[2 * LANES :]], 0)
        field = jnp.dot(doubled(middle[rows, :]), table, preferred_element_type=jnp.float32)
        for item in range(2):
            turned[item, rows, :] = field[:, item * LANES : (item + 1) * LANES]

    turns = points // 16 - 1
    piece = sorter.shape[0] // (count * turns)
    for part in range(2):
        first_axis(part)

    @pl.loop(1, turns + 1)
    def _(turn):
        begin = pl.multiple_of((band * turns + turn - 1) * piece, 16)
        at = lax.broadcasted_iota(jnp.int32, (piece, sorter.shape[1]), 0) + begin
        sorter[pl.ds(begin, piece), :] = jnp.where(at == place_ref[...], 1.0, 0.0).astype(jnp.bfloat16)
        for part in range(2):
            second_axis(2 * turn - 2 + part)
        for part in range(2):
            first_axis(2 * turn + part)

    for part in range(2):
        second_axis(2 * turns + part)

    for begin in range(0, KEEP, 4):
        both = []
        for pair in range(2):
            items = [
                turned[item, pl.ds(begin + 2 * pair + k3, points // 2, stride=KEEP), :]
                for k3 in range(2)
                for item in range(2)
            ]
            turn = jnp.concatenate(items, 0).T
            both.append((turn[:KEEP], turn[HALF : HALF + KEEP]))
        store_split(last, slice(begin // 2 * KEEP, (begin // 2 + 2) * KEEP), list(zip(*both)))

    bands = val_energy_ref.shape[0] * cond_energy_ref.shape[0]
    gap = cond_energy_ref[owner_ref[0]] - val_energy_ref[first_band + band]
    weight = -2.0 / (math.sqrt(bands) * jnp.full((1, LANES), gap, jnp.float32))
    slab = slab_tiles(plan)
    tiles = PARITY_LANES // LANES
    field = contract_last(third_ref[...], last[...])
    band_rows = pl.ds(pl.multiple_of(band * 2 * KEEP, 2 * KEEP), 2 * KEEP)
    for odd in range(2):
        value = field[odd * 2 * KEEP : (odd + 1) * 2 * KEEP]
        plain_rows[band_rows, odd * PARITY_LANES : (odd + 1) * PARITY_LANES] = value.astype(jnp.bfloat16)
        for place, tile in enumerate(slab):
            if tile // tiles == odd:
                inside = value[:, tile % tiles * LANES : (tile % tiles + 1) * LANES]
                weighted_rows[band_rows, place * LANES : (place + 1) * LANES] = (weight * inside).astype(jnp.bfloat16)

    @pl.when(band == count - 1)
    def _():
        def sort_rows(rows, which, target):
            value = jnp.dot(rows, which, preferred_element_type=jnp.float32)
            for tile in range(target.shape[0]):
                target[tile] = value[:, tile * LANES : (tile + 1) * LANES]

        which = [sorter[tile * LANES : (tile + 1) * LANES, : weighted_sorted.shape[0] * LANES] for tile in slab]
        sort_rows(plain_rows[...], sorter[: 2 * PARITY_LANES, :], plain_sorted)
        sort_rows(weighted_rows[...], jnp.concatenate(which, 0), weighted_sorted)

        def plain_at(index, tile):
            return plain_sorted[tile, pl.ds(index, 2 * count, stride=KEEP), :]

        def weighted_at(index, tile):
            return weighted_sorted[tile, pl.ds(index, 2 * count, stride=KEEP), :]

        for block, bucket in enumerate(plan["buckets"]):

            def keep(tile, value):
                send_ref[block, :, tile * LANES : (tile + 1) * LANES] = value.astype(jnp.bfloat16)

            pack_pieces(bucket.pieces, plan["lanes"], plain_at, 2 * count, lane, keep)
        for block, bucket in enumerate(plan["slabs"]):

            def keep_slab(tile, value):
                slab_ref[block, :, tile * LANES : (tile + 1) * LANES] = value.astype(jnp.bfloat16)

            pack_pieces(bucket.pieces, plan["slab_lanes"], weighted_at, 2 * count, lane, keep_slab)


def spectra(plan, val_wave, cond_wave, energies, first_band, count):
    points = val_wave.shape[1]
    turns = points // 16 - 1
    depth = round_up(-(-2 * PARITY_LANES // (count * turns)), 16) * count * turns
    columns = round_up(plan["column_place"].shape[0], 256)
    slab_columns = round_up(plan["slab_columns"], LANES)
    slab_depth = len(slab_tiles(plan)) * LANES
    place = np.full((1, columns), -1, np.int32)
    place[0, : plan["column_place"].shape[0]] = plan["column_place"]
    grid_rows = points * points
    tables = dft_tables(points)
    send_shape = (len(plan["buckets"]), 2 * count, plan["lanes"])
    slab_shape = (len(plan["slabs"]), 2 * count, plan["slab_lanes"])
    kernel = lambda *refs: spectrum_kernel(plan, points, first_band, count, *refs)
    return pl.pallas_call(
        kernel,
        grid=(count,),
        in_specs=[
            pl.BlockSpec(memory_space=pltpu.SMEM),
            pl.BlockSpec(memory_space=pltpu.SMEM),
            pl.BlockSpec(memory_space=pltpu.SMEM),
            pl.BlockSpec((1, points, points, 2 * points), lambda v: (first_band + v, 0, 0, 0)),
            pl.BlockSpec((1, points, points, 2 * points), lambda v: (0, 0, 0, 0)),
            pl.BlockSpec((1, columns), lambda v: (0, 0)),
            *[pl.BlockSpec(table.shape, lambda v: (0, 0)) for table in tables],
        ],
        out_specs=[pl.BlockSpec(send_shape, lambda v: (0, 0, 0)), pl.BlockSpec(slab_shape, lambda v: (0, 0, 0))],
        out_shape=[jax.ShapeDtypeStruct(send_shape, jnp.bfloat16), jax.ShapeDtypeStruct(slab_shape, jnp.bfloat16)],
        scratch_shapes=[
            pltpu.VMEM((grid_rows, LANES), jnp.float32),
            pltpu.VMEM((grid_rows, LANES), jnp.float32),
            pltpu.VMEM((points // 2 * KEEP, 4 * LANES), jnp.bfloat16),
            pltpu.VMEM((2, points // 2 * KEEP, LANES), jnp.float32),
            pltpu.VMEM((PARITY_LANES, 4 * LANES), jnp.bfloat16),
            pltpu.VMEM((depth, columns), jnp.bfloat16),
            pltpu.VMEM((2 * count * KEEP, 2 * PARITY_LANES), jnp.bfloat16),
            pltpu.VMEM((2 * count * KEEP, slab_depth), jnp.bfloat16),
            pltpu.VMEM((columns // LANES, 2 * count * KEEP, LANES), jnp.float32),
            pltpu.VMEM((slab_columns // LANES, 2 * count * KEEP, LANES), jnp.float32),
        ],
        compiler_params=pltpu.CompilerParams(vmem_limit_bytes=VMEM_BYTES, dimension_semantics=("arbitrary",)),
        cost_estimate=pl.CostEstimate(flops=1, bytes_accessed=1, transcendentals=0),
        name="spectra",
    )(*energies, val_wave, cond_wave, jnp.asarray(place), *tables)


def one_hot(ids, wanted):
    ids = jnp.broadcast_to(ids, (LANES, LANES)).T
    ids = jnp.concatenate([ids] * (wanted.shape[1] // LANES), 1)
    return jnp.where(ids == wanted, 1.0, 0.0).astype(jnp.bfloat16)


def make_left(row_count, slab_ref, ids_ref, wanted_ref, left):
    rows = wanted_ref.shape[1]
    col_count = slab_ref.shape[0]
    group = slab_ref.shape[1] // (2 * row_count)
    order = [(col, 2 * row) for col in range(col_count) for row in range(row_count)]
    order += [(col, 2 * row + 1) for row in range(row_count) for col in range(col_count)]
    slab = [slab_ref[col, at * group : (at + 1) * group, :].astype(jnp.float32) for col, at in order]
    ids = ids_ref[0]
    choice = [one_hot(ids[:, begin : begin + LANES], wanted_ref[...]) for begin in range(0, ids.shape[1], LANES)]
    chosen = jnp.dot(
        jnp.concatenate(slab, 0).astype(jnp.bfloat16), jnp.concatenate(choice, 0), preferred_element_type=jnp.float32
    )
    lane = lax.broadcasted_iota(jnp.int32, (1, LANES), 1)
    real_lanes = lane % 2 == 0
    for begin in range(0, chosen.shape[0], LANES):
        turned = chosen[begin : begin + LANES].T
        after = pltpu.roll(turned, LANES - 1, 1)
        before = pltpu.roll(turned, 1, 1)
        left[:rows, begin : begin + LANES] = turned.astype(jnp.bfloat16)
        left[rows:, begin : begin + LANES] = jnp.where(real_lanes, after, -before).astype(jnp.bfloat16)


def order_kernel(place_ref, starts_ref, ids_ref, wanted_ref, panel_ref, out_ref, hot):
    start = pl.multiple_of(starts_ref[place_ref[0] * PARTS + pl.program_id(0)], LANES)
    wanted = wanted_ref[...]
    window = hot.shape[0]
    for begin in range(0, window, LANES):
        ids = ids_ref[0, :, pl.ds(pl.multiple_of(start + begin, LANES), LANES)]
        hot[begin : begin + LANES, :] = one_hot(ids, wanted)
    ordered = jnp.dot(panel_ref[:, pl.ds(start, window)], hot[...], preferred_element_type=jnp.float32)
    out_ref[...] = ordered.astype(jnp.bfloat16)


def put_in_order(plan, place, points_map, panel):
    columns = points_map.shape[1] // len(plan["buckets"])
    block = columns // PARTS
    ids = jnp.asarray(plan["ids"])[:, None]
    return pl.pallas_call(
        order_kernel,
        grid_spec=pltpu.PrefetchScalarGridSpec(
            num_scalar_prefetch=2,
            grid=(PARTS,),
            in_specs=[
                pl.BlockSpec((1, *ids.shape[1:]), lambda n, place, starts: (place[0], 0, 0)),
                pl.BlockSpec((1, block), lambda n, place, starts: (0, place[0] * PARTS + n)),
                pl.BlockSpec(panel.shape, lambda n, place, starts: (0, 0)),
            ],
            out_specs=pl.BlockSpec((panel.shape[0], block), lambda n, place, starts: (0, n)),
            scratch_shapes=[pltpu.VMEM((plan["window"], block), jnp.bfloat16)],
        ),
        out_shape=jax.ShapeDtypeStruct((panel.shape[0], columns), jnp.bfloat16),
        compiler_params=pltpu.CompilerParams(vmem_limit_bytes=VMEM_BYTES, dimension_semantics=("arbitrary",)),
        cost_estimate=pl.CostEstimate(flops=1, bytes_accessed=1, transcendentals=0),
        name="in_order",
    )(place, jnp.asarray(plan["starts"].reshape(-1)), ids, points_map, panel)


def product_kernel(row_count, place_ref, slab_ref, ids_ref, wanted_ref, early_ref, last_ref, out_ref, left):
    rows = out_ref.shape[1]

    @pl.when(pl.program_id(0) == 0)
    def _():
        make_left(row_count, slab_ref, ids_ref, wanted_ref, left)

    right = jnp.concatenate([early_ref[...], last_ref[...]], 0)
    chi = jnp.dot(left[...], right, preferred_element_type=jnp.float32)
    out_ref[0] = chi[:rows]
    out_ref[1] = chi[rows:]


def product(plan, place, points_map, slab, early, last):
    pairs, columns = slab.shape[0] * slab.shape[1], early.shape[1]
    block = 6 * LANES
    ids = jnp.asarray(plan["slab_ids"])[:, None]
    return pl.pallas_call(
        lambda *refs: product_kernel(ids.shape[0], *refs),
        grid_spec=pltpu.PrefetchScalarGridSpec(
            num_scalar_prefetch=1,
            grid=(pl.cdiv(columns, block),),
            in_specs=[
                pl.BlockSpec(slab.shape, lambda n, place: (0, 0, 0)),
                pl.BlockSpec((1, *ids.shape[1:]), lambda n, place: (place[1], 0, 0)),
                pl.BlockSpec((1, ROWS_DEV), lambda n, place: (0, place[1])),
                pl.BlockSpec((early.shape[0], block), lambda n, place: (0, n)),
                pl.BlockSpec((last.shape[0], block), lambda n, place: (0, n)),
            ],
            out_specs=pl.BlockSpec((2, ROWS_DEV, block), lambda n, place: (0, 0, n)),
            scratch_shapes=[pltpu.VMEM((2 * ROWS_DEV, pairs), jnp.bfloat16)],
        ),
        out_shape=jax.ShapeDtypeStruct((2, ROWS_DEV, columns), jnp.float32),
        compiler_params=pltpu.CompilerParams(vmem_limit_bytes=VMEM_BYTES, dimension_semantics=("arbitrary",)),
        cost_estimate=pl.CostEstimate(flops=1, bytes_accessed=1, transcendentals=0),
        name="product",
    )(place, slab, ids, points_map, early, last)


def on_device(val_wave, cond_wave, val_energy, cond_energy, band_owner, grid_map):
    bands, points = val_wave.shape[0], val_wave.shape[1]
    row_count = lax.axis_size("row")
    col_count = lax.axis_size("col")
    col, row = lax.axis_index("col"), lax.axis_index("row")
    plan = make_plan(points, grid_map.shape[0], col_count, ROWS_DEV * row_count, row_count)
    place = jnp.stack([col, row]).astype(jnp.int32)
    points_map = grid_map[None]
    chunk = bands // 2
    energies = (band_owner, cond_energy, val_energy)
    slabs = []
    for part in range(2):
        send, slab = spectra(plan, val_wave, cond_wave, energies, part * chunk, chunk)
        slabs.append(slab)
        if part == 0:
            send, cond_wave = lax.optimization_barrier((send, cond_wave))
            early = lax.all_gather(send, "row", axis=1)
        else:
            mine = lax.all_to_all(send, "col", split_axis=0, concat_axis=0, tiled=True).reshape(-1, plan["lanes"])
            mine = put_in_order(plan, place, points_map, mine)
            last = lax.all_gather(mine, "row", axis=0, tiled=True)
    slab, _ = lax.optimization_barrier((jnp.concatenate(slabs, 1), mine))
    slab = lax.all_to_all(slab, "row", split_axis=0, concat_axis=0, tiled=True).reshape(-1, plan["slab_lanes"])
    slab = jnp.broadcast_to(slab, (col_count, *slab.shape))
    early, slab = lax.optimization_barrier((early, slab))
    early = lax.all_to_all(early, "col", split_axis=0, concat_axis=0, tiled=True).reshape(-1, plan["lanes"])
    early, slab = lax.optimization_barrier((early, slab))
    slab = lax.all_to_all(slab, "col", split_axis=0, concat_axis=0, tiled=True)
    early = put_in_order(plan, place, points_map, early)
    return product(plan, place, points_map, slab, early, last)


def solution(mesh):
    in_specs = (P(), P(("row", "col"), None, None, None), P(), P(), P(("row", "col")), P())
    out_specs = P(None, "row", "col")
    return jax.shard_map(
        on_device, mesh=mesh, in_specs=in_specs, out_specs=out_specs, check_vma=False
    )
```

```python
import math

import jax
import jax.numpy as jnp
import numpy as np
from jax import lax
from jax.experimental import pallas as pl
from jax.experimental.pallas import tpu as pltpu
from jax.sharding import PartitionSpec as P

ROWS_DEV = 256
LANES = 128
VMEM_BYTES = 56 * 1024 * 1024
HALF = 64
KEEP = 40
ORIGIN = KEEP // 2
PARTS = 3


def round_up(value, step):
    return -(-value // step) * step


def length_counts(points):
    freq = np.arange(points) - points // 2
    square = freq * freq
    lengths = square[:, None, None] + square[None, :, None] + square[None, None, :]
    return np.cumsum(np.bincount(lengths.reshape(-1)))


def column_order(top):
    freq = np.arange(KEEP) - ORIGIN
    first, second = np.meshgrid(freq, freq, indexing="ij")
    length = (first * first + second * second).reshape(-1)
    order = np.argsort(length, kind="stable")
    order = order[length[order] <= top]
    return first.reshape(-1)[order], second.reshape(-1)[order], length[order]


class Columns:
    def __init__(self, top):
        self.windows = []
        offset = 0
        for begin in range(0, KEEP, 4):
            nearest = min(abs(index - ORIGIN) for index in range(begin, begin + 4))
            reach = math.isqrt(max(top - nearest * nearest, 0))
            low = (ORIGIN - reach) // 8 * 8
            high = min(round_up(ORIGIN + reach + 1, 8), KEEP)
            self.windows.append((low, high, offset))
            offset += 2 * (high - low)
        self.used = offset
        self.parity = round_up(offset, 2 * LANES)

    def place(self, index_2, index_3):
        low, high, offset = np.array(self.windows)[index_3 // 4].T
        return index_3 % 2 * self.parity + offset + index_3 // 2 % 2 * (high - low) + index_2 - low


class Bucket:
    def __init__(self, ranges, column_length):
        self.pieces = []
        self.edges = {}
        offset = 0
        for low, high in ranges:
            begin = offset
            for index in range(KEEP):
                freq = index - ORIGIN
                start = int(np.searchsorted(column_length, low - freq * freq, side="left"))
                stop = int(np.searchsorted(column_length, high - freq * freq, side="right"))
                if stop > start:
                    self.pieces.append((index, start, stop, offset))
                    offset += stop - start
            for length in range(low, high + 1):
                self.edges[length] = (begin, offset)
        self.size = offset

    def ids(self, column_2, column_3, points, width):
        out = np.full((width,), -1, np.int32)
        for index, start, stop, offset in self.pieces:
            k1 = (index - ORIGIN) % points
            k2 = column_2[start:stop] % points
            k3 = column_3[start:stop] % points
            out[offset : offset + stop - start] = (k1 * points + k2) * points + k3
        return out


def length_ranges(cumulative, first, step, count):
    shell = lambda rank: int(np.searchsorted(cumulative, rank, side="right"))
    ranges, low = [], shell(first)
    for part in range(1, count):
        before, after = shell(first + part * step - 1), shell(first + part * step)
        if before == after:
            if low < before:
                ranges.append((low, before - 1))
            if low <= before:
                ranges.append((before, before))
        elif low <= before:
            ranges.append((low, before))
        low = before + 1
    high = shell(first + count * step - 1)
    if low <= high:
        ranges.append((low, high))
    return ranges


def make_plan(points, total, blocks, slab, slab_blocks):
    cumulative = length_counts(points)
    shell = lambda rank: int(np.searchsorted(cumulative, rank, side="right"))
    width, slab_width = total // blocks, slab // slab_blocks
    step = width // PARTS
    column_2, column_3, column_length = column_order(shell(total - 1))
    buckets = [Bucket(length_ranges(cumulative, n * width, step, PARTS), column_length) for n in range(blocks)]
    slabs = [Bucket(length_ranges(cumulative, n * slab_width, slab_width, 1), column_length) for n in range(slab_blocks)]
    slab_top = shell(slab - 1)
    columns = Columns(shell(total - 1))
    place = columns.place(column_2 + ORIGIN, column_3 + ORIGIN)
    slab_columns = int(np.searchsorted(column_length, slab_top, side="right"))
    lanes = round_up(max(bucket.size for bucket in buckets), LANES)
    slab_lanes = round_up(max(bucket.size for bucket in slabs), LANES)
    windows = np.zeros((blocks, PARTS, 2), np.int64)
    for n, bucket in enumerate(buckets):
        for part in range(PARTS):
            rank = n * width + part * step
            windows[n, part, 0] = bucket.edges[shell(rank)][0] // LANES * LANES
            windows[n, part, 1] = round_up(bucket.edges[shell(rank + step - 1)][1], LANES)
    window = int((windows[..., 1] - windows[..., 0]).max())
    return dict(
        buckets=buckets,
        slabs=slabs,
        slab_columns=slab_columns,
        slab_tiles=sorted({int(value) for value in place[:slab_columns] // LANES}),
        columns=columns,
        lanes=lanes,
        slab_lanes=slab_lanes,
        window=window,
        starts=np.minimum(windows[..., 0], lanes - window).astype(np.int32),
        ids=np.stack([bucket.ids(column_2, column_3, points, lanes) for bucket in buckets]),
        slab_ids=np.stack([bucket.ids(column_2, column_3, points, slab_lanes) for bucket in slabs]),
        column_place=place.astype(np.int32),
    )


def dft_tables(points):
    n = np.arange(points)
    freq = np.arange(KEEP) - ORIGIN
    angle = (n[:, None] * freq[None, :] % points) * (2.0 * np.pi / points)
    cosine, sine = np.cos(angle), np.sin(angle)
    one = np.zeros((2, points, 2, HALF))
    one[0, :, 0, :KEEP] = cosine
    one[1, :, 0, :KEEP] = sine
    one[0, :, 1, :KEEP] = -sine
    one[1, :, 1, :KEEP] = cosine
    two = np.zeros((2, 2, points, 2, 2, HALF))
    for item in range(2):
        two[:, item, :, item] = one

    def parts(table):
        high = table.astype(jnp.bfloat16)
        return high, (table - high.astype(np.float64)).astype(jnp.bfloat16)

    high, low = parts(one[..., :KEEP].reshape(2 * points, 2 * KEEP).T)
    first = np.block([[high, high], [low, np.zeros_like(low)]])
    second = np.concatenate(parts(two.reshape(4 * points, 4 * HALF)), 0)
    halves = two[..., :KEEP].reshape(2, 2, points // 2, 2, 4 * KEEP).transpose(0, 1, 3, 2, 4)
    high, low = parts(halves.reshape(4 * points, 4 * KEEP).T)
    third = np.block([[high, high], [low, np.zeros_like(low)]])
    return [jnp.asarray(table) for table in (first, second, third)]


def split_parts(value):
    high = value.astype(jnp.bfloat16)
    low = (value - high.astype(jnp.float32)).astype(jnp.bfloat16)
    return high, low


def store_split(target, rows, blocks):
    for part, block in enumerate(blocks):
        high, low = split_parts(jnp.concatenate(block, 0))
        target[rows, part * LANES : (part + 1) * LANES] = high
        target[rows, (part + 2) * LANES : (part + 3) * LANES] = low


def doubled(stored):
    return jnp.concatenate([stored, stored[:, : stored.shape[1] // 2]], 1)


def contract_last(table, stored):
    both = lax.dot_general(table, stored, (((1,), (1,)), ((), ())), preferred_element_type=jnp.float32)
    rows = both.shape[0] // 2
    return both[:rows] + both[rows:]


def pack_pieces(pieces, width, source, rows, lane, out):
    for tile in range(width // LANES):
        left, right = tile * LANES, (tile + 1) * LANES
        value = jnp.zeros((rows, LANES), jnp.float32)
        for index, start, stop, offset in pieces:
            begin, end = max(left, offset), min(right, offset + stop - start)
            while begin < end:
                at = start + begin - offset
                block = source(index, at // LANES)
                shift = (begin - at) % LANES
                if shift:
                    block = pltpu.roll(block, shift, 1)
                value = block if begin == left else jnp.where(lane >= begin - left, block, value)
                begin = min(end, begin + LANES - at % LANES)
        out(tile, value)


def spectrum_kernel(plan, points, first_band, count, owner_ref, cond_energy_ref, val_energy_ref, val_ref, cond_ref, place_ref, first_ref,
                    second_ref, third_ref, send_ref, slab_ref, cond_a, cond_b, middle, turned, last, sorter, plain_rows, weighted_rows,
                    plain_sorted, weighted_sorted):
    band = pl.program_id(0)
    columns = plan["columns"]
    planes = 8
    pairs = planes // 2
    lane = lax.broadcasted_iota(jnp.int32, (1, LANES), 1)
    low_lanes = lane < HALF

    @pl.when(band == 0)
    def _():
        scale = 1.0 / float(points) ** 1.5
        sign = jnp.where(low_lanes, scale, -scale)

        @pl.loop(0, points // planes)
        def _(block):
            rows = pl.ds(pl.multiple_of(block * planes * points, planes * points), planes * points)
            wave = cond_ref[0, pl.ds(block * planes, planes)].reshape(planes * points, LANES).astype(jnp.float32)
            cond_a[rows, :] = wave * scale
            cond_b[rows, :] = pltpu.roll(wave, HALF, 1) * sign

        last[columns.used :, :] = jnp.zeros((columns.parity - columns.used, 4 * LANES), jnp.bfloat16)

    def first_axis(block):
        rows = pl.ds(pl.multiple_of(block * planes * points, planes * points), planes * points)
        wave = val_ref[0, pl.ds(block * planes, planes)].reshape(planes * points, LANES).astype(jnp.float32)
        other = pltpu.roll(wave, HALF, 1)
        density = jnp.where(low_lanes, wave, other) * cond_a[rows, :] + jnp.where(low_lanes, other, wave) * cond_b[rows, :]
        high, low = split_parts(density)
        field = contract_last(first_ref[...], jnp.concatenate([high, low], 1))
        for begin in range(0, pairs, 2):
            blocks = [
                [field[part * KEEP : (part + 1) * KEEP, pair * LANES : (pair + 1) * LANES] for pair in (begin, begin + 1)]
                for part in range(2)
            ]
            at = pl.ds(pl.multiple_of((block * pairs + begin) * KEEP, 2 * KEEP), 2 * KEEP)
            store_split(middle, at, blocks)

    def second_axis(block):
        rows = pl.ds(pl.multiple_of(block * 4 * KEEP, 4 * KEEP), 4 * KEEP)
        high = second_ref[: 2 * LANES]
        table = jnp.concatenate([high, high, second_ref[2 * LANES :]], 0)
        field = jnp.dot(doubled(middle[rows, :]), table, preferred_element_type=jnp.float32)
        for item in range(2):
            turned[item, rows, :] = field[:, item * LANES : (item + 1) * LANES]

    turns = points // 16 - 1
    piece = sorter.shape[0] // (count * turns)
    for part in range(2):
        first_axis(part)

    @pl.loop(1, turns + 1)
    def _(turn):
        begin = pl.multiple_of((band * turns + turn - 1) * piece, 16)
        at = lax.broadcasted_iota(jnp.int32, (piece, sorter.shape[1]), 0) + begin
        sorter[pl.ds(begin, piece), :] = jnp.where(at == place_ref[...], 1.0, 0.0).astype(jnp.bfloat16)
        for part in range(2):
            second_axis(2 * turn - 2 + part)
        for part in range(2):
            first_axis(2 * turn + part)

    for part in range(2):
        second_axis(2 * turns + part)

    for begin, (low, high, offset) in zip(range(0, KEEP, 4), columns.windows):
        both = []
        for pair in range(2):
            items = [
                turned[item, pl.ds(begin + 2 * pair + k3, points // 2, stride=KEEP), :]
                for k3 in range(2)
                for item in range(2)
            ]
            turn = jnp.concatenate(items, 0).T
            both.append((turn[low:high], turn[HALF + low : HALF + high]))
        store_split(last, slice(offset, offset + 2 * (high - low)), list(zip(*both)))

    bands = val_energy_ref.shape[0] * cond_energy_ref.shape[0]
    gap = cond_energy_ref[owner_ref[0]] - val_energy_ref[first_band + band]
    weight = -2.0 / (math.sqrt(bands) * jnp.full((1, LANES), gap, jnp.float32))
    slab = plan["slab_tiles"]
    tiles = columns.parity // LANES
    field = contract_last(third_ref[...], last[...])
    band_rows = pl.ds(pl.multiple_of(band * 2 * KEEP, 2 * KEEP), 2 * KEEP)
    for odd in range(2):
        value = field[odd * 2 * KEEP : (odd + 1) * 2 * KEEP]
        plain_rows[band_rows, odd * columns.parity : (odd + 1) * columns.parity] = value.astype(jnp.bfloat16)
        for place, tile in enumerate(slab):
            if tile // tiles == odd:
                inside = value[:, tile % tiles * LANES : (tile % tiles + 1) * LANES]
                weighted_rows[band_rows, place * LANES : (place + 1) * LANES] = (weight * inside).astype(jnp.bfloat16)

    @pl.when(band == count - 1)
    def _():
        def sort_rows(rows, which, target):
            value = jnp.dot(rows, which, preferred_element_type=jnp.float32)
            for tile in range(target.shape[0]):
                target[tile] = value[:, tile * LANES : (tile + 1) * LANES]

        which = [sorter[tile * LANES : (tile + 1) * LANES, : weighted_sorted.shape[0] * LANES] for tile in slab]
        sort_rows(plain_rows[...], sorter[: 2 * columns.parity, :], plain_sorted)
        sort_rows(weighted_rows[...], jnp.concatenate(which, 0), weighted_sorted)

        def plain_at(index, tile):
            return plain_sorted[tile, pl.ds(index, 2 * count, stride=KEEP), :]

        def weighted_at(index, tile):
            return weighted_sorted[tile, pl.ds(index, 2 * count, stride=KEEP), :]

        for block, bucket in enumerate(plan["buckets"]):

            def keep(tile, value):
                send_ref[block, :, tile * LANES : (tile + 1) * LANES] = value.astype(jnp.bfloat16)

            pack_pieces(bucket.pieces, plan["lanes"], plain_at, 2 * count, lane, keep)
        for block, bucket in enumerate(plan["slabs"]):

            def keep_slab(tile, value):
                slab_ref[block, :, tile * LANES : (tile + 1) * LANES] = value.astype(jnp.bfloat16)

            pack_pieces(bucket.pieces, plan["slab_lanes"], weighted_at, 2 * count, lane, keep_slab)


def spectra(plan, val_wave, cond_wave, energies, first_band, count):
    points = val_wave.shape[1]
    turns = points // 16 - 1
    parity = plan["columns"].parity
    depth = round_up(-(-2 * parity // (count * turns)), 16) * count * turns
    columns = round_up(plan["column_place"].shape[0], 256)
    slab_columns = round_up(plan["slab_columns"], LANES)
    slab_depth = len(plan["slab_tiles"]) * LANES
    place = np.full((1, columns), -1, np.int32)
    place[0, : plan["column_place"].shape[0]] = plan["column_place"]
    grid_rows = points * points
    tables = dft_tables(points)
    send_shape = (len(plan["buckets"]), 2 * count, plan["lanes"])
    slab_shape = (len(plan["slabs"]), 2 * count, plan["slab_lanes"])
    kernel = lambda *refs: spectrum_kernel(plan, points, first_band, count, *refs)
    return pl.pallas_call(
        kernel,
        grid=(count,),
        in_specs=[
            pl.BlockSpec(memory_space=pltpu.SMEM),
            pl.BlockSpec(memory_space=pltpu.SMEM),
            pl.BlockSpec(memory_space=pltpu.SMEM),
            pl.BlockSpec((1, points, points, 2 * points), lambda v: (first_band + v, 0, 0, 0)),
            pl.BlockSpec((1, points, points, 2 * points), lambda v: (0, 0, 0, 0)),
            pl.BlockSpec((1, columns), lambda v: (0, 0)),
            *[pl.BlockSpec(table.shape, lambda v: (0, 0)) for table in tables],
        ],
        out_specs=[pl.BlockSpec(send_shape, lambda v: (0, 0, 0)), pl.BlockSpec(slab_shape, lambda v: (0, 0, 0))],
        out_shape=[jax.ShapeDtypeStruct(send_shape, jnp.bfloat16), jax.ShapeDtypeStruct(slab_shape, jnp.bfloat16)],
        scratch_shapes=[
            pltpu.VMEM((grid_rows, LANES), jnp.float32),
            pltpu.VMEM((grid_rows, LANES), jnp.float32),
            pltpu.VMEM((points // 2 * KEEP, 4 * LANES), jnp.bfloat16),
            pltpu.VMEM((2, points // 2 * KEEP, LANES), jnp.float32),
            pltpu.VMEM((parity, 4 * LANES), jnp.bfloat16),
            pltpu.VMEM((depth, columns), jnp.bfloat16),
            pltpu.VMEM((2 * count * KEEP, 2 * parity), jnp.bfloat16),
            pltpu.VMEM((2 * count * KEEP, slab_depth), jnp.bfloat16),
            pltpu.VMEM((columns // LANES, 2 * count * KEEP, LANES), jnp.float32),
            pltpu.VMEM((slab_columns // LANES, 2 * count * KEEP, LANES), jnp.float32),
        ],
        compiler_params=pltpu.CompilerParams(vmem_limit_bytes=VMEM_BYTES, dimension_semantics=("arbitrary",)),
        cost_estimate=pl.CostEstimate(flops=1, bytes_accessed=1, transcendentals=0),
        name="spectra",
    )(*energies, val_wave, cond_wave, jnp.asarray(place), *tables)


def one_hot(ids, wanted):
    ids = jnp.broadcast_to(ids, (LANES, LANES)).T
    ids = jnp.concatenate([ids] * (wanted.shape[1] // LANES), 1)
    return jnp.where(ids == wanted, 1.0, 0.0).astype(jnp.bfloat16)


def make_left(row_count, slab_ref, ids_ref, wanted_ref, left):
    rows = wanted_ref.shape[1]
    col_count = slab_ref.shape[0]
    group = slab_ref.shape[1] // (2 * row_count)
    order = [(col, 2 * row) for col in range(col_count) for row in range(row_count)]
    order += [(col, 2 * row + 1) for row in range(row_count) for col in range(col_count)]
    slab = [slab_ref[col, at * group : (at + 1) * group, :].astype(jnp.float32) for col, at in order]
    ids = ids_ref[0]
    choice = [one_hot(ids[:, begin : begin + LANES], wanted_ref[...]) for begin in range(0, ids.shape[1], LANES)]
    chosen = jnp.dot(
        jnp.concatenate(slab, 0).astype(jnp.bfloat16), jnp.concatenate(choice, 0), preferred_element_type=jnp.float32
    )
    lane = lax.broadcasted_iota(jnp.int32, (1, LANES), 1)
    real_lanes = lane % 2 == 0
    for begin in range(0, chosen.shape[0], LANES):
        turned = chosen[begin : begin + LANES].T
        after = pltpu.roll(turned, LANES - 1, 1)
        before = pltpu.roll(turned, 1, 1)
        left[:rows, begin : begin + LANES] = turned.astype(jnp.bfloat16)
        left[rows:, begin : begin + LANES] = jnp.where(real_lanes, after, -before).astype(jnp.bfloat16)


def order_kernel(place_ref, starts_ref, ids_ref, wanted_ref, panel_ref, out_ref, hot):
    start = pl.multiple_of(starts_ref[place_ref[0] * PARTS + pl.program_id(0)], LANES)
    wanted = wanted_ref[...]
    window = hot.shape[0]
    for begin in range(0, window, LANES):
        ids = ids_ref[0, :, pl.ds(pl.multiple_of(start + begin, LANES), LANES)]
        hot[begin : begin + LANES, :] = one_hot(ids, wanted)
    ordered = jnp.dot(panel_ref[:, pl.ds(start, window)], hot[...], preferred_element_type=jnp.float32)
    out_ref[...] = ordered.astype(jnp.bfloat16)


def put_in_order(plan, place, points_map, panel):
    columns = points_map.shape[1] // len(plan["buckets"])
    block = columns // PARTS
    ids = jnp.asarray(plan["ids"])[:, None]
    return pl.pallas_call(
        order_kernel,
        grid_spec=pltpu.PrefetchScalarGridSpec(
            num_scalar_prefetch=2,
            grid=(PARTS,),
            in_specs=[
                pl.BlockSpec((1, *ids.shape[1:]), lambda n, place, starts: (place[0], 0, 0)),
                pl.BlockSpec((1, block), lambda n, place, starts: (0, place[0] * PARTS + n)),
                pl.BlockSpec(panel.shape, lambda n, place, starts: (0, 0)),
            ],
            out_specs=pl.BlockSpec((panel.shape[0], block), lambda n, place, starts: (0, n)),
            scratch_shapes=[pltpu.VMEM((plan["window"], block), jnp.bfloat16)],
        ),
        out_shape=jax.ShapeDtypeStruct((panel.shape[0], columns), jnp.bfloat16),
        compiler_params=pltpu.CompilerParams(vmem_limit_bytes=VMEM_BYTES, dimension_semantics=("arbitrary",)),
        cost_estimate=pl.CostEstimate(flops=1, bytes_accessed=1, transcendentals=0),
        name="in_order",
    )(place, jnp.asarray(plan["starts"].reshape(-1)), ids, points_map, panel)


def product_kernel(row_count, place_ref, slab_ref, ids_ref, wanted_ref, early_ref, last_ref, out_ref, left):
    rows = out_ref.shape[1]

    @pl.when(pl.program_id(0) == 0)
    def _():
        make_left(row_count, slab_ref, ids_ref, wanted_ref, left)

    right = jnp.concatenate([early_ref[...], last_ref[...]], 0)
    chi = jnp.dot(left[...], right, preferred_element_type=jnp.float32)
    out_ref[0] = chi[:rows]
    out_ref[1] = chi[rows:]


def product(plan, place, points_map, slab, early, last):
    pairs, columns = slab.shape[0] * slab.shape[1], early.shape[1]
    block = 6 * LANES
    ids = jnp.asarray(plan["slab_ids"])[:, None]
    return pl.pallas_call(
        lambda *refs: product_kernel(ids.shape[0], *refs),
        grid_spec=pltpu.PrefetchScalarGridSpec(
            num_scalar_prefetch=1,
            grid=(pl.cdiv(columns, block),),
            in_specs=[
                pl.BlockSpec(slab.shape, lambda n, place: (0, 0, 0)),
                pl.BlockSpec((1, *ids.shape[1:]), lambda n, place: (place[1], 0, 0)),
                pl.BlockSpec((1, ROWS_DEV), lambda n, place: (0, place[1])),
                pl.BlockSpec((early.shape[0], block), lambda n, place: (0, n)),
                pl.BlockSpec((last.shape[0], block), lambda n, place: (0, n)),
            ],
            out_specs=pl.BlockSpec((2, ROWS_DEV, block), lambda n, place: (0, 0, n)),
            scratch_shapes=[pltpu.VMEM((2 * ROWS_DEV, pairs), jnp.bfloat16)],
        ),
        out_shape=jax.ShapeDtypeStruct((2, ROWS_DEV, columns), jnp.float32),
        compiler_params=pltpu.CompilerParams(vmem_limit_bytes=VMEM_BYTES, dimension_semantics=("arbitrary",)),
        cost_estimate=pl.CostEstimate(flops=1, bytes_accessed=1, transcendentals=0),
        name="product",
    )(place, slab, ids, points_map, early, last)


def on_device(val_wave, cond_wave, val_energy, cond_energy, band_owner, grid_map):
    bands, points = val_wave.shape[0], val_wave.shape[1]
    row_count = lax.axis_size("row")
    col_count = lax.axis_size("col")
    col, row = lax.axis_index("col"), lax.axis_index("row")
    plan = make_plan(points, grid_map.shape[0], col_count, ROWS_DEV * row_count, row_count)
    place = jnp.stack([col, row]).astype(jnp.int32)
    points_map = grid_map[None]
    chunk = bands // 2
    energies = (band_owner, cond_energy, val_energy)
    slabs = []
    for part in range(2):
        send, slab = spectra(plan, val_wave, cond_wave, energies, part * chunk, chunk)
        slabs.append(slab)
        if part == 0:
            send, cond_wave = lax.optimization_barrier((send, cond_wave))
            early = lax.all_gather(send, "row", axis=1)
        else:
            mine = lax.all_to_all(send, "col", split_axis=0, concat_axis=0, tiled=True).reshape(-1, plan["lanes"])
            mine = put_in_order(plan, place, points_map, mine)
            last = lax.all_gather(mine, "row", axis=0, tiled=True)
    slab, _ = lax.optimization_barrier((jnp.concatenate(slabs, 1), mine))
    slab = lax.all_to_all(slab, "row", split_axis=0, concat_axis=0, tiled=True).reshape(-1, plan["slab_lanes"])
    slab = jnp.broadcast_to(slab, (col_count, *slab.shape))
    early, slab = lax.optimization_barrier((early, slab))
    early = lax.all_to_all(early, "col", split_axis=0, concat_axis=0, tiled=True).reshape(-1, plan["lanes"])
    early, slab = lax.optimization_barrier((early, slab))
    slab = lax.all_to_all(slab, "col", split_axis=0, concat_axis=0, tiled=True)
    early = put_in_order(plan, place, points_map, early)
    return product(plan, place, points_map, slab, early, last)


def solution(mesh):
    in_specs = (P(), P(("row", "col"), None, None, None), P(), P(), P(("row", "col")), P())
    out_specs = P(None, "row", "col")
    return jax.shard_map(
        on_device, mesh=mesh, in_specs=in_specs, out_specs=out_specs, check_vma=False
    )
```

```python
import math

import jax
import jax.numpy as jnp
import numpy as np
from jax import lax
from jax.experimental import pallas as pl
from jax.experimental.pallas import tpu as pltpu
from jax.sharding import PartitionSpec as P

ROWS_DEV = 256
LANES = 128
VMEM_BYTES = 56 * 1024 * 1024
HALF = 64
KEEP = 40
ORIGIN = KEEP // 2
PARTS = 3


def round_up(value, step):
    return -(-value // step) * step


def length_counts(points):
    freq = np.arange(points) - points // 2
    square = freq * freq
    lengths = square[:, None, None] + square[None, :, None] + square[None, None, :]
    return np.cumsum(np.bincount(lengths.reshape(-1)))


def column_order(top):
    freq = np.arange(KEEP) - ORIGIN
    first, second = np.meshgrid(freq, freq, indexing="ij")
    length = (first * first + second * second).reshape(-1)
    order = np.argsort(length, kind="stable")
    order = order[length[order] <= top]
    return first.reshape(-1)[order], second.reshape(-1)[order], length[order]


class Columns:
    def __init__(self, top):
        self.windows = []
        offset = 0
        for begin in range(0, KEEP, 4):
            nearest = min(abs(index - ORIGIN) for index in range(begin, begin + 4))
            reach = math.isqrt(max(top - nearest * nearest, 0))
            low = (ORIGIN - reach) // 8 * 8
            high = min(round_up(ORIGIN + reach + 1, 8), KEEP)
            self.windows.append((low, high, offset))
            offset += 2 * (high - low)
        self.used = offset
        self.parity = round_up(offset, 2 * LANES)

    def place(self, index_2, index_3):
        low, high, offset = np.array(self.windows)[index_3 // 4].T
        return index_3 % 2 * self.parity + offset + index_3 // 2 % 2 * (high - low) + index_2 - low


class Bucket:
    def __init__(self, ranges, column_length):
        self.pieces = []
        self.edges = {}
        offset = 0
        for low, high in ranges:
            begin = offset
            for index in range(KEEP):
                freq = index - ORIGIN
                start = int(np.searchsorted(column_length, low - freq * freq, side="left"))
                stop = int(np.searchsorted(column_length, high - freq * freq, side="right"))
                if stop > start:
                    self.pieces.append((index, start, stop, offset))
                    offset += stop - start
            for length in range(low, high + 1):
                self.edges[length] = (begin, offset)
        self.size = offset

    def ids(self, column_2, column_3, points, width):
        out = np.full((width,), -1, np.int32)
        for index, start, stop, offset in self.pieces:
            k1 = (index - ORIGIN) % points
            k2 = column_2[start:stop] % points
            k3 = column_3[start:stop] % points
            out[offset : offset + stop - start] = (k1 * points + k2) * points + k3
        return out


def length_ranges(cumulative, first, step, count):
    shell = lambda rank: int(np.searchsorted(cumulative, rank, side="right"))
    ranges, low = [], shell(first)
    for part in range(1, count):
        before, after = shell(first + part * step - 1), shell(first + part * step)
        if before == after:
            if low < before:
                ranges.append((low, before - 1))
            if low <= before:
                ranges.append((before, before))
        elif low <= before:
            ranges.append((low, before))
        low = before + 1
    high = shell(first + count * step - 1)
    if low <= high:
        ranges.append((low, high))
    return ranges


def make_plan(points, total, blocks, slab, slab_blocks):
    cumulative = length_counts(points)
    shell = lambda rank: int(np.searchsorted(cumulative, rank, side="right"))
    width, slab_width = total // blocks, slab // slab_blocks
    step = width // PARTS
    column_2, column_3, column_length = column_order(shell(total - 1))
    buckets = [Bucket(length_ranges(cumulative, n * width, step, PARTS), column_length) for n in range(blocks)]
    slabs = [Bucket(length_ranges(cumulative, n * slab_width, slab_width, 1), column_length) for n in range(slab_blocks)]
    slab_top = shell(slab - 1)
    columns = Columns(shell(total - 1))
    place = columns.place(column_2 + ORIGIN, column_3 + ORIGIN)
    slab_columns = int(np.searchsorted(column_length, slab_top, side="right"))
    lanes = round_up(max(bucket.size for bucket in buckets), LANES)
    slab_lanes = round_up(max(bucket.size for bucket in slabs), LANES)
    windows = np.zeros((blocks, PARTS, 2), np.int64)
    for n, bucket in enumerate(buckets):
        for part in range(PARTS):
            rank = n * width + part * step
            windows[n, part, 0] = bucket.edges[shell(rank)][0] // LANES * LANES
            windows[n, part, 1] = round_up(bucket.edges[shell(rank + step - 1)][1], LANES)
    window = int((windows[..., 1] - windows[..., 0]).max())
    return dict(
        buckets=buckets,
        slabs=slabs,
        slab_columns=slab_columns,
        slab_tiles=sorted({int(value) for value in place[:slab_columns] // LANES}),
        columns=columns,
        lanes=lanes,
        slab_lanes=slab_lanes,
        window=window,
        starts=np.minimum(windows[..., 0], lanes - window).astype(np.int32),
        ids=np.stack([bucket.ids(column_2, column_3, points, lanes) for bucket in buckets]),
        slab_ids=np.stack([bucket.ids(column_2, column_3, points, slab_lanes) for bucket in slabs]),
        column_place=place.astype(np.int32),
    )


def dft_tables(points):
    n = np.arange(points)
    freq = np.arange(KEEP) - ORIGIN
    angle = (n[:, None] * freq[None, :] % points) * (2.0 * np.pi / points)
    cosine, sine = np.cos(angle), np.sin(angle)
    one = np.zeros((2, points, 2, HALF))
    one[0, :, 0, :KEEP] = cosine
    one[1, :, 0, :KEEP] = sine
    one[0, :, 1, :KEEP] = -sine
    one[1, :, 1, :KEEP] = cosine
    two = np.zeros((2, 2, points, 2, 2, HALF))
    for item in range(2):
        two[:, item, :, item] = one

    def parts(table):
        high = table.astype(jnp.bfloat16)
        return high, (table - high.astype(np.float64)).astype(jnp.bfloat16)

    high, low = parts(one[..., :KEEP].reshape(2 * points, 2 * KEEP).T)
    first = np.block([[high, high], [low, np.zeros_like(low)]])
    second = np.concatenate(parts(two.reshape(4 * points, 4 * HALF)), 0)
    halves = two[..., :KEEP].reshape(2, 2, points // 2, 2, 4 * KEEP).transpose(0, 1, 3, 2, 4)
    high, low = parts(halves.reshape(4 * points, 4 * KEEP).T)
    third = np.block([[high, high], [low, np.zeros_like(low)]])
    return [jnp.asarray(table) for table in (first, second, third)]


def split_parts(value):
    high = value.astype(jnp.bfloat16)
    low = (value - high.astype(jnp.float32)).astype(jnp.bfloat16)
    return high, low


def store_split(target, rows, blocks):
    for part, block in enumerate(blocks):
        high, low = split_parts(jnp.concatenate(block, 0))
        target[rows, part * LANES : (part + 1) * LANES] = high
        target[rows, (part + 2) * LANES : (part + 3) * LANES] = low


def doubled(stored):
    return jnp.concatenate([stored, stored[:, : stored.shape[1] // 2]], 1)


def contract_last(table, stored):
    both = lax.dot_general(table, stored, (((1,), (1,)), ((), ())), preferred_element_type=jnp.float32)
    rows = both.shape[0] // 2
    return both[:rows] + both[rows:]


def pack_pieces(pieces, width, source, rows, lane, out):
    for tile in range(width // LANES):
        left, right = tile * LANES, (tile + 1) * LANES
        value = jnp.zeros((rows, LANES), jnp.float32)
        for index, start, stop, offset in pieces:
            begin, end = max(left, offset), min(right, offset + stop - start)
            while begin < end:
                at = start + begin - offset
                block = source(index, at // LANES)
                shift = (begin - at) % LANES
                if shift:
                    block = pltpu.roll(block, shift, 1)
                value = block if begin == left else jnp.where(lane >= begin - left, block, value)
                begin = min(end, begin + LANES - at % LANES)
        out(tile, value)


def spectrum_kernel(plan, points, first_band, count, owner_ref, cond_energy_ref, val_energy_ref, val_ref, cond_ref, place_ref, first_ref,
                    second_ref, third_ref, send_ref, slab_ref, cond_a, cond_b, middle, turned, last, sorter, plain_rows, weighted_rows,
                    plain_sorted, weighted_sorted):
    band = pl.program_id(0)
    columns = plan["columns"]
    planes = 8
    pairs = planes // 2
    lane = lax.broadcasted_iota(jnp.int32, (1, LANES), 1)
    low_lanes = lane < HALF

    @pl.when(band == 0)
    def _():
        scale = 1.0 / float(points) ** 1.5
        sign = jnp.where(low_lanes, scale, -scale)

        @pl.loop(0, points // planes, unroll=4)
        def _(block):
            rows = pl.ds(pl.multiple_of(block * planes * points, planes * points), planes * points)
            wave = cond_ref[0, pl.ds(block * planes, planes)].reshape(planes * points, LANES).astype(jnp.float32)
            other = pltpu.roll(wave, HALF, 1)
            cond_a[rows, :] = jnp.where(low_lanes, wave, other) * sign
            cond_b[rows, :] = jnp.where(low_lanes, other, wave) * scale

        last[columns.used :, :] = jnp.zeros((columns.parity - columns.used, 4 * LANES), jnp.bfloat16)

    def first_axis(block):
        rows = pl.ds(pl.multiple_of(block * planes * points, planes * points), planes * points)
        wave = val_ref[0, pl.ds(block * planes, planes)].reshape(planes * points, LANES).astype(jnp.float32)
        density = wave * cond_a[rows, :] + pltpu.roll(wave, HALF, 1) * cond_b[rows, :]
        high, low = split_parts(density)
        field = contract_last(first_ref[...], jnp.concatenate([high, low], 1))
        for begin in range(0, pairs, 2):
            blocks = [
                [field[part * KEEP : (part + 1) * KEEP, pair * LANES : (pair + 1) * LANES] for pair in (begin, begin + 1)]
                for part in range(2)
            ]
            at = pl.ds(pl.multiple_of((block * pairs + begin) * KEEP, 2 * KEEP), 2 * KEEP)
            store_split(middle, at, blocks)

    def second_axis(block):
        rows = pl.ds(pl.multiple_of(block * 4 * KEEP, 4 * KEEP), 4 * KEEP)
        high = second_ref[: 2 * LANES]
        table = jnp.concatenate([high, high, second_ref[2 * LANES :]], 0)
        field = jnp.dot(doubled(middle[rows, :]), table, preferred_element_type=jnp.float32)
        for item in range(2):
            turned[item, rows, :] = field[:, item * LANES : (item + 1) * LANES]

    turns = points // 16 - 1
    piece = sorter.shape[0] // (count * turns)
    for part in range(2):
        first_axis(part)

    @pl.loop(1, turns + 1)
    def _(turn):
        begin = pl.multiple_of((band * turns + turn - 1) * piece, 16)
        at = lax.broadcasted_iota(jnp.int32, (piece, sorter.shape[1]), 0) + begin
        sorter[pl.ds(begin, piece), :] = jnp.where(at == place_ref[...], 1.0, 0.0).astype(jnp.bfloat16)
        for part in range(2):
            second_axis(2 * turn - 2 + part)
        for part in range(2):
            first_axis(2 * turn + part)

    for part in range(2):
        second_axis(2 * turns + part)

    for begin, (low, high, offset) in zip(range(0, KEEP, 4), columns.windows):
        both = []
        for pair in range(2):
            items = [
                turned[item, pl.ds(begin + 2 * pair + k3, points // 2, stride=KEEP), :]
                for k3 in range(2)
                for item in range(2)
            ]
            turn = jnp.concatenate(items, 0).T
            both.append((turn[low:high], turn[HALF + low : HALF + high]))
        store_split(last, slice(offset, offset + 2 * (high - low)), list(zip(*both)))

    bands = val_energy_ref.shape[0] * cond_energy_ref.shape[0]
    gap = cond_energy_ref[owner_ref[0]] - val_energy_ref[first_band + band]
    weight = -2.0 / (math.sqrt(bands) * jnp.full((1, LANES), gap, jnp.float32))
    slab = plan["slab_tiles"]
    tiles = columns.parity // LANES
    field = contract_last(third_ref[...], last[...])
    band_rows = pl.ds(pl.multiple_of(band * 2 * KEEP, 2 * KEEP), 2 * KEEP)
    for odd in range(2):
        value = field[odd * 2 * KEEP : (odd + 1) * 2 * KEEP]
        plain_rows[band_rows, odd * columns.parity : (odd + 1) * columns.parity] = value.astype(jnp.bfloat16)
        for place, tile in enumerate(slab):
            if tile // tiles == odd:
                inside = value[:, tile % tiles * LANES : (tile % tiles + 1) * LANES]
                weighted_rows[band_rows, place * LANES : (place + 1) * LANES] = (weight * inside).astype(jnp.bfloat16)

    @pl.when(band == count - 1)
    def _():
        def sort_rows(rows, which, target):
            value = jnp.dot(rows, which, preferred_element_type=jnp.float32)
            for tile in range(target.shape[0]):
                target[tile] = value[:, tile * LANES : (tile + 1) * LANES]

        which = [sorter[tile * LANES : (tile + 1) * LANES, : weighted_sorted.shape[0] * LANES] for tile in slab]
        sort_rows(plain_rows[...], sorter[: 2 * columns.parity, :], plain_sorted)
        sort_rows(weighted_rows[...], jnp.concatenate(which, 0), weighted_sorted)

        def plain_at(index, tile):
            return plain_sorted[tile, pl.ds(index, 2 * count, stride=KEEP), :]

        def weighted_at(index, tile):
            return weighted_sorted[tile, pl.ds(index, 2 * count, stride=KEEP), :]

        for block, bucket in enumerate(plan["buckets"]):

            def keep(tile, value):
                send_ref[block, :, tile * LANES : (tile + 1) * LANES] = value.astype(jnp.bfloat16)

            pack_pieces(bucket.pieces, plan["lanes"], plain_at, 2 * count, lane, keep)
        for block, bucket in enumerate(plan["slabs"]):

            def keep_slab(tile, value):
                slab_ref[block, :, tile * LANES : (tile + 1) * LANES] = value.astype(jnp.bfloat16)

            pack_pieces(bucket.pieces, plan["slab_lanes"], weighted_at, 2 * count, lane, keep_slab)


def spectra(plan, val_wave, cond_wave, energies, first_band, count):
    points = val_wave.shape[1]
    turns = points // 16 - 1
    parity = plan["columns"].parity
    depth = round_up(-(-2 * parity // (count * turns)), 16) * count * turns
    columns = round_up(plan["column_place"].shape[0], 256)
    slab_columns = round_up(plan["slab_columns"], LANES)
    slab_depth = len(plan["slab_tiles"]) * LANES
    place = np.full((1, columns), -1, np.int32)
    place[0, : plan["column_place"].shape[0]] = plan["column_place"]
    grid_rows = points * points
    tables = dft_tables(points)
    send_shape = (len(plan["buckets"]), 2 * count, plan["lanes"])
    slab_shape = (len(plan["slabs"]), 2 * count, plan["slab_lanes"])
    kernel = lambda *refs: spectrum_kernel(plan, points, first_band, count, *refs)
    return pl.pallas_call(
        kernel,
        grid=(count,),
        in_specs=[
            pl.BlockSpec(memory_space=pltpu.SMEM),
            pl.BlockSpec(memory_space=pltpu.SMEM),
            pl.BlockSpec(memory_space=pltpu.SMEM),
            pl.BlockSpec((1, points, points, 2 * points), lambda v: (first_band + v, 0, 0, 0)),
            pl.BlockSpec((1, points, points, 2 * points), lambda v: (0, 0, 0, 0)),
            pl.BlockSpec((1, columns), lambda v: (0, 0)),
            *[pl.BlockSpec(table.shape, lambda v: (0, 0)) for table in tables],
        ],
        out_specs=[pl.BlockSpec(send_shape, lambda v: (0, 0, 0)), pl.BlockSpec(slab_shape, lambda v: (0, 0, 0))],
        out_shape=[jax.ShapeDtypeStruct(send_shape, jnp.bfloat16), jax.ShapeDtypeStruct(slab_shape, jnp.bfloat16)],
        scratch_shapes=[
            pltpu.VMEM((grid_rows, LANES), jnp.float32),
            pltpu.VMEM((grid_rows, LANES), jnp.float32),
            pltpu.VMEM((points // 2 * KEEP, 4 * LANES), jnp.bfloat16),
            pltpu.VMEM((2, points // 2 * KEEP, LANES), jnp.float32),
            pltpu.VMEM((parity, 4 * LANES), jnp.bfloat16),
            pltpu.VMEM((depth, columns), jnp.bfloat16),
            pltpu.VMEM((2 * count * KEEP, 2 * parity), jnp.bfloat16),
            pltpu.VMEM((2 * count * KEEP, slab_depth), jnp.bfloat16),
            pltpu.VMEM((columns // LANES, 2 * count * KEEP, LANES), jnp.float32),
            pltpu.VMEM((slab_columns // LANES, 2 * count * KEEP, LANES), jnp.float32),
        ],
        compiler_params=pltpu.CompilerParams(vmem_limit_bytes=VMEM_BYTES, dimension_semantics=("arbitrary",)),
        cost_estimate=pl.CostEstimate(flops=1, bytes_accessed=1, transcendentals=0),
        name="spectra",
    )(*energies, val_wave, cond_wave, jnp.asarray(place), *tables)


def one_hot(ids, wanted):
    ids = jnp.broadcast_to(ids, (LANES, LANES)).T
    ids = jnp.concatenate([ids] * (wanted.shape[1] // LANES), 1)
    return jnp.where(ids == wanted, 1.0, 0.0).astype(jnp.bfloat16)


def make_left(row_count, slab_ref, ids_ref, wanted_ref, left):
    rows = wanted_ref.shape[1]
    col_count = slab_ref.shape[0]
    group = slab_ref.shape[1] // (2 * row_count)
    order = [(col, 2 * row) for col in range(col_count) for row in range(row_count)]
    order += [(col, 2 * row + 1) for row in range(row_count) for col in range(col_count)]
    slab = [slab_ref[col, at * group : (at + 1) * group, :].astype(jnp.float32) for col, at in order]
    wanted = [
        jnp.broadcast_to(wanted_ref[:, begin : begin + LANES], (LANES, LANES)).T for begin in range(0, rows, LANES)
    ]
    wanted = jnp.concatenate([jnp.concatenate(wanted, 0)] * (ids_ref.shape[2] // LANES), 1)
    choice = jnp.where(wanted == ids_ref[0], 1.0, 0.0).astype(jnp.bfloat16)
    chosen = lax.dot_general(
        choice,
        jnp.concatenate(slab, 0).astype(jnp.bfloat16),
        (((1,), (1,)), ((), ())),
        preferred_element_type=jnp.float32,
    )
    lane = lax.broadcasted_iota(jnp.int32, (1, LANES), 1)
    real_lanes = lane % 2 == 0
    for begin in range(0, chosen.shape[1], LANES):
        part = chosen[:, begin : begin + LANES]
        after = pltpu.roll(part, LANES - 1, 1)
        before = pltpu.roll(part, 1, 1)
        left[:rows, begin : begin + LANES] = part.astype(jnp.bfloat16)
        left[rows:, begin : begin + LANES] = jnp.where(real_lanes, after, -before).astype(jnp.bfloat16)


def order_kernel(place_ref, starts_ref, ids_ref, wanted_ref, panel_ref, out_ref, hot):
    start = pl.multiple_of(starts_ref[place_ref[0] * PARTS + pl.program_id(0)], LANES)
    wanted = wanted_ref[...]
    window = hot.shape[0]
    for begin in range(0, window, LANES):
        ids = ids_ref[0, :, pl.ds(pl.multiple_of(start + begin, LANES), LANES)]
        hot[begin : begin + LANES, :] = one_hot(ids, wanted)
    ordered = jnp.dot(panel_ref[:, pl.ds(start, window)], hot[...], preferred_element_type=jnp.float32)
    out_ref[...] = ordered.astype(jnp.bfloat16)


def put_in_order(plan, place, points_map, panel):
    columns = points_map.shape[1] // len(plan["buckets"])
    block = columns // PARTS
    ids = jnp.asarray(plan["ids"])[:, None]
    return pl.pallas_call(
        order_kernel,
        grid_spec=pltpu.PrefetchScalarGridSpec(
            num_scalar_prefetch=2,
            grid=(PARTS,),
            in_specs=[
                pl.BlockSpec((1, *ids.shape[1:]), lambda n, place, starts: (place[0], 0, 0)),
                pl.BlockSpec((1, block), lambda n, place, starts: (0, place[0] * PARTS + n)),
                pl.BlockSpec(panel.shape, lambda n, place, starts: (0, 0)),
            ],
            out_specs=pl.BlockSpec((panel.shape[0], block), lambda n, place, starts: (0, n)),
            scratch_shapes=[pltpu.VMEM((plan["window"], block), jnp.bfloat16)],
        ),
        out_shape=jax.ShapeDtypeStruct((panel.shape[0], columns), jnp.bfloat16),
        compiler_params=pltpu.CompilerParams(vmem_limit_bytes=VMEM_BYTES, dimension_semantics=("arbitrary",)),
        cost_estimate=pl.CostEstimate(flops=1, bytes_accessed=1, transcendentals=0),
        name="in_order",
    )(place, jnp.asarray(plan["starts"].reshape(-1)), ids, points_map, panel)


def product_kernel(row_count, place_ref, slab_ref, ids_ref, wanted_ref, early_ref, last_ref, out_ref, left):
    rows = out_ref.shape[1]

    @pl.when(pl.program_id(0) == 0)
    def _():
        make_left(row_count, slab_ref, ids_ref, wanted_ref, left)

    right = jnp.concatenate([early_ref[...], last_ref[...]], 0)
    chi = jnp.dot(left[...], right, preferred_element_type=jnp.float32)
    out_ref[0] = chi[:rows]
    out_ref[1] = chi[rows:]


def product(plan, place, points_map, slab, early, last):
    pairs, columns = slab.shape[0] * slab.shape[1], early.shape[1]
    block = 6 * LANES
    ids = jnp.asarray(plan["slab_ids"])[:, None]
    return pl.pallas_call(
        lambda *refs: product_kernel(ids.shape[0], *refs),
        grid_spec=pltpu.PrefetchScalarGridSpec(
            num_scalar_prefetch=1,
            grid=(pl.cdiv(columns, block),),
            in_specs=[
                pl.BlockSpec(slab.shape, lambda n, place: (0, 0, 0)),
                pl.BlockSpec((1, *ids.shape[1:]), lambda n, place: (place[1], 0, 0)),
                pl.BlockSpec((1, ROWS_DEV), lambda n, place: (0, place[1])),
                pl.BlockSpec((early.shape[0], block), lambda n, place: (0, n)),
                pl.BlockSpec((last.shape[0], block), lambda n, place: (0, n)),
            ],
            out_specs=pl.BlockSpec((2, ROWS_DEV, block), lambda n, place: (0, 0, n)),
            scratch_shapes=[pltpu.VMEM((2 * ROWS_DEV, pairs), jnp.bfloat16)],
        ),
        out_shape=jax.ShapeDtypeStruct((2, ROWS_DEV, columns), jnp.float32),
        compiler_params=pltpu.CompilerParams(vmem_limit_bytes=VMEM_BYTES, dimension_semantics=("arbitrary",)),
        cost_estimate=pl.CostEstimate(flops=1, bytes_accessed=1, transcendentals=0),
        name="product",
    )(place, slab, ids, points_map, early, last)


def on_device(val_wave, cond_wave, val_energy, cond_energy, band_owner, grid_map):
    bands, points = val_wave.shape[0], val_wave.shape[1]
    row_count = lax.axis_size("row")
    col_count = lax.axis_size("col")
    col, row = lax.axis_index("col"), lax.axis_index("row")
    plan = make_plan(points, grid_map.shape[0], col_count, ROWS_DEV * row_count, row_count)
    place = jnp.stack([col, row]).astype(jnp.int32)
    points_map = grid_map[None]
    chunk = bands // 2
    energies = (band_owner, cond_energy, val_energy)
    slabs = []
    for part in range(2):
        send, slab = spectra(plan, val_wave, cond_wave, energies, part * chunk, chunk)
        slabs.append(slab)
        if part == 0:
            send, cond_wave = lax.optimization_barrier((send, cond_wave))
            early = lax.all_gather(send, "row", axis=1)
        else:
            mine = lax.all_to_all(send, "col", split_axis=0, concat_axis=0, tiled=True).reshape(-1, plan["lanes"])
            mine = put_in_order(plan, place, points_map, mine)
            last = lax.all_gather(mine, "row", axis=0, tiled=True)
    slab, _ = lax.optimization_barrier((jnp.concatenate(slabs, 1), mine))
    slab = lax.all_to_all(slab, "row", split_axis=0, concat_axis=0, tiled=True).reshape(-1, plan["slab_lanes"])
    slab = jnp.broadcast_to(slab, (col_count, *slab.shape))
    early, slab = lax.optimization_barrier((early, slab))
    early = lax.all_to_all(early, "col", split_axis=0, concat_axis=0, tiled=True).reshape(-1, plan["lanes"])
    early, slab = lax.optimization_barrier((early, slab))
    slab = lax.all_to_all(slab, "col", split_axis=0, concat_axis=0, tiled=True)
    early = put_in_order(plan, place, points_map, early)
    return product(plan, place, points_map, slab, early, last)


def solution(mesh):
    in_specs = (P(), P(("row", "col"), None, None, None), P(), P(), P(("row", "col")), P())
    out_specs = P(None, "row", "col")
    return jax.shard_map(
        on_device, mesh=mesh, in_specs=in_specs, out_specs=out_specs, check_vma=False
    )
```

```python
import math

import jax
import jax.numpy as jnp
import numpy as np
from jax import lax
from jax.experimental import pallas as pl
from jax.experimental.pallas import tpu as pltpu
from jax.sharding import PartitionSpec as P

ROWS_DEV = 256
LANES = 128
VMEM_BYTES = 56 * 1024 * 1024
HALF = 64
KEEP = 40
ORIGIN = KEEP // 2
PARTS = 3


def round_up(value, step):
    return -(-value // step) * step


def length_counts(points):
    freq = np.arange(points) - points // 2
    square = freq * freq
    lengths = square[:, None, None] + square[None, :, None] + square[None, None, :]
    return np.cumsum(np.bincount(lengths.reshape(-1)))


def column_order(top):
    freq = np.arange(KEEP) - ORIGIN
    first, second = np.meshgrid(freq, freq, indexing="ij")
    length = (first * first + second * second).reshape(-1)
    order = np.argsort(length, kind="stable")
    order = order[length[order] <= top]
    return first.reshape(-1)[order], second.reshape(-1)[order], length[order]


class Columns:
    def __init__(self, top):
        self.windows = []
        offset = 0
        for begin in range(0, KEEP, 4):
            nearest = min(abs(index - ORIGIN) for index in range(begin, begin + 4))
            reach = math.isqrt(max(top - nearest * nearest, 0))
            low = (ORIGIN - reach) // 8 * 8
            high = min(round_up(ORIGIN + reach + 1, 8), KEEP)
            self.windows.append((low, high, offset))
            offset += 2 * (high - low)
        self.used = offset
        self.parity = round_up(offset, 2 * LANES)

    def place(self, index_2, index_3):
        low, high, offset = np.array(self.windows)[index_3 // 4].T
        return index_3 % 2 * self.parity + offset + index_3 // 2 % 2 * (high - low) + index_2 - low


class Bucket:
    def __init__(self, ranges, column_length):
        self.pieces = []
        self.edges = {}
        offset = 0
        for low, high in ranges:
            begin = offset
            for index in range(KEEP):
                freq = index - ORIGIN
                start = int(np.searchsorted(column_length, low - freq * freq, side="left"))
                stop = int(np.searchsorted(column_length, high - freq * freq, side="right"))
                if stop > start:
                    self.pieces.append((index, start, stop, offset))
                    offset += stop - start
            for length in range(low, high + 1):
                self.edges[length] = (begin, offset)
        self.size = offset

    def ids(self, column_2, column_3, points, width):
        out = np.full((width,), -1, np.int32)
        for index, start, stop, offset in self.pieces:
            k1 = (index - ORIGIN) % points
            k2 = column_2[start:stop] % points
            k3 = column_3[start:stop] % points
            out[offset : offset + stop - start] = (k1 * points + k2) * points + k3
        return out


def length_ranges(cumulative, first, step, count):
    shell = lambda rank: int(np.searchsorted(cumulative, rank, side="right"))
    ranges, low = [], shell(first)
    for part in range(1, count):
        before, after = shell(first + part * step - 1), shell(first + part * step)
        if before == after:
            if low < before:
                ranges.append((low, before - 1))
            if low <= before:
                ranges.append((before, before))
        elif low <= before:
            ranges.append((low, before))
        low = before + 1
    high = shell(first + count * step - 1)
    if low <= high:
        ranges.append((low, high))
    return ranges


def make_plan(points, total, blocks, slab, slab_blocks):
    cumulative = length_counts(points)
    shell = lambda rank: int(np.searchsorted(cumulative, rank, side="right"))
    width, slab_width = total // blocks, slab // slab_blocks
    step = width // PARTS
    column_2, column_3, column_length = column_order(shell(total - 1))
    buckets = [Bucket(length_ranges(cumulative, n * width, step, PARTS), column_length) for n in range(blocks)]
    slabs = [Bucket(length_ranges(cumulative, n * slab_width, slab_width, 1), column_length) for n in range(slab_blocks)]
    slab_top = shell(slab - 1)
    columns = Columns(shell(total - 1))
    place = columns.place(column_2 + ORIGIN, column_3 + ORIGIN)
    slab_columns = int(np.searchsorted(column_length, slab_top, side="right"))
    lanes = round_up(max(bucket.size for bucket in buckets), LANES)
    slab_lanes = round_up(max(bucket.size for bucket in slabs), LANES)
    windows = np.zeros((blocks, PARTS, 2), np.int64)
    for n, bucket in enumerate(buckets):
        for part in range(PARTS):
            rank = n * width + part * step
            windows[n, part, 0] = bucket.edges[shell(rank)][0] // LANES * LANES
            windows[n, part, 1] = round_up(bucket.edges[shell(rank + step - 1)][1], LANES)
    window = int((windows[..., 1] - windows[..., 0]).max())
    return dict(
        buckets=buckets,
        slabs=slabs,
        slab_columns=slab_columns,
        slab_tiles=sorted({int(value) for value in place[:slab_columns] // LANES}),
        columns=columns,
        lanes=lanes,
        slab_lanes=slab_lanes,
        window=window,
        starts=np.minimum(windows[..., 0], lanes - window).astype(np.int32),
        ids=np.stack([bucket.ids(column_2, column_3, points, lanes) for bucket in buckets]),
        slab_ids=np.stack([bucket.ids(column_2, column_3, points, slab_lanes) for bucket in slabs]),
        column_place=place.astype(np.int32),
    )


def dft_tables(points):
    n = np.arange(points)
    freq = np.arange(KEEP) - ORIGIN
    angle = (n[:, None] * freq[None, :] % points) * (2.0 * np.pi / points)
    cosine, sine = np.cos(angle), np.sin(angle)
    one = np.zeros((2, points, 2, HALF))
    one[0, :, 0, :KEEP] = cosine
    one[1, :, 0, :KEEP] = sine
    one[0, :, 1, :KEEP] = -sine
    one[1, :, 1, :KEEP] = cosine
    two = np.zeros((2, 2, points, 2, 2, HALF))
    for item in range(2):
        two[:, item, :, item] = one

    def parts(table):
        high = table.astype(jnp.bfloat16)
        return high, (table - high.astype(np.float64)).astype(jnp.bfloat16)

    high, low = parts(one[..., :KEEP].reshape(2 * points, 2 * KEEP).T)
    first = np.block([[high, high], [low, np.zeros_like(low)]])
    second = np.concatenate(parts(two.reshape(4 * points, 4 * HALF)), 0)
    halves = two[..., :KEEP].reshape(2, 2, points // 2, 2, 4 * KEEP).transpose(0, 1, 3, 2, 4)
    high, low = parts(halves.reshape(4 * points, 4 * KEEP).T)
    third = np.block([[high, high], [low, np.zeros_like(low)]])
    return [jnp.asarray(table) for table in (first, second, third)]


def split_parts(value):
    high = value.astype(jnp.bfloat16)
    low = (value - high.astype(jnp.float32)).astype(jnp.bfloat16)
    return high, low


def store_split(target, rows, blocks):
    for part, block in enumerate(blocks):
        high, low = split_parts(jnp.concatenate(block, 0))
        target[rows, part * LANES : (part + 1) * LANES] = high
        target[rows, (part + 2) * LANES : (part + 3) * LANES] = low


def doubled(stored):
    return jnp.concatenate([stored, stored[:, : stored.shape[1] // 2]], 1)


def contract_last(table, stored):
    both = lax.dot_general(table, stored, (((1,), (1,)), ((), ())), preferred_element_type=jnp.float32)
    rows = both.shape[0] // 2
    return both[:rows] + both[rows:]


def pack_pieces(pieces, width, source, rows, lane, out):
    for tile in range(width // LANES):
        left, right = tile * LANES, (tile + 1) * LANES
        value = jnp.zeros((rows, LANES), jnp.float32)
        for index, start, stop, offset in pieces:
            begin, end = max(left, offset), min(right, offset + stop - start)
            while begin < end:
                at = start + begin - offset
                block = source(index, at // LANES)
                shift = (begin - at) % LANES
                if shift:
                    block = pltpu.roll(block, shift, 1)
                value = block if begin == left else jnp.where(lane >= begin - left, block, value)
                begin = min(end, begin + LANES - at % LANES)
        out(tile, value)


def spectrum_kernel(plan, points, first_band, count, owner_ref, cond_energy_ref, val_energy_ref, val_ref, cond_ref, place_ref, first_ref,
                    second_ref, third_ref, send_ref, slab_ref, cond_a, cond_b, middle, turned, last, sorter, plain_rows, weighted_rows,
                    plain_sorted, weighted_sorted):
    band = pl.program_id(0)
    columns = plan["columns"]
    planes = 8
    pairs = planes // 2
    lane = lax.broadcasted_iota(jnp.int32, (1, LANES), 1)
    low_lanes = lane < HALF

    @pl.when(band == 0)
    def _():
        scale = 1.0 / float(points) ** 1.5
        sign = jnp.where(low_lanes, scale, -scale)

        @pl.loop(0, points // planes, unroll=4)
        def _(block):
            rows = pl.ds(pl.multiple_of(block * planes * points, planes * points), planes * points)
            wave = cond_ref[0, pl.ds(block * planes, planes)].reshape(planes * points, LANES).astype(jnp.float32)
            other = pltpu.roll(wave, HALF, 1)
            cond_a[rows, :] = jnp.where(low_lanes, wave, other) * sign
            cond_b[rows, :] = jnp.where(low_lanes, other, wave) * scale

        last[columns.used :, :] = jnp.zeros((columns.parity - columns.used, 4 * LANES), jnp.bfloat16)

    def first_axis(block):
        rows = pl.ds(pl.multiple_of(block * planes * points, planes * points), planes * points)
        wave = val_ref[0, pl.ds(block * planes, planes)].reshape(planes * points, LANES).astype(jnp.float32)
        density = wave * cond_a[rows, :] + pltpu.roll(wave, HALF, 1) * cond_b[rows, :]
        high, low = split_parts(density)
        field = contract_last(first_ref[...], jnp.concatenate([high, low], 1))
        for begin in range(0, pairs, 2):
            blocks = [
                [field[part * KEEP : (part + 1) * KEEP, pair * LANES : (pair + 1) * LANES] for pair in (begin, begin + 1)]
                for part in range(2)
            ]
            at = pl.ds(pl.multiple_of((block * pairs + begin) * KEEP, 2 * KEEP), 2 * KEEP)
            store_split(middle, at, blocks)

    def second_axis(turn):
        rows = pl.ds(pl.multiple_of(turn * 8 * KEEP, 8 * KEEP), 8 * KEEP)
        high = second_ref[: 2 * LANES]
        table = jnp.concatenate([high, high, second_ref[2 * LANES :]], 0)
        field = jnp.dot(doubled(middle[rows, :]), table, preferred_element_type=jnp.float32)
        for item in range(2):
            turned[item, rows, :] = field[:, item * LANES : (item + 1) * LANES]

    turns = points // 16 - 1
    piece = sorter.shape[0] // (count * turns)
    for part in range(2):
        first_axis(part)

    @pl.loop(1, turns + 1)
    def _(turn):
        begin = pl.multiple_of((band * turns + turn - 1) * piece, 16)
        at = lax.broadcasted_iota(jnp.int32, (piece, sorter.shape[1]), 0) + begin
        sorter[pl.ds(begin, piece), :] = jnp.where(at == place_ref[...], 1.0, 0.0).astype(jnp.bfloat16)
        second_axis(turn - 1)
        for part in range(2):
            first_axis(2 * turn + part)

    second_axis(turns)

    for begin, (low, high, offset) in zip(range(0, KEEP, 4), columns.windows):
        both = []
        for pair in range(2):
            items = [
                turned[item, pl.ds(begin + 2 * pair + k3, points // 2, stride=KEEP), :]
                for k3 in range(2)
                for item in range(2)
            ]
            turn = jnp.concatenate(items, 0).T
            both.append((turn[low:high], turn[HALF + low : HALF + high]))
        store_split(last, slice(offset, offset + 2 * (high - low)), list(zip(*both)))

    bands = val_energy_ref.shape[0] * cond_energy_ref.shape[0]
    gap = cond_energy_ref[owner_ref[0]] - val_energy_ref[first_band + band]
    weight = -2.0 / (math.sqrt(bands) * jnp.full((1, LANES), gap, jnp.float32))
    slab = plan["slab_tiles"]
    tiles = columns.parity // LANES
    field = contract_last(third_ref[...], last[...])
    band_rows = pl.ds(pl.multiple_of(band * 2 * KEEP, 2 * KEEP), 2 * KEEP)
    for odd in range(2):
        value = field[odd * 2 * KEEP : (odd + 1) * 2 * KEEP]
        plain_rows[band_rows, odd * columns.parity : (odd + 1) * columns.parity] = value.astype(jnp.bfloat16)
        for place, tile in enumerate(slab):
            if tile // tiles == odd:
                inside = value[:, tile % tiles * LANES : (tile % tiles + 1) * LANES]
                weighted_rows[band_rows, place * LANES : (place + 1) * LANES] = (weight * inside).astype(jnp.bfloat16)

    @pl.when(band == count - 1)
    def _():
        def sort_rows(rows, which, target):
            value = jnp.dot(rows, which, preferred_element_type=jnp.float32)
            for tile in range(target.shape[0]):
                target[tile] = value[:, tile * LANES : (tile + 1) * LANES]

        which = [sorter[tile * LANES : (tile + 1) * LANES, : weighted_sorted.shape[0] * LANES] for tile in slab]
        sort_rows(plain_rows[...], sorter[: 2 * columns.parity, :], plain_sorted)
        sort_rows(weighted_rows[...], jnp.concatenate(which, 0), weighted_sorted)

        def plain_at(index, tile):
            return plain_sorted[tile, pl.ds(index, 2 * count, stride=KEEP), :]

        def weighted_at(index, tile):
            return weighted_sorted[tile, pl.ds(index, 2 * count, stride=KEEP), :]

        for block, bucket in enumerate(plan["buckets"]):

            def keep(tile, value):
                send_ref[block, :, tile * LANES : (tile + 1) * LANES] = value.astype(jnp.bfloat16)

            pack_pieces(bucket.pieces, plan["lanes"], plain_at, 2 * count, lane, keep)
        for block, bucket in enumerate(plan["slabs"]):

            def keep_slab(tile, value):
                slab_ref[block, :, tile * LANES : (tile + 1) * LANES] = value.astype(jnp.bfloat16)

            pack_pieces(bucket.pieces, plan["slab_lanes"], weighted_at, 2 * count, lane, keep_slab)


def spectra(plan, val_wave, cond_wave, energies, first_band, count):
    points = val_wave.shape[1]
    turns = points // 16 - 1
    parity = plan["columns"].parity
    depth = round_up(-(-2 * parity // (count * turns)), 16) * count * turns
    columns = round_up(plan["column_place"].shape[0], 256)
    slab_columns = round_up(plan["slab_columns"], LANES)
    slab_depth = len(plan["slab_tiles"]) * LANES
    place = np.full((1, columns), -1, np.int32)
    place[0, : plan["column_place"].shape[0]] = plan["column_place"]
    grid_rows = points * points
    tables = dft_tables(points)
    send_shape = (len(plan["buckets"]), 2 * count, plan["lanes"])
    slab_shape = (len(plan["slabs"]), 2 * count, plan["slab_lanes"])
    kernel = lambda *refs: spectrum_kernel(plan, points, first_band, count, *refs)
    return pl.pallas_call(
        kernel,
        grid=(count,),
        in_specs=[
            pl.BlockSpec(memory_space=pltpu.SMEM),
            pl.BlockSpec(memory_space=pltpu.SMEM),
            pl.BlockSpec(memory_space=pltpu.SMEM),
            pl.BlockSpec((1, points, points, 2 * points), lambda v: (first_band + v, 0, 0, 0)),
            pl.BlockSpec((1, points, points, 2 * points), lambda v: (0, 0, 0, 0)),
            pl.BlockSpec((1, columns), lambda v: (0, 0)),
            *[pl.BlockSpec(table.shape, lambda v: (0, 0)) for table in tables],
        ],
        out_specs=[pl.BlockSpec(send_shape, lambda v: (0, 0, 0)), pl.BlockSpec(slab_shape, lambda v: (0, 0, 0))],
        out_shape=[jax.ShapeDtypeStruct(send_shape, jnp.bfloat16), jax.ShapeDtypeStruct(slab_shape, jnp.bfloat16)],
        scratch_shapes=[
            pltpu.VMEM((grid_rows, LANES), jnp.float32),
            pltpu.VMEM((grid_rows, LANES), jnp.float32),
            pltpu.VMEM((points // 2 * KEEP, 4 * LANES), jnp.bfloat16),
            pltpu.VMEM((2, points // 2 * KEEP, LANES), jnp.float32),
            pltpu.VMEM((parity, 4 * LANES), jnp.bfloat16),
            pltpu.VMEM((depth, columns), jnp.bfloat16),
            pltpu.VMEM((2 * count * KEEP, 2 * parity), jnp.bfloat16),
            pltpu.VMEM((2 * count * KEEP, slab_depth), jnp.bfloat16),
            pltpu.VMEM((columns // LANES, 2 * count * KEEP, LANES), jnp.float32),
            pltpu.VMEM((slab_columns // LANES, 2 * count * KEEP, LANES), jnp.float32),
        ],
        compiler_params=pltpu.CompilerParams(vmem_limit_bytes=VMEM_BYTES, dimension_semantics=("arbitrary",)),
        cost_estimate=pl.CostEstimate(flops=1, bytes_accessed=1, transcendentals=0),
        name="spectra",
    )(*energies, val_wave, cond_wave, jnp.asarray(place), *tables)


def one_hot(ids, wanted):
    ids = jnp.broadcast_to(ids, (LANES, LANES)).T
    ids = jnp.concatenate([ids] * (wanted.shape[1] // LANES), 1)
    return jnp.where(ids == wanted, 1.0, 0.0).astype(jnp.bfloat16)


def make_left(row_count, slab_ref, ids_ref, wanted_ref, left):
    rows = wanted_ref.shape[1]
    col_count = slab_ref.shape[0]
    group = slab_ref.shape[1] // (2 * row_count)
    order = [(col, 2 * row) for col in range(col_count) for row in range(row_count)]
    order += [(col, 2 * row + 1) for row in range(row_count) for col in range(col_count)]
    slab = [slab_ref[col, at * group : (at + 1) * group, :].astype(jnp.float32) for col, at in order]
    wanted = [
        jnp.broadcast_to(wanted_ref[:, begin : begin + LANES], (LANES, LANES)).T for begin in range(0, rows, LANES)
    ]
    wanted = jnp.concatenate([jnp.concatenate(wanted, 0)] * (ids_ref.shape[2] // LANES), 1)
    choice = jnp.where(wanted == ids_ref[0], 1.0, 0.0).astype(jnp.bfloat16)
    chosen = lax.dot_general(
        choice,
        jnp.concatenate(slab, 0).astype(jnp.bfloat16),
        (((1,), (1,)), ((), ())),
        preferred_element_type=jnp.float32,
    )
    lane = lax.broadcasted_iota(jnp.int32, (1, LANES), 1)
    real_lanes = lane % 2 == 0
    for begin in range(0, chosen.shape[1], LANES):
        part = chosen[:, begin : begin + LANES]
        after = pltpu.roll(part, LANES - 1, 1)
        before = pltpu.roll(part, 1, 1)
        left[:rows, begin : begin + LANES] = part.astype(jnp.bfloat16)
        left[rows:, begin : begin + LANES] = jnp.where(real_lanes, after, -before).astype(jnp.bfloat16)


def order_kernel(place_ref, starts_ref, ids_ref, wanted_ref, panel_ref, out_ref, hot):
    start = pl.multiple_of(starts_ref[place_ref[0] * PARTS + pl.program_id(0)], LANES)
    wanted = wanted_ref[...]
    window = hot.shape[0]
    for begin in range(0, window, LANES):
        ids = ids_ref[0, :, pl.ds(pl.multiple_of(start + begin, LANES), LANES)]
        hot[begin : begin + LANES, :] = one_hot(ids, wanted)
    ordered = jnp.dot(panel_ref[:, pl.ds(start, window)], hot[...], preferred_element_type=jnp.float32)
    out_ref[...] = ordered.astype(jnp.bfloat16)


def put_in_order(plan, place, points_map, panel):
    columns = points_map.shape[1] // len(plan["buckets"])
    block = columns // PARTS
    ids = jnp.asarray(plan["ids"])[:, None]
    return pl.pallas_call(
        order_kernel,
        grid_spec=pltpu.PrefetchScalarGridSpec(
            num_scalar_prefetch=2,
            grid=(PARTS,),
            in_specs=[
                pl.BlockSpec((1, *ids.shape[1:]), lambda n, place, starts: (place[0], 0, 0)),
                pl.BlockSpec((1, block), lambda n, place, starts: (0, place[0] * PARTS + n)),
                pl.BlockSpec(panel.shape, lambda n, place, starts: (0, 0)),
            ],
            out_specs=pl.BlockSpec((panel.shape[0], block), lambda n, place, starts: (0, n)),
            scratch_shapes=[pltpu.VMEM((plan["window"], block), jnp.bfloat16)],
        ),
        out_shape=jax.ShapeDtypeStruct((panel.shape[0], columns), jnp.bfloat16),
        compiler_params=pltpu.CompilerParams(vmem_limit_bytes=VMEM_BYTES, dimension_semantics=("arbitrary",)),
        cost_estimate=pl.CostEstimate(flops=1, bytes_accessed=1, transcendentals=0),
        name="in_order",
    )(place, jnp.asarray(plan["starts"].reshape(-1)), ids, points_map, panel)


def product_kernel(row_count, place_ref, slab_ref, ids_ref, wanted_ref, early_ref, last_ref, out_ref, left):
    rows = out_ref.shape[1]

    @pl.when(pl.program_id(0) == 0)
    def _():
        make_left(row_count, slab_ref, ids_ref, wanted_ref, left)

    right = jnp.concatenate([early_ref[...], last_ref[...]], 0)
    chi = jnp.dot(left[...], right, preferred_element_type=jnp.float32)
    out_ref[0] = chi[:rows]
    out_ref[1] = chi[rows:]


def product(plan, place, points_map, slab, early, last):
    pairs, columns = slab.shape[0] * slab.shape[1], early.shape[1]
    block = 6 * LANES
    ids = jnp.asarray(plan["slab_ids"])[:, None]
    return pl.pallas_call(
        lambda *refs: product_kernel(ids.shape[0], *refs),
        grid_spec=pltpu.PrefetchScalarGridSpec(
            num_scalar_prefetch=1,
            grid=(pl.cdiv(columns, block),),
            in_specs=[
                pl.BlockSpec(slab.shape, lambda n, place: (0, 0, 0)),
                pl.BlockSpec((1, *ids.shape[1:]), lambda n, place: (place[1], 0, 0)),
                pl.BlockSpec((1, ROWS_DEV), lambda n, place: (0, place[1])),
                pl.BlockSpec((early.shape[0], block), lambda n, place: (0, n)),
                pl.BlockSpec((last.shape[0], block), lambda n, place: (0, n)),
            ],
            out_specs=pl.BlockSpec((2, ROWS_DEV, block), lambda n, place: (0, 0, n)),
            scratch_shapes=[pltpu.VMEM((2 * ROWS_DEV, pairs), jnp.bfloat16)],
        ),
        out_shape=jax.ShapeDtypeStruct((2, ROWS_DEV, columns), jnp.float32),
        compiler_params=pltpu.CompilerParams(vmem_limit_bytes=VMEM_BYTES, dimension_semantics=("arbitrary",)),
        cost_estimate=pl.CostEstimate(flops=1, bytes_accessed=1, transcendentals=0),
        name="product",
    )(place, slab, ids, points_map, early, last)


def on_device(val_wave, cond_wave, val_energy, cond_energy, band_owner, grid_map):
    bands, points = val_wave.shape[0], val_wave.shape[1]
    row_count = lax.axis_size("row")
    col_count = lax.axis_size("col")
    col, row = lax.axis_index("col"), lax.axis_index("row")
    plan = make_plan(points, grid_map.shape[0], col_count, ROWS_DEV * row_count, row_count)
    place = jnp.stack([col, row]).astype(jnp.int32)
    points_map = grid_map[None]
    chunk = bands // 2
    energies = (band_owner, cond_energy, val_energy)
    slabs = []
    for part in range(2):
        send, slab = spectra(plan, val_wave, cond_wave, energies, part * chunk, chunk)
        slabs.append(slab)
        if part == 0:
            send, cond_wave = lax.optimization_barrier((send, cond_wave))
            early = lax.all_gather(send, "row", axis=1)
        else:
            mine = lax.all_to_all(send, "col", split_axis=0, concat_axis=0, tiled=True).reshape(-1, plan["lanes"])
            mine = put_in_order(plan, place, points_map, mine)
            last = lax.all_gather(mine, "row", axis=0, tiled=True)
    slab, _ = lax.optimization_barrier((jnp.concatenate(slabs, 1), mine))
    slab = lax.all_to_all(slab, "row", split_axis=0, concat_axis=0, tiled=True).reshape(-1, plan["slab_lanes"])
    slab = jnp.broadcast_to(slab, (col_count, *slab.shape))
    early, slab = lax.optimization_barrier((early, slab))
    early = lax.all_to_all(early, "col", split_axis=0, concat_axis=0, tiled=True).reshape(-1, plan["lanes"])
    early, slab = lax.optimization_barrier((early, slab))
    slab = lax.all_to_all(slab, "col", split_axis=0, concat_axis=0, tiled=True)
    early = put_in_order(plan, place, points_map, early)
    return product(plan, place, points_map, slab, early, last)


def solution(mesh):
    in_specs = (P(), P(("row", "col"), None, None, None), P(), P(), P(("row", "col")), P())
    out_specs = P(None, "row", "col")
    return jax.shard_map(
        on_device, mesh=mesh, in_specs=in_specs, out_specs=out_specs, check_vma=False
    )
```

```python
import math

import jax
import jax.numpy as jnp
import numpy as np
from jax import lax
from jax.experimental import pallas as pl
from jax.experimental.pallas import tpu as pltpu
from jax.sharding import PartitionSpec as P

ROWS_DEV = 256
LANES = 128
VMEM_BYTES = 56 * 1024 * 1024
HALF = 64
KEEP = 40
ORIGIN = KEEP // 2
PARTS = 3


def round_up(value, step):
    return -(-value // step) * step


def length_counts(points):
    freq = np.arange(points) - points // 2
    square = freq * freq
    lengths = square[:, None, None] + square[None, :, None] + square[None, None, :]
    return np.cumsum(np.bincount(lengths.reshape(-1)))


def column_order(top):
    freq = np.arange(KEEP) - ORIGIN
    first, second = np.meshgrid(freq, freq, indexing="ij")
    length = (first * first + second * second).reshape(-1)
    order = np.argsort(length, kind="stable")
    order = order[length[order] <= top]
    return first.reshape(-1)[order], second.reshape(-1)[order], length[order]


class Columns:
    def __init__(self, top):
        self.windows = []
        offset = 0
        for begin in range(0, KEEP, 4):
            nearest = min(abs(index - ORIGIN) for index in range(begin, begin + 4))
            reach = math.isqrt(max(top - nearest * nearest, 0))
            low = (ORIGIN - reach) // 8 * 8
            high = min(round_up(ORIGIN + reach + 1, 8), KEEP)
            self.windows.append((low, high, offset))
            offset += 2 * (high - low)
        self.used = offset
        self.parity = round_up(offset, 2 * LANES)

    def place(self, index_2, index_3):
        low, high, offset = np.array(self.windows)[index_3 // 4].T
        return index_3 % 2 * self.parity + offset + index_3 // 2 % 2 * (high - low) + index_2 - low


class Bucket:
    def __init__(self, ranges, column_length):
        self.pieces = []
        self.edges = {}
        offset = 0
        for low, high in ranges:
            begin = offset
            for index in range(KEEP):
                freq = index - ORIGIN
                start = int(np.searchsorted(column_length, low - freq * freq, side="left"))
                stop = int(np.searchsorted(column_length, high - freq * freq, side="right"))
                if stop > start:
                    self.pieces.append((index, start, stop, offset))
                    offset += stop - start
            for length in range(low, high + 1):
                self.edges[length] = (begin, offset)
        self.size = offset

    def ids(self, column_2, column_3, points, width):
        out = np.full((width,), -1, np.int32)
        for index, start, stop, offset in self.pieces:
            k1 = (index - ORIGIN) % points
            k2 = column_2[start:stop] % points
            k3 = column_3[start:stop] % points
            out[offset : offset + stop - start] = (k1 * points + k2) * points + k3
        return out


def length_ranges(cumulative, first, step, count):
    shell = lambda rank: int(np.searchsorted(cumulative, rank, side="right"))
    ranges, low = [], shell(first)
    for part in range(1, count):
        before, after = shell(first + part * step - 1), shell(first + part * step)
        if before == after:
            if low < before:
                ranges.append((low, before - 1))
            if low <= before:
                ranges.append((before, before))
        elif low <= before:
            ranges.append((low, before))
        low = before + 1
    high = shell(first + count * step - 1)
    if low <= high:
        ranges.append((low, high))
    return ranges


def make_plan(points, total, blocks, slab, slab_blocks):
    cumulative = length_counts(points)
    shell = lambda rank: int(np.searchsorted(cumulative, rank, side="right"))
    width, slab_width = total // blocks, slab // slab_blocks
    step = width // PARTS
    column_2, column_3, column_length = column_order(shell(total - 1))
    buckets = [Bucket(length_ranges(cumulative, n * width, step, PARTS), column_length) for n in range(blocks)]
    slabs = [Bucket(length_ranges(cumulative, n * slab_width, slab_width, 1), column_length) for n in range(slab_blocks)]
    slab_top = shell(slab - 1)
    columns = Columns(shell(total - 1))
    place = columns.place(column_2 + ORIGIN, column_3 + ORIGIN)
    slab_columns = int(np.searchsorted(column_length, slab_top, side="right"))
    lanes = round_up(max(bucket.size for bucket in buckets), LANES)
    slab_lanes = round_up(max(bucket.size for bucket in slabs), LANES)
    windows = np.zeros((blocks, PARTS, 2), np.int64)
    for n, bucket in enumerate(buckets):
        for part in range(PARTS):
            rank = n * width + part * step
            windows[n, part, 0] = bucket.edges[shell(rank)][0] // LANES * LANES
            windows[n, part, 1] = round_up(bucket.edges[shell(rank + step - 1)][1], LANES)
    window = int((windows[..., 1] - windows[..., 0]).max())
    return dict(
        buckets=buckets,
        slabs=slabs,
        slab_columns=slab_columns,
        slab_tiles=sorted({int(value) for value in place[:slab_columns] // LANES}),
        columns=columns,
        lanes=lanes,
        slab_lanes=slab_lanes,
        window=window,
        starts=np.minimum(windows[..., 0], lanes - window).astype(np.int32),
        ids=np.stack([bucket.ids(column_2, column_3, points, lanes) for bucket in buckets]),
        slab_ids=np.stack([bucket.ids(column_2, column_3, points, slab_lanes) for bucket in slabs]),
        column_place=place.astype(np.int32),
    )


def dft_tables(points):
    n = np.arange(points)
    freq = np.arange(KEEP) - ORIGIN
    angle = (n[:, None] * freq[None, :] % points) * (2.0 * np.pi / points)
    cosine, sine = np.cos(angle), np.sin(angle)
    one = np.zeros((2, points, 2, HALF))
    one[0, :, 0, :KEEP] = cosine
    one[1, :, 0, :KEEP] = sine
    one[0, :, 1, :KEEP] = -sine
    one[1, :, 1, :KEEP] = cosine
    two = np.zeros((2, 2, points, 2, 2, HALF))
    for item in range(2):
        two[:, item, :, item] = one

    def parts(table):
        high = table.astype(jnp.bfloat16)
        return high, (table - high.astype(np.float64)).astype(jnp.bfloat16)

    high, low = parts(one[..., :KEEP].reshape(2 * points, 2 * KEEP).T)
    first = np.block([[high, high], [low, np.zeros_like(low)]])
    second = np.concatenate(parts(two.reshape(4 * points, 4 * HALF)), 0)
    halves = two[..., :KEEP].reshape(2, 2, points // 2, 2, 4 * KEEP).transpose(0, 1, 3, 2, 4)
    high, low = parts(halves.reshape(4 * points, 4 * KEEP).T)
    third = np.block([[high, high], [low, np.zeros_like(low)]])
    return [jnp.asarray(table) for table in (first, second, third)]


def split_parts(value):
    high = value.astype(jnp.bfloat16)
    low = (value - high.astype(jnp.float32)).astype(jnp.bfloat16)
    return high, low


def store_split(target, rows, blocks):
    for part, block in enumerate(blocks):
        high, low = split_parts(jnp.concatenate(block, 0))
        target[rows, part * LANES : (part + 1) * LANES] = high
        target[rows, (part + 2) * LANES : (part + 3) * LANES] = low


def doubled(stored):
    return jnp.concatenate([stored, stored[:, : stored.shape[1] // 2]], 1)


def contract_last(table, stored):
    both = lax.dot_general(table, stored, (((1,), (1,)), ((), ())), preferred_element_type=jnp.float32)
    rows = both.shape[0] // 2
    return both[:rows] + both[rows:]


def pack_pieces(pieces, width, source, rows, lane, out):
    for tile in range(width // LANES):
        left, right = tile * LANES, (tile + 1) * LANES
        value = jnp.zeros((rows, LANES), jnp.float32)
        for index, start, stop, offset in pieces:
            begin, end = max(left, offset), min(right, offset + stop - start)
            while begin < end:
                at = start + begin - offset
                block = source(index, at // LANES)
                shift = (begin - at) % LANES
                if shift:
                    block = pltpu.roll(block, shift, 1)
                value = block if begin == left else jnp.where(lane >= begin - left, block, value)
                begin = min(end, begin + LANES - at % LANES)
        out(tile, value)


def spectrum_kernel(plan, points, first_band, count, owner_ref, cond_energy_ref, val_energy_ref, val_ref, cond_ref, place_ref, first_ref,
                    second_ref, third_ref, send_ref, slab_ref, cond_a, cond_b, middle, turned, last, sorter, plain_rows, weighted_rows,
                    plain_sorted, weighted_sorted):
    band = pl.program_id(0)
    columns = plan["columns"]
    planes = 8
    pairs = planes // 2
    lane = lax.broadcasted_iota(jnp.int32, (1, LANES), 1)
    low_lanes = lane < HALF

    @pl.when(band == 0)
    def _():
        scale = 1.0 / float(points) ** 1.5
        sign = jnp.where(low_lanes, scale, -scale)

        @pl.loop(0, points // planes, unroll=4)
        def _(block):
            rows = pl.ds(pl.multiple_of(block * planes * points, planes * points), planes * points)
            wave = cond_ref[0, pl.ds(block * planes, planes)].reshape(planes * points, LANES).astype(jnp.float32)
            other = pltpu.roll(wave, HALF, 1)
            cond_a[rows, :] = jnp.where(low_lanes, wave, other) * sign
            cond_b[rows, :] = jnp.where(low_lanes, other, wave) * scale

        last[columns.used :, :] = jnp.zeros((columns.parity - columns.used, 4 * LANES), jnp.bfloat16)

    def first_axis(block):
        rows = pl.ds(pl.multiple_of(block * planes * points, planes * points), planes * points)
        wave = val_ref[0, pl.ds(block * planes, planes)].reshape(planes * points, LANES).astype(jnp.float32)
        density = wave * cond_a[rows, :] + pltpu.roll(wave, HALF, 1) * cond_b[rows, :]
        high, low = split_parts(density)
        field = contract_last(first_ref[...], jnp.concatenate([high, low], 1))
        for begin in range(0, pairs, 2):
            blocks = [
                [field[part * KEEP : (part + 1) * KEEP, pair * LANES : (pair + 1) * LANES] for pair in (begin, begin + 1)]
                for part in range(2)
            ]
            at = pl.ds(pl.multiple_of((block * pairs + begin) * KEEP, 2 * KEEP), 2 * KEEP)
            store_split(middle, at, blocks)

    def second_axis(block):
        rows = pl.ds(pl.multiple_of(block * 4 * KEEP, 4 * KEEP), 4 * KEEP)
        high = second_ref[: 2 * LANES]
        table = jnp.concatenate([high, high, second_ref[2 * LANES :]], 0)
        field = jnp.dot(doubled(middle[rows, :]), table, preferred_element_type=jnp.float32)
        for item in range(2):
            turned[item, rows, :] = field[:, item * LANES : (item + 1) * LANES]

    turns = points // 16 - 1
    piece = sorter.shape[0] // (count * turns)
    for part in range(2):
        first_axis(part)

    @pl.loop(1, turns + 1)
    def _(turn):
        begin = pl.multiple_of((band * turns + turn - 1) * piece, 16)
        at = lax.broadcasted_iota(jnp.int32, (piece, sorter.shape[1]), 0) + begin
        sorter[pl.ds(begin, piece), :] = jnp.where(at == place_ref[...], 1.0, 0.0).astype(jnp.bfloat16)
        for part in range(2):
            second_axis(2 * turn - 2 + part)
        for part in range(2):
            first_axis(2 * turn + part)

    for part in range(2):
        second_axis(2 * turns + part)

    for begin, (low, high, offset) in zip(range(0, KEEP, 4), columns.windows):
        both = []
        for pair in range(2):
            items = [
                turned[item, pl.ds(begin + 2 * pair + k3, points // 2, stride=KEEP), :]
                for k3 in range(2)
                for item in range(2)
            ]
            turn = jnp.concatenate(items, 0).T
            both.append((turn[low:high], turn[HALF + low : HALF + high]))
        store_split(last, slice(offset, offset + 2 * (high - low)), list(zip(*both)))

    bands = val_energy_ref.shape[0] * cond_energy_ref.shape[0]
    gap = cond_energy_ref[owner_ref[0]] - val_energy_ref[first_band + band]
    weight = -2.0 / (math.sqrt(bands) * jnp.full((1, LANES), gap, jnp.float32))
    slab = plan["slab_tiles"]
    band_rows = pl.ds(pl.multiple_of(band * 2 * KEEP, 2 * KEEP), 2 * KEEP)
    for begin in range(0, columns.parity, 2 * LANES):
        field = contract_last(third_ref[...], last[begin : begin + 2 * LANES, :])
        for odd in range(2):
            value = field[odd * 2 * KEEP : (odd + 1) * 2 * KEEP]
            first = odd * columns.parity + begin
            plain_rows[band_rows, first : first + 2 * LANES] = value.astype(jnp.bfloat16)
            for place, tile in enumerate(slab):
                at = tile * LANES - first
                if 0 <= at < 2 * LANES:
                    inside = (weight * value[:, at : at + LANES]).astype(jnp.bfloat16)
                    weighted_rows[band_rows, place * LANES : (place + 1) * LANES] = inside

    @pl.when(band == count - 1)
    def _():
        def sort_rows(rows, which, target):
            for tile in range(0, target.shape[0], 2):
                lanes = slice(tile * LANES, (tile + 2) * LANES)
                value = jnp.dot(rows, which(lanes), preferred_element_type=jnp.float32)
                target[tile] = value[:, :LANES]
                target[tile + 1] = value[:, LANES:]

        def slab_places(lanes):
            return jnp.concatenate([sorter[tile * LANES : (tile + 1) * LANES, lanes] for tile in slab], 0)

        sort_rows(plain_rows[...], lambda lanes: sorter[: 2 * columns.parity, lanes], plain_sorted)
        sort_rows(weighted_rows[...], slab_places, weighted_sorted)

        def plain_at(index, tile):
            return plain_sorted[tile, pl.ds(index, 2 * count, stride=KEEP), :]

        def weighted_at(index, tile):
            return weighted_sorted[tile, pl.ds(index, 2 * count, stride=KEEP), :]

        for block, bucket in enumerate(plan["buckets"]):

            def keep(tile, value):
                send_ref[block, :, tile * LANES : (tile + 1) * LANES] = value.astype(jnp.bfloat16)

            pack_pieces(bucket.pieces, plan["lanes"], plain_at, 2 * count, lane, keep)
        for block, bucket in enumerate(plan["slabs"]):

            def keep_slab(tile, value):
                slab_ref[block, :, tile * LANES : (tile + 1) * LANES] = value.astype(jnp.bfloat16)

            pack_pieces(bucket.pieces, plan["slab_lanes"], weighted_at, 2 * count, lane, keep_slab)


def spectra(plan, val_wave, cond_wave, energies, first_band, count):
    points = val_wave.shape[1]
    turns = points // 16 - 1
    parity = plan["columns"].parity
    depth = round_up(-(-2 * parity // (count * turns)), 16) * count * turns
    columns = round_up(plan["column_place"].shape[0], 256)
    slab_columns = round_up(plan["slab_columns"], 2 * LANES)
    slab_depth = len(plan["slab_tiles"]) * LANES
    place = np.full((1, columns), -1, np.int32)
    place[0, : plan["column_place"].shape[0]] = plan["column_place"]
    grid_rows = points * points
    tables = dft_tables(points)
    send_shape = (len(plan["buckets"]), 2 * count, plan["lanes"])
    slab_shape = (len(plan["slabs"]), 2 * count, plan["slab_lanes"])
    kernel = lambda *refs: spectrum_kernel(plan, points, first_band, count, *refs)
    return pl.pallas_call(
        kernel,
        grid=(count,),
        in_specs=[
            pl.BlockSpec(memory_space=pltpu.SMEM),
            pl.BlockSpec(memory_space=pltpu.SMEM),
            pl.BlockSpec(memory_space=pltpu.SMEM),
            pl.BlockSpec((1, points, points, 2 * points), lambda v: (first_band + v, 0, 0, 0)),
            pl.BlockSpec((1, points, points, 2 * points), lambda v: (0, 0, 0, 0)),
            pl.BlockSpec((1, columns), lambda v: (0, 0)),
            *[pl.BlockSpec(table.shape, lambda v: (0, 0)) for table in tables],
        ],
        out_specs=[pl.BlockSpec(send_shape, lambda v: (0, 0, 0)), pl.BlockSpec(slab_shape, lambda v: (0, 0, 0))],
        out_shape=[jax.ShapeDtypeStruct(send_shape, jnp.bfloat16), jax.ShapeDtypeStruct(slab_shape, jnp.bfloat16)],
        scratch_shapes=[
            pltpu.VMEM((grid_rows, LANES), jnp.float32),
            pltpu.VMEM((grid_rows, LANES), jnp.float32),
            pltpu.VMEM((points // 2 * KEEP, 4 * LANES), jnp.bfloat16),
            pltpu.VMEM((2, points // 2 * KEEP, LANES), jnp.float32),
            pltpu.VMEM((parity, 4 * LANES), jnp.bfloat16),
            pltpu.VMEM((depth, columns), jnp.bfloat16),
            pltpu.VMEM((2 * count * KEEP, 2 * parity), jnp.bfloat16),
            pltpu.VMEM((2 * count * KEEP, slab_depth), jnp.bfloat16),
            pltpu.VMEM((columns // LANES, 2 * count * KEEP, LANES), jnp.float32),
            pltpu.VMEM((slab_columns // LANES, 2 * count * KEEP, LANES), jnp.float32),
        ],
        compiler_params=pltpu.CompilerParams(vmem_limit_bytes=VMEM_BYTES, dimension_semantics=("arbitrary",)),
        cost_estimate=pl.CostEstimate(flops=1, bytes_accessed=1, transcendentals=0),
        name="spectra",
    )(*energies, val_wave, cond_wave, jnp.asarray(place), *tables)


def one_hot(ids, wanted):
    ids = jnp.broadcast_to(ids, (LANES, LANES)).T
    ids = jnp.concatenate([ids] * (wanted.shape[1] // LANES), 1)
    return jnp.where(ids == wanted, 1.0, 0.0).astype(jnp.bfloat16)


def make_left(row_count, slab_ref, ids_ref, wanted_ref, left):
    rows = wanted_ref.shape[1]
    col_count = slab_ref.shape[0]
    group = slab_ref.shape[1] // (2 * row_count)
    order = [(col, 2 * row) for col in range(col_count) for row in range(row_count)]
    order += [(col, 2 * row + 1) for row in range(row_count) for col in range(col_count)]
    slab = [slab_ref[col, at * group : (at + 1) * group, :].astype(jnp.float32) for col, at in order]
    wanted = [
        jnp.broadcast_to(wanted_ref[:, begin : begin + LANES], (LANES, LANES)).T for begin in range(0, rows, LANES)
    ]
    wanted = jnp.concatenate([jnp.concatenate(wanted, 0)] * (ids_ref.shape[2] // LANES), 1)
    choice = jnp.where(wanted == ids_ref[0], 1.0, 0.0).astype(jnp.bfloat16)
    chosen = lax.dot_general(
        choice,
        jnp.concatenate(slab, 0).astype(jnp.bfloat16),
        (((1,), (1,)), ((), ())),
        preferred_element_type=jnp.float32,
    )
    lane = lax.broadcasted_iota(jnp.int32, (1, LANES), 1)
    real_lanes = lane % 2 == 0
    for begin in range(0, chosen.shape[1], LANES):
        part = chosen[:, begin : begin + LANES]
        after = pltpu.roll(part, LANES - 1, 1)
        before = pltpu.roll(part, 1, 1)
        left[:rows, begin : begin + LANES] = part.astype(jnp.bfloat16)
        left[rows:, begin : begin + LANES] = jnp.where(real_lanes, after, -before).astype(jnp.bfloat16)


def order_kernel(place_ref, starts_ref, ids_ref, wanted_ref, panel_ref, out_ref, hot):
    start = pl.multiple_of(starts_ref[place_ref[0] * PARTS + pl.program_id(0)], LANES)
    window = hot.shape[0]
    for column in range(0, hot.shape[1], 2 * LANES):
        lanes = slice(column, min(column + 2 * LANES, hot.shape[1]))
        for begin in range(0, window, LANES):
            ids = ids_ref[0, :, pl.ds(pl.multiple_of(start + begin, LANES), LANES)]
            hot[begin : begin + LANES, lanes] = one_hot(ids, wanted_ref[:, lanes])
        ordered = jnp.dot(panel_ref[:, pl.ds(start, window)], hot[:, lanes], preferred_element_type=jnp.float32)
        out_ref[:, lanes] = ordered.astype(jnp.bfloat16)


def put_in_order(plan, place, points_map, panel):
    columns = points_map.shape[1] // len(plan["buckets"])
    block = columns // PARTS
    ids = jnp.asarray(plan["ids"])[:, None]
    return pl.pallas_call(
        order_kernel,
        grid_spec=pltpu.PrefetchScalarGridSpec(
            num_scalar_prefetch=2,
            grid=(PARTS,),
            in_specs=[
                pl.BlockSpec((1, *ids.shape[1:]), lambda n, place, starts: (place[0], 0, 0)),
                pl.BlockSpec((1, block), lambda n, place, starts: (0, place[0] * PARTS + n)),
                pl.BlockSpec(panel.shape, lambda n, place, starts: (0, 0)),
            ],
            out_specs=pl.BlockSpec((panel.shape[0], block), lambda n, place, starts: (0, n)),
            scratch_shapes=[pltpu.VMEM((plan["window"], block), jnp.bfloat16)],
        ),
        out_shape=jax.ShapeDtypeStruct((panel.shape[0], columns), jnp.bfloat16),
        compiler_params=pltpu.CompilerParams(vmem_limit_bytes=VMEM_BYTES, dimension_semantics=("arbitrary",)),
        cost_estimate=pl.CostEstimate(flops=1, bytes_accessed=1, transcendentals=0),
        name="in_order",
    )(place, jnp.asarray(plan["starts"].reshape(-1)), ids, points_map, panel)


def product_kernel(row_count, place_ref, slab_ref, ids_ref, wanted_ref, early_ref, last_ref, out_ref, left):
    rows = out_ref.shape[1]

    @pl.when(pl.program_id(0) == 0)
    def _():
        make_left(row_count, slab_ref, ids_ref, wanted_ref, left)

    for begin in range(0, out_ref.shape[2], 2 * LANES):
        lanes = slice(begin, begin + 2 * LANES)
        right = jnp.concatenate([early_ref[:, lanes], last_ref[:, lanes]], 0)
        for part in range(2):
            half = left[part * rows : (part + 1) * rows, :]
            out_ref[part, :, lanes] = jnp.dot(half, right, preferred_element_type=jnp.float32)


def product(plan, place, points_map, slab, early, last):
    pairs, columns = slab.shape[0] * slab.shape[1], early.shape[1]
    block = 6 * LANES
    ids = jnp.asarray(plan["slab_ids"])[:, None]
    return pl.pallas_call(
        lambda *refs: product_kernel(ids.shape[0], *refs),
        grid_spec=pltpu.PrefetchScalarGridSpec(
            num_scalar_prefetch=1,
            grid=(pl.cdiv(columns, block),),
            in_specs=[
                pl.BlockSpec(slab.shape, lambda n, place: (0, 0, 0)),
                pl.BlockSpec((1, *ids.shape[1:]), lambda n, place: (place[1], 0, 0)),
                pl.BlockSpec((1, ROWS_DEV), lambda n, place: (0, place[1])),
                pl.BlockSpec((early.shape[0], block), lambda n, place: (0, n)),
                pl.BlockSpec((last.shape[0], block), lambda n, place: (0, n)),
            ],
            out_specs=pl.BlockSpec((2, ROWS_DEV, block), lambda n, place: (0, 0, n)),
            scratch_shapes=[pltpu.VMEM((2 * ROWS_DEV, pairs), jnp.bfloat16)],
        ),
        out_shape=jax.ShapeDtypeStruct((2, ROWS_DEV, columns), jnp.float32),
        compiler_params=pltpu.CompilerParams(vmem_limit_bytes=VMEM_BYTES, dimension_semantics=("arbitrary",)),
        cost_estimate=pl.CostEstimate(flops=1, bytes_accessed=1, transcendentals=0),
        name="product",
    )(place, slab, ids, points_map, early, last)


def on_device(val_wave, cond_wave, val_energy, cond_energy, band_owner, grid_map):
    bands, points = val_wave.shape[0], val_wave.shape[1]
    row_count = lax.axis_size("row")
    col_count = lax.axis_size("col")
    col, row = lax.axis_index("col"), lax.axis_index("row")
    plan = make_plan(points, grid_map.shape[0], col_count, ROWS_DEV * row_count, row_count)
    place = jnp.stack([col, row]).astype(jnp.int32)
    points_map = grid_map[None]
    chunk = bands // 2
    energies = (band_owner, cond_energy, val_energy)
    slabs = []
    for part in range(2):
        send, slab = spectra(plan, val_wave, cond_wave, energies, part * chunk, chunk)
        slabs.append(slab)
        if part == 0:
            send, cond_wave = lax.optimization_barrier((send, cond_wave))
            early = lax.all_gather(send, "row", axis=1)
        else:
            mine = lax.all_to_all(send, "col", split_axis=0, concat_axis=0, tiled=True).reshape(-1, plan["lanes"])
            mine = put_in_order(plan, place, points_map, mine)
            last = lax.all_gather(mine, "row", axis=0, tiled=True)
    slab, _ = lax.optimization_barrier((jnp.concatenate(slabs, 1), mine))
    slab = lax.all_to_all(slab, "row", split_axis=0, concat_axis=0, tiled=True).reshape(-1, plan["slab_lanes"])
    slab = jnp.broadcast_to(slab, (col_count, *slab.shape))
    early, slab = lax.optimization_barrier((early, slab))
    early = lax.all_to_all(early, "col", split_axis=0, concat_axis=0, tiled=True).reshape(-1, plan["lanes"])
    early, slab = lax.optimization_barrier((early, slab))
    slab = lax.all_to_all(slab, "col", split_axis=0, concat_axis=0, tiled=True)
    early = put_in_order(plan, place, points_map, early)
    return product(plan, place, points_map, slab, early, last)


def solution(mesh):
    in_specs = (P(), P(("row", "col"), None, None, None), P(), P(), P(("row", "col")), P())
    out_specs = P(None, "row", "col")
    return jax.shard_map(
        on_device, mesh=mesh, in_specs=in_specs, out_specs=out_specs, check_vma=False
    )
```

```python
import math

import jax
import jax.numpy as jnp
import numpy as np
from jax import lax
from jax.experimental import pallas as pl
from jax.experimental.pallas import tpu as pltpu
from jax.sharding import PartitionSpec as P

ROWS_DEV = 256
LANES = 128
VMEM_BYTES = 56 * 1024 * 1024
HALF = 64
KEEP = 40
ORIGIN = KEEP // 2
PARTS = 3


def round_up(value, step):
    return -(-value // step) * step


def length_counts(points):
    freq = np.arange(points) - points // 2
    square = freq * freq
    lengths = square[:, None, None] + square[None, :, None] + square[None, None, :]
    return np.cumsum(np.bincount(lengths.reshape(-1)))


def column_order(top):
    freq = np.arange(KEEP) - ORIGIN
    first, second = np.meshgrid(freq, freq, indexing="ij")
    length = (first * first + second * second).reshape(-1)
    order = np.argsort(length, kind="stable")
    order = order[length[order] <= top]
    return first.reshape(-1)[order], second.reshape(-1)[order], length[order]


class Columns:
    def __init__(self, top):
        self.windows = []
        offset = 0
        for begin in range(0, KEEP, 4):
            nearest = min(abs(index - ORIGIN) for index in range(begin, begin + 4))
            reach = math.isqrt(max(top - nearest * nearest, 0))
            low = (ORIGIN - reach) // 8 * 8
            high = min(round_up(ORIGIN + reach + 1, 8), KEEP)
            self.windows.append((low, high, offset))
            offset += 2 * (high - low)
        self.used = offset
        self.parity = round_up(offset, 2 * LANES)

    def place(self, index_2, index_3):
        low, high, offset = np.array(self.windows)[index_3 // 4].T
        return index_3 % 2 * self.parity + offset + index_3 // 2 % 2 * (high - low) + index_2 - low


class Bucket:
    def __init__(self, ranges, column_length):
        self.pieces = []
        self.edges = {}
        offset = 0
        for low, high in ranges:
            begin = offset
            for index in range(KEEP):
                freq = index - ORIGIN
                start = int(np.searchsorted(column_length, low - freq * freq, side="left"))
                stop = int(np.searchsorted(column_length, high - freq * freq, side="right"))
                if stop > start:
                    self.pieces.append((index, start, stop, offset))
                    offset += stop - start
            for length in range(low, high + 1):
                self.edges[length] = (begin, offset)
        self.size = offset

    def ids(self, column_2, column_3, points, width):
        out = np.full((width,), -1, np.int32)
        for index, start, stop, offset in self.pieces:
            k1 = (index - ORIGIN) % points
            k2 = column_2[start:stop] % points
            k3 = column_3[start:stop] % points
            out[offset : offset + stop - start] = (k1 * points + k2) * points + k3
        return out


def length_ranges(cumulative, first, step, count):
    shell = lambda rank: int(np.searchsorted(cumulative, rank, side="right"))
    ranges, low = [], shell(first)
    for part in range(1, count):
        before, after = shell(first + part * step - 1), shell(first + part * step)
        if before == after:
            if low < before:
                ranges.append((low, before - 1))
            if low <= before:
                ranges.append((before, before))
        elif low <= before:
            ranges.append((low, before))
        low = before + 1
    high = shell(first + count * step - 1)
    if low <= high:
        ranges.append((low, high))
    return ranges


def make_plan(points, total, blocks, slab, slab_blocks):
    cumulative = length_counts(points)
    shell = lambda rank: int(np.searchsorted(cumulative, rank, side="right"))
    width, slab_width = total // blocks, slab // slab_blocks
    step = width // PARTS
    column_2, column_3, column_length = column_order(shell(total - 1))
    buckets = [Bucket(length_ranges(cumulative, n * width, step, PARTS), column_length) for n in range(blocks)]
    slabs = [Bucket(length_ranges(cumulative, n * slab_width, slab_width, 1), column_length) for n in range(slab_blocks)]
    slab_top = shell(slab - 1)
    columns = Columns(shell(total - 1))
    place = columns.place(column_2 + ORIGIN, column_3 + ORIGIN)
    slab_columns = int(np.searchsorted(column_length, slab_top, side="right"))
    lanes = round_up(max(bucket.size for bucket in buckets), LANES)
    slab_lanes = round_up(max(bucket.size for bucket in slabs), LANES)
    windows = np.zeros((blocks, PARTS, 2), np.int64)
    for n, bucket in enumerate(buckets):
        for part in range(PARTS):
            rank = n * width + part * step
            windows[n, part, 0] = bucket.edges[shell(rank)][0] // LANES * LANES
            windows[n, part, 1] = round_up(bucket.edges[shell(rank + step - 1)][1], LANES)
    window = int((windows[..., 1] - windows[..., 0]).max())
    return dict(
        buckets=buckets,
        slabs=slabs,
        slab_columns=slab_columns,
        slab_tiles=sorted({int(value) for value in place[:slab_columns] // LANES}),
        columns=columns,
        lanes=lanes,
        slab_lanes=slab_lanes,
        window=window,
        starts=np.minimum(windows[..., 0], lanes - window).astype(np.int32),
        ids=np.stack([bucket.ids(column_2, column_3, points, lanes) for bucket in buckets]),
        slab_ids=np.stack([bucket.ids(column_2, column_3, points, slab_lanes) for bucket in slabs]),
        column_place=place.astype(np.int32),
    )


def dft_tables(points):
    n = np.arange(points)
    freq = np.arange(KEEP) - ORIGIN
    angle = (n[:, None] * freq[None, :] % points) * (2.0 * np.pi / points)
    cosine, sine = np.cos(angle), np.sin(angle)
    one = np.zeros((2, points, 2, HALF))
    one[0, :, 0, :KEEP] = cosine
    one[1, :, 0, :KEEP] = sine
    one[0, :, 1, :KEEP] = -sine
    one[1, :, 1, :KEEP] = cosine
    two = np.zeros((2, 2, points, 2, 2, HALF))
    for item in range(2):
        two[:, item, :, item] = one

    def parts(table):
        high = table.astype(jnp.bfloat16)
        return high, (table - high.astype(np.float64)).astype(jnp.bfloat16)

    high, low = parts(one[..., :KEEP].reshape(2 * points, 2 * KEEP).T)
    first = np.block([[high, high], [low, np.zeros_like(low)]])
    second = np.concatenate(parts(two.reshape(4 * points, 4 * HALF)), 0)
    halves = two[..., :KEEP].reshape(2, 2, points // 2, 2, 4 * KEEP).transpose(0, 1, 3, 2, 4)
    high, low = parts(halves.reshape(4 * points, 4 * KEEP).T)
    third = np.block([[high, high], [low, np.zeros_like(low)]])
    return [jnp.asarray(table) for table in (first, second, third)]


def split_parts(value):
    high = value.astype(jnp.bfloat16)
    low = (value - high.astype(jnp.float32)).astype(jnp.bfloat16)
    return high, low


def store_split(target, rows, blocks):
    for part, block in enumerate(blocks):
        high, low = split_parts(jnp.concatenate(block, 0))
        target[rows, part * LANES : (part + 1) * LANES] = high
        target[rows, (part + 2) * LANES : (part + 3) * LANES] = low


def doubled(stored):
    return jnp.concatenate([stored, stored[:, : stored.shape[1] // 2]], 1)


def contract_last(table, stored):
    both = lax.dot_general(table, stored, (((1,), (1,)), ((), ())), preferred_element_type=jnp.float32)
    rows = both.shape[0] // 2
    return both[:rows] + both[rows:]


def pack_pieces(pieces, width, source, rows, lane, out):
    for tile in range(width // LANES):
        left, right = tile * LANES, (tile + 1) * LANES
        value = jnp.zeros((rows, LANES), jnp.float32)
        for index, start, stop, offset in pieces:
            begin, end = max(left, offset), min(right, offset + stop - start)
            while begin < end:
                at = start + begin - offset
                block = source(index, at // LANES)
                shift = (begin - at) % LANES
                if shift:
                    block = pltpu.roll(block, shift, 1)
                value = block if begin == left else jnp.where(lane >= begin - left, block, value)
                begin = min(end, begin + LANES - at % LANES)
        out(tile, value)


def spectrum_kernel(plan, points, first_band, count, owner_ref, cond_energy_ref, val_energy_ref, val_ref, cond_ref, place_ref, first_ref,
                    second_ref, third_ref, send_ref, slab_ref, cond_a, cond_b, middle, turned, last, sorter, plain_rows, weighted_rows,
                    plain_sorted, weighted_sorted):
    band = pl.program_id(0)
    columns = plan["columns"]
    planes = 8
    pairs = planes // 2
    lane = lax.broadcasted_iota(jnp.int32, (1, LANES), 1)
    low_lanes = lane < HALF

    @pl.when(band == 0)
    def _():
        scale = 1.0 / float(points) ** 1.5
        sign = jnp.where(low_lanes, scale, -scale)

        @pl.loop(0, points // planes, unroll=4)
        def _(block):
            rows = pl.ds(pl.multiple_of(block * planes * points, planes * points), planes * points)
            wave = cond_ref[0, pl.ds(block * planes, planes)].reshape(planes * points, LANES).astype(jnp.float32)
            other = pltpu.roll(wave, HALF, 1)
            cond_a[rows, :] = jnp.where(low_lanes, wave, other) * sign
            cond_b[rows, :] = jnp.where(low_lanes, other, wave) * scale

        last[columns.used :, :] = jnp.zeros((columns.parity - columns.used, 4 * LANES), jnp.bfloat16)

    def first_axis(block):
        rows = pl.ds(pl.multiple_of(block * planes * points, planes * points), planes * points)
        wave = val_ref[0, pl.ds(block * planes, planes)].reshape(planes * points, LANES).astype(jnp.float32)
        density = wave * cond_a[rows, :] + pltpu.roll(wave, HALF, 1) * cond_b[rows, :]
        high, low = split_parts(density)
        field = contract_last(first_ref[...], jnp.concatenate([high, low], 1))
        for begin in range(0, pairs, 2):
            blocks = [
                [field[part * KEEP : (part + 1) * KEEP, pair * LANES : (pair + 1) * LANES] for pair in (begin, begin + 1)]
                for part in range(2)
            ]
            at = pl.ds(pl.multiple_of((block * pairs + begin) * KEEP, 2 * KEEP), 2 * KEEP)
            store_split(middle, at, blocks)

    def second_axis(block):
        rows = pl.ds(pl.multiple_of(block * 4 * KEEP, 4 * KEEP), 4 * KEEP)
        high = second_ref[: 2 * LANES]
        table = jnp.concatenate([high, high, second_ref[2 * LANES :]], 0)
        field = jnp.dot(doubled(middle[rows, :]), table, preferred_element_type=jnp.float32)
        for item in range(2):
            turned[item, rows, :] = field[:, item * LANES : (item + 1) * LANES]

    turns = points // 16 - 1
    piece = sorter.shape[0] // (count * turns)
    for part in range(2):
        first_axis(part)

    @pl.loop(1, turns + 1)
    def _(turn):
        begin = pl.multiple_of((band * turns + turn - 1) * piece, 16)
        at = lax.broadcasted_iota(jnp.int32, (piece, sorter.shape[1]), 0) + begin
        sorter[pl.ds(begin, piece), :] = jnp.where(at == place_ref[...], 1.0, 0.0).astype(jnp.bfloat16)
        for part in range(2):
            second_axis(2 * turn - 2 + part)
        for part in range(2):
            first_axis(2 * turn + part)

    for part in range(2):
        second_axis(2 * turns + part)

    for begin, (low, high, offset) in zip(range(0, KEEP, 4), columns.windows):
        both = []
        for pair in range(2):
            items = [
                turned[item, pl.ds(begin + 2 * pair + k3, points // 2, stride=KEEP), :]
                for k3 in range(2)
                for item in range(2)
            ]
            turn = jnp.concatenate(items, 0).T
            both.append((turn[low:high], turn[HALF + low : HALF + high]))
        store_split(last, slice(offset, offset + 2 * (high - low)), list(zip(*both)))

    bands = val_energy_ref.shape[0] * cond_energy_ref.shape[0]
    gap = cond_energy_ref[owner_ref[0]] - val_energy_ref[first_band + band]
    weight = -2.0 / (math.sqrt(bands) * jnp.full((1, LANES), gap, jnp.float32))
    slab = plan["slab_tiles"]
    band_rows = pl.ds(pl.multiple_of(band * 2 * KEEP, 2 * KEEP), 2 * KEEP)
    for begin in range(0, columns.parity, 2 * LANES):
        field = contract_last(third_ref[...], last[begin : begin + 2 * LANES, :])
        for odd in range(2):
            value = field[odd * 2 * KEEP : (odd + 1) * 2 * KEEP]
            first = odd * columns.parity + begin
            plain_rows[band_rows, first : first + 2 * LANES] = value.astype(jnp.bfloat16)
            for place, tile in enumerate(slab):
                at = tile * LANES - first
                if 0 <= at < 2 * LANES:
                    inside = (weight * value[:, at : at + LANES]).astype(jnp.bfloat16)
                    weighted_rows[band_rows, place * LANES : (place + 1) * LANES] = inside

    @pl.when(band == count - 1)
    def _():
        def sort_rows(rows, which, target):
            for tile in range(0, target.shape[0], 2):
                lanes = slice(tile * LANES, (tile + 2) * LANES)
                value = jnp.dot(rows, which(lanes), preferred_element_type=jnp.float32)
                target[tile] = value[:, :LANES]
                target[tile + 1] = value[:, LANES:]

        def slab_places(lanes):
            return jnp.concatenate([sorter[tile * LANES : (tile + 1) * LANES, lanes] for tile in slab], 0)

        sort_rows(plain_rows[...], lambda lanes: sorter[: 2 * columns.parity, lanes], plain_sorted)
        sort_rows(weighted_rows[...], slab_places, weighted_sorted)

        def plain_at(index, tile):
            return plain_sorted[tile, pl.ds(index, 2 * count, stride=KEEP), :]

        def weighted_at(index, tile):
            return weighted_sorted[tile, pl.ds(index, 2 * count, stride=KEEP), :]

        for block, bucket in enumerate(plan["buckets"]):

            def keep(tile, value):
                send_ref[block, :, tile * LANES : (tile + 1) * LANES] = value.astype(jnp.bfloat16)

            pack_pieces(bucket.pieces, plan["lanes"], plain_at, 2 * count, lane, keep)
        for block, bucket in enumerate(plan["slabs"]):

            def keep_slab(tile, value):
                slab_ref[block, :, tile * LANES : (tile + 1) * LANES] = value.astype(jnp.bfloat16)

            pack_pieces(bucket.pieces, plan["slab_lanes"], weighted_at, 2 * count, lane, keep_slab)


def spectra(plan, val_wave, cond_wave, energies, first_band, count):
    points = val_wave.shape[1]
    turns = points // 16 - 1
    parity = plan["columns"].parity
    depth = round_up(-(-2 * parity // (count * turns)), 16) * count * turns
    columns = round_up(plan["column_place"].shape[0], 256)
    slab_columns = round_up(plan["slab_columns"], 2 * LANES)
    slab_depth = len(plan["slab_tiles"]) * LANES
    place = np.full((1, columns), -1, np.int32)
    place[0, : plan["column_place"].shape[0]] = plan["column_place"]
    grid_rows = points * points
    tables = dft_tables(points)
    send_shape = (len(plan["buckets"]), 2 * count, plan["lanes"])
    slab_shape = (len(plan["slabs"]), 2 * count, plan["slab_lanes"])
    kernel = lambda *refs: spectrum_kernel(plan, points, first_band, count, *refs)
    return pl.pallas_call(
        kernel,
        grid=(count,),
        in_specs=[
            pl.BlockSpec(memory_space=pltpu.SMEM),
            pl.BlockSpec(memory_space=pltpu.SMEM),
            pl.BlockSpec(memory_space=pltpu.SMEM),
            pl.BlockSpec((1, points, points, 2 * points), lambda v: (first_band + v, 0, 0, 0)),
            pl.BlockSpec((1, points, points, 2 * points), lambda v: (0, 0, 0, 0)),
            pl.BlockSpec((1, columns), lambda v: (0, 0)),
            *[pl.BlockSpec(table.shape, lambda v: (0, 0)) for table in tables],
        ],
        out_specs=[pl.BlockSpec(send_shape, lambda v: (0, 0, 0)), pl.BlockSpec(slab_shape, lambda v: (0, 0, 0))],
        out_shape=[jax.ShapeDtypeStruct(send_shape, jnp.bfloat16), jax.ShapeDtypeStruct(slab_shape, jnp.bfloat16)],
        scratch_shapes=[
            pltpu.VMEM((grid_rows, LANES), jnp.float32),
            pltpu.VMEM((grid_rows, LANES), jnp.float32),
            pltpu.VMEM((points // 2 * KEEP, 4 * LANES), jnp.bfloat16),
            pltpu.VMEM((2, points // 2 * KEEP, LANES), jnp.float32),
            pltpu.VMEM((parity, 4 * LANES), jnp.bfloat16),
            pltpu.VMEM((depth, columns), jnp.bfloat16),
            pltpu.VMEM((2 * count * KEEP, 2 * parity), jnp.bfloat16),
            pltpu.VMEM((2 * count * KEEP, slab_depth), jnp.bfloat16),
            pltpu.VMEM((columns // LANES, 2 * count * KEEP, LANES), jnp.float32),
            pltpu.VMEM((slab_columns // LANES, 2 * count * KEEP, LANES), jnp.float32),
        ],
        compiler_params=pltpu.CompilerParams(vmem_limit_bytes=VMEM_BYTES, dimension_semantics=("arbitrary",)),
        cost_estimate=pl.CostEstimate(flops=1, bytes_accessed=1, transcendentals=0),
        name="spectra",
    )(*energies, val_wave, cond_wave, jnp.asarray(place), *tables)


def one_hot(ids, wanted):
    ids = jnp.broadcast_to(ids, (LANES, LANES)).T
    ids = jnp.concatenate([ids] * (wanted.shape[1] // LANES), 1)
    return jnp.where(ids == wanted, 1.0, 0.0).astype(jnp.bfloat16)


def make_left(row_count, slab_ref, ids_ref, wanted_ref, left):
    rows = wanted_ref.shape[1]
    col_count = slab_ref.shape[0]
    group = slab_ref.shape[1] // (2 * row_count)
    order = [(col, 2 * row) for col in range(col_count) for row in range(row_count)]
    order += [(col, 2 * row + 1) for row in range(row_count) for col in range(col_count)]
    slab = [slab_ref[col, at * group : (at + 1) * group, :].astype(jnp.float32) for col, at in order]
    wanted = [
        jnp.broadcast_to(wanted_ref[:, begin : begin + LANES], (LANES, LANES)).T for begin in range(0, rows, LANES)
    ]
    wanted = jnp.concatenate([jnp.concatenate(wanted, 0)] * (ids_ref.shape[2] // LANES), 1)
    choice = jnp.where(wanted == ids_ref[0], 1.0, 0.0).astype(jnp.bfloat16)
    chosen = lax.dot_general(
        choice,
        jnp.concatenate(slab, 0).astype(jnp.bfloat16),
        (((1,), (1,)), ((), ())),
        preferred_element_type=jnp.float32,
    )
    lane = lax.broadcasted_iota(jnp.int32, (1, LANES), 1)
    real_lanes = lane % 2 == 0
    for begin in range(0, chosen.shape[1], LANES):
        part = chosen[:, begin : begin + LANES]
        after = pltpu.roll(part, LANES - 1, 1)
        before = pltpu.roll(part, 1, 1)
        left[:rows, begin : begin + LANES] = part.astype(jnp.bfloat16)
        left[rows:, begin : begin + LANES] = jnp.where(real_lanes, after, -before).astype(jnp.bfloat16)


def order_kernel(place_ref, starts_ref, ids_ref, wanted_ref, panel_ref, out_ref, hot):
    start = pl.multiple_of(starts_ref[place_ref[0] * PARTS + pl.program_id(0)], LANES)
    wanted = wanted_ref[...]
    window = hot.shape[0]
    for begin in range(0, window, LANES):
        ids = ids_ref[0, :, pl.ds(pl.multiple_of(start + begin, LANES), LANES)]
        hot[begin : begin + LANES, :] = one_hot(ids, wanted)
    ordered = jnp.dot(panel_ref[:, pl.ds(start, window)], hot[...], preferred_element_type=jnp.float32)
    out_ref[...] = ordered.astype(jnp.bfloat16)


def put_in_order(plan, place, points_map, panel):
    columns = points_map.shape[1] // len(plan["buckets"])
    block = columns // PARTS
    ids = jnp.asarray(plan["ids"])[:, None]
    return pl.pallas_call(
        order_kernel,
        grid_spec=pltpu.PrefetchScalarGridSpec(
            num_scalar_prefetch=2,
            grid=(PARTS,),
            in_specs=[
                pl.BlockSpec((1, *ids.shape[1:]), lambda n, place, starts: (place[0], 0, 0)),
                pl.BlockSpec((1, block), lambda n, place, starts: (0, place[0] * PARTS + n)),
                pl.BlockSpec(panel.shape, lambda n, place, starts: (0, 0)),
            ],
            out_specs=pl.BlockSpec((panel.shape[0], block), lambda n, place, starts: (0, n)),
            scratch_shapes=[pltpu.VMEM((plan["window"], block), jnp.bfloat16)],
        ),
        out_shape=jax.ShapeDtypeStruct((panel.shape[0], columns), jnp.bfloat16),
        compiler_params=pltpu.CompilerParams(vmem_limit_bytes=VMEM_BYTES, dimension_semantics=("arbitrary",)),
        cost_estimate=pl.CostEstimate(flops=1, bytes_accessed=1, transcendentals=0),
        name="in_order",
    )(place, jnp.asarray(plan["starts"].reshape(-1)), ids, points_map, panel)


def product_kernel(row_count, place_ref, slab_ref, ids_ref, wanted_ref, early_ref, last_ref, out_ref, left):
    rows = out_ref.shape[1]

    @pl.when(pl.program_id(0) == 0)
    def _():
        make_left(row_count, slab_ref, ids_ref, wanted_ref, left)

    for begin in range(0, out_ref.shape[2], 2 * LANES):
        lanes = slice(begin, begin + 2 * LANES)
        right = jnp.concatenate([early_ref[:, lanes], last_ref[:, lanes]], 0)
        for part in range(2):
            half = left[part * rows : (part + 1) * rows, :]
            out_ref[part, :, lanes] = jnp.dot(half, right, preferred_element_type=jnp.float32)


def product(plan, place, points_map, slab, early, last):
    pairs, columns = slab.shape[0] * slab.shape[1], early.shape[1]
    block = 6 * LANES
    ids = jnp.asarray(plan["slab_ids"])[:, None]
    return pl.pallas_call(
        lambda *refs: product_kernel(ids.shape[0], *refs),
        grid_spec=pltpu.PrefetchScalarGridSpec(
            num_scalar_prefetch=1,
            grid=(pl.cdiv(columns, block),),
            in_specs=[
                pl.BlockSpec(slab.shape, lambda n, place: (0, 0, 0)),
                pl.BlockSpec((1, *ids.shape[1:]), lambda n, place: (place[1], 0, 0)),
                pl.BlockSpec((1, ROWS_DEV), lambda n, place: (0, place[1])),
                pl.BlockSpec((early.shape[0], block), lambda n, place: (0, n)),
                pl.BlockSpec((last.shape[0], block), lambda n, place: (0, n)),
            ],
            out_specs=pl.BlockSpec((2, ROWS_DEV, block), lambda n, place: (0, 0, n)),
            scratch_shapes=[pltpu.VMEM((2 * ROWS_DEV, pairs), jnp.bfloat16)],
        ),
        out_shape=jax.ShapeDtypeStruct((2, ROWS_DEV, columns), jnp.float32),
        compiler_params=pltpu.CompilerParams(vmem_limit_bytes=VMEM_BYTES, dimension_semantics=("arbitrary",)),
        cost_estimate=pl.CostEstimate(flops=1, bytes_accessed=1, transcendentals=0),
        name="product",
    )(place, slab, ids, points_map, early, last)


def on_device(val_wave, cond_wave, val_energy, cond_energy, band_owner, grid_map):
    bands, points = val_wave.shape[0], val_wave.shape[1]
    row_count = lax.axis_size("row")
    col_count = lax.axis_size("col")
    col, row = lax.axis_index("col"), lax.axis_index("row")
    plan = make_plan(points, grid_map.shape[0], col_count, ROWS_DEV * row_count, row_count)
    place = jnp.stack([col, row]).astype(jnp.int32)
    points_map = grid_map[None]
    chunk = bands // 2
    energies = (band_owner, cond_energy, val_energy)
    slabs = []
    for part in range(2):
        send, slab = spectra(plan, val_wave, cond_wave, energies, part * chunk, chunk)
        slabs.append(slab)
        if part == 0:
            send, cond_wave = lax.optimization_barrier((send, cond_wave))
            early = lax.all_gather(send, "row", axis=1)
        else:
            mine = lax.all_to_all(send, "col", split_axis=0, concat_axis=0, tiled=True).reshape(-1, plan["lanes"])
            mine = put_in_order(plan, place, points_map, mine)
            last = lax.all_gather(mine, "row", axis=0, tiled=True)
    slab, _ = lax.optimization_barrier((jnp.concatenate(slabs, 1), mine))
    slab = lax.all_to_all(slab, "row", split_axis=0, concat_axis=0, tiled=True).reshape(-1, plan["slab_lanes"])
    early, slab = lax.optimization_barrier((early, slab))
    early = lax.all_to_all(early, "col", split_axis=0, concat_axis=0, tiled=True).reshape(-1, plan["lanes"])
    slab = jnp.broadcast_to(slab, (col_count, *slab.shape))
    early, slab = lax.optimization_barrier((early, slab))
    slab = lax.all_to_all(slab, "col", split_axis=0, concat_axis=0, tiled=True)
    early = put_in_order(plan, place, points_map, early)
    return product(plan, place, points_map, slab, early, last)


def solution(mesh):
    in_specs = (P(), P(("row", "col"), None, None, None), P(), P(), P(("row", "col")), P())
    out_specs = P(None, "row", "col")
    return jax.shard_map(
        on_device, mesh=mesh, in_specs=in_specs, out_specs=out_specs, check_vma=False
    )
```

```python
import math

import jax
import jax.numpy as jnp
import numpy as np
from jax import lax
from jax.experimental import pallas as pl
from jax.experimental.pallas import tpu as pltpu
from jax.sharding import PartitionSpec as P

ROWS_DEV = 256
LANES = 128
VMEM_BYTES = 56 * 1024 * 1024
HALF = 64
KEEP = 40
ORIGIN = KEEP // 2
PARTS = 3


def round_up(value, step):
    return -(-value // step) * step


def length_counts(points):
    freq = np.arange(points) - points // 2
    square = freq * freq
    lengths = square[:, None, None] + square[None, :, None] + square[None, None, :]
    return np.cumsum(np.bincount(lengths.reshape(-1)))


def column_order(top):
    freq = np.arange(KEEP) - ORIGIN
    first, second = np.meshgrid(freq, freq, indexing="ij")
    length = (first * first + second * second).reshape(-1)
    order = np.argsort(length, kind="stable")
    order = order[length[order] <= top]
    return first.reshape(-1)[order], second.reshape(-1)[order], length[order]


class Columns:
    def __init__(self, top):
        self.windows = []
        offset = 0
        for begin in range(0, KEEP, 4):
            nearest = min(abs(index - ORIGIN) for index in range(begin, begin + 4))
            reach = math.isqrt(max(top - nearest * nearest, 0))
            low = (ORIGIN - reach) // 8 * 8
            high = min(round_up(ORIGIN + reach + 1, 8), KEEP)
            self.windows.append((low, high, offset))
            offset += 2 * (high - low)
        self.used = offset
        self.parity = round_up(offset, 2 * LANES)

    def place(self, index_2, index_3):
        low, high, offset = np.array(self.windows)[index_3 // 4].T
        return index_3 % 2 * self.parity + offset + index_3 // 2 % 2 * (high - low) + index_2 - low


class Bucket:
    def __init__(self, ranges, column_length):
        self.pieces = []
        self.edges = {}
        offset = 0
        for low, high in ranges:
            begin = offset
            for index in range(KEEP):
                freq = index - ORIGIN
                start = int(np.searchsorted(column_length, low - freq * freq, side="left"))
                stop = int(np.searchsorted(column_length, high - freq * freq, side="right"))
                if stop > start:
                    self.pieces.append((index, start, stop, offset))
                    offset += stop - start
            for length in range(low, high + 1):
                self.edges[length] = (begin, offset)
        self.size = offset

    def ids(self, column_2, column_3, points, width):
        out = np.full((width,), -1, np.int32)
        for index, start, stop, offset in self.pieces:
            k1 = (index - ORIGIN) % points
            k2 = column_2[start:stop] % points
            k3 = column_3[start:stop] % points
            out[offset : offset + stop - start] = (k1 * points + k2) * points + k3
        return out


def length_ranges(cumulative, first, step, count):
    shell = lambda rank: int(np.searchsorted(cumulative, rank, side="right"))
    ranges, low = [], shell(first)
    for part in range(1, count):
        before, after = shell(first + part * step - 1), shell(first + part * step)
        if before == after:
            if low < before:
                ranges.append((low, before - 1))
            if low <= before:
                ranges.append((before, before))
        elif low <= before:
            ranges.append((low, before))
        low = before + 1
    high = shell(first + count * step - 1)
    if low <= high:
        ranges.append((low, high))
    return ranges


def make_plan(points, total, blocks, slab, slab_blocks):
    cumulative = length_counts(points)
    shell = lambda rank: int(np.searchsorted(cumulative, rank, side="right"))
    width, slab_width = total // blocks, slab // slab_blocks
    step = width // PARTS
    column_2, column_3, column_length = column_order(shell(total - 1))
    buckets = [Bucket(length_ranges(cumulative, n * width, step, PARTS), column_length) for n in range(blocks)]
    slabs = [Bucket(length_ranges(cumulative, n * slab_width, slab_width, 1), column_length) for n in range(slab_blocks)]
    slab_top = shell(slab - 1)
    columns = Columns(shell(total - 1))
    place = columns.place(column_2 + ORIGIN, column_3 + ORIGIN)
    slab_columns = int(np.searchsorted(column_length, slab_top, side="right"))
    lanes = round_up(max(bucket.size for bucket in buckets), LANES)
    slab_lanes = round_up(max(bucket.size for bucket in slabs), LANES)
    windows = np.zeros((blocks, PARTS, 2), np.int64)
    for n, bucket in enumerate(buckets):
        for part in range(PARTS):
            rank = n * width + part * step
            windows[n, part, 0] = bucket.edges[shell(rank)][0] // LANES * LANES
            windows[n, part, 1] = round_up(bucket.edges[shell(rank + step - 1)][1], LANES)
    window = int((windows[..., 1] - windows[..., 0]).max())
    return dict(
        buckets=buckets,
        slabs=slabs,
        slab_columns=slab_columns,
        slab_tiles=sorted({int(value) for value in place[:slab_columns] // LANES}),
        columns=columns,
        lanes=lanes,
        slab_lanes=slab_lanes,
        window=window,
        starts=np.minimum(windows[..., 0], lanes - window).astype(np.int32),
        ids=np.stack([bucket.ids(column_2, column_3, points, lanes) for bucket in buckets]),
        slab_ids=np.stack([bucket.ids(column_2, column_3, points, slab_lanes) for bucket in slabs]),
        column_place=place.astype(np.int32),
    )


def dft_tables(points):
    n = np.arange(points)
    freq = np.arange(KEEP) - ORIGIN
    angle = (n[:, None] * freq[None, :] % points) * (2.0 * np.pi / points)
    cosine, sine = np.cos(angle), np.sin(angle)
    one = np.zeros((2, points, 2, HALF))
    one[0, :, 0, :KEEP] = cosine
    one[1, :, 0, :KEEP] = sine
    one[0, :, 1, :KEEP] = -sine
    one[1, :, 1, :KEEP] = cosine
    two = np.zeros((2, 2, points, 2, 2, HALF))
    for item in range(2):
        two[:, item, :, item] = one

    def parts(table):
        high = table.astype(jnp.bfloat16)
        return high, (table - high.astype(np.float64)).astype(jnp.bfloat16)

    high, low = parts(one[..., :KEEP].reshape(2 * points, 2 * KEEP).T)
    first = np.block([[high, high], [low, np.zeros_like(low)]])
    second = np.concatenate(parts(two.reshape(4 * points, 4 * HALF)), 0)
    halves = two[..., :KEEP].reshape(2, 2, points // 2, 2, 4 * KEEP).transpose(0, 1, 3, 2, 4)
    high, low = parts(halves.reshape(4 * points, 4 * KEEP).T)
    third = np.block([[high, high], [low, np.zeros_like(low)]])
    return [jnp.asarray(table) for table in (first, second, third)]


def split_parts(value):
    high = value.astype(jnp.bfloat16)
    low = (value - high.astype(jnp.float32)).astype(jnp.bfloat16)
    return high, low


def store_split(target, rows, blocks):
    for part, block in enumerate(blocks):
        high, low = split_parts(jnp.concatenate(block, 0))
        target[rows, part * LANES : (part + 1) * LANES] = high
        target[rows, (part + 2) * LANES : (part + 3) * LANES] = low


def doubled(stored):
    return jnp.concatenate([stored, stored[:, : stored.shape[1] // 2]], 1)


def contract_last(table, stored):
    both = lax.dot_general(table, stored, (((1,), (1,)), ((), ())), preferred_element_type=jnp.float32)
    rows = both.shape[0] // 2
    return both[:rows] + both[rows:]


def pack_pieces(pieces, width, source, rows, lane, out):
    for tile in range(width // LANES):
        left, right = tile * LANES, (tile + 1) * LANES
        value = jnp.zeros((rows, LANES), jnp.float32)
        for index, start, stop, offset in pieces:
            begin, end = max(left, offset), min(right, offset + stop - start)
            while begin < end:
                at = start + begin - offset
                block = source(index, at // LANES)
                shift = (begin - at) % LANES
                if shift:
                    block = pltpu.roll(block, shift, 1)
                value = block if begin == left else jnp.where(lane >= begin - left, block, value)
                begin = min(end, begin + LANES - at % LANES)
        out(tile, value)


def spectrum_kernel(plan, points, first_band, count, owner_ref, cond_energy_ref, val_energy_ref, val_ref, cond_ref, place_ref, first_ref,
                    second_ref, third_ref, send_ref, slab_ref, cond_a, cond_b, middle, turned, last, sorter, plain_rows, weighted_rows,
                    plain_sorted, weighted_sorted):
    band = pl.program_id(0)
    columns = plan["columns"]
    planes = 8
    pairs = planes // 2
    lane = lax.broadcasted_iota(jnp.int32, (1, LANES), 1)
    low_lanes = lane < HALF

    @pl.when(band == 0)
    def _():
        scale = 1.0 / float(points) ** 1.5
        sign = jnp.where(low_lanes, scale, -scale)

        @pl.loop(0, points // planes, unroll=4)
        def _(block):
            rows = pl.ds(pl.multiple_of(block * planes * points, planes * points), planes * points)
            wave = cond_ref[0, pl.ds(block * planes, planes)].reshape(planes * points, LANES).astype(jnp.float32)
            other = pltpu.roll(wave, HALF, 1)
            cond_a[rows, :] = jnp.where(low_lanes, wave, other) * sign
            cond_b[rows, :] = jnp.where(low_lanes, other, wave) * scale

        last[columns.used :, :] = jnp.zeros((columns.parity - columns.used, 4 * LANES), jnp.bfloat16)

    def first_axis(block):
        stored = []
        for part in range(pairs):
            at = block * planes + 2 * part
            rows = pl.ds(pl.multiple_of(at * points, 2 * points), 2 * points)
            wave = val_ref[0, pl.ds(at, 2)].reshape(2 * points, LANES).astype(jnp.float32)
            density = wave * cond_a[rows, :] + pltpu.roll(wave, HALF, 1) * cond_b[rows, :]
            stored.append(jnp.concatenate(split_parts(density), 1))
        field = contract_last(first_ref[...], jnp.concatenate(stored, 0))
        for begin in range(0, pairs, 2):
            blocks = [
                [field[part * KEEP : (part + 1) * KEEP, pair * LANES : (pair + 1) * LANES] for pair in (begin, begin + 1)]
                for part in range(2)
            ]
            at = pl.ds(pl.multiple_of((block * pairs + begin) * KEEP, 2 * KEEP), 2 * KEEP)
            store_split(middle, at, blocks)

    def second_axis(block):
        rows = pl.ds(pl.multiple_of(block * 4 * KEEP, 4 * KEEP), 4 * KEEP)
        high = second_ref[: 2 * LANES]
        table = jnp.concatenate([high, high, second_ref[2 * LANES :]], 0)
        field = jnp.dot(doubled(middle[rows, :]), table, preferred_element_type=jnp.float32)
        for item in range(2):
            turned[item, rows, :] = field[:, item * LANES : (item + 1) * LANES]

    turns = points // 16 - 1
    piece = sorter.shape[0] // (count * turns)
    for part in range(2):
        first_axis(part)

    @pl.loop(1, turns + 1)
    def _(turn):
        begin = pl.multiple_of((band * turns + turn - 1) * piece, 16)
        at = lax.broadcasted_iota(jnp.int32, (piece, sorter.shape[1]), 0) + begin
        sorter[pl.ds(begin, piece), :] = jnp.where(at == place_ref[...], 1.0, 0.0).astype(jnp.bfloat16)
        for part in range(2):
            second_axis(2 * turn - 2 + part)
        for part in range(2):
            first_axis(2 * turn + part)

    for part in range(2):
        second_axis(2 * turns + part)

    for begin, (low, high, offset) in zip(range(0, KEEP, 4), columns.windows):
        both = []
        for pair in range(2):
            items = [
                turned[item, pl.ds(begin + 2 * pair + k3, points // 2, stride=KEEP), :]
                for k3 in range(2)
                for item in range(2)
            ]
            turn = jnp.concatenate(items, 0).T
            both.append((turn[low:high], turn[HALF + low : HALF + high]))
        store_split(last, slice(offset, offset + 2 * (high - low)), list(zip(*both)))

    bands = val_energy_ref.shape[0] * cond_energy_ref.shape[0]
    gap = cond_energy_ref[owner_ref[0]] - val_energy_ref[first_band + band]
    weight = -2.0 / (math.sqrt(bands) * jnp.full((1, LANES), gap, jnp.float32))
    slab = plan["slab_tiles"]
    band_rows = pl.ds(pl.multiple_of(band * 2 * KEEP, 2 * KEEP), 2 * KEEP)
    for begin in range(0, columns.parity, 2 * LANES):
        field = contract_last(third_ref[...], last[begin : begin + 2 * LANES, :])
        for odd in range(2):
            value = field[odd * 2 * KEEP : (odd + 1) * 2 * KEEP]
            first = odd * columns.parity + begin
            plain_rows[band_rows, first : first + 2 * LANES] = value.astype(jnp.bfloat16)
            for place, tile in enumerate(slab):
                at = tile * LANES - first
                if 0 <= at < 2 * LANES:
                    inside = (weight * value[:, at : at + LANES]).astype(jnp.bfloat16)
                    weighted_rows[band_rows, place * LANES : (place + 1) * LANES] = inside

    @pl.when(band == count - 1)
    def _():
        def sort_rows(rows, which, target):
            for tile in range(0, target.shape[0], 2):
                lanes = slice(tile * LANES, (tile + 2) * LANES)
                value = jnp.dot(rows, which(lanes), preferred_element_type=jnp.float32)
                target[tile] = value[:, :LANES]
                target[tile + 1] = value[:, LANES:]

        def slab_places(lanes):
            return jnp.concatenate([sorter[tile * LANES : (tile + 1) * LANES, lanes] for tile in slab], 0)

        sort_rows(plain_rows[...], lambda lanes: sorter[: 2 * columns.parity, lanes], plain_sorted)
        sort_rows(weighted_rows[...], slab_places, weighted_sorted)

        def plain_at(index, tile):
            return plain_sorted[tile, pl.ds(index, 2 * count, stride=KEEP), :]

        def weighted_at(index, tile):
            return weighted_sorted[tile, pl.ds(index, 2 * count, stride=KEEP), :]

        for block, bucket in enumerate(plan["buckets"]):

            def keep(tile, value):
                send_ref[block, :, tile * LANES : (tile + 1) * LANES] = value.astype(jnp.bfloat16)

            pack_pieces(bucket.pieces, plan["lanes"], plain_at, 2 * count, lane, keep)
        for block, bucket in enumerate(plan["slabs"]):

            def keep_slab(tile, value):
                slab_ref[block, :, tile * LANES : (tile + 1) * LANES] = value.astype(jnp.bfloat16)

            pack_pieces(bucket.pieces, plan["slab_lanes"], weighted_at, 2 * count, lane, keep_slab)


def spectra(plan, val_wave, cond_wave, energies, first_band, count):
    points = val_wave.shape[1]
    turns = points // 16 - 1
    parity = plan["columns"].parity
    depth = round_up(-(-2 * parity // (count * turns)), 16) * count * turns
    columns = round_up(plan["column_place"].shape[0], 256)
    slab_columns = round_up(plan["slab_columns"], 2 * LANES)
    slab_depth = len(plan["slab_tiles"]) * LANES
    place = np.full((1, columns), -1, np.int32)
    place[0, : plan["column_place"].shape[0]] = plan["column_place"]
    grid_rows = points * points
    tables = dft_tables(points)
    send_shape = (len(plan["buckets"]), 2 * count, plan["lanes"])
    slab_shape = (len(plan["slabs"]), 2 * count, plan["slab_lanes"])
    kernel = lambda *refs: spectrum_kernel(plan, points, first_band, count, *refs)
    return pl.pallas_call(
        kernel,
        grid=(count,),
        in_specs=[
            pl.BlockSpec(memory_space=pltpu.SMEM),
            pl.BlockSpec(memory_space=pltpu.SMEM),
            pl.BlockSpec(memory_space=pltpu.SMEM),
            pl.BlockSpec((1, points, points, 2 * points), lambda v: (first_band + v, 0, 0, 0)),
            pl.BlockSpec((1, points, points, 2 * points), lambda v: (0, 0, 0, 0)),
            pl.BlockSpec((1, columns), lambda v: (0, 0)),
            *[pl.BlockSpec(table.shape, lambda v: (0, 0)) for table in tables],
        ],
        out_specs=[pl.BlockSpec(send_shape, lambda v: (0, 0, 0)), pl.BlockSpec(slab_shape, lambda v: (0, 0, 0))],
        out_shape=[jax.ShapeDtypeStruct(send_shape, jnp.bfloat16), jax.ShapeDtypeStruct(slab_shape, jnp.bfloat16)],
        scratch_shapes=[
            pltpu.VMEM((grid_rows, LANES), jnp.float32),
            pltpu.VMEM((grid_rows, LANES), jnp.float32),
            pltpu.VMEM((points // 2 * KEEP, 4 * LANES), jnp.bfloat16),
            pltpu.VMEM((2, points // 2 * KEEP, LANES), jnp.float32),
            pltpu.VMEM((parity, 4 * LANES), jnp.bfloat16),
            pltpu.VMEM((depth, columns), jnp.bfloat16),
            pltpu.VMEM((2 * count * KEEP, 2 * parity), jnp.bfloat16),
            pltpu.VMEM((2 * count * KEEP, slab_depth), jnp.bfloat16),
            pltpu.VMEM((columns // LANES, 2 * count * KEEP, LANES), jnp.float32),
            pltpu.VMEM((slab_columns // LANES, 2 * count * KEEP, LANES), jnp.float32),
        ],
        compiler_params=pltpu.CompilerParams(vmem_limit_bytes=VMEM_BYTES, dimension_semantics=("arbitrary",)),
        cost_estimate=pl.CostEstimate(flops=1, bytes_accessed=1, transcendentals=0),
        name="spectra",
    )(*energies, val_wave, cond_wave, jnp.asarray(place), *tables)


def one_hot(ids, wanted):
    ids = jnp.broadcast_to(ids, (LANES, LANES)).T
    ids = jnp.concatenate([ids] * (wanted.shape[1] // LANES), 1)
    return jnp.where(ids == wanted, 1.0, 0.0).astype(jnp.bfloat16)


def make_left(row_count, slab_ref, ids_ref, wanted_ref, left):
    rows = wanted_ref.shape[1]
    col_count = slab_ref.shape[0]
    group = slab_ref.shape[1] // (2 * row_count)
    order = [(col, 2 * row) for col in range(col_count) for row in range(row_count)]
    order += [(col, 2 * row + 1) for row in range(row_count) for col in range(col_count)]
    slab = [slab_ref[col, at * group : (at + 1) * group, :].astype(jnp.float32) for col, at in order]
    wanted = [
        jnp.broadcast_to(wanted_ref[:, begin : begin + LANES], (LANES, LANES)).T for begin in range(0, rows, LANES)
    ]
    wanted = jnp.concatenate([jnp.concatenate(wanted, 0)] * (ids_ref.shape[2] // LANES), 1)
    choice = jnp.where(wanted == ids_ref[0], 1.0, 0.0).astype(jnp.bfloat16)
    chosen = lax.dot_general(
        choice,
        jnp.concatenate(slab, 0).astype(jnp.bfloat16),
        (((1,), (1,)), ((), ())),
        preferred_element_type=jnp.float32,
    )
    lane = lax.broadcasted_iota(jnp.int32, (1, LANES), 1)
    real_lanes = lane % 2 == 0
    for begin in range(0, chosen.shape[1], LANES):
        part = chosen[:, begin : begin + LANES]
        after = pltpu.roll(part, LANES - 1, 1)
        before = pltpu.roll(part, 1, 1)
        left[:rows, begin : begin + LANES] = part.astype(jnp.bfloat16)
        left[rows:, begin : begin + LANES] = jnp.where(real_lanes, after, -before).astype(jnp.bfloat16)


def order_kernel(place_ref, starts_ref, ids_ref, wanted_ref, panel_ref, out_ref, hot):
    start = pl.multiple_of(starts_ref[place_ref[0] * PARTS + pl.program_id(0)], LANES)
    wanted = wanted_ref[...]
    window = hot.shape[0]
    for begin in range(0, window, LANES):
        ids = ids_ref[0, :, pl.ds(pl.multiple_of(start + begin, LANES), LANES)]
        hot[begin : begin + LANES, :] = one_hot(ids, wanted)
    ordered = jnp.dot(panel_ref[:, pl.ds(start, window)], hot[...], preferred_element_type=jnp.float32)
    out_ref[...] = ordered.astype(jnp.bfloat16)


def put_in_order(plan, place, points_map, panel):
    columns = points_map.shape[1] // len(plan["buckets"])
    block = columns // PARTS
    ids = jnp.asarray(plan["ids"])[:, None]
    return pl.pallas_call(
        order_kernel,
        grid_spec=pltpu.PrefetchScalarGridSpec(
            num_scalar_prefetch=2,
            grid=(PARTS,),
            in_specs=[
                pl.BlockSpec((1, *ids.shape[1:]), lambda n, place, starts: (place[0], 0, 0)),
                pl.BlockSpec((1, block), lambda n, place, starts: (0, place[0] * PARTS + n)),
                pl.BlockSpec(panel.shape, lambda n, place, starts: (0, 0)),
            ],
            out_specs=pl.BlockSpec((panel.shape[0], block), lambda n, place, starts: (0, n)),
            scratch_shapes=[pltpu.VMEM((plan["window"], block), jnp.bfloat16)],
        ),
        out_shape=jax.ShapeDtypeStruct((panel.shape[0], columns), jnp.bfloat16),
        compiler_params=pltpu.CompilerParams(vmem_limit_bytes=VMEM_BYTES, dimension_semantics=("arbitrary",)),
        cost_estimate=pl.CostEstimate(flops=1, bytes_accessed=1, transcendentals=0),
        name="in_order",
    )(place, jnp.asarray(plan["starts"].reshape(-1)), ids, points_map, panel)


def product_kernel(row_count, place_ref, slab_ref, ids_ref, wanted_ref, early_ref, last_ref, out_ref, left):
    rows = out_ref.shape[1]

    @pl.when(pl.program_id(0) == 0)
    def _():
        make_left(row_count, slab_ref, ids_ref, wanted_ref, left)

    for begin in range(0, out_ref.shape[2], 2 * LANES):
        lanes = slice(begin, begin + 2 * LANES)
        right = jnp.concatenate([early_ref[:, lanes], last_ref[:, lanes]], 0)
        for part in range(2):
            half = left[part * rows : (part + 1) * rows, :]
            out_ref[part, :, lanes] = jnp.dot(half, right, preferred_element_type=jnp.float32)


def product(plan, place, points_map, slab, early, last):
    pairs, columns = slab.shape[0] * slab.shape[1], early.shape[1]
    block = 6 * LANES
    ids = jnp.asarray(plan["slab_ids"])[:, None]
    return pl.pallas_call(
        lambda *refs: product_kernel(ids.shape[0], *refs),
        grid_spec=pltpu.PrefetchScalarGridSpec(
            num_scalar_prefetch=1,
            grid=(pl.cdiv(columns, block),),
            in_specs=[
                pl.BlockSpec(slab.shape, lambda n, place: (0, 0, 0)),
                pl.BlockSpec((1, *ids.shape[1:]), lambda n, place: (place[1], 0, 0)),
                pl.BlockSpec((1, ROWS_DEV), lambda n, place: (0, place[1])),
                pl.BlockSpec((early.shape[0], block), lambda n, place: (0, n)),
                pl.BlockSpec((last.shape[0], block), lambda n, place: (0, n)),
            ],
            out_specs=pl.BlockSpec((2, ROWS_DEV, block), lambda n, place: (0, 0, n)),
            scratch_shapes=[pltpu.VMEM((2 * ROWS_DEV, pairs), jnp.bfloat16)],
        ),
        out_shape=jax.ShapeDtypeStruct((2, ROWS_DEV, columns), jnp.float32),
        compiler_params=pltpu.CompilerParams(vmem_limit_bytes=VMEM_BYTES, dimension_semantics=("arbitrary",)),
        cost_estimate=pl.CostEstimate(flops=1, bytes_accessed=1, transcendentals=0),
        name="product",
    )(place, slab, ids, points_map, early, last)


def on_device(val_wave, cond_wave, val_energy, cond_energy, band_owner, grid_map):
    bands, points = val_wave.shape[0], val_wave.shape[1]
    row_count = lax.axis_size("row")
    col_count = lax.axis_size("col")
    col, row = lax.axis_index("col"), lax.axis_index("row")
    plan = make_plan(points, grid_map.shape[0], col_count, ROWS_DEV * row_count, row_count)
    place = jnp.stack([col, row]).astype(jnp.int32)
    points_map = grid_map[None]
    chunk = bands // 2
    energies = (band_owner, cond_energy, val_energy)
    slabs = []
    for part in range(2):
        send, slab = spectra(plan, val_wave, cond_wave, energies, part * chunk, chunk)
        slabs.append(slab)
        if part == 0:
            send, cond_wave = lax.optimization_barrier((send, cond_wave))
            early = lax.all_gather(send, "row", axis=1)
        else:
            mine = lax.all_to_all(send, "col", split_axis=0, concat_axis=0, tiled=True).reshape(-1, plan["lanes"])
            mine = put_in_order(plan, place, points_map, mine)
            last = lax.all_gather(mine, "row", axis=0, tiled=True)
    slab, _ = lax.optimization_barrier((jnp.concatenate(slabs, 1), mine))
    slab = lax.all_to_all(slab, "row", split_axis=0, concat_axis=0, tiled=True).reshape(-1, plan["slab_lanes"])
    early, slab = lax.optimization_barrier((early, slab))
    early = lax.all_to_all(early, "col", split_axis=0, concat_axis=0, tiled=True).reshape(-1, plan["lanes"])
    slab = jnp.broadcast_to(slab, (col_count, *slab.shape))
    early, slab = lax.optimization_barrier((early, slab))
    slab = lax.all_to_all(slab, "col", split_axis=0, concat_axis=0, tiled=True)
    early = put_in_order(plan, place, points_map, early)
    return product(plan, place, points_map, slab, early, last)


def solution(mesh):
    in_specs = (P(), P(("row", "col"), None, None, None), P(), P(), P(("row", "col")), P())
    out_specs = P(None, "row", "col")
    return jax.shard_map(
        on_device, mesh=mesh, in_specs=in_specs, out_specs=out_specs, check_vma=False
    )
```
